32 devices in a mesh: dp: 16 (over z, y, x), tensor: 2 (over core).
Axes of the slice: x: 2, y: 2, z: 4, core: 2. Of those that a mesh axis runs over, the one named last changes fastest.
Arguments:
- tokens: bfloat16 [4096, 2048], P(('dp', 'tensor')), may hold values from -6 to 6
- segments: int32 [16, 256], P('dp'), may hold values from 0 to 3, as said below
- weights: bfloat16 [256, 2048, 128], P(('dp', 'tensor'))
- momentum: float32 [256, 2048, 128], P(('dp', 'tensor'))
- gains: float32 [2, 2048], replicated, may hold values from 0.5 to 1.5
- gain_first: float32 [2, 2048], replicated
- gain_second: float32 [2, 2048], replicated
- cotangent: bfloat16 [4096, 2048], P(('dp', 'tensor')), may hold values from -6 to 6
Outputs:
- output: bfloat16 [4096, 2048], P(('dp', 'tensor'))
- input_grad: float32 [4096, 2048], P(('dp', 'tensor'))
- weight_grads: float32 [256, 2048, 128], P(('dp', 'tensor'))
- new_momentum: float32 [256, 2048, 128], P(('dp', 'tensor'))
- new_weights: float32 [256, 2048, 128], P(('dp', 'tensor'))
- new_gain_first: float32 [2, 2048], replicated
- new_gain_second: float32 [2, 2048], replicated
- new_gains: float32 [2, 2048], replicated
The draws below stay inside these ranges and needn't reach their ends.
Inputs may be any that keep to these rules, and one draw needn't show every extreme that they name: `segments`: in each row the document numbers start at 0, never fall and rise 4 - 1 times, each time by one; they never change between positions 64 and 192.
All inputs are finite; a program needn't handle non-finite values.
Results may differ from the reference program's by a relative error of at most 0.017.
Values may be sent and summed in bfloat16 or wider, within the bound.
No kernel may reach another device: no remote copies, remote signals or barrier semaphores. Data moves between devices by JAX's collectives and lax.ppermute only.
A program may use at most 384 MiB of HBM per device.

```python
import math
import jax
import jax.numpy as jnp
from jax import lax

D = 2048
FF = 8192
HD = 64
BW = 128
TOK = 256
DOCS = 4
NS_ITERS = 5
STEP = 10
HEADS = 32
NB = 256
TOKENS = 4096


def block_scales():
    position = jnp.arange(NB)
    attn_count = D // BW
    inner_scale = 1.0 / math.sqrt(D)
    outer_scale = 4.0 / math.sqrt(D)
    down_scale = 1.0 / math.sqrt(FF)
    scales = jnp.where(position < 3 * attn_count, inner_scale, jnp.where(position < 4 * attn_count, outer_scale, jnp.where(position < NB - FF // BW, inner_scale, down_scale)))
    return scales.astype(jnp.float32)


def draw_weights(key, part):
    key = jax.random.fold_in(key, 11)
    noise = jnp.clip(jax.random.normal(key, (NB, D, BW), jnp.float32), -6.0, 6.0)
    return (noise * block_scales()[:, None, None]).astype(jnp.bfloat16)


def draw_momentum(key, part):
    key = jax.random.fold_in(key, 23)
    noise = jnp.clip(jax.random.normal(key, (NB, D, BW), jnp.float32), -6.0, 6.0)
    return (noise * (0.3 * math.sqrt(TOKENS))).astype(jnp.float32)


def draw_gain_first(key, part):
    key = jax.random.fold_in(key, 37)
    noise = jnp.clip(jax.random.normal(key, (2, D), jnp.float32), -6.0, 6.0)
    return (noise * (0.1 / 0.9 * math.sqrt(TOKENS))).astype(jnp.float32)


def draw_gain_second(key, part):
    key = jax.random.fold_in(key, 41)
    factor = jax.random.uniform(key, (2, D), jnp.float32, 1.0, 4.0)
    return (factor * (0.05 / 0.95 * TOKENS)).astype(jnp.float32)


def draw_segments(key, part):
    key = jax.random.fold_in(key, 5)
    rows_total = TOKENS // TOK
    quarter = TOK // 4
    early_places = jnp.arange(1, quarter, dtype=jnp.int32)
    late_places = jnp.arange(TOK - quarter + 1, TOK, dtype=jnp.int32)
    places = jnp.concatenate([early_places, late_places])
    position = jnp.arange(TOK, dtype=jnp.int32)

    def one_row(row_key):
        chosen = jax.random.permutation(row_key, places)[:DOCS - 1]
        flags = jnp.sum((position[:, None] == chosen[None, :]).astype(jnp.int32), axis=1)
        return jnp.cumsum(flags).astype(jnp.int32)
    return jax.vmap(one_row)(jax.random.split(key, rows_total)).astype(jnp.int32)


def level_of(rng, extent, pieces, smallest, top_value):
    level = 1.0
    for axis_at, shards_of in pieces:
        heights = jax.random.uniform(jax.random.fold_in(jax.random.fold_in(rng, 6), axis_at), (shards_of,), jnp.float32, smallest / len(pieces), top_value / len(pieces))
        level = level * jnp.repeat(jnp.exp(heights), extent[axis_at] // shards_of).reshape((-1,) + (1,) * (len(extent) - 1 - axis_at))
    return level


def gaussian(own_key, dims, spread, bound, pieces=(), held_as=jnp.bfloat16):
    entries = jax.random.normal(own_key, dims, jnp.float32) * spread
    if len(pieces) > 0:
        entries = level_of(own_key, dims, pieces, -0.22, 0.18) * entries
    return jnp.clip(entries, min=-bound, max=bound).astype(held_as)


def setup_inputs(seed: int = 0) -> dict:
    keys = jax.random.split(jax.random.key(seed), 9)
    return {
        "tokens": gaussian(keys[0], (TOKENS, D), 1.0, 6.0, ((0, 32),)),
        "segments": draw_segments(jax.random.fold_in(keys[8], 71), 0),
        "weights": draw_weights(jax.random.fold_in(keys[8], 71), 0),
        "momentum": draw_momentum(jax.random.fold_in(keys[8], 71), 0),
        "gains": jnp.clip(1.0 + 0.1 * jax.random.normal(keys[4], (2, D), jnp.float32), 0.5, 1.5),
        "gain_first": draw_gain_first(jax.random.fold_in(keys[8], 71), 0),
        "gain_second": draw_gain_second(jax.random.fold_in(keys[8], 71), 0),
        "cotangent": gaussian(keys[7], (TOKENS, D), 1.0, 6.0, ((0, 32),)),
    }


@jax.custom_vjp
def low(v):
    return lax.optimization_barrier(v.astype(jnp.bfloat16)).astype(jnp.float32)

@jax.custom_vjp
def low_back(v):
    return v

def low_keep(v):
    return (low(v), None)

def low_pass(kept, grad):
    return (grad,)

def back_keep(v):
    return (v, None)

def back_low(kept, grad):
    return (low(grad),)
low.defvjp(low_keep, low_pass)
low_back.defvjp(back_keep, back_low)
HIGHEST = lax.Precision.HIGHEST
ROPE_BASE = 130000.0
NORM_EPS = 1e-05
NEG_LARGE = -1e+30
MOMENTUM_DECAY = 0.95
MUON_RATE = 0.25
COEFF_A = 3.4445
COEFF_B = -4.775
COEFF_C = 2.0315
BETA_FIRST = 0.9
BETA_SECOND = 0.95
ADAM_RATE = 1.0
ADAM_EPS = 1e-08

def rms_norm(values, gain):
    return values * lax.rsqrt(lax.optimization_barrier(jnp.mean(values * values, axis=-1, keepdims=True)) + NORM_EPS) * gain

def rope_tables(length):
    position = jnp.arange(length).astype(jnp.float32)
    exponent = jnp.arange(HD // 2).astype(jnp.float32) * (2.0 / HD)
    inverse = jnp.exp(-exponent * math.log(ROPE_BASE))
    angle = position[:, None] * inverse[None, :]
    return (jnp.cos(angle)[:, None, :], jnp.sin(angle)[:, None, :])

def rotate(values, cosine, sine):
    half = values.shape[-1] // 2
    first = values[..., :half]
    second = values[..., half:]
    return jnp.concatenate([first * cosine - second * sine, second * cosine + first * sine], axis=-1)

def attend(parts):
    queries, key_rot, value_rows, segment_row = parts
    scores = jnp.einsum('thd,shd->hts', queries, key_rot, precision=HIGHEST)
    scores = low_back(scores * (1.0 / math.sqrt(HD)))
    length = segment_row.shape[0]
    place = jnp.arange(length)
    allowed = (place[None, :] <= place[:, None]) & (segment_row[None, :] == segment_row[:, None])
    scores = jnp.where(allowed[None], scores, NEG_LARGE)
    probs = jax.nn.softmax(scores, axis=-1)
    context = jnp.einsum('hts,shd->thd', low(probs), value_rows, precision=HIGHEST)
    return low_back(low(context))

def block_forward(rows_value, matrices, gain_pair, segment_rows):
    w_query, w_key, w_value, w_out_t, w_gate, w_up, w_down_t = matrices
    group = rows_value.shape[0]
    length = rows_value.shape[1]
    flat = rows_value.reshape(group * length, D)
    normed_one = low(rms_norm(flat, gain_pair[0]))
    query_lin = low_back(jnp.dot(normed_one, w_query, precision=HIGHEST))
    key_lin = low_back(jnp.dot(normed_one, w_key, precision=HIGHEST))
    value_rows = low(low_back(jnp.dot(normed_one, w_value, precision=HIGHEST)))
    cosine, sine = rope_tables(length)
    head_shape = (group, length, HEADS, HD)
    query_rot = low(rotate(query_lin.reshape(head_shape), cosine, sine))
    key_rot = low(rotate(key_lin.reshape(head_shape), cosine, sine))
    context = lax.map(jax.checkpoint(attend), (query_rot, key_rot, value_rows.reshape(head_shape), segment_rows))
    mixed = low_back(jnp.dot(context.reshape(group * length, D), w_out_t.T, precision=HIGHEST))
    middle = flat + mixed
    normed_two = low(rms_norm(middle, gain_pair[1]))
    gate_act = low_back(jnp.dot(normed_two, w_gate, precision=HIGHEST))
    up_act = low_back(jnp.dot(normed_two, w_up, precision=HIGHEST))
    hidden = low(jax.nn.silu(gate_act) * up_act)
    output = middle + low_back(jnp.dot(hidden, w_down_t.T, precision=HIGHEST))
    return output.reshape(rows_value.shape)

def orthogonalize(block):
    current = block / (jnp.sqrt(jnp.sum(block * block)) + 1e-07)
    for turn_index in range(NS_ITERS):
        gram = jnp.einsum('dc,de->ce', current, current, precision=HIGHEST)
        mixer = COEFF_B * gram + COEFF_C * jnp.dot(gram, gram, precision=HIGHEST)
        current = COEFF_A * current + jnp.dot(current, mixer, precision=HIGHEST)
    return current

def reference(tokens, segments, weights, momentum, gains, gain_first, gain_second, cotangent):
    blocks = weights.astype(jnp.float32)
    attn_count = D // BW
    mlp_count = FF // BW
    counts = [attn_count] * 4 + [mlp_count] * 3
    starts = [0]
    for count_of in counts:
        starts.append(starts[-1] + count_of)
    matrices = tuple((blocks[starts[position]:starts[position + 1]].transpose(1, 0, 2).reshape(D, counts[position] * BW) for position in range(7)))
    rows_total = TOKENS // TOK
    group = min(rows_total, max(1, 4096 // TOK))
    batches = rows_total // group
    rows_all = tokens.astype(jnp.float32).reshape(batches, group, TOK, D)
    cot_all = cotangent.astype(jnp.float32).reshape(batches, group, TOK, D)
    seg_all = segments.reshape(batches, group, TOK)

    def one_group(carry, inputs):
        grad_mats, grad_gains = carry
        rows_in, segment_rows, cot_rows = inputs

        def forward(rows_value, mats, gain_pair):
            return block_forward(rows_value, mats, gain_pair, segment_rows)
        result, pullback = jax.vjp(forward, rows_in, matrices, gains)
        d_rows, d_mats, d_gains = pullback(cot_rows)
        grad_mats = jax.tree.map(lambda total_part, added_part: total_part + added_part, grad_mats, d_mats)
        return ((grad_mats, grad_gains + d_gains), (result, d_rows))
    zero_mats = tuple((jnp.zeros_like(matrix_one) for matrix_one in matrices))
    carry_out, outputs = lax.scan(one_group, (zero_mats, jnp.zeros_like(gains)), (rows_all, seg_all, cot_all))
    grad_mats, gain_grads = carry_out
    results, d_rows = outputs
    output = results.reshape(TOKENS, D).astype(jnp.bfloat16)
    input_grad = d_rows.reshape(TOKENS, D)
    weight_grads = jnp.concatenate([grad_mats[position].reshape(D, counts[position], BW).transpose(1, 0, 2) for position in range(7)], axis=0)
    new_momentum = MOMENTUM_DECAY * momentum + weight_grads
    ortho = lax.map(orthogonalize, new_momentum)
    new_weights = blocks - MUON_RATE * math.sqrt(D / BW) * ortho
    new_gain_first = BETA_FIRST * gain_first + (1.0 - BETA_FIRST) * gain_grads
    new_gain_second = BETA_SECOND * gain_second + (1.0 - BETA_SECOND) * gain_grads * gain_grads
    first_hat = new_gain_first / (1.0 - BETA_FIRST ** STEP)
    second_hat = new_gain_second / (1.0 - BETA_SECOND ** STEP)
    new_gains = gains - ADAM_RATE * first_hat / (jnp.sqrt(second_hat) + ADAM_EPS)
    return (output, input_grad, weight_grads, new_momentum, new_weights, new_gain_first, new_gain_second, new_gains)
```

```python
import math

import jax
import jax.numpy as jnp
import numpy as np
from jax import lax
from jax.sharding import Mesh
from jax.sharding import PartitionSpec as P

D = 2048
FF = 8192
HD = 64
BW = 128
NS_ITERS = 5
STEP = 10

HIGHEST = lax.Precision.HIGHEST
ROPE_BASE = 130000.0
NORM_EPS = 1e-05
NEG_LARGE = -1e30
MOMENTUM_DECAY = 0.95
MUON_RATE = 0.25
COEFF_A = 3.4445
COEFF_B = -4.775
COEFF_C = 2.0315
BETA_FIRST = 0.9
BETA_SECOND = 0.95
ADAM_RATE = 1.0
ADAM_EPS = 1e-08

F32 = jnp.float32
BF16 = jnp.bfloat16
PLANE = ("m", "r", "tensor")


def rms_norm(values, gain):
    return values * lax.rsqrt(jnp.mean(values * values, axis=-1, keepdims=True) + NORM_EPS) * gain


def rms_norm_back(values, gain, grad):
    scale = lax.rsqrt(jnp.mean(values * values, axis=-1, keepdims=True) + NORM_EPS)
    scaled = gain * grad
    inner = jnp.mean(scaled * values, axis=-1, keepdims=True)
    gain_grad = jnp.sum(grad * values * scale, axis=0)
    return scale * scaled - values * (scale * scale * scale * inner), gain_grad


def rope_tables(length):
    position = jnp.arange(length).astype(F32)
    exponent = jnp.arange(HD // 2).astype(F32) * (2.0 / HD)
    inverse = jnp.exp(-exponent * math.log(ROPE_BASE))
    angle = position[:, None] * inverse[None, :]
    return (jnp.cos(angle)[:, None, :], jnp.sin(angle)[:, None, :])


def rotate(values, cosine, sine):
    half = values.shape[-1] // 2
    first = values[..., :half]
    second = values[..., half:]
    return jnp.concatenate(
        [first * cosine - second * sine, second * cosine + first * sine], axis=-1
    )


def unrotate(values, cosine, sine):
    return rotate(values, cosine, -sine)


def gather_rows(rows):
    return lax.all_gather(rows, PLANE, axis=0, tiled=True)


def scatter_rows(partial_sum):
    return lax.psum_scatter(
        partial_sum.astype(BF16), PLANE, scatter_dimension=0, tiled=True
    ).astype(F32)


def dot(a, b):
    return jnp.dot(a, b, preferred_element_type=F32)


def dot_t(a, b):
    return lax.dot_general(a, b, (((1,), (1,)), ((), ())), preferred_element_type=F32)


def t_dot(a, b):
    return lax.dot_general(a, b, (((0,), (0,)), ((), ())), preferred_element_type=F32)


def orthogonalize(blocks):
    norm = jnp.sqrt(jnp.sum(blocks * blocks, axis=(1, 2), keepdims=True))
    current = blocks / (norm + 1e-07)
    gram = jnp.einsum("bdc,bde->bce", current, current, precision=HIGHEST)
    eye = jnp.eye(BW, dtype=F32)
    total = None
    for turn in range(NS_ITERS):
        square = jnp.einsum("bij,bjk->bik", gram, gram, precision=HIGHEST)
        mixer = COEFF_A * eye + COEFF_B * gram + COEFF_C * square
        if total is None:
            total = mixer
        else:
            total = jnp.einsum("bij,bjk->bik", total, mixer, precision=HIGHEST)
        if turn < NS_ITERS - 1:
            half = jnp.einsum("bij,bjk->bik", mixer, gram, precision=HIGHEST)
            gram = jnp.einsum("bij,bjk->bik", half, mixer, precision=HIGHEST)
    return jnp.einsum("bdc,bce->bde", current, total, precision=HIGHEST)


def blocks_to_matrix(blocks):
    return blocks.transpose(1, 0, 2).reshape(D, -1)


def matrix_to_blocks(matrix):
    return matrix.reshape(D, -1, BW).transpose(1, 0, 2)


def local(tokens, segments, weights, momentum, gains, gain_first, gain_second, cotangent):
    gathered = lax.all_gather(weights, "z", axis=0, tiled=False)
    attn_own = blocks_to_matrix(gathered[0])
    width = attn_own.shape[1] // 4
    attn_parts = attn_own.reshape(D, 4, width).transpose(1, 0, 2)
    attn_mats = lax.all_to_all(attn_parts, "m", 0, 0, tiled=True)
    w_query, w_key, w_value, w_out = (attn_mats[i] for i in range(4))
    w_gate, w_up, w_down = (blocks_to_matrix(gathered[i]) for i in (1, 2, 3))
    segment_rows = lax.all_gather(segments, ("m", "r"), axis=0, tiled=True)
    group, length = segment_rows.shape
    heads = width // HD
    head_shape = (group, length, heads, HD)

    rows_in = tokens.astype(F32)
    seen_one = gather_rows(rms_norm(rows_in, gains[0]).astype(BF16))
    d_mlp = gather_rows(cotangent)
    cosine, sine = rope_tables(length)
    query = rotate(dot(seen_one, w_query).reshape(head_shape), cosine, sine).astype(BF16)
    key = rotate(dot(seen_one, w_key).reshape(head_shape), cosine, sine).astype(BF16)
    value = dot(seen_one, w_value).astype(BF16).reshape(head_shape)
    score_scale = 1.0 / math.sqrt(HD)
    place = jnp.arange(length)
    allowed = (place[None, None, :] <= place[None, :, None]) & (
        segment_rows[:, None, :] == segment_rows[:, :, None]
    )
    scores = jnp.einsum("gthd,gshd->ghts", query, key, preferred_element_type=F32) * score_scale
    scores = jnp.where(allowed[:, None], scores, NEG_LARGE)
    probs = jax.nn.softmax(scores, axis=-1)
    probs_low = probs.astype(BF16)
    context = jnp.einsum("ghts,gshd->gthd", probs_low, value, preferred_element_type=F32)
    context = context.astype(BF16).reshape(group * length, width)
    middle = rows_in + scatter_rows(dot_t(context, w_out))
    seen_two = gather_rows(rms_norm(middle, gains[1]).astype(BF16))
    gate_act = dot(seen_two, w_gate)
    up_act = dot(seen_two, w_up)
    sigmoid_gate = jax.nn.sigmoid(gate_act)
    hidden = (gate_act * sigmoid_gate * up_act).astype(BF16)
    output = (middle + scatter_rows(dot_t(hidden, w_down))).astype(BF16)
    d_output = cotangent.astype(F32)
    d_hidden = dot(d_mlp, w_down)
    d_gate = (d_hidden * up_act * sigmoid_gate * (1.0 + gate_act * (1.0 - sigmoid_gate))).astype(BF16)
    d_up = (d_hidden * (gate_act * sigmoid_gate)).astype(BF16)
    d_normed_two = scatter_rows(dot_t(d_gate, w_gate) + dot_t(d_up, w_up))
    d_middle_norm, d_gain_two = rms_norm_back(middle, gains[1], d_normed_two)
    d_middle = d_output + d_middle_norm
    d_attn = gather_rows(d_middle.astype(BF16))
    d_context = dot(d_attn, w_out).astype(BF16).reshape(head_shape)
    d_value = jnp.einsum("ghts,gthd->gshd", probs_low, d_context, preferred_element_type=F32)
    d_probs = jnp.einsum("gthd,gshd->ghts", d_context, value, preferred_element_type=F32)
    inner = jnp.sum(probs * d_probs, axis=-1, keepdims=True)
    d_scores = (probs * (d_probs - inner)).astype(BF16)
    d_query = jnp.einsum("ghts,gshd->gthd", d_scores, key, preferred_element_type=F32) * score_scale
    d_key = jnp.einsum("ghts,gthd->gshd", d_scores, query, preferred_element_type=F32) * score_scale
    flat = (group * length, width)
    d_query = unrotate(d_query, cosine, sine).astype(BF16).reshape(flat)
    d_key = unrotate(d_key, cosine, sine).astype(BF16).reshape(flat)
    d_value = d_value.astype(BF16).reshape(flat)
    d_normed_one = scatter_rows(dot_t(d_query, w_query) + dot_t(d_key, w_key) + dot_t(d_value, w_value))
    d_rows_norm, d_gain_one = rms_norm_back(rows_in, gains[0], d_normed_one)
    input_grad = d_middle + d_rows_norm

    attn_grads = jnp.stack(
        [
            t_dot(seen_one, d_query),
            t_dot(seen_one, d_key),
            t_dot(seen_one, d_value),
            t_dot(d_attn, context),
        ]
    ).astype(BF16)
    attn_grads = lax.all_to_all(attn_grads, "m", 0, 0, tiled=True)
    attn_grads = attn_grads.transpose(1, 0, 2).reshape(D, 4 * width)
    stacked = jnp.stack(
        [
            matrix_to_blocks(attn_grads),
            matrix_to_blocks(t_dot(seen_two, d_gate).astype(BF16)),
            matrix_to_blocks(t_dot(seen_two, d_up).astype(BF16)),
            matrix_to_blocks(t_dot(d_mlp, hidden).astype(BF16)),
        ]
    )
    weight_grads = lax.psum_scatter(stacked, "z", scatter_dimension=0, tiled=False).astype(F32)
    gain_grads = lax.psum(jnp.stack([d_gain_one, d_gain_two]), ("z",) + PLANE)
    new_momentum = MOMENTUM_DECAY * momentum + weight_grads
    ortho = orthogonalize(new_momentum)
    new_weights = weights.astype(F32) - MUON_RATE * math.sqrt(D / BW) * ortho
    new_gain_first = BETA_FIRST * gain_first + (1.0 - BETA_FIRST) * gain_grads
    new_gain_second = BETA_SECOND * gain_second + (1.0 - BETA_SECOND) * gain_grads * gain_grads
    first_hat = new_gain_first / (1.0 - BETA_FIRST**STEP)
    second_hat = new_gain_second / (1.0 - BETA_SECOND**STEP)
    new_gains = gains - ADAM_RATE * first_hat / (jnp.sqrt(second_hat) + ADAM_EPS)
    return (
        output,
        input_grad,
        weight_grads,
        new_momentum,
        new_weights,
        new_gain_first,
        new_gain_second,
        new_gains,
    )


def solution(mesh):
    count = mesh.shape["dp"]
    fine = Mesh(
        np.asarray(mesh.devices).reshape(4, 4, count // 16, mesh.shape["tensor"]),
        ("z",) + PLANE,
    )
    every = ("z",) + PLANE
    in_specs = (
        P(every, None),
        P(every[:3], None),
        P(every, None, None),
        P(every, None, None),
        P(),
        P(),
        P(),
        P(every, None),
    )
    out_specs = (
        P(every, None),
        P(every, None),
        P(every, None, None),
        P(every, None, None),
        P(every, None, None),
        P(),
        P(),
        P(),
    )
    return jax.shard_map(local, mesh=fine, in_specs=in_specs, out_specs=out_specs, check_vma=False)
```

```python
import math

import jax
import jax.numpy as jnp
import numpy as np
from jax import lax
from jax.sharding import Mesh
from jax.sharding import PartitionSpec as P

D = 2048
FF = 8192
HD = 64
BW = 128
NS_ITERS = 5
STEP = 10

HIGHEST = lax.Precision.HIGHEST
ROPE_BASE = 130000.0
NORM_EPS = 1e-05
NEG_LARGE = -1e30
MOMENTUM_DECAY = 0.95
MUON_RATE = 0.25
COEFF_A = 3.4445
COEFF_B = -4.775
COEFF_C = 2.0315
BETA_FIRST = 0.9
BETA_SECOND = 0.95
ADAM_RATE = 1.0
ADAM_EPS = 1e-08

F32 = jnp.float32
BF16 = jnp.bfloat16
PLANE = ("m", "r", "tensor")
SWAP = [(0, 1), (1, 0)]


def rms_norm(values, gain):
    return values * lax.rsqrt(jnp.mean(values * values, axis=-1, keepdims=True) + NORM_EPS) * gain


def rms_norm_back(values, gain, grad):
    scale = lax.rsqrt(jnp.mean(values * values, axis=-1, keepdims=True) + NORM_EPS)
    scaled = gain * grad
    inner = jnp.mean(scaled * values, axis=-1, keepdims=True)
    gain_grad = jnp.sum(grad * values * scale, axis=0)
    return scale * scaled - values * (scale * scale * scale * inner), gain_grad


def rope_tables(place):
    position = place.astype(F32)
    exponent = jnp.arange(HD // 2).astype(F32) * (2.0 / HD)
    inverse = jnp.exp(-exponent * math.log(ROPE_BASE))
    angle = position[:, None] * inverse[None, :]
    return (jnp.cos(angle)[:, None, :], jnp.sin(angle)[:, None, :])


def rotate(values, cosine, sine):
    half = values.shape[-1] // 2
    first = values[..., :half]
    second = values[..., half:]
    return jnp.concatenate(
        [first * cosine - second * sine, second * cosine + first * sine], axis=-1
    )


def unrotate(values, cosine, sine):
    return rotate(values, cosine, -sine)


def dot(a, b):
    return jnp.dot(a, b, preferred_element_type=F32)


def dot_t(a, b):
    return lax.dot_general(a, b, (((1,), (1,)), ((), ())), preferred_element_type=F32)


def t_dot(a, b):
    return lax.dot_general(a, b, (((0,), (0,)), ((), ())), preferred_element_type=F32)


def orthogonalize(blocks):
    norm = jnp.sqrt(jnp.sum(blocks * blocks, axis=(1, 2), keepdims=True))
    current = blocks / (norm + 1e-07)
    gram = jnp.einsum("bdc,bde->bce", current, current, precision=HIGHEST)
    eye = jnp.eye(BW, dtype=F32)
    total = None
    for turn in range(NS_ITERS):
        square = jnp.einsum("bij,bjk->bik", gram, gram, precision=HIGHEST)
        mixer = COEFF_A * eye + COEFF_B * gram + COEFF_C * square
        if total is None:
            total = mixer
        else:
            total = jnp.einsum("bij,bjk->bik", total, mixer, precision=HIGHEST)
        if turn < NS_ITERS - 1:
            half = jnp.einsum("bij,bjk->bik", mixer, gram, precision=HIGHEST)
            gram = jnp.einsum("bij,bjk->bik", half, mixer, precision=HIGHEST)
    return jnp.einsum("bdc,bce->bde", current, total, precision=HIGHEST)


def mirror(step):
    return [(place, place ^ step) for place in range(4)]


def gather_rows(rows, row_major):
    if lax.axis_size("r") > 1:
        rows = lax.all_gather(rows, "r", axis=0, tiled=False)
    else:
        rows = rows[None]
    mine = [rows] + [lax.ppermute(rows, "m", mirror(step)) for step in (1, 2, 3)]
    other = [lax.ppermute(part, "tensor", SWAP) for part in mine]
    if row_major:
        pieces = [jnp.stack([a, b], axis=1) for a, b in zip(mine, other)]
    else:
        pieces = mine + other
    return jnp.concatenate([piece.reshape(-1, D) for piece in pieces], axis=0)


def scatter_rows(own_half, other_half):
    total = own_half + lax.ppermute(other_half, "tensor", SWAP).astype(F32)
    low = total.astype(BF16)
    arrived = [lax.ppermute(low[step], "m", mirror(step)) for step in (1, 2, 3)]
    result = total[0] + arrived[0].astype(F32) + arrived[1].astype(F32) + arrived[2].astype(F32)
    if lax.axis_size("r") > 1:
        return lax.psum_scatter(result.astype(BF16), "r", scatter_dimension=0, tiled=False).astype(F32)
    return result[0]


def after(value, *others):
    return lax.optimization_barrier((value,) + others)[0]


def up_one(value, pairs):
    return lax.ppermute(value, "z", [(a, a + 1) for a in pairs])


def down_one(value, pairs):
    return lax.ppermute(value, "z", [(a, a - 1) for a in pairs])


def local(tokens, segments, weights, momentum, gains, gain_first, gain_second, cotangent):
    plane = lax.axis_index("z")
    core = lax.axis_index("tensor")
    block_count = weights.shape[0]
    chunk_count = block_count // 2
    width = block_count * BW // 4
    own = weights.reshape(chunk_count, 2, D, BW).transpose(0, 2, 1, 3).reshape(chunk_count, D, 2 * BW)
    if width == 2 * BW:
        attn_parts = own
    else:
        attn_parts = own.transpose(1, 0, 2).reshape(D, 4, width).transpose(1, 0, 2)
    attn_first = lax.all_to_all(attn_parts, "m", 0, 0, tiled=True)

    def choose(*cases):
        return lax.select_n(plane, *cases)

    attn_mats = []
    gate_token = None
    for index in range(4):
        hop_one = up_one(attn_first[index], [0])
        hop_two = up_one(hop_one, [1])
        hop_three = up_one(hop_two, [2])
        attn_mats.append(choose(attn_first[index], hop_one, hop_two, hop_three))
        gate_token = hop_two
    w_query, w_key, w_value, w_out = attn_mats

    mlp_mats = []
    hold_down = None
    hold_up = None
    for index in range(chunk_count):
        mine = own[index]
        mine_down = mine if hold_down is None else after(mine, hold_down)
        mine_up = mine if index == 0 else after(mine, gate_token, *(() if hold_up is None else (hold_up,)))
        down_a = down_one(mine_down, [1, 2, 3])
        down_b = down_one(down_a, [1, 2])
        down_c = down_one(down_b, [1])
        up_a = up_one(mine_up, [1, 2])
        up_b = up_one(up_a, [2])
        hold_down = down_b
        if index > 0:
            hold_up = up_a
        mlp_mats.append(
            (
                choose(down_a, mine, up_a, up_b),
                choose(down_b, down_a, mine, up_a),
                choose(down_c, down_b, down_a, mine),
            )
        )

    ring = lax.axis_size("r")
    segment_own = lax.all_gather(segments, "r", axis=0, tiled=True) if ring > 1 else segments
    segment_parts = [segment_own] + [lax.ppermute(segment_own, "m", mirror(step)) for step in (1, 2, 3)]
    segment_rows = jnp.concatenate(segment_parts, axis=0)
    group, length = segment_rows.shape
    half = length // 2
    part_shape = (4, ring, half, D)
    place = jnp.arange(length)
    place = jnp.where(core == 0, place, (place + half) % length)
    segment_rows = jnp.where(core == 0, segment_rows, jnp.roll(segment_rows, half, axis=1))
    heads = width // HD
    head_shape = (group, length, heads, HD)

    rows_in = tokens.astype(F32)
    seen_one = gather_rows(rms_norm(rows_in, gains[0]).astype(BF16), True)
    d_mlp = gather_rows(cotangent, False)
    cosine, sine = rope_tables(place)
    query = rotate(dot(seen_one, w_query).reshape(head_shape), cosine, sine).astype(BF16)
    key = rotate(dot(seen_one, w_key).reshape(head_shape), cosine, sine).astype(BF16)
    value = dot(seen_one, w_value).astype(BF16).reshape(head_shape)
    score_scale = 1.0 / math.sqrt(HD)
    allowed = (place[None, None, :] <= place[None, :, None]) & (
        segment_rows[:, None, :] == segment_rows[:, :, None]
    )
    scores = jnp.einsum("gthd,gshd->ghts", query, key, preferred_element_type=F32) * score_scale
    scores = jnp.where(allowed[:, None], scores, NEG_LARGE)
    probs = jax.nn.softmax(scores, axis=-1)
    probs_low = probs.astype(BF16)
    context = jnp.einsum("ghts,gshd->gthd", probs_low, value, preferred_element_type=F32)
    context = context.astype(BF16).reshape(group * length, width)

    def halves(rows):
        parts = rows.reshape(group, 2, half, rows.shape[-1])
        return (parts[:, 0].reshape(group * half, -1), parts[:, 1].reshape(group * half, -1))

    context_own, context_other = halves(context)
    mixed = scatter_rows(
        dot_t(context_own, w_out).reshape(part_shape),
        dot_t(context_other, w_out).astype(BF16).reshape(part_shape),
    )
    middle = rows_in + mixed
    seen_two = gather_rows(rms_norm(middle, gains[1]).astype(BF16), False)

    count = group * half
    output_own = output_other = d_two_own = d_two_other = None
    mlp_grads = []
    for index in range(chunk_count):
        w_gate, w_up, w_down = mlp_mats[index]
        gate_act = dot(seen_two, w_gate)
        up_act = dot(seen_two, w_up)
        d_hidden = dot(d_mlp, w_down)
        sigmoid_gate = jax.nn.sigmoid(gate_act)
        silu = gate_act * sigmoid_gate
        hidden = (silu * up_act).astype(BF16)
        d_gate = (d_hidden * up_act * sigmoid_gate * (1.0 + gate_act * (1.0 - sigmoid_gate))).astype(BF16)
        d_up = (d_hidden * silu).astype(BF16)
        mlp_grads.append((t_dot(seen_two, d_gate), t_dot(seen_two, d_up), t_dot(d_mlp, hidden)))
        parts = (
            dot_t(hidden[:count], w_down),
            dot_t(hidden[count:], w_down),
            dot_t(d_gate[:count], w_gate) + dot_t(d_up[:count], w_up),
            dot_t(d_gate[count:], w_gate) + dot_t(d_up[count:], w_up),
        )
        if index == 0:
            output_own, output_other, d_two_own, d_two_other = parts
        else:
            output_own += parts[0]
            output_other += parts[1]
            d_two_own += parts[2]
            d_two_other += parts[3]
    d_normed_two = scatter_rows(d_two_own.reshape(part_shape), d_two_other.astype(BF16).reshape(part_shape))

    mlp_totals = []
    for index in range(chunk_count):
        grads = [grad.astype(BF16) for grad in mlp_grads[index]]
        first, second, third = grads
        hop_up = up_one(third, [0])
        hop_up = up_one((choose(second, third, third, third).astype(F32) + hop_up.astype(F32)).astype(BF16), [0, 1])
        hop_up = up_one((choose(first, second, third, third).astype(F32) + hop_up.astype(F32)).astype(BF16), [0, 1, 2])
        hop_down = down_one(first, [3])
        hop_down = down_one((choose(first, first, first, second).astype(F32) + hop_down.astype(F32)).astype(BF16), [2, 3])
        mlp_totals.append(choose(first, first, second, third).astype(F32) + hop_up.astype(F32) + hop_down.astype(F32))

    d_output = cotangent.astype(F32)
    d_middle_norm, d_gain_two = rms_norm_back(middle, gains[1], d_normed_two)
    d_middle = d_output + d_middle_norm
    d_attn = gather_rows(d_middle.astype(BF16), True)
    d_context = dot(d_attn, w_out).astype(BF16).reshape(head_shape)
    d_value = jnp.einsum("ghts,gthd->gshd", probs_low, d_context, preferred_element_type=F32)
    d_probs = jnp.einsum("gthd,gshd->ghts", d_context, value, preferred_element_type=F32)
    inner = jnp.sum(probs * d_probs, axis=-1, keepdims=True)
    d_scores = (probs * (d_probs - inner)).astype(BF16)
    d_query = jnp.einsum("ghts,gshd->gthd", d_scores, key, preferred_element_type=F32) * score_scale
    d_key = jnp.einsum("ghts,gthd->gshd", d_scores, query, preferred_element_type=F32) * score_scale
    flat = (group * length, width)
    d_query = unrotate(d_query, cosine, sine).astype(BF16).reshape(flat)
    d_key = unrotate(d_key, cosine, sine).astype(BF16).reshape(flat)
    d_value = d_value.astype(BF16).reshape(flat)

    attn_totals = [None] * 4
    for index, (rows, columns) in (
        (3, (d_attn, context)),
        (2, (seen_one, d_value)),
        (0, (seen_one, d_query)),
        (1, (seen_one, d_key)),
    ):
        grad = t_dot(rows, columns)
        hop = down_one(grad.astype(BF16), [3])
        hop = down_one((grad + hop.astype(F32)).astype(BF16), [2])
        hop = down_one((grad + hop.astype(F32)).astype(BF16), [1])
        attn_totals[index] = (grad + hop.astype(F32)).astype(BF16)
    attn_back = lax.all_to_all(jnp.stack(attn_totals), "m", 0, 0, tiled=True)
    if width != 2 * BW:
        attn_back = attn_back.transpose(1, 0, 2).reshape(D, chunk_count, 2 * BW).transpose(1, 0, 2)

    d_one_parts = [halves(rows) for rows in (d_query, d_key, d_value)]
    d_one = [
        dot_t(d_one_parts[0][side], w_query)
        + dot_t(d_one_parts[1][side], w_key)
        + dot_t(d_one_parts[2][side], w_value)
        for side in (0, 1)
    ]
    d_normed_one = scatter_rows(d_one[0].reshape(part_shape), d_one[1].astype(BF16).reshape(part_shape))
    d_rows_norm, d_gain_one = rms_norm_back(rows_in, gains[0], d_normed_one)
    input_grad = d_middle + d_rows_norm
    output = middle + scatter_rows(output_own.reshape(part_shape), output_other.astype(BF16).reshape(part_shape))
    output = output.astype(BF16)

    weight_grads = jnp.where(plane == 0, attn_back.astype(F32), jnp.stack(mlp_totals))
    weight_grads = weight_grads.reshape(chunk_count, D, 2, BW).transpose(0, 2, 1, 3).reshape(block_count, D, BW)
    gain_parts = lax.all_gather(jnp.stack([d_gain_one, d_gain_two]), ("z",) + PLANE, axis=0, tiled=False)
    gain_grads = jnp.sum(gain_parts, axis=0)
    new_momentum = MOMENTUM_DECAY * momentum + weight_grads
    ortho = orthogonalize(new_momentum)
    new_weights = weights.astype(F32) - MUON_RATE * math.sqrt(D / BW) * ortho
    new_gain_first = BETA_FIRST * gain_first + (1.0 - BETA_FIRST) * gain_grads
    new_gain_second = BETA_SECOND * gain_second + (1.0 - BETA_SECOND) * gain_grads * gain_grads
    first_hat = new_gain_first / (1.0 - BETA_FIRST**STEP)
    second_hat = new_gain_second / (1.0 - BETA_SECOND**STEP)
    new_gains = gains - ADAM_RATE * first_hat / (jnp.sqrt(second_hat) + ADAM_EPS)
    return (
        output,
        input_grad,
        weight_grads,
        new_momentum,
        new_weights,
        new_gain_first,
        new_gain_second,
        new_gains,
    )


def solution(mesh):
    count = mesh.shape["dp"]
    fine = Mesh(
        np.asarray(mesh.devices).reshape(4, 4, count // 16, mesh.shape["tensor"]),
        ("z",) + PLANE,
    )
    every = ("z",) + PLANE
    in_specs = (
        P(every, None),
        P(every[:3], None),
        P(every, None, None),
        P(every, None, None),
        P(),
        P(),
        P(),
        P(every, None),
    )
    out_specs = (
        P(every, None),
        P(every, None),
        P(every, None, None),
        P(every, None, None),
        P(every, None, None),
        P(),
        P(),
        P(),
    )
    return jax.shard_map(local, mesh=fine, in_specs=in_specs, out_specs=out_specs, check_vma=False)
```

```python
import math

import jax
import jax.numpy as jnp
import numpy as np
from jax import lax
from jax.sharding import Mesh
from jax.sharding import PartitionSpec as P

D = 2048
FF = 8192
HD = 64
BW = 128
NS_ITERS = 5
STEP = 10

HIGHEST = lax.Precision.HIGHEST
ROPE_BASE = 130000.0
NORM_EPS = 1e-05
NEG_LARGE = -1e30
MOMENTUM_DECAY = 0.95
MUON_RATE = 0.25
COEFF_A = 3.4445
COEFF_B = -4.775
COEFF_C = 2.0315
BETA_FIRST = 0.9
BETA_SECOND = 0.95
ADAM_RATE = 1.0
ADAM_EPS = 1e-08

F32 = jnp.float32
BF16 = jnp.bfloat16
PLANE = ("m", "r", "tensor")
SWAP = [(0, 1), (1, 0)]


def rms_norm(values, gain):
    return values * lax.rsqrt(jnp.mean(values * values, axis=-1, keepdims=True) + NORM_EPS) * gain


def rms_norm_back(values, gain, grad):
    scale = lax.rsqrt(jnp.mean(values * values, axis=-1, keepdims=True) + NORM_EPS)
    scaled = gain * grad
    inner = jnp.mean(scaled * values, axis=-1, keepdims=True)
    gain_grad = jnp.sum(grad * values * scale, axis=0)
    return scale * scaled - values * (scale * scale * scale * inner), gain_grad


def rope_tables(place):
    position = place.astype(F32)
    exponent = jnp.arange(HD // 2).astype(F32) * (2.0 / HD)
    inverse = jnp.exp(-exponent * math.log(ROPE_BASE))
    angle = position[:, None] * inverse[None, :]
    return (jnp.cos(angle)[:, None, :], jnp.sin(angle)[:, None, :])


def rotate(values, cosine, sine):
    half = values.shape[-1] // 2
    first = values[..., :half]
    second = values[..., half:]
    return jnp.concatenate(
        [first * cosine - second * sine, second * cosine + first * sine], axis=-1
    )


def unrotate(values, cosine, sine):
    return rotate(values, cosine, -sine)


def dot(a, b):
    return jnp.dot(a, b, preferred_element_type=F32)


def dot_t(a, b):
    return lax.dot_general(a, b, (((1,), (1,)), ((), ())), preferred_element_type=F32)


def t_dot(a, b):
    return lax.dot_general(a, b, (((0,), (0,)), ((), ())), preferred_element_type=F32)


def orthogonalize(blocks):
    norm = jnp.sqrt(jnp.sum(blocks * blocks, axis=(1, 2), keepdims=True))
    current = blocks / (norm + 1e-07)
    gram = jnp.einsum("bdc,bde->bce", current, current, precision=HIGHEST)
    eye = jnp.eye(BW, dtype=F32)
    total = None
    for turn in range(NS_ITERS):
        square = jnp.einsum("bij,bjk->bik", gram, gram, precision=HIGHEST)
        mixer = COEFF_A * eye + COEFF_B * gram + COEFF_C * square
        if total is None:
            total = mixer
        else:
            total = jnp.einsum("bij,bjk->bik", total, mixer, precision=HIGHEST)
        if turn < NS_ITERS - 1:
            half = jnp.einsum("bij,bjk->bik", mixer, gram, precision=HIGHEST)
            gram = jnp.einsum("bij,bjk->bik", half, mixer, precision=HIGHEST)
    return jnp.einsum("bdc,bce->bde", current, total, precision=HIGHEST)


def mirror(step):
    return [(place, place ^ step) for place in range(4)]


def ring(value, step=1):
    return lax.ppermute(value, "z", [(place, (place + step) % 4) for place in range(4)])


def gather_rows(rows, row_major):
    mine = [rows]
    for _ in range(3):
        mine.append(ring(mine[-1]))
    other = [lax.ppermute(part, "tensor", SWAP) for part in mine]
    if row_major:
        pieces = [piece for pair in zip(mine, other) for piece in pair]
    else:
        pieces = mine + other
    return jnp.concatenate(pieces, axis=0)


def scatter_rows(own_half, other_half):
    total = own_half + lax.ppermute(other_half, "tensor", SWAP).astype(F32)
    moving = ring(total[1].astype(BF16))
    for step in (2, 3):
        moving = ring((total[step] + moving.astype(F32)).astype(BF16))
    return total[0] + moving.astype(F32)


def everywhere(value):
    value = value + lax.ppermute(value, "tensor", SWAP)
    for axis in ("m", "z"):
        for step in (1, 2):
            value = value + lax.ppermute(value, axis, mirror(step))
    if lax.axis_size("r") > 1:
        value = lax.psum(value, "r")
    return value


def widen(parts, width):
    if width == 2 * BW:
        return parts
    return parts.reshape(4, -1, D, width).transpose(0, 2, 1, 3).reshape(4, D, 2 * BW)


def narrow(parts, width):
    if width == 2 * BW:
        return parts
    return parts.reshape(4, D, -1, width).transpose(0, 2, 1, 3).reshape(-1, D, width)


def gather_kind(kind, width):
    return widen(lax.all_gather(kind, ("m", "r"), axis=0, tiled=False), width)


def scatter_kind(grads, width):
    grads = narrow(grads, width)
    return lax.psum_scatter(grads, ("m", "r"), scatter_dimension=0, tiled=False)


def local(tokens, segments, weights, momentum, gains, gain_first, gain_second, cotangent):
    plane = lax.axis_index("z")
    core = lax.axis_index("tensor")
    block_count = weights.shape[0]
    width = block_count * BW // 4

    def choose(*cases):
        return lax.select_n(plane, *cases)

    if width == 2 * BW:
        own = weights.reshape(4, 2, D, BW).transpose(0, 2, 1, 3).reshape(4, D, width)
    else:
        own = weights.reshape(block_count, D, 2, width).transpose(0, 2, 1, 3).reshape(4, D, width)
    from_attn = [lax.ppermute(own[k], "z", [(0, k)]) for k in (1, 2, 3)]
    w_attn = gather_kind(choose(own[0], *from_attn), width)
    to_plane = lambda shift: lax.dynamic_index_in_dim(own, (plane + shift) % 4, 0, keepdims=False)
    moved = {}
    for shift in (1, 2, 3):
        moved[shift] = lax.ppermute(
            to_plane(shift), "z", [(a, (a + shift) % 4) for a in (1, 2, 3)]
        )
    kept = to_plane(0)
    w_gate = gather_kind(choose(moved[3], kept, moved[1], moved[2]), width)
    w_up = gather_kind(choose(moved[2], moved[3], kept, moved[1]), width)
    w_down = gather_kind(choose(moved[1], moved[2], moved[3], kept), width)
    w_query, w_key, w_value, w_out = (w_attn[index] for index in range(4))

    segment_parts = [segments]
    for _ in range(3):
        segment_parts.append(ring(segment_parts[-1]))
    segment_rows = jnp.concatenate(segment_parts, axis=0)
    group, length = segment_rows.shape
    half = length // 2
    part_shape = (4, half, D)
    place = jnp.arange(length)
    place = jnp.where(core == 0, place, (place + half) % length)
    segment_rows = jnp.where(core == 0, segment_rows, jnp.roll(segment_rows, half, axis=1))
    span = w_query.shape[1]
    heads = span // HD
    head_shape = (group, length, heads, HD)

    rows_in = tokens.astype(F32)
    seen_one = gather_rows(rms_norm(rows_in, gains[0]).astype(BF16), True)
    d_mlp = gather_rows(cotangent, False)
    cosine, sine = rope_tables(place)
    query = rotate(dot(seen_one, w_query).reshape(head_shape), cosine, sine).astype(BF16)
    key = rotate(dot(seen_one, w_key).reshape(head_shape), cosine, sine).astype(BF16)
    value = dot(seen_one, w_value).astype(BF16).reshape(head_shape)
    score_scale = 1.0 / math.sqrt(HD)
    allowed = (place[None, None, :] <= place[None, :, None]) & (
        segment_rows[:, None, :] == segment_rows[:, :, None]
    )
    scores = jnp.einsum("gthd,gshd->ghts", query, key, preferred_element_type=F32) * score_scale
    scores = jnp.where(allowed[:, None], scores, NEG_LARGE)
    probs = jax.nn.softmax(scores, axis=-1)
    probs_low = probs.astype(BF16)
    context = jnp.einsum("ghts,gshd->gthd", probs_low, value, preferred_element_type=F32)
    context = context.astype(BF16).reshape(group * length, span)

    def halves(rows):
        parts = rows.reshape(group, 2, half, rows.shape[-1])
        return (parts[:, 0].reshape(group * half, -1), parts[:, 1].reshape(group * half, -1))

    context_own, context_other = halves(context)
    mixed = scatter_rows(
        dot_t(context_own, w_out).reshape(part_shape),
        dot_t(context_other, w_out).astype(BF16).reshape(part_shape),
    )
    middle = rows_in + mixed
    seen_two = gather_rows(rms_norm(middle, gains[1]).astype(BF16), False)

    count = group * half
    output_own = output_other = d_two_own = d_two_other = None
    mlp_grads = []
    for index in range(4):
        gate_act = dot(seen_two, w_gate[index])
        up_act = dot(seen_two, w_up[index])
        d_hidden = dot(d_mlp, w_down[index])
        sigmoid_gate = jax.nn.sigmoid(gate_act)
        silu = gate_act * sigmoid_gate
        hidden = (silu * up_act).astype(BF16)
        d_gate = (d_hidden * up_act * sigmoid_gate * (1.0 + gate_act * (1.0 - sigmoid_gate))).astype(BF16)
        d_up = (d_hidden * silu).astype(BF16)
        mlp_grads.append(
            (
                t_dot(seen_two, d_gate).astype(BF16),
                t_dot(seen_two, d_up).astype(BF16),
                t_dot(d_mlp, hidden).astype(BF16),
            )
        )
        parts = (
            dot_t(hidden[:count], w_down[index]),
            dot_t(hidden[count:], w_down[index]),
            dot_t(d_gate[:count], w_gate[index]) + dot_t(d_up[:count], w_up[index]),
            dot_t(d_gate[count:], w_gate[index]) + dot_t(d_up[count:], w_up[index]),
        )
        if index == 0:
            output_own, output_other, d_two_own, d_two_other = parts
        else:
            output_own += parts[0]
            output_other += parts[1]
            d_two_own += parts[2]
            d_two_other += parts[3]
    d_normed_two = scatter_rows(d_two_own.reshape(part_shape), d_two_other.astype(BF16).reshape(part_shape))
    kind_grads = [None] + [
        scatter_kind(jnp.stack([mlp_grads[index][kind] for index in range(4)]), width) for kind in range(3)
    ]

    d_output = cotangent.astype(F32)
    d_middle_norm, d_gain_two = rms_norm_back(middle, gains[1], d_normed_two)
    d_middle = d_output + d_middle_norm
    d_attn = gather_rows(d_middle.astype(BF16), True)
    d_context = dot(d_attn, w_out).astype(BF16).reshape(head_shape)
    d_value = jnp.einsum("ghts,gthd->gshd", probs_low, d_context, preferred_element_type=F32)
    d_probs = jnp.einsum("gthd,gshd->ghts", d_context, value, preferred_element_type=F32)
    inner = jnp.sum(probs * d_probs, axis=-1, keepdims=True)
    d_scores = (probs * (d_probs - inner)).astype(BF16)
    d_query = jnp.einsum("ghts,gshd->gthd", d_scores, key, preferred_element_type=F32) * score_scale
    d_key = jnp.einsum("ghts,gthd->gshd", d_scores, query, preferred_element_type=F32) * score_scale
    flat = (group * length, span)
    d_query = unrotate(d_query, cosine, sine).astype(BF16).reshape(flat)
    d_key = unrotate(d_key, cosine, sine).astype(BF16).reshape(flat)
    d_value = d_value.astype(BF16).reshape(flat)

    attn_grads = jnp.stack(
        [
            t_dot(seen_one, d_query).astype(BF16),
            t_dot(seen_one, d_key).astype(BF16),
            t_dot(seen_one, d_value).astype(BF16),
            t_dot(d_attn, context).astype(BF16),
        ]
    )
    kind_grads[0] = scatter_kind(attn_grads, width)
    to_attn = [lax.ppermute(kind_grads[0], "z", [(k, 0)]) for k in (1, 2, 3)]
    stacked = jnp.stack(kind_grads[1:] + kind_grads[1:2])
    back = {}
    for shift in (1, 2, 3):
        target = (plane + shift) % 4
        payload = lax.dynamic_index_in_dim(stacked, (target + 3) % 4, 0, keepdims=False)
        back[shift] = lax.ppermute(payload, "z", [(a, (a + shift) % 4) for a in range(4) if (a + shift) % 4])
    mine = lax.dynamic_index_in_dim(stacked, (plane + 3) % 4, 0, keepdims=False)
    received = [
        choose(kind_grads[0], back[1], back[2], back[3]),
        choose(to_attn[0], mine, back[1], back[2]),
        choose(to_attn[1], back[3], mine, back[1]),
        choose(to_attn[2], back[2], back[3], mine),
    ]

    d_one_parts = [halves(rows) for rows in (d_query, d_key, d_value)]
    d_one = [
        dot_t(d_one_parts[0][side], w_query)
        + dot_t(d_one_parts[1][side], w_key)
        + dot_t(d_one_parts[2][side], w_value)
        for side in (0, 1)
    ]
    d_normed_one = scatter_rows(d_one[0].reshape(part_shape), d_one[1].astype(BF16).reshape(part_shape))
    d_rows_norm, d_gain_one = rms_norm_back(rows_in, gains[0], d_normed_one)
    input_grad = d_middle + d_rows_norm
    output = middle + scatter_rows(output_own.reshape(part_shape), output_other.astype(BF16).reshape(part_shape))
    output = output.astype(BF16)

    weight_grads = jnp.stack(received).astype(F32)
    if width == 2 * BW:
        weight_grads = weight_grads.reshape(4, D, 2, BW).transpose(0, 2, 1, 3)
    else:
        weight_grads = weight_grads.reshape(block_count, 2, D, width).transpose(0, 2, 1, 3)
    weight_grads = weight_grads.reshape(block_count, D, BW)
    gain_grads = everywhere(jnp.stack([d_gain_one, d_gain_two]))
    new_momentum = MOMENTUM_DECAY * momentum + weight_grads
    ortho = orthogonalize(new_momentum)
    new_weights = weights.astype(F32) - MUON_RATE * math.sqrt(D / BW) * ortho
    new_gain_first = BETA_FIRST * gain_first + (1.0 - BETA_FIRST) * gain_grads
    new_gain_second = BETA_SECOND * gain_second + (1.0 - BETA_SECOND) * gain_grads * gain_grads
    first_hat = new_gain_first / (1.0 - BETA_FIRST**STEP)
    second_hat = new_gain_second / (1.0 - BETA_SECOND**STEP)
    new_gains = gains - ADAM_RATE * first_hat / (jnp.sqrt(second_hat) + ADAM_EPS)
    return (
        output,
        input_grad,
        weight_grads,
        new_momentum,
        new_weights,
        new_gain_first,
        new_gain_second,
        new_gains,
    )


def solution(mesh):
    count = mesh.shape["dp"]
    fine = Mesh(
        np.asarray(mesh.devices).reshape(4, 4, count // 16, mesh.shape["tensor"]),
        ("z",) + PLANE,
    )
    every = ("z",) + PLANE
    in_specs = (
        P(every, None),
        P(every[:3], None),
        P(every, None, None),
        P(every, None, None),
        P(),
        P(),
        P(),
        P(every, None),
    )
    out_specs = (
        P(every, None),
        P(every, None),
        P(every, None, None),
        P(every, None, None),
        P(every, None, None),
        P(),
        P(),
        P(),
    )
    return jax.shard_map(local, mesh=fine, in_specs=in_specs, out_specs=out_specs, check_vma=False)
```

```python
import functools
import math

import jax
import jax.numpy as jnp
import numpy as np
from jax import lax
from jax.experimental import pallas as pl
from jax.experimental.pallas import tpu as pltpu
from jax.sharding import Mesh
from jax.sharding import PartitionSpec as P

D = 2048
FF = 8192
HD = 64
BW = 128
NS_ITERS = 5
STEP = 10

HIGHEST = lax.Precision.HIGHEST
ROPE_BASE = 130000.0
NORM_EPS = 1e-05
NEG_LARGE = -1e30
MOMENTUM_DECAY = 0.95
MUON_RATE = 0.25
COEFF_A = 3.4445
COEFF_B = -4.775
COEFF_C = 2.0315
BETA_FIRST = 0.9
BETA_SECOND = 0.95
ADAM_RATE = 1.0
ADAM_EPS = 1e-08

F32 = jnp.float32
BF16 = jnp.bfloat16
PLANE = ("m", "r", "tensor")
SWAP = [(0, 1), (1, 0)]
TILE = 256
SCORE_SCALE = 1.0 / math.sqrt(HD)


def rms_norm(values, gain):
    return values * lax.rsqrt(jnp.mean(values * values, axis=-1, keepdims=True) + NORM_EPS) * gain


def rms_norm_back(values, gain, grad):
    scale = lax.rsqrt(jnp.mean(values * values, axis=-1, keepdims=True) + NORM_EPS)
    scaled = gain * grad
    inner = jnp.mean(scaled * values, axis=-1, keepdims=True)
    gain_grad = jnp.sum(grad * values * scale, axis=0)
    return scale * scaled - values * (scale * scale * scale * inner), gain_grad


def rope_tables(place):
    exponent = jnp.arange(HD // 2).astype(F32) * (2.0 / HD)
    inverse = jnp.exp(-exponent * math.log(ROPE_BASE))
    angle = place.astype(F32)[:, None] * inverse[None, :]
    cosine, sine = jnp.cos(angle), jnp.sin(angle)
    heads = 2 * BW // HD
    return (
        jnp.tile(jnp.concatenate([cosine, cosine], axis=1), (1, heads)),
        jnp.tile(jnp.concatenate([-sine, sine], axis=1), (1, heads)),
    )


def dims(lhs, rhs):
    return (((lhs,), (rhs,)), ((), ()))


def mul(a, b):
    return lax.dot_general(a, b, dims(1, 0), preferred_element_type=F32)


def mul_bt(a, b):
    return lax.dot_general(a, b, dims(1, 1), preferred_element_type=F32)


def mul_at(a, b):
    return lax.dot_general(a, b, dims(0, 0), preferred_element_type=F32)


def side_by_side(ref, *index):
    return jnp.concatenate([ref[index + (0,)], ref[index + (1,)]], axis=-1)


def pair_rows(own_ref, other_ref):
    return jnp.concatenate([own_ref[...], other_ref[...]], axis=0)


def swap_halves(values):
    lane = lax.broadcasted_iota(jnp.int32, values.shape, 1)
    span = values.shape[1]
    ahead = pltpu.roll(values, span - HD // 2, 1)
    behind = pltpu.roll(values, HD // 2, 1)
    return jnp.where(lane % HD < HD // 2, ahead, behind)


def head_only(values, head):
    lane = lax.broadcasted_iota(jnp.int32, values.shape, 1)
    return jnp.where((lane >= head * HD) & (lane < (head + 1) * HD), values, jnp.zeros_like(values))


def head_probs(query, key, bias, head):
    scores = mul_bt(head_only(query, head), key) * SCORE_SCALE + bias
    weights = jnp.exp(scores - jnp.max(scores, axis=-1, keepdims=True))
    return weights / jnp.sum(weights, axis=-1, keepdims=True)


def attn_forward_kernel(
    own_ref, other_ref, w_ref, bias_ref, cos_ref, sin_ref, q_ref, k_ref, v_ref, c_ref, mine_ref, theirs_ref
):
    rows = pair_rows(own_ref, other_ref)
    cosine, sine = cos_ref[...], sin_ref[...]
    lin = mul(rows, side_by_side(w_ref, 0))
    query = (lin * cosine + swap_halves(lin) * sine).astype(BF16)
    lin = mul(rows, side_by_side(w_ref, 1))
    key = (lin * cosine + swap_halves(lin) * sine).astype(BF16)
    value = mul(rows, side_by_side(w_ref, 2)).astype(BF16)
    q_ref[...] = query
    k_ref[...] = key
    v_ref[...] = value
    context = jnp.zeros(query.shape, F32)
    for head in range(query.shape[1] // HD):
        probs = head_probs(query, key, bias_ref[...], head)
        context = context + mul(probs.astype(BF16), head_only(value, head))
    context = context.astype(BF16)
    c_ref[...] = context
    half = own_ref.shape[0]
    for tile in range(D // TILE):
        at = pl.ds(tile * TILE, TILE)
        w_out = jnp.concatenate([w_ref[3, 0, at, :], w_ref[3, 1, at, :]], axis=-1)
        mixed = mul_bt(context, w_out)
        mine_ref[:, at] = mixed[:half]
        theirs_ref[:, at] = mixed[half:].astype(BF16)


def attn_backward_kernel(
    own_ref, other_ref, w_ref, bias_ref, cos_ref, sin_ref, q_ref, k_ref, v_ref,
    dq_ref, dk_ref, dv_ref, mine_ref, theirs_ref,
):
    rows = pair_rows(own_ref, other_ref)
    query, key, value = q_ref[...], k_ref[...], v_ref[...]
    d_context = mul(rows, side_by_side(w_ref, 3)).astype(BF16)
    d_query = jnp.zeros(query.shape, F32)
    d_key = jnp.zeros(query.shape, F32)
    d_value = jnp.zeros(query.shape, F32)
    for head in range(query.shape[1] // HD):
        probs = head_probs(query, key, bias_ref[...], head)
        d_here = head_only(d_context, head)
        d_value = d_value + mul_at(probs.astype(BF16), d_here)
        d_probs = mul_bt(d_here, value)
        inner = jnp.sum(probs * d_probs, axis=-1, keepdims=True)
        d_scores = (probs * (d_probs - inner)).astype(BF16)
        d_query = d_query + mul(d_scores, head_only(key, head))
        d_key = d_key + mul_at(d_scores, head_only(query, head))
    cosine, sine = cos_ref[...], sin_ref[...]
    d_query = d_query * SCORE_SCALE
    d_key = d_key * SCORE_SCALE
    d_query = (d_query * cosine - swap_halves(d_query) * sine).astype(BF16)
    d_key = (d_key * cosine - swap_halves(d_key) * sine).astype(BF16)
    d_value = d_value.astype(BF16)
    dq_ref[...] = d_query
    dk_ref[...] = d_key
    dv_ref[...] = d_value
    half = own_ref.shape[0]
    for tile in range(D // TILE):
        at = pl.ds(tile * TILE, TILE)
        total = jnp.zeros((2 * half, TILE), F32)
        for matrix, columns in ((0, d_query), (1, d_key), (2, d_value)):
            w_here = jnp.concatenate([w_ref[matrix, 0, at, :], w_ref[matrix, 1, at, :]], axis=-1)
            total = total + mul_bt(columns, w_here)
        mine_ref[:, at] = total[:half]
        theirs_ref[:, at] = total[half:].astype(BF16)


def mlp_kernel(
    own_ref, other_ref, d_own_ref, d_other_ref, gate_ref, up_ref, down_ref,
    hid_ref, dgate_ref, dup_ref, dn_mine_ref, dn_theirs_ref, out_mine_ref, out_theirs_ref, dn_acc, out_acc,
):
    step = pl.program_id(0)
    rows = pair_rows(own_ref, other_ref)
    d_rows = pair_rows(d_own_ref, d_other_ref)
    w_gate = side_by_side(gate_ref)
    w_up = side_by_side(up_ref)
    w_down = side_by_side(down_ref)
    gate = mul(rows, w_gate)
    up = mul(rows, w_up)
    d_hidden = mul(d_rows, w_down)
    sigmoid = 1.0 / (1.0 + jnp.exp(-gate))
    silu = gate * sigmoid
    hidden = (silu * up).astype(BF16)
    d_gate = (d_hidden * up * sigmoid * (1.0 + gate * (1.0 - sigmoid))).astype(BF16)
    d_up = (d_hidden * silu).astype(BF16)
    hid_ref[...] = hidden
    dgate_ref[...] = d_gate
    dup_ref[...] = d_up

    @pl.when(step == 0)
    def _():
        dn_acc[...] = jnp.zeros_like(dn_acc)
        out_acc[...] = jnp.zeros_like(out_acc)

    dn_acc[...] += mul_bt(d_gate, w_gate) + mul_bt(d_up, w_up)
    out_acc[...] += mul_bt(hidden, w_down)

    @pl.when(step == pl.num_programs(0) - 1)
    def _():
        half = own_ref.shape[0]
        dn_mine_ref[...] = dn_acc[:half]
        dn_theirs_ref[...] = dn_acc[half:].astype(BF16)
        out_mine_ref[...] = out_acc[:half]
        out_theirs_ref[...] = out_acc[half:].astype(BF16)


def grads_kernel(sources, *refs):
    first, second = refs[:8], refs[8:16]
    columns = refs[16:-1]
    out_ref = refs[-1]
    row_sets = [jnp.concatenate([ref[...] for ref in part], axis=0) for part in (first, second)]
    for index, source in enumerate(sources):
        stacked = jnp.concatenate([ref[...] for ref in columns[4 * index : 4 * index + 4]], axis=0)
        grad = mul_at(row_sets[source], stacked).astype(BF16)
        for block in range(grad.shape[1] // BW):
            out_ref[block // 2, index, block % 2] = grad[:, block * BW : (block + 1) * BW]


def split(values):
    high = values.astype(BF16)
    return high, (values - high.astype(F32)).astype(BF16)


def mul_split(a, b):
    return mul(a[0], b[0]) + (mul(a[0], b[1]) + mul(a[1], b[0]))


def muon_kernel(grad_ref, momentum_ref, weight_ref, wg_ref, nm_ref, nw_ref, held, mixers):
    step = pl.program_id(0)
    count = held.shape[0]

    @pl.when(step < count)
    def _():
        grad = grad_ref[...].astype(F32)
        wg_ref[...] = grad
        block = MOMENTUM_DECAY * momentum_ref[...] + grad
        nm_ref[...] = block
        block = block * (1.0 / (jnp.sqrt(jnp.sum(block * block)) + 1e-07))
        held[step] = block
        high, low = split(block)
        cross = mul_at(high, low)
        mixers[step] = mul_at(high, high) + (cross + cross.T)

    @pl.when(step == count - 1)
    def _():
        row = lax.broadcasted_iota(jnp.int32, (BW, BW), 0)
        column = lax.broadcasted_iota(jnp.int32, (BW, BW), 1)
        eye = jnp.where(row == column, COEFF_A, 0.0).astype(F32)
        grams = [mixers[index] for index in range(count)]
        totals = [None] * count
        for turn in range(NS_ITERS):
            for index in range(count):
                pair = split(grams[index])
                mixer = eye + COEFF_B * grams[index] + COEFF_C * mul_split(pair, pair)
                mixed = split(mixer)
                if turn == 0:
                    totals[index] = mixer
                else:
                    totals[index] = mul_split(split(totals[index]), mixed)
                if turn < NS_ITERS - 1:
                    grams[index] = mul_split(split(mul_split(mixed, pair)), mixed)
        for index in range(count):
            mixers[index] = totals[index]

    @pl.when(step >= count)
    def _():
        at = step - count
        ortho = mul_split(split(held[at]), split(mixers[at]))
        nw_ref[...] = weight_ref[...].astype(F32) - (MUON_RATE * math.sqrt(D / BW)) * ortho


def params(mebibytes):
    return pltpu.CompilerParams(vmem_limit_bytes=mebibytes * 1024 * 1024)


def whole_specs(arrays):
    return [pl.BlockSpec(memory_space=pltpu.VMEM) for _ in arrays]


def shaped(shape, dtype):
    return jax.ShapeDtypeStruct(shape, dtype)


def attn_forward(own, other, w_attn, bias, cosine, sine):
    half = own.shape[0]
    span = w_attn.shape[1] * w_attn.shape[3]
    square = shaped((2 * half, span), BF16)
    args = (own, other, w_attn, bias, cosine, sine)
    return pl.pallas_call(
        attn_forward_kernel,
        out_shape=(square,) * 4 + (shaped((half, D), F32), shaped((half, D), BF16)),
        in_specs=whole_specs(args),
        out_specs=tuple(whole_specs(range(6))),
        compiler_params=params(40),
        cost_estimate=pl.CostEstimate(flops=1_300_000_000, bytes_accessed=9_000_000, transcendentals=262_144),
        name="attn_forward",
    )(*args)


def attn_backward(own, other, w_attn, bias, cosine, sine, query, key, value):
    half = own.shape[0]
    square = shaped(query.shape, BF16)
    args = (own, other, w_attn, bias, cosine, sine, query, key, value)
    return pl.pallas_call(
        attn_backward_kernel,
        out_shape=(square,) * 3 + (shaped((half, D), F32), shaped((half, D), BF16)),
        in_specs=whole_specs(args),
        out_specs=tuple(whole_specs(range(5))),
        compiler_params=params(40),
        cost_estimate=pl.CostEstimate(flops=1_600_000_000, bytes_accessed=9_000_000, transcendentals=262_144),
        name="attn_backward",
    )(*args)


def mlp_piece(own, other, d_own, d_other, w_mlp):
    half = own.shape[0]
    chunks = w_mlp.shape[0]
    wide = 2 * BW
    keep = pl.BlockSpec((half, D), lambda j: (0, 0))
    weights = [
        pl.BlockSpec((None, None, 2, D, BW), lambda j, kind=kind: (j, kind, 0, 0, 0)) for kind in range(3)
    ]
    column = pl.BlockSpec((2 * half, wide), lambda j: (0, j))
    columns = shaped((2 * half, chunks * wide), BF16)
    return pl.pallas_call(
        mlp_kernel,
        grid=(chunks,),
        out_shape=(columns,) * 3 + (shaped((half, D), F32), shaped((half, D), BF16)) * 2,
        in_specs=[keep] * 4 + weights,
        out_specs=(column,) * 3 + (keep,) * 4,
        scratch_shapes=[pltpu.VMEM((2 * half, D), F32)] * 2,
        compiler_params=params(40),
        cost_estimate=pl.CostEstimate(flops=6_400_000_000, bytes_accessed=20_000_000, transcendentals=262_144),
        name="mlp_piece",
    )(own, other, d_own, d_other, w_mlp, w_mlp, w_mlp)


def weight_products(first, second, column_sets, sources, name):
    half = first[0].shape[0]
    span = column_sets[0][0].shape[1]
    pairs = span // (2 * BW)
    row_spec = pl.BlockSpec((half, TILE), lambda i: (0, i))
    column_spec = pl.BlockSpec((2 * half, span), lambda i: (0, 0))
    flat = [piece for pieces in column_sets for piece in pieces]
    return pl.pallas_call(
        functools.partial(grads_kernel, sources),
        grid=(D // TILE,),
        out_shape=shaped((pairs, len(sources), 2, D, BW), BF16),
        in_specs=[row_spec] * 16 + [column_spec] * len(flat),
        out_specs=pl.BlockSpec((pairs, len(sources), 2, TILE, BW), lambda i: (0, 0, 0, i, 0)),
        compiler_params=params(40),
        cost_estimate=pl.CostEstimate(
            flops=2 * 8 * half * D * span * len(sources), bytes_accessed=20_000_000, transcendentals=0
        ),
        name=name,
    )(*first, *second, *flat)


def muon(grads, momentum, weights):
    count = grads.shape[0]
    early = pl.BlockSpec((None, D, BW), lambda i: (jnp.minimum(i, count - 1), 0, 0))
    late = pl.BlockSpec((None, D, BW), lambda i: (jnp.maximum(i - count, 0), 0, 0))
    full = shaped(grads.shape, F32)
    return pl.pallas_call(
        muon_kernel,
        grid=(2 * count,),
        out_shape=(full,) * 3,
        in_specs=[early, early, late],
        out_specs=(early, early, late),
        scratch_shapes=[pltpu.VMEM((count, D, BW), F32), pltpu.VMEM((count, BW, BW), F32)],
        compiler_params=params(40),
        cost_estimate=pl.CostEstimate(flops=8_000_000_000, bytes_accessed=45_000_000, transcendentals=0),
        name="muon",
    )(grads, momentum, weights)


def mirror(step):
    return [(place, place ^ step) for place in range(4)]


def ring(value, step=1):
    return lax.ppermute(value, "z", [(place, (place + step) % 4) for place in range(4)])


def swap(value):
    return lax.ppermute(value, "tensor", SWAP)


def nothing(value):
    first = value[(0,) * value.ndim].astype(F32)
    return (first * 0.0).astype(jnp.int32)


def hold(value, *others):
    zero = sum(nothing(other) for other in others)
    return value + zero.astype(value.dtype)


def gather_rows(rows):
    mine = [rows]
    for _ in range(3):
        mine.append(ring(mine[-1]))
    return mine, [swap(part) for part in mine]


def scatter_rows(pieces):
    total = [mine + swap(theirs).astype(F32) for mine, theirs in pieces]
    moving = ring(total[1].astype(BF16))
    for step in (2, 3):
        moving = ring((total[step] + moving.astype(F32)).astype(BF16))
    return total[0] + moving.astype(F32)


def everywhere(value):
    value = value + swap(value)
    for axis in ("m", "z"):
        for step in (1, 2):
            value = value + lax.ppermute(value, axis, mirror(step))
    if lax.axis_size("r") > 1:
        value = lax.psum(value, "r")
    return value


def join(parts):
    if parts.shape[0] == 4:
        return parts
    width = parts.shape[3]
    parts = parts.reshape(4, 2, -1, D, width).transpose(0, 1, 3, 2, 4)
    return parts.reshape(4, 2, D, BW)


def unjoin(grads, width):
    if width == BW:
        return grads
    grads = grads.reshape(4, 2, D, -1, width).transpose(0, 1, 3, 2, 4)
    return grads.reshape(-1, 1, D, width)


def gather_kinds(kinds):
    stack = jnp.stack([part for parts in kinds for part in parts])
    gathered = lax.all_gather(stack, ("m", "r"), axis=0, tiled=False)
    gathered = gathered.reshape((gathered.shape[0], len(kinds), -1) + gathered.shape[2:])
    if len(kinds[0]) == 2:
        return gathered
    return jnp.stack([join(gathered[:, index]) for index in range(len(kinds))], axis=1)


def gather_kind_direct(parts):
    if lax.axis_size("r") > 1:
        return gather_kinds([parts])[:, 0]
    chip = lax.axis_index("m")
    result = jnp.zeros((4, len(parts)) + parts[0].shape, parts[0].dtype)
    for index, part in enumerate(parts):
        result = lax.dynamic_update_slice(result, part[None, None], (chip, index, 0, 0))
        for step in (1, 2, 3):
            got = lax.ppermute(part, "m", mirror(step))
            result = lax.dynamic_update_slice(result, got[None, None], (chip ^ step, index, 0, 0))
    return result


def scatter_kind(grads, width):
    grads = unjoin(grads, width)
    share = lax.psum_scatter(
        grads.reshape(grads.shape[0], -1, width), ("m", "r"), scatter_dimension=0, tiled=False
    )
    return share.reshape(grads.shape[1:])


def scatter_kind_direct(grads, width):
    if lax.axis_size("r") > 1:
        share = scatter_kind(grads, width)
        return [share[index] for index in range(share.shape[0])]
    chip = lax.axis_index("m")

    def part_for(step, index):
        return lax.dynamic_slice(grads, (chip ^ step, index, 0, 0), (1, 1, D, BW))[0, 0]

    result = []
    for index in range(2):
        total = part_for(0, index).astype(F32)
        for step in (1, 2, 3):
            total = total + lax.ppermute(part_for(step, index), "m", mirror(step)).astype(F32)
        result.append(total.astype(BF16))
    return result


def interleave(mine, other):
    return [rows for pair in zip(mine, other) for rows in pair]


def local(tokens, segments, weights, momentum, gains, gain_first, gain_second, cotangent):
    plane = lax.axis_index("z")
    core = lax.axis_index("tensor")
    block_count = weights.shape[0]

    def choose(*cases):
        return lax.select_n(plane, *cases)

    if block_count == 8:
        shards = weights.reshape(4, 2, D, BW)
    else:
        width = block_count * BW // 4
        shards = weights.reshape(block_count, D, -1, width).transpose(0, 2, 1, 3).reshape(4, 1, D, width)
    parts, width = shards.shape[1], shards.shape[3]

    def shard(shift, part):
        return lax.dynamic_slice(shards, ((plane + shift) % 4, part, 0, 0), (1, 1, D, width))[0, 0]

    moved = [[ring(shard(shift, part), shift) if shift else shard(0, part) for part in range(parts)] for shift in range(4)]
    kinds = [
        [choose(*(moved[(at - source) % 4][part] for at in range(4))) for part in range(parts)]
        for source in range(4)
    ]
    w_attn = gather_kind_direct(kinds[0])
    w_mlp = gather_kinds(kinds[1:])

    rows_in = tokens.astype(F32)
    one_mine, one_other = gather_rows(rms_norm(rows_in, gains[0]).astype(BF16))
    d_mine, d_other = gather_rows(hold(cotangent, kinds[0][-1]))

    segment_parts = [segments]
    for _ in range(3):
        segment_parts.append(ring(segment_parts[-1]))
    segment_rows = jnp.concatenate(segment_parts, axis=0)
    length = segment_rows.shape[1]
    half = length // 2
    place = jnp.arange(length)
    place = jnp.where(core == 0, place, (place + half) % length)
    segment_rows = jnp.where(core == 0, segment_rows, jnp.roll(segment_rows, half, axis=1))
    allowed = (place[None, None, :] <= place[None, :, None]) & (
        segment_rows[:, None, :] == segment_rows[:, :, None]
    )
    bias = jnp.where(allowed, 0.0, NEG_LARGE).astype(F32)
    cosine, sine = rope_tables(place)

    query, key, value, context, mixed = ([None] * 4 for _ in range(5))
    for s in (1, 2, 3, 0):
        query[s], key[s], value[s], context[s], *both = attn_forward(
            one_mine[s], one_other[s], w_attn, bias[s], cosine, sine
        )
        mixed[s] = both
    middle = rows_in + scatter_rows(mixed)
    two_mine, two_other = gather_rows(rms_norm(middle, gains[1]).astype(BF16))

    hidden, d_gate, d_up, d_two, outward = ([None] * 4 for _ in range(5))
    for s in range(4):
        hidden[s], d_gate[s], d_up[s], *both = mlp_piece(
            two_mine[s], two_other[s], d_mine[s], d_other[s], w_mlp
        )
        d_two[s], outward[s] = both[:2], both[2:]
    d_normed_two = scatter_rows(d_two)
    mlp_grads = weight_products(
        interleave(two_mine, two_other), interleave(d_mine, d_other), (d_gate, d_up, hidden), (0, 0, 1), "mlp_products"
    )
    if parts == 2:
        mlp_share = scatter_kind(mlp_grads.reshape(4, 6, D, BW), BW).reshape(3, 2, D, BW)
    else:
        mlp_share = jnp.stack([scatter_kind(mlp_grads[:, kind], width) for kind in range(3)])

    d_output = cotangent.astype(F32)
    d_middle_norm, d_gain_two = rms_norm_back(middle, gains[1], d_normed_two)
    d_middle = d_output + d_middle_norm
    e_mine, e_other = gather_rows(d_middle.astype(BF16))
    d_query, d_key, d_value, d_one = ([None] * 4 for _ in range(4))
    for s in range(4):
        d_query[s], d_key[s], d_value[s], *both = attn_backward(
            e_mine[s], e_other[s], w_attn, bias[s], cosine, sine, query[s], key[s], value[s]
        )
        d_one[s] = both
    attn_grads = weight_products(
        interleave(one_mine, one_other),
        interleave(e_mine, e_other),
        (d_query, d_key, d_value, context),
        (0, 0, 0, 1),
        "attn_products",
    )
    attn_share = scatter_kind_direct(attn_grads[0], width)

    def share_of(target):
        return lax.dynamic_index_in_dim(mlp_share, (target + 3) % 4 % 3, 0, keepdims=False)

    back = [share_of(plane)]
    for shift in (1, 2, 3):
        pairs = [(at, (at + shift) % 4) for at in range(4) if (at + shift) % 4]
        back.append(lax.ppermute(share_of((plane + shift) % 4), "z", pairs))
    mlp_back = jnp.stack([choose(*(back[(at - source) % 4] for at in range(4))) for source in range(4)])
    mlp_back = mlp_back.reshape((4 * parts,) + mlp_back.shape[2:])
    attn_parts = [
        attn_share if source == 0 else [lax.ppermute(part, "z", [(source, 0)]) for part in attn_share]
        for source in range(4)
    ]
    attn_back = jnp.stack([attn_parts[source][part] for source in range(4) for part in range(parts)])
    summed = jnp.where(plane == 0, attn_back, mlp_back)
    if parts == 1:
        summed = summed.reshape(block_count, -1, D, width).transpose(0, 2, 1, 3).reshape(block_count, D, BW)
    weight_grads, new_momentum, new_weights = muon(summed, momentum, weights)

    d_normed_one = scatter_rows(d_one)
    d_rows_norm, d_gain_one = rms_norm_back(rows_in, gains[0], d_normed_one)
    input_grad = d_middle + d_rows_norm
    late = [(hold(mine, e_other[3]), hold(theirs, e_other[3])) for mine, theirs in outward]
    output = (middle + scatter_rows(late)).astype(BF16)
    gain_grads = everywhere(jnp.stack([d_gain_one, d_gain_two]))
    new_gain_first = BETA_FIRST * gain_first + (1.0 - BETA_FIRST) * gain_grads
    new_gain_second = BETA_SECOND * gain_second + (1.0 - BETA_SECOND) * gain_grads * gain_grads
    first_hat = new_gain_first / (1.0 - BETA_FIRST**STEP)
    second_hat = new_gain_second / (1.0 - BETA_SECOND**STEP)
    new_gains = gains - ADAM_RATE * first_hat / (jnp.sqrt(second_hat) + ADAM_EPS)
    return (
        output,
        input_grad,
        weight_grads,
        new_momentum,
        new_weights,
        new_gain_first,
        new_gain_second,
        new_gains,
    )


def solution(mesh):
    count = mesh.shape["dp"]
    fine = Mesh(
        np.asarray(mesh.devices).reshape(4, 4, count // 16, mesh.shape["tensor"]),
        ("z",) + PLANE,
    )
    every = ("z",) + PLANE
    in_specs = (
        P(every, None),
        P(every[:3], None),
        P(every, None, None),
        P(every, None, None),
        P(),
        P(),
        P(),
        P(every, None),
    )
    out_specs = (
        P(every, None),
        P(every, None),
        P(every, None, None),
        P(every, None, None),
        P(every, None, None),
        P(),
        P(),
        P(),
    )
    return jax.shard_map(local, mesh=fine, in_specs=in_specs, out_specs=out_specs, check_vma=False)
```

```python
import functools
import math

import jax
import jax.numpy as jnp
import numpy as np
from jax import lax
from jax.experimental import pallas as pl
from jax.experimental.pallas import tpu as pltpu
from jax.sharding import Mesh
from jax.sharding import PartitionSpec as P

D = 2048
FF = 8192
HD = 64
BW = 128
NS_ITERS = 5
STEP = 10

HIGHEST = lax.Precision.HIGHEST
ROPE_BASE = 130000.0
NORM_EPS = 1e-05
NEG_LARGE = -1e30
MOMENTUM_DECAY = 0.95
MUON_RATE = 0.25
COEFF_A = 3.4445
COEFF_B = -4.775
COEFF_C = 2.0315
BETA_FIRST = 0.9
BETA_SECOND = 0.95
ADAM_RATE = 1.0
ADAM_EPS = 1e-08

F32 = jnp.float32
BF16 = jnp.bfloat16
PLANE = ("m", "r", "tensor")
SWAP = [(0, 1), (1, 0)]
TILE = 256
SCORE_SCALE = 1.0 / math.sqrt(HD)


def rms_norm(values, gain):
    return values * lax.rsqrt(jnp.mean(values * values, axis=-1, keepdims=True) + NORM_EPS) * gain


def rms_norm_back(values, gain, grad):
    scale = lax.rsqrt(jnp.mean(values * values, axis=-1, keepdims=True) + NORM_EPS)
    scaled = gain * grad
    inner = jnp.mean(scaled * values, axis=-1, keepdims=True)
    gain_grad = jnp.sum(grad * values * scale, axis=0)
    return scale * scaled - values * (scale * scale * scale * inner), gain_grad


def rope_tables(place):
    exponent = jnp.arange(HD // 2).astype(F32) * (2.0 / HD)
    inverse = jnp.exp(-exponent * math.log(ROPE_BASE))
    angle = place.astype(F32)[:, None] * inverse[None, :]
    cosine, sine = jnp.cos(angle), jnp.sin(angle)
    heads = 2 * BW // HD
    return (
        jnp.tile(jnp.concatenate([cosine, cosine], axis=1), (1, heads)),
        jnp.tile(jnp.concatenate([-sine, sine], axis=1), (1, heads)),
    )


def dims(lhs, rhs):
    return (((lhs,), (rhs,)), ((), ()))


def mul(a, b):
    return lax.dot_general(a, b, dims(1, 0), preferred_element_type=F32)


def mul_bt(a, b):
    return lax.dot_general(a, b, dims(1, 1), preferred_element_type=F32)


def mul_at(a, b):
    return lax.dot_general(a, b, dims(0, 0), preferred_element_type=F32)


def side_by_side(ref, *index):
    return jnp.concatenate([ref[index + (0,)], ref[index + (1,)]], axis=-1)


def pair_rows(own_ref, other_ref):
    return jnp.concatenate([own_ref[...], other_ref[...]], axis=0)


def swap_halves(values):
    lane = lax.broadcasted_iota(jnp.int32, values.shape, 1)
    span = values.shape[1]
    ahead = pltpu.roll(values, span - HD // 2, 1)
    behind = pltpu.roll(values, HD // 2, 1)
    return jnp.where(lane % HD < HD // 2, ahead, behind)


def head_only(values, head):
    lane = lax.broadcasted_iota(jnp.int32, values.shape, 1)
    return jnp.where((lane >= head * HD) & (lane < (head + 1) * HD), values, jnp.zeros_like(values))


def head_probs(query, key, bias, head):
    scores = mul_bt(head_only(query, head), key) * SCORE_SCALE + bias
    weights = jnp.exp(scores - jnp.max(scores, axis=-1, keepdims=True))
    return weights / jnp.sum(weights, axis=-1, keepdims=True)


def attn_forward_kernel(
    own_ref, other_ref, w_ref, bias_ref, cos_ref, sin_ref, q_ref, k_ref, v_ref, c_ref, mine_ref, theirs_ref
):
    rows = pair_rows(own_ref, other_ref)
    cosine, sine = cos_ref[...], sin_ref[...]
    lin = mul(rows, side_by_side(w_ref, 0))
    query = (lin * cosine + swap_halves(lin) * sine).astype(BF16)
    lin = mul(rows, side_by_side(w_ref, 1))
    key = (lin * cosine + swap_halves(lin) * sine).astype(BF16)
    value = mul(rows, side_by_side(w_ref, 2)).astype(BF16)
    q_ref[...] = query
    k_ref[...] = key
    v_ref[...] = value
    context = jnp.zeros(query.shape, F32)
    for head in range(query.shape[1] // HD):
        probs = head_probs(query, key, bias_ref[...], head)
        context = context + mul(probs.astype(BF16), head_only(value, head))
    context = context.astype(BF16)
    c_ref[...] = context
    half = own_ref.shape[0]
    for tile in range(D // TILE):
        at = pl.ds(tile * TILE, TILE)
        w_out = jnp.concatenate([w_ref[3, 0, at, :], w_ref[3, 1, at, :]], axis=-1)
        mixed = mul_bt(context, w_out)
        mine_ref[:, at] = mixed[:half]
        theirs_ref[:, at] = mixed[half:].astype(BF16)


def attn_backward_kernel(
    own_ref, other_ref, w_ref, bias_ref, cos_ref, sin_ref, q_ref, k_ref, v_ref,
    dq_ref, dk_ref, dv_ref, mine_ref, theirs_ref,
):
    rows = pair_rows(own_ref, other_ref)
    query, key, value = q_ref[...], k_ref[...], v_ref[...]
    d_context = mul(rows, side_by_side(w_ref, 3)).astype(BF16)
    d_query = jnp.zeros(query.shape, F32)
    d_key = jnp.zeros(query.shape, F32)
    d_value = jnp.zeros(query.shape, F32)
    for head in range(query.shape[1] // HD):
        probs = head_probs(query, key, bias_ref[...], head)
        d_here = head_only(d_context, head)
        d_value = d_value + mul_at(probs.astype(BF16), d_here)
        d_probs = mul_bt(d_here, value)
        inner = jnp.sum(probs * d_probs, axis=-1, keepdims=True)
        d_scores = (probs * (d_probs - inner)).astype(BF16)
        d_query = d_query + mul(d_scores, head_only(key, head))
        d_key = d_key + mul_at(d_scores, head_only(query, head))
    cosine, sine = cos_ref[...], sin_ref[...]
    d_query = d_query * SCORE_SCALE
    d_key = d_key * SCORE_SCALE
    d_query = (d_query * cosine - swap_halves(d_query) * sine).astype(BF16)
    d_key = (d_key * cosine - swap_halves(d_key) * sine).astype(BF16)
    d_value = d_value.astype(BF16)
    dq_ref[...] = d_query
    dk_ref[...] = d_key
    dv_ref[...] = d_value
    half = own_ref.shape[0]
    for tile in range(D // TILE):
        at = pl.ds(tile * TILE, TILE)
        total = jnp.zeros((2 * half, TILE), F32)
        for matrix, columns in ((0, d_query), (1, d_key), (2, d_value)):
            w_here = jnp.concatenate([w_ref[matrix, 0, at, :], w_ref[matrix, 1, at, :]], axis=-1)
            total = total + mul_bt(columns, w_here)
        mine_ref[:, at] = total[:half]
        theirs_ref[:, at] = total[half:].astype(BF16)


def mlp_kernel(
    own_ref, other_ref, d_own_ref, d_other_ref, gate_even, gate_odd, up_even, up_odd, down_even, down_odd,
    hid_ref, dgate_ref, dup_ref, dn_mine_ref, dn_theirs_ref, out_mine_ref, out_theirs_ref, dn_acc, out_acc,
):
    step = pl.program_id(0)
    rows = pair_rows(own_ref, other_ref)
    d_rows = pair_rows(d_own_ref, d_other_ref)
    w_gate = jnp.concatenate([gate_even[...], gate_odd[...]], axis=-1)
    w_up = jnp.concatenate([up_even[...], up_odd[...]], axis=-1)
    w_down = jnp.concatenate([down_even[...], down_odd[...]], axis=-1)
    gate = mul(rows, w_gate)
    up = mul(rows, w_up)
    d_hidden = mul(d_rows, w_down)
    sigmoid = 1.0 / (1.0 + jnp.exp(-gate))
    silu = gate * sigmoid
    hidden = (silu * up).astype(BF16)
    d_gate = (d_hidden * up * sigmoid * (1.0 + gate * (1.0 - sigmoid))).astype(BF16)
    d_up = (d_hidden * silu).astype(BF16)
    hid_ref[...] = hidden
    dgate_ref[...] = d_gate
    dup_ref[...] = d_up

    @pl.when(step == 0)
    def _():
        dn_acc[...] = jnp.zeros_like(dn_acc)
        out_acc[...] = jnp.zeros_like(out_acc)

    dn_acc[...] += mul_bt(d_gate, w_gate) + mul_bt(d_up, w_up)
    out_acc[...] += mul_bt(hidden, w_down)

    @pl.when(step == pl.num_programs(0) - 1)
    def _():
        half = own_ref.shape[0]
        dn_mine_ref[...] = dn_acc[:half]
        dn_theirs_ref[...] = dn_acc[half:].astype(BF16)
        out_mine_ref[...] = out_acc[:half]
        out_theirs_ref[...] = out_acc[half:].astype(BF16)


def grads_kernel(sources, *refs):
    first, second = refs[:8], refs[8:16]
    columns = refs[16:-2]
    outs = refs[-2:]
    row_sets = [jnp.concatenate([ref[...] for ref in part], axis=0) for part in (first, second)]
    for index, source in enumerate(sources):
        stacked = jnp.concatenate([ref[...] for ref in columns[4 * index : 4 * index + 4]], axis=0)
        grad = mul_at(row_sets[source], stacked).astype(BF16)
        for block in range(grad.shape[1] // BW):
            outs[block % 2][block // 2, index] = grad[:, block * BW : (block + 1) * BW]


def split(values):
    high = values.astype(BF16)
    return high, (values - high.astype(F32)).astype(BF16)


def mul_split(a, b):
    return mul(a[0], b[0]) + (mul(a[0], b[1]) + mul(a[1], b[0]))


def muon_kernel(grad_ref, momentum_ref, weight_ref, wg_ref, nm_ref, nw_ref, held, mixers):
    step = pl.program_id(0)
    count = held.shape[0]

    @pl.when(step < count)
    def _():
        grad = grad_ref[...].astype(F32)
        wg_ref[...] = grad
        block = MOMENTUM_DECAY * momentum_ref[...] + grad
        nm_ref[...] = block
        block = block * (1.0 / (jnp.sqrt(jnp.sum(block * block)) + 1e-07))
        held[step] = block
        high, low = split(block)
        cross = mul_at(high, low)
        mixers[step] = mul_at(high, high) + (cross + cross.T)

    @pl.when(step == count - 1)
    def _():
        row = lax.broadcasted_iota(jnp.int32, (BW, BW), 0)
        column = lax.broadcasted_iota(jnp.int32, (BW, BW), 1)
        eye = jnp.where(row == column, COEFF_A, 0.0).astype(F32)
        grams = [mixers[index] for index in range(count)]
        totals = [None] * count
        for turn in range(NS_ITERS):
            for index in range(count):
                pair = split(grams[index])
                mixer = eye + COEFF_B * grams[index] + COEFF_C * mul_split(pair, pair)
                mixed = split(mixer)
                if turn == 0:
                    totals[index] = mixer
                else:
                    totals[index] = mul_split(split(totals[index]), mixed)
                if turn < NS_ITERS - 1:
                    grams[index] = mul_split(split(mul_split(mixed, pair)), mixed)
        for index in range(count):
            mixers[index] = totals[index]

    @pl.when(step >= count)
    def _():
        at = step - count
        ortho = mul_split(split(held[at]), split(mixers[at]))
        nw_ref[...] = weight_ref[...].astype(F32) - (MUON_RATE * math.sqrt(D / BW)) * ortho


def deferred(kernel, inputs, unread):
    return lambda *refs: kernel(*refs[:inputs], *refs[inputs + unread :])


def unread_specs(after):
    return [pl.BlockSpec(memory_space=pl.ANY) for _ in after]


def params(mebibytes):
    return pltpu.CompilerParams(vmem_limit_bytes=mebibytes * 1024 * 1024)


def whole_specs(arrays):
    return [pl.BlockSpec(memory_space=pltpu.VMEM) for _ in arrays]


def shaped(shape, dtype):
    return jax.ShapeDtypeStruct(shape, dtype)


def attn_forward(own, other, w_attn, bias, cosine, sine, after=()):
    half = own.shape[0]
    span = w_attn.shape[1] * w_attn.shape[3]
    square = shaped((2 * half, span), BF16)
    args = (own, other, w_attn, bias, cosine, sine)
    return pl.pallas_call(
        deferred(attn_forward_kernel, len(args), len(after)),
        out_shape=(square,) * 4 + (shaped((half, D), F32), shaped((half, D), BF16)),
        in_specs=whole_specs(args) + unread_specs(after),
        out_specs=tuple(whole_specs(range(6))),
        compiler_params=params(40),
        cost_estimate=pl.CostEstimate(flops=1_300_000_000, bytes_accessed=9_000_000, transcendentals=262_144),
        name="attn_forward",
    )(*args, *after)


def attn_backward(own, other, w_attn, bias, cosine, sine, query, key, value):
    half = own.shape[0]
    square = shaped(query.shape, BF16)
    args = (own, other, w_attn, bias, cosine, sine, query, key, value)
    return pl.pallas_call(
        attn_backward_kernel,
        out_shape=(square,) * 3 + (shaped((half, D), F32), shaped((half, D), BF16)),
        in_specs=whole_specs(args),
        out_specs=tuple(whole_specs(range(5))),
        compiler_params=params(40),
        cost_estimate=pl.CostEstimate(flops=1_600_000_000, bytes_accessed=9_000_000, transcendentals=262_144),
        name="attn_backward",
    )(*args)


def mlp_piece(own, other, d_own, d_other, w_even, w_odd, after=()):
    half = own.shape[0]
    chunks = w_even.shape[0]
    wide = 2 * BW
    keep = pl.BlockSpec((half, D), lambda j: (0, 0))
    weights = [
        pl.BlockSpec((None, None, D, BW), lambda j, kind=kind: (j, kind, 0, 0)) for kind in (0, 0, 1, 1, 2, 2)
    ]
    column = pl.BlockSpec((2 * half, wide), lambda j: (0, j))
    columns = shaped((2 * half, chunks * wide), BF16)
    return pl.pallas_call(
        deferred(mlp_kernel, 10, len(after)),
        grid=(chunks,),
        out_shape=(columns,) * 3 + (shaped((half, D), F32), shaped((half, D), BF16)) * 2,
        in_specs=[keep] * 4 + weights + unread_specs(after),
        out_specs=(column,) * 3 + (keep,) * 4,
        scratch_shapes=[pltpu.VMEM((2 * half, D), F32)] * 2,
        compiler_params=params(40),
        cost_estimate=pl.CostEstimate(flops=6_400_000_000, bytes_accessed=20_000_000, transcendentals=262_144),
        name="mlp_piece",
    )(own, other, d_own, d_other, w_even, w_odd, w_even, w_odd, w_even, w_odd, *after)


def weight_products(first, second, column_sets, sources, name, after=()):
    half = first[0].shape[0]
    span = column_sets[0][0].shape[1]
    pairs = span // (2 * BW)
    row_spec = pl.BlockSpec((half, TILE), lambda i: (0, i))
    column_spec = pl.BlockSpec((2 * half, span), lambda i: (0, 0))
    flat = [piece for pieces in column_sets for piece in pieces]
    return pl.pallas_call(
        deferred(functools.partial(grads_kernel, sources), 16 + len(flat), len(after)),
        grid=(D // TILE,),
        out_shape=(shaped((pairs, len(sources), D, BW), BF16),) * 2,
        in_specs=[row_spec] * 16 + [column_spec] * len(flat) + unread_specs(after),
        out_specs=(pl.BlockSpec((pairs, len(sources), TILE, BW), lambda i: (0, 0, i, 0)),) * 2,
        compiler_params=params(40),
        cost_estimate=pl.CostEstimate(
            flops=2 * 8 * half * D * span * len(sources), bytes_accessed=20_000_000, transcendentals=0
        ),
        name=name,
    )(*first, *second, *flat, *after)


def muon(grads, momentum, weights, offset, stride, begun=()):
    count = grads.shape[0]
    now = lambda i: jnp.minimum(i, count - 1)
    then = lambda i: jnp.maximum(i - count, 0)
    block = (None, D, BW)
    compact = pl.BlockSpec(block, lambda i: (now(i), 0, 0))
    early = pl.BlockSpec(block, lambda i: (stride * now(i) + offset, 0, 0))
    late = pl.BlockSpec(block, lambda i: (stride * then(i) + offset, 0, 0))
    return pl.pallas_call(
        deferred(muon_kernel, 3, len(begun)),
        grid=(2 * count,),
        out_shape=(shaped(momentum.shape, F32),) * 3,
        in_specs=[compact, early, late] + unread_specs(begun),
        out_specs=(early, early, late),
        input_output_aliases={3 + index: index for index in range(len(begun))},
        scratch_shapes=[pltpu.VMEM((count, D, BW), F32), pltpu.VMEM((count, BW, BW), F32)],
        compiler_params=params(40),
        cost_estimate=pl.CostEstimate(flops=1_000_000_000 * count, bytes_accessed=5_500_000 * count, transcendentals=0),
        name="muon",
    )(grads, momentum, weights, *begun)


def mirror(step):
    return [(place, place ^ step) for place in range(4)]


def ring(value, step=1):
    return lax.ppermute(value, "z", [(place, (place + step) % 4) for place in range(4)])


def swap(value):
    return lax.ppermute(value, "tensor", SWAP)


def nothing(value):
    first = value[(0,) * value.ndim].astype(F32)
    return (first * 0.0).astype(jnp.int32)


def hold(value, *others):
    zero = sum(nothing(other) for other in others)
    return value + zero.astype(value.dtype)


def gather_rows(rows):
    mine = [rows]
    for _ in range(3):
        mine.append(ring(mine[-1]))
    return mine, [swap(part) for part in mine]


def scatter_rows(pieces):
    scatter = Scatter()
    for step in (1, 2, 3, 0):
        scatter.add(step, *pieces[step])
    return scatter.result


class Scatter:
    def __init__(self):
        self.moving = self.result = None
        self.payloads = []

    def add(self, step, mine, theirs):
        total = mine + swap(theirs).astype(F32)
        if self.moving is not None:
            total = total + self.moving.astype(F32)
        if step:
            self.payloads.append(total.astype(BF16))
            self.moving = ring(self.payloads[-1])
        else:
            self.result = total


def everywhere(value):
    value = value + swap(value)
    for axis in ("m", "z"):
        for step in (1, 2):
            value = value + lax.ppermute(value, axis, mirror(step))
    if lax.axis_size("r") > 1:
        value = lax.psum(value, "r")
    return value


def join(parts):
    if parts.shape[0] == 4:
        return parts
    width = parts.shape[3]
    parts = parts.reshape(4, 2, -1, D, width).transpose(0, 1, 3, 2, 4)
    return parts.reshape(4, 2, D, BW)


def unjoin(grads, width):
    if width == BW:
        return grads
    grads = grads.reshape(4, 2, D, -1, width).transpose(0, 1, 3, 2, 4)
    return grads.reshape(-1, 1, D, width)


def gather_plane(parts):
    return lax.all_gather(jnp.stack(parts), ("m", "r"), axis=0, tiled=False)


def gather_part_direct(part, index, result):
    chip = lax.axis_index("m")
    result = lax.dynamic_update_slice(result, part[None, None], (chip, index, 0, 0))
    for step in (1, 2, 3):
        got = lax.ppermute(part, "m", mirror(step))
        result = lax.dynamic_update_slice(result, got[None, None], (chip ^ step, index, 0, 0))
    return result


def scatter_plane(grads):
    share = lax.psum_scatter(
        grads.reshape(grads.shape[0], -1, grads.shape[3]), ("m", "r"), scatter_dimension=0, tiled=False
    )
    return share.reshape(grads.shape[1:])


def scatter_plane_direct(grads):
    chip = lax.axis_index("m")

    def share_for(step):
        return lax.dynamic_index_in_dim(grads, chip ^ step, 0, keepdims=False)

    total = share_for(0).astype(F32)
    for step in (1, 2, 3):
        total = total + lax.ppermute(share_for(step), "m", mirror(step)).astype(F32)
    return total.astype(BF16)


def interleave(mine, other):
    return [rows for pair in zip(mine, other) for rows in pair]


def local(tokens, segments, weights, momentum, gains, gain_first, gain_second, cotangent):
    plane = lax.axis_index("z")
    core = lax.axis_index("tensor")
    block_count = weights.shape[0]

    def choose(*cases):
        return lax.select_n(plane, *cases)

    if block_count == 8:
        shards = weights.reshape(4, 2, D, BW)
    else:
        width = block_count * BW // 4
        shards = weights.reshape(block_count, D, -1, width).transpose(0, 2, 1, 3).reshape(4, 1, D, width)
    parts, width = shards.shape[1], shards.shape[3]

    def shard(shift, part):
        return lax.dynamic_slice(shards, ((plane + shift) % 4, part, 0, 0), (1, 1, D, width))[0, 0]

    rows_in = tokens.astype(F32)
    one_mine, one_other = gather_rows(rms_norm(rows_in, gains[0]).astype(BF16))

    moved = [
        [ring(shard(shift, part), shift) if shift else shard(0, part) for shift in range(4)] for part in range(parts)
    ]

    def kind_part(source, part, *others):
        at = sum((nothing(other) for other in others), plane)
        return lax.select_n(at, *(moved[part][(here - source) % 4] for here in range(4)))

    if parts == 2:
        w_attn = jnp.zeros((4, 2, D, BW), BF16)
        w_mlp = []
        for part, waits in enumerate(((), (one_mine[1],))):
            w_attn = gather_part_direct(kind_part(0, part, *waits), part, w_attn)
            later = (one_mine[2],) if part else ()
            w_mlp.append(gather_plane([kind_part(kind, part, *later) for kind in (1, 2, 3)]))
    else:
        w_attn = join(gather_plane([kind_part(0, 0)]))
        w_mlp = gather_plane([kind_part(kind, 0) for kind in (1, 2, 3)])
        w_mlp = jnp.stack([join(w_mlp[:, kind : kind + 1]) for kind in range(3)], axis=1)
        w_mlp = [w_mlp[:, :, 0], w_mlp[:, :, 1]]

    segment_parts = [segments]
    for _ in range(3):
        segment_parts.append(ring(segment_parts[-1]))
    segment_rows = jnp.concatenate(segment_parts, axis=0)
    length = segment_rows.shape[1]
    half = length // 2
    place = jnp.arange(length)
    place = jnp.where(core == 0, place, (place + half) % length)
    segment_rows = jnp.where(core == 0, segment_rows, jnp.roll(segment_rows, half, axis=1))
    allowed = (place[None, None, :] <= place[None, :, None]) & (
        segment_rows[:, None, :] == segment_rows[:, :, None]
    )
    bias = jnp.where(allowed, 0.0, NEG_LARGE).astype(F32)
    cosine, sine = rope_tables(place)

    query, key, value, context = ([None] * 4 for _ in range(4))
    mixed = Scatter()
    for s in (1, 2, 3, 0):
        query[s], key[s], value[s], context[s], *both = attn_forward(
            one_mine[s], one_other[s], w_attn, bias[s], cosine, sine, mixed.payloads[:1] if s == 3 else ()
        )
        mixed.add(s, *both)
    middle = rows_in + mixed.result
    two_mine, two_other = gather_rows(rms_norm(middle, gains[1]).astype(BF16))
    d_mine, d_other = gather_rows(hold(cotangent, two_mine[1]))

    hidden, d_gate, d_up, d_two, outward = ([None] * 4 for _ in range(5))
    d_normed = Scatter()
    for s in range(4):
        hidden[s], d_gate[s], d_up[s], *both = mlp_piece(
            two_mine[s], two_other[s], d_mine[s], d_other[s], *w_mlp, d_normed.payloads[:1] if s == 3 else ()
        )
        d_two[s], outward[s] = both[:2], both[2:]
        if s:
            d_normed.add(s, *d_two[s])
    mlp_grads = weight_products(
        interleave(two_mine, two_other),
        interleave(d_mine, d_other),
        (d_gate, d_up, hidden),
        (0, 0, 1),
        "mlp_products",
        d_normed.payloads[-1:],
    )
    d_normed.add(0, *d_two[0])
    d_normed_two = d_normed.result
    if parts == 2:
        mlp_share = [scatter_plane(mlp_grads[0]), scatter_plane_direct(mlp_grads[1])]
    else:
        mlp_grads = jnp.stack(mlp_grads, axis=2)
        mlp_share = [
            jnp.concatenate([scatter_plane(unjoin(mlp_grads[:, kind], width)) for kind in range(3)])
        ]

    d_output = cotangent.astype(F32)
    d_middle_norm, d_gain_two = rms_norm_back(middle, gains[1], d_normed_two)
    d_middle = d_output + d_middle_norm
    e_mine, e_other = gather_rows(d_middle.astype(BF16))
    d_query, d_key, d_value, d_one = ([None] * 4 for _ in range(4))
    for s in range(4):
        d_query[s], d_key[s], d_value[s], *both = attn_backward(
            e_mine[s], e_other[s], w_attn, bias[s], cosine, sine, query[s], key[s], value[s]
        )
        d_one[s] = both
    attn_grads = weight_products(
        interleave(one_mine, one_other),
        interleave(e_mine, e_other),
        (d_query, d_key, d_value, context),
        (0, 0, 0, 1),
        "attn_products",
    )
    if parts == 2:
        attn_share = [scatter_plane_direct(grads[0]) for grads in attn_grads]
    else:
        attn_share = [scatter_plane(unjoin(jnp.stack([grads[0] for grads in attn_grads], axis=1), width))[0]]

    results = ()
    for part in range(parts):

        def share_of(target):
            return lax.dynamic_index_in_dim(mlp_share[part], (target + 3) % 4 % 3, 0, keepdims=False)

        back = [share_of(plane)]
        for shift in (1, 2, 3):
            pairs = [(at, (at + shift) % 4) for at in range(4) if (at + shift) % 4]
            back.append(lax.ppermute(share_of((plane + shift) % 4), "z", pairs))
        mlp_back = jnp.stack([choose(*(back[(at - source) % 4] for at in range(4))) for source in range(4)])
        attn_back = [attn_share[part]]
        attn_back += [lax.ppermute(attn_share[part], "z", [(source, 0)]) for source in (1, 2, 3)]
        summed = jnp.where(plane == 0, jnp.stack(attn_back), mlp_back)
        if parts == 1:
            summed = summed.reshape(block_count, -1, D, width).transpose(0, 2, 1, 3).reshape(block_count, D, BW)
        results = muon(summed, momentum, weights, part, parts, results)
    weight_grads, new_momentum, new_weights = results

    d_normed_one = scatter_rows(d_one)
    d_rows_norm, d_gain_one = rms_norm_back(rows_in, gains[0], d_normed_one)
    input_grad = d_middle + d_rows_norm
    late = [(hold(mine, e_other[3]), hold(theirs, e_other[3])) for mine, theirs in outward]
    output = (middle + scatter_rows(late)).astype(BF16)
    gain_grads = everywhere(jnp.stack([d_gain_one, d_gain_two]))
    new_gain_first = BETA_FIRST * gain_first + (1.0 - BETA_FIRST) * gain_grads
    new_gain_second = BETA_SECOND * gain_second + (1.0 - BETA_SECOND) * gain_grads * gain_grads
    first_hat = new_gain_first / (1.0 - BETA_FIRST**STEP)
    second_hat = new_gain_second / (1.0 - BETA_SECOND**STEP)
    new_gains = gains - ADAM_RATE * first_hat / (jnp.sqrt(second_hat) + ADAM_EPS)
    return (
        output,
        input_grad,
        weight_grads,
        new_momentum,
        new_weights,
        new_gain_first,
        new_gain_second,
        new_gains,
    )


def solution(mesh):
    count = mesh.shape["dp"]
    fine = Mesh(
        np.asarray(mesh.devices).reshape(4, 4, count // 16, mesh.shape["tensor"]),
        ("z",) + PLANE,
    )
    every = ("z",) + PLANE
    in_specs = (
        P(every, None),
        P(every[:3], None),
        P(every, None, None),
        P(every, None, None),
        P(),
        P(),
        P(),
        P(every, None),
    )
    out_specs = (
        P(every, None),
        P(every, None),
        P(every, None, None),
        P(every, None, None),
        P(every, None, None),
        P(),
        P(),
        P(),
    )
    return jax.shard_map(local, mesh=fine, in_specs=in_specs, out_specs=out_specs, check_vma=False)
```

```python
import functools
import math

import jax
import jax.numpy as jnp
import numpy as np
from jax import lax
from jax.experimental import pallas as pl
from jax.experimental.pallas import tpu as pltpu
from jax.sharding import Mesh
from jax.sharding import PartitionSpec as P

D = 2048
FF = 8192
HD = 64
BW = 128
NS_ITERS = 5
STEP = 10

HIGHEST = lax.Precision.HIGHEST
ROPE_BASE = 130000.0
NORM_EPS = 1e-05
NEG_LARGE = -1e30
MOMENTUM_DECAY = 0.95
MUON_RATE = 0.25
COEFF_A = 3.4445
COEFF_B = -4.775
COEFF_C = 2.0315
BETA_FIRST = 0.9
BETA_SECOND = 0.95
ADAM_RATE = 1.0
ADAM_EPS = 1e-08

F32 = jnp.float32
BF16 = jnp.bfloat16
PLANE = ("m", "r", "tensor")
SWAP = [(0, 1), (1, 0)]
TILE = 256
SCORE_SCALE = 1.0 / math.sqrt(HD)


def rms_norm(values, gain):
    return values * lax.rsqrt(jnp.mean(values * values, axis=-1, keepdims=True) + NORM_EPS) * gain


def rms_norm_back(values, gain, grad):
    scale = lax.rsqrt(jnp.mean(values * values, axis=-1, keepdims=True) + NORM_EPS)
    scaled = gain * grad
    inner = jnp.mean(scaled * values, axis=-1, keepdims=True)
    gain_grad = jnp.sum(grad * values * scale, axis=0)
    return scale * scaled - values * (scale * scale * scale * inner), gain_grad


def rope_tables(place):
    exponent = jnp.arange(HD // 2).astype(F32) * (2.0 / HD)
    inverse = jnp.exp(-exponent * math.log(ROPE_BASE))
    angle = place.astype(F32)[:, None] * inverse[None, :]
    cosine, sine = jnp.cos(angle), jnp.sin(angle)
    heads = 2 * BW // HD
    return (
        jnp.tile(jnp.concatenate([cosine, cosine], axis=1), (1, heads)),
        jnp.tile(jnp.concatenate([-sine, sine], axis=1), (1, heads)),
    )


def dims(lhs, rhs):
    return (((lhs,), (rhs,)), ((), ()))


def mul(a, b):
    return lax.dot_general(a, b, dims(1, 0), preferred_element_type=F32)


def mul_bt(a, b):
    return lax.dot_general(a, b, dims(1, 1), preferred_element_type=F32)


def mul_at(a, b):
    return lax.dot_general(a, b, dims(0, 0), preferred_element_type=F32)


def side_by_side(ref, *index):
    return jnp.concatenate([ref[index + (0,)], ref[index + (1,)]], axis=-1)


def pair_rows(own_ref, other_ref):
    return jnp.concatenate([own_ref[...], other_ref[...]], axis=0)


def swap_halves(values):
    lane = lax.broadcasted_iota(jnp.int32, values.shape, 1)
    span = values.shape[1]
    ahead = pltpu.roll(values, span - HD // 2, 1)
    behind = pltpu.roll(values, HD // 2, 1)
    return jnp.where(lane % HD < HD // 2, ahead, behind)


def head_only(values, head):
    lane = lax.broadcasted_iota(jnp.int32, values.shape, 1)
    return jnp.where((lane >= head * HD) & (lane < (head + 1) * HD), values, jnp.zeros_like(values))


def head_probs(query, key, bias, head):
    scores = mul_bt(head_only(query, head), key) * SCORE_SCALE + bias
    weights = jnp.exp(scores - jnp.max(scores, axis=-1, keepdims=True))
    return weights / jnp.sum(weights, axis=-1, keepdims=True)


def attn_forward_kernel(
    own_ref, other_ref, w_ref, bias_ref, cos_ref, sin_ref, q_ref, k_ref, v_ref, c_ref, mine_ref, theirs_ref
):
    rows = pair_rows(own_ref, other_ref)
    cosine, sine = cos_ref[...], sin_ref[...]
    lin = mul(rows, side_by_side(w_ref, 0))
    query = (lin * cosine + swap_halves(lin) * sine).astype(BF16)
    lin = mul(rows, side_by_side(w_ref, 1))
    key = (lin * cosine + swap_halves(lin) * sine).astype(BF16)
    value = mul(rows, side_by_side(w_ref, 2)).astype(BF16)
    q_ref[...] = query
    k_ref[...] = key
    v_ref[...] = value
    context = jnp.zeros(query.shape, F32)
    for head in range(query.shape[1] // HD):
        probs = head_probs(query, key, bias_ref[...], head)
        context = context + mul(probs.astype(BF16), head_only(value, head))
    context = context.astype(BF16)
    c_ref[...] = context
    half = own_ref.shape[0]
    for tile in range(D // TILE):
        at = pl.ds(tile * TILE, TILE)
        w_out = jnp.concatenate([w_ref[3, 0, at, :], w_ref[3, 1, at, :]], axis=-1)
        mixed = mul_bt(context, w_out)
        mine_ref[:, at] = mixed[:half]
        theirs_ref[:, at] = mixed[half:].astype(BF16)


def attn_backward_kernel(
    own_ref, other_ref, w_ref, bias_ref, cos_ref, sin_ref, q_ref, k_ref, v_ref,
    dq_ref, dk_ref, dv_ref, mine_ref, theirs_ref,
):
    rows = pair_rows(own_ref, other_ref)
    query, key, value = q_ref[...], k_ref[...], v_ref[...]
    d_context = mul(rows, side_by_side(w_ref, 3)).astype(BF16)
    d_query = jnp.zeros(query.shape, F32)
    d_key = jnp.zeros(query.shape, F32)
    d_value = jnp.zeros(query.shape, F32)
    for head in range(query.shape[1] // HD):
        probs = head_probs(query, key, bias_ref[...], head)
        d_here = head_only(d_context, head)
        d_value = d_value + mul_at(probs.astype(BF16), d_here)
        d_probs = mul_bt(d_here, value)
        inner = jnp.sum(probs * d_probs, axis=-1, keepdims=True)
        d_scores = (probs * (d_probs - inner)).astype(BF16)
        d_query = d_query + mul(d_scores, head_only(key, head))
        d_key = d_key + mul_at(d_scores, head_only(query, head))
    cosine, sine = cos_ref[...], sin_ref[...]
    d_query = d_query * SCORE_SCALE
    d_key = d_key * SCORE_SCALE
    d_query = (d_query * cosine - swap_halves(d_query) * sine).astype(BF16)
    d_key = (d_key * cosine - swap_halves(d_key) * sine).astype(BF16)
    d_value = d_value.astype(BF16)
    dq_ref[...] = d_query
    dk_ref[...] = d_key
    dv_ref[...] = d_value
    half = own_ref.shape[0]
    for tile in range(D // TILE):
        at = pl.ds(tile * TILE, TILE)
        total = jnp.zeros((2 * half, TILE), F32)
        for matrix, columns in ((0, d_query), (1, d_key), (2, d_value)):
            w_here = jnp.concatenate([w_ref[matrix, 0, at, :], w_ref[matrix, 1, at, :]], axis=-1)
            total = total + mul_bt(columns, w_here)
        mine_ref[:, at] = total[:half]
        theirs_ref[:, at] = total[half:].astype(BF16)


def mlp_kernel(
    own_ref, other_ref, d_own_ref, d_other_ref, gate_even, gate_odd, up_even, up_odd, down_even, down_odd,
    hid_ref, dgate_ref, dup_ref, dn_mine_ref, dn_theirs_ref, out_mine_ref, out_theirs_ref, dn_acc, out_acc,
):
    step = pl.program_id(0)
    rows = pair_rows(own_ref, other_ref)
    d_rows = pair_rows(d_own_ref, d_other_ref)
    w_gate = jnp.concatenate([gate_even[...], gate_odd[...]], axis=-1)
    w_up = jnp.concatenate([up_even[...], up_odd[...]], axis=-1)
    w_down = jnp.concatenate([down_even[...], down_odd[...]], axis=-1)
    gate = mul(rows, w_gate)
    up = mul(rows, w_up)
    d_hidden = mul(d_rows, w_down)
    sigmoid = 1.0 / (1.0 + jnp.exp(-gate))
    silu = gate * sigmoid
    hidden = (silu * up).astype(BF16)
    d_gate = (d_hidden * up * sigmoid * (1.0 + gate * (1.0 - sigmoid))).astype(BF16)
    d_up = (d_hidden * silu).astype(BF16)
    hid_ref[...] = hidden
    dgate_ref[...] = d_gate
    dup_ref[...] = d_up

    @pl.when(step == 0)
    def _():
        dn_acc[...] = jnp.zeros_like(dn_acc)
        out_acc[...] = jnp.zeros_like(out_acc)

    dn_acc[...] += mul_bt(d_gate, w_gate) + mul_bt(d_up, w_up)
    out_acc[...] += mul_bt(hidden, w_down)

    @pl.when(step == pl.num_programs(0) - 1)
    def _():
        half = own_ref.shape[0]
        dn_mine_ref[...] = dn_acc[:half]
        dn_theirs_ref[...] = dn_acc[half:].astype(BF16)
        out_mine_ref[...] = out_acc[:half]
        out_theirs_ref[...] = out_acc[half:].astype(BF16)


def grads_kernel(sources, *refs):
    first, second = refs[:8], refs[8:16]
    columns = refs[16:-1]
    out_ref = refs[-1]
    row_sets = [jnp.concatenate([ref[...] for ref in part], axis=0) for part in (first, second)]
    for index, source in enumerate(sources):
        stacked = jnp.concatenate([ref[...] for ref in columns[4 * index : 4 * index + 4]], axis=0)
        grad = mul_at(row_sets[source], stacked).astype(BF16)
        for block in range(grad.shape[1] // BW):
            out_ref[block // 2, index, block % 2] = grad[:, block * BW : (block + 1) * BW]


def split(values):
    high = values.astype(BF16)
    return high, (values - high.astype(F32)).astype(BF16)


def mul_split(a, b):
    return mul(a[0], b[0]) + (mul(a[0], b[1]) + mul(a[1], b[0]))


def muon_kernel(grad_ref, momentum_ref, weight_ref, wg_ref, nm_ref, nw_ref, held, mixers):
    step = pl.program_id(0)
    count = held.shape[0]

    @pl.when(step < count)
    def _():
        grad = grad_ref[...].astype(F32)
        wg_ref[...] = grad
        block = MOMENTUM_DECAY * momentum_ref[...] + grad
        nm_ref[...] = block
        block = block * (1.0 / (jnp.sqrt(jnp.sum(block * block)) + 1e-07))
        held[step] = block
        high, low = split(block)
        cross = mul_at(high, low)
        mixers[step] = mul_at(high, high) + (cross + cross.T)

    @pl.when(step == count - 1)
    def _():
        row = lax.broadcasted_iota(jnp.int32, (BW, BW), 0)
        column = lax.broadcasted_iota(jnp.int32, (BW, BW), 1)
        eye = jnp.where(row == column, COEFF_A, 0.0).astype(F32)
        grams = [mixers[index] for index in range(count)]
        totals = [None] * count
        for turn in range(NS_ITERS):
            for index in range(count):
                pair = split(grams[index])
                mixer = eye + COEFF_B * grams[index] + COEFF_C * mul_split(pair, pair)
                mixed = split(mixer)
                if turn == 0:
                    totals[index] = mixer
                else:
                    totals[index] = mul_split(split(totals[index]), mixed)
                if turn < NS_ITERS - 1:
                    grams[index] = mul_split(split(mul_split(mixed, pair)), mixed)
        for index in range(count):
            mixers[index] = totals[index]

    @pl.when(step >= count)
    def _():
        at = step - count
        ortho = mul_split(split(held[at]), split(mixers[at]))
        nw_ref[...] = weight_ref[...].astype(F32) - (MUON_RATE * math.sqrt(D / BW)) * ortho


def deferred(kernel, inputs, unread):
    return lambda *refs: kernel(*refs[:inputs], *refs[inputs + unread :])


def unread_specs(after):
    return [pl.BlockSpec(memory_space=pl.ANY) for _ in after]


def params(mebibytes):
    return pltpu.CompilerParams(vmem_limit_bytes=mebibytes * 1024 * 1024)


def whole_specs(arrays):
    return [pl.BlockSpec(memory_space=pltpu.VMEM) for _ in arrays]


def shaped(shape, dtype):
    return jax.ShapeDtypeStruct(shape, dtype)


def attn_forward(own, other, w_attn, bias, cosine, sine, after=()):
    half = own.shape[0]
    span = w_attn.shape[1] * w_attn.shape[3]
    square = shaped((2 * half, span), BF16)
    args = (own, other, w_attn, bias, cosine, sine)
    return pl.pallas_call(
        deferred(attn_forward_kernel, len(args), len(after)),
        out_shape=(square,) * 4 + (shaped((half, D), F32), shaped((half, D), BF16)),
        in_specs=whole_specs(args) + unread_specs(after),
        out_specs=tuple(whole_specs(range(6))),
        compiler_params=params(40),
        cost_estimate=pl.CostEstimate(flops=1_300_000_000, bytes_accessed=9_000_000, transcendentals=262_144),
        name="attn_forward",
    )(*args, *after)


def attn_backward(own, other, w_attn, bias, cosine, sine, query, key, value):
    half = own.shape[0]
    square = shaped(query.shape, BF16)
    args = (own, other, w_attn, bias, cosine, sine, query, key, value)
    return pl.pallas_call(
        attn_backward_kernel,
        out_shape=(square,) * 3 + (shaped((half, D), F32), shaped((half, D), BF16)),
        in_specs=whole_specs(args),
        out_specs=tuple(whole_specs(range(5))),
        compiler_params=params(40),
        cost_estimate=pl.CostEstimate(flops=1_600_000_000, bytes_accessed=9_000_000, transcendentals=262_144),
        name="attn_backward",
    )(*args)


def mlp_piece(own, other, d_own, d_other, w_even, w_odd, after=()):
    half = own.shape[0]
    chunks = w_even.shape[0]
    wide = 2 * BW
    keep = pl.BlockSpec((half, D), lambda j: (0, 0))
    weights = [
        pl.BlockSpec((None, None, D, BW), lambda j, kind=kind: (j, kind, 0, 0)) for kind in (0, 0, 1, 1, 2, 2)
    ]
    column = pl.BlockSpec((2 * half, wide), lambda j: (0, j))
    columns = shaped((2 * half, chunks * wide), BF16)
    return pl.pallas_call(
        deferred(mlp_kernel, 10, len(after)),
        grid=(chunks,),
        out_shape=(columns,) * 3 + (shaped((half, D), F32), shaped((half, D), BF16)) * 2,
        in_specs=[keep] * 4 + weights + unread_specs(after),
        out_specs=(column,) * 3 + (keep,) * 4,
        scratch_shapes=[pltpu.VMEM((2 * half, D), F32)] * 2,
        compiler_params=params(40),
        cost_estimate=pl.CostEstimate(flops=6_400_000_000, bytes_accessed=20_000_000, transcendentals=262_144),
        name="mlp_piece",
    )(own, other, d_own, d_other, w_even, w_odd, w_even, w_odd, w_even, w_odd, *after)


def weight_products(first, second, column_sets, sources, name, after=()):
    half = first[0].shape[0]
    span = column_sets[0][0].shape[1]
    pairs = span // (2 * BW)
    row_spec = pl.BlockSpec((half, TILE), lambda i: (0, i))
    column_spec = pl.BlockSpec((2 * half, span), lambda i: (0, 0))
    flat = [piece for pieces in column_sets for piece in pieces]
    return pl.pallas_call(
        deferred(functools.partial(grads_kernel, sources), 16 + len(flat), len(after)),
        grid=(D // TILE,),
        out_shape=shaped((pairs, len(sources), 2, D, BW), BF16),
        in_specs=[row_spec] * 16 + [column_spec] * len(flat) + unread_specs(after),
        out_specs=pl.BlockSpec((pairs, len(sources), 2, TILE, BW), lambda i: (0, 0, 0, i, 0)),
        compiler_params=params(40),
        cost_estimate=pl.CostEstimate(
            flops=2 * 8 * half * D * span * len(sources), bytes_accessed=20_000_000, transcendentals=0
        ),
        name=name,
    )(*first, *second, *flat, *after)


def muon(grads, momentum, weights, offset, stride, begun=(), after=()):
    count = grads.shape[0]
    now = lambda i: jnp.minimum(i, count - 1)
    then = lambda i: jnp.maximum(i - count, 0)
    block = (None, D, BW)
    compact = pl.BlockSpec(block, lambda i: (now(i), 0, 0))
    early = pl.BlockSpec(block, lambda i: (stride * now(i) + offset, 0, 0))
    late = pl.BlockSpec(block, lambda i: (stride * then(i) + offset, 0, 0))
    return pl.pallas_call(
        deferred(muon_kernel, 3, len(begun) + len(after)),
        grid=(2 * count,),
        out_shape=(shaped(momentum.shape, F32),) * 3,
        in_specs=[compact, early, late] + unread_specs(begun) + unread_specs(after),
        out_specs=(early, early, late),
        input_output_aliases={3 + index: index for index in range(len(begun))},
        scratch_shapes=[pltpu.VMEM((count, D, BW), F32), pltpu.VMEM((count, BW, BW), F32)],
        compiler_params=params(40),
        cost_estimate=pl.CostEstimate(flops=1_000_000_000 * count, bytes_accessed=5_500_000 * count, transcendentals=0),
        name="muon",
    )(grads, momentum, weights, *begun, *after)


def mirror(step):
    return [(place, place ^ step) for place in range(4)]


def ring(value, step=1):
    return lax.ppermute(value, "z", [(place, (place + step) % 4) for place in range(4)])


def swap(value):
    return lax.ppermute(value, "tensor", SWAP)


def nothing(value):
    first = value[(0,) * value.ndim].astype(F32)
    return (first * 0.0).astype(jnp.int32)


def hold(value, *others):
    zero = sum((nothing(other) for other in others), jnp.int32(0))
    return value + zero.astype(value.dtype)


def gather_rows(rows):
    mine = [rows]
    for _ in range(3):
        mine.append(ring(mine[-1]))
    return mine, [swap(part) for part in mine]


def scatter_rows(pieces):
    scatter = Scatter()
    for step in (1, 2, 3, 0):
        scatter.add(step, *pieces[step])
    return scatter.result


def gather_rows_at_once(rows):
    plane = lax.axis_index("z")
    mine = lax.all_gather(rows, "z", axis=0, tiled=False)
    other = swap(mine)
    pick = lambda stack, s: lax.dynamic_index_in_dim(stack, (plane + 4 - s) % 4, 0, keepdims=False)
    return [pick(mine, s) for s in range(4)], [pick(other, s) for s in range(4)]


def gather_rows_direct(rows):
    mine = [rows] + [ring(rows, shift) for shift in (1, 2, 3)]
    return mine, [swap(part) for part in mine]


class Scatter:
    def __init__(self):
        self.moving = self.result = None
        self.payloads = []

    def add(self, step, mine, theirs):
        total = mine + swap(theirs).astype(F32)
        if self.moving is not None:
            total = total + self.moving.astype(F32)
        if step:
            self.payloads.append(total.astype(BF16))
            self.moving = ring(self.payloads[-1])
        else:
            self.result = total


def everywhere(value):
    value = value + swap(value)
    for axis in ("m", "z"):
        for step in (1, 2):
            value = value + lax.ppermute(value, axis, mirror(step))
    if lax.axis_size("r") > 1:
        value = lax.psum(value, "r")
    return value


def join(parts):
    if parts.shape[0] == 4:
        return parts
    width = parts.shape[3]
    parts = parts.reshape(4, 2, -1, D, width).transpose(0, 1, 3, 2, 4)
    return parts.reshape(4, 2, D, BW)


def unjoin(grads, width):
    if width == BW:
        return grads
    grads = grads.reshape(4, 2, D, -1, width).transpose(0, 1, 3, 2, 4)
    return grads.reshape(-1, 1, D, width)


def gather_plane(parts):
    return lax.all_gather(jnp.stack(parts), ("m", "r"), axis=0, tiled=False)


def gather_part_direct(part, index, result):
    chip = lax.axis_index("m")
    result = lax.dynamic_update_slice(result, part[None, None], (chip, index, 0, 0))
    for step in (1, 2, 3):
        got = lax.ppermute(part, "m", mirror(step))
        result = lax.dynamic_update_slice(result, got[None, None], (chip ^ step, index, 0, 0))
    return result


def scatter_plane(grads):
    share = lax.psum_scatter(
        grads.reshape(grads.shape[0], -1, grads.shape[3]), ("m", "r"), scatter_dimension=0, tiled=False
    )
    return share.reshape(grads.shape[1:])


def scatter_plane_direct(grads):
    chip = lax.axis_index("m")

    def share_for(step):
        return lax.dynamic_index_in_dim(grads, chip ^ step, 0, keepdims=False)

    total = share_for(0).astype(F32)
    for step in (1, 2, 3):
        total = total + lax.ppermute(share_for(step), "m", mirror(step)).astype(F32)
    return total.astype(BF16)


def interleave(mine, other):
    return [rows for pair in zip(mine, other) for rows in pair]


def local(tokens, segments, weights, momentum, gains, gain_first, gain_second, cotangent):
    plane = lax.axis_index("z")
    core = lax.axis_index("tensor")
    block_count = weights.shape[0]

    def choose(*cases):
        return lax.select_n(plane, *cases)

    if block_count == 8:
        shards = weights.reshape(4, 2, D, BW)
    else:
        width = block_count * BW // 4
        shards = weights.reshape(block_count, D, -1, width).transpose(0, 2, 1, 3).reshape(4, 1, D, width)
    parts, width = shards.shape[1], shards.shape[3]

    def shard(shift, part):
        return lax.dynamic_slice(shards, ((plane + shift) % 4, part, 0, 0), (1, 1, D, width))[0, 0]

    rows_in = tokens.astype(F32)
    one_mine, one_other = gather_rows_at_once(rms_norm(rows_in, gains[0]).astype(BF16))

    moved = [
        [ring(shard(shift, part), shift) if shift else shard(0, part) for shift in range(4)] for part in range(parts)
    ]

    def kind_part(source, part, *others):
        at = sum((nothing(other) for other in others), plane)
        return lax.select_n(at, *(moved[part][(here - source) % 4] for here in range(4)))

    if parts == 2:
        mlp_parts = [[kind_part(kind, 0) for kind in (1, 2, 3)]]
        w_attn = gather_part_direct(kind_part(0, 0), 0, jnp.zeros((4, 2, D, BW), BF16))
        waits = (w_attn, mlp_parts[0][0], one_mine[1])
        w_attn = gather_part_direct(kind_part(0, 1, *waits), 1, w_attn)
        mlp_parts.append([kind_part(kind, 1) for kind in (1, 2, 3)])
        begun = [mlp_parts[1][0]]
        w_mlp = [gather_plane(kinds) for kinds in mlp_parts]
    else:
        w_attn = join(gather_plane([kind_part(0, 0)]))
        w_mlp = gather_plane([kind_part(kind, 0) for kind in (1, 2, 3)])
        w_mlp = jnp.stack([join(w_mlp[:, kind : kind + 1]) for kind in range(3)], axis=1)
        w_mlp = [w_mlp[:, :, 0], w_mlp[:, :, 1]]
        begun = []
    d_mine, d_other = gather_rows_direct(hold(cotangent, *begun))

    segment_parts = [segments] + [ring(segments, shift) for shift in (1, 2, 3)]
    segment_rows = jnp.concatenate(segment_parts, axis=0)
    length = segment_rows.shape[1]
    half = length // 2
    place = jnp.arange(length)
    place = jnp.where(core == 0, place, (place + half) % length)
    segment_rows = jnp.where(core == 0, segment_rows, jnp.roll(segment_rows, half, axis=1))
    allowed = (place[None, None, :] <= place[None, :, None]) & (
        segment_rows[:, None, :] == segment_rows[:, :, None]
    )
    bias = jnp.where(allowed, 0.0, NEG_LARGE).astype(F32)
    cosine, sine = rope_tables(place)

    query, key, value, context = ([None] * 4 for _ in range(4))
    mixed = Scatter()
    for s in (1, 2, 3, 0):
        query[s], key[s], value[s], context[s], *both = attn_forward(
            one_mine[s], one_other[s], w_attn, bias[s], cosine, sine, mixed.payloads[:1] if s == 3 else begun if s == 1 else ()
        )
        mixed.add(s, *both)
    middle = rows_in + mixed.result
    two_mine, two_other = gather_rows(hold(rms_norm(middle, gains[1]), d_mine[1], d_mine[3]).astype(BF16))

    hidden, d_gate, d_up, d_two, outward = ([None] * 4 for _ in range(5))
    d_normed = Scatter()
    for s in range(4):
        hidden[s], d_gate[s], d_up[s], *both = mlp_piece(
            two_mine[s], two_other[s], d_mine[s], d_other[s], *w_mlp, d_normed.payloads[:1] if s == 3 else ()
        )
        d_two[s], outward[s] = both[:2], both[2:]
        if s:
            d_normed.add(s, *d_two[s])
    mlp_grads = weight_products(
        interleave(two_mine, two_other),
        interleave(d_mine, d_other),
        (d_gate, d_up, hidden),
        (0, 0, 1),
        "mlp_products",
        d_normed.payloads[-1:],
    )
    d_normed.add(0, *d_two[0])
    d_normed_two = d_normed.result
    if parts == 2:
        mlp_share = scatter_plane(mlp_grads.reshape(4, 6, D, BW)).reshape(3, 2, D, BW)
    else:
        mlp_share = jnp.stack([scatter_plane(unjoin(mlp_grads[:, kind], width)) for kind in range(3)])

    d_output = cotangent.astype(F32)
    d_middle_norm, d_gain_two = rms_norm_back(middle, gains[1], d_normed_two)
    d_middle = d_output + d_middle_norm
    e_mine, e_other = gather_rows(d_middle.astype(BF16))
    d_query, d_key, d_value, d_one = ([None] * 4 for _ in range(4))
    for s in range(4):
        d_query[s], d_key[s], d_value[s], *both = attn_backward(
            e_mine[s], e_other[s], w_attn, bias[s], cosine, sine, query[s], key[s], value[s]
        )
        d_one[s] = both
    attn_grads = weight_products(
        interleave(one_mine, one_other),
        interleave(e_mine, e_other),
        (d_query, d_key, d_value, context),
        (0, 0, 0, 1),
        "attn_products",
    )
    if parts == 2:
        attn_share = [scatter_plane_direct(attn_grads[0][:, part]) for part in range(2)]
    else:
        attn_share = [scatter_plane(unjoin(attn_grads[0], width))[0]]

    d_normed_one = scatter_rows(d_one)
    d_rows_norm, d_gain_one = rms_norm_back(rows_in, gains[0], d_normed_one)
    input_grad = d_middle + d_rows_norm
    late = [(hold(mine, e_other[3]), hold(theirs, e_other[3])) for mine, theirs in outward]
    output = (middle + scatter_rows(late)).astype(BF16)
    gain_grads = everywhere(jnp.stack([d_gain_one, d_gain_two]))

    results = ()
    for part in range(parts):
        shares = jnp.stack([attn_share[part]] + [mlp_share[kind, part] for kind in range(3)])
        at = plane + nothing(output) if part == 0 else plane

        def share_of(shift):
            return lax.dynamic_index_in_dim(shares, (at + shift) % 4, 0, keepdims=False)

        back = [share_of(0)] + [ring(share_of(shift), shift) for shift in (1, 2, 3)]
        summed = jnp.stack([choose(*(back[(here - source) % 4] for here in range(4))) for source in range(4)])
        if parts == 1:
            summed = summed.reshape(block_count, -1, D, width).transpose(0, 2, 1, 3).reshape(block_count, D, BW)
        results = muon(summed, momentum, weights, part, parts, results, (gain_grads,) if part == 0 else ())
    weight_grads, new_momentum, new_weights = results

    new_gain_first = BETA_FIRST * gain_first + (1.0 - BETA_FIRST) * gain_grads
    new_gain_second = BETA_SECOND * gain_second + (1.0 - BETA_SECOND) * gain_grads * gain_grads
    first_hat = new_gain_first / (1.0 - BETA_FIRST**STEP)
    second_hat = new_gain_second / (1.0 - BETA_SECOND**STEP)
    new_gains = gains - ADAM_RATE * first_hat / (jnp.sqrt(second_hat) + ADAM_EPS)
    return (
        output,
        input_grad,
        weight_grads,
        new_momentum,
        new_weights,
        new_gain_first,
        new_gain_second,
        new_gains,
    )


def solution(mesh):
    count = mesh.shape["dp"]
    fine = Mesh(
        np.asarray(mesh.devices).reshape(4, 4, count // 16, mesh.shape["tensor"]),
        ("z",) + PLANE,
    )
    every = ("z",) + PLANE
    in_specs = (
        P(every, None),
        P(every[:3], None),
        P(every, None, None),
        P(every, None, None),
        P(),
        P(),
        P(),
        P(every, None),
    )
    out_specs = (
        P(every, None),
        P(every, None),
        P(every, None, None),
        P(every, None, None),
        P(every, None, None),
        P(),
        P(),
        P(),
    )
    return jax.shard_map(local, mesh=fine, in_specs=in_specs, out_specs=out_specs, check_vma=False)
```

```python
import functools
import math

import jax
import jax.numpy as jnp
import numpy as np
from jax import lax
from jax.experimental import pallas as pl
from jax.experimental.pallas import tpu as pltpu
from jax.sharding import Mesh
from jax.sharding import PartitionSpec as P

D = 2048
FF = 8192
HD = 64
BW = 128
NS_ITERS = 5
STEP = 10

HIGHEST = lax.Precision.HIGHEST
ROPE_BASE = 130000.0
NORM_EPS = 1e-05
NEG_LARGE = -1e30
MOMENTUM_DECAY = 0.95
MUON_RATE = 0.25
COEFF_A = 3.4445
COEFF_B = -4.775
COEFF_C = 2.0315
BETA_FIRST = 0.9
BETA_SECOND = 0.95
ADAM_RATE = 1.0
ADAM_EPS = 1e-08

F32 = jnp.float32
BF16 = jnp.bfloat16
PLANE = ("m", "r", "tensor")
SWAP = [(0, 1), (1, 0)]
TILE = 256
SCORE_SCALE = 1.0 / math.sqrt(HD)


def rms_norm(values, gain):
    return values * lax.rsqrt(jnp.mean(values * values, axis=-1, keepdims=True) + NORM_EPS) * gain


def rms_norm_back(values, gain, grad):
    scale = lax.rsqrt(jnp.mean(values * values, axis=-1, keepdims=True) + NORM_EPS)
    scaled = gain * grad
    inner = jnp.mean(scaled * values, axis=-1, keepdims=True)
    gain_grad = jnp.sum(grad * values * scale, axis=0)
    return scale * scaled - values * (scale * scale * scale * inner), gain_grad


def rope_tables(place):
    exponent = jnp.arange(HD // 2).astype(F32) * (2.0 / HD)
    inverse = jnp.exp(-exponent * math.log(ROPE_BASE))
    angle = place.astype(F32)[:, None] * inverse[None, :]
    cosine, sine = jnp.cos(angle), jnp.sin(angle)
    heads = 2 * BW // HD
    return (
        jnp.tile(jnp.concatenate([cosine, cosine], axis=1), (1, heads)),
        jnp.tile(jnp.concatenate([-sine, sine], axis=1), (1, heads)),
    )


def dims(lhs, rhs):
    return (((lhs,), (rhs,)), ((), ()))


def mul(a, b):
    return lax.dot_general(a, b, dims(1, 0), preferred_element_type=F32)


def mul_bt(a, b):
    return lax.dot_general(a, b, dims(1, 1), preferred_element_type=F32)


def mul_at(a, b):
    return lax.dot_general(a, b, dims(0, 0), preferred_element_type=F32)


def side_by_side(ref, *index):
    return jnp.concatenate([ref[index + (0,)], ref[index + (1,)]], axis=-1)


def pair_rows(own_ref, other_ref):
    return jnp.concatenate([own_ref[...], other_ref[...]], axis=0)


def swap_halves(values):
    lane = lax.broadcasted_iota(jnp.int32, values.shape, 1)
    span = values.shape[1]
    ahead = pltpu.roll(values, span - HD // 2, 1)
    behind = pltpu.roll(values, HD // 2, 1)
    return jnp.where(lane % HD < HD // 2, ahead, behind)


def head_only(values, head):
    lane = lax.broadcasted_iota(jnp.int32, values.shape, 1)
    return jnp.where((lane >= head * HD) & (lane < (head + 1) * HD), values, jnp.zeros_like(values))


def head_probs(query, key, bias, head):
    scores = mul_bt(head_only(query, head), key) * SCORE_SCALE + bias
    weights = jnp.exp(scores - jnp.max(scores, axis=-1, keepdims=True))
    return weights / jnp.sum(weights, axis=-1, keepdims=True)


def attn_forward_kernel(
    own_ref, other_ref, w_ref, bias_ref, cos_ref, sin_ref, q_ref, k_ref, v_ref, c_ref, mine_ref, theirs_ref
):
    rows = pair_rows(own_ref, other_ref)
    cosine, sine = cos_ref[...], sin_ref[...]
    lin = mul(rows, side_by_side(w_ref, 0))
    query = (lin * cosine + swap_halves(lin) * sine).astype(BF16)
    lin = mul(rows, side_by_side(w_ref, 1))
    key = (lin * cosine + swap_halves(lin) * sine).astype(BF16)
    value = mul(rows, side_by_side(w_ref, 2)).astype(BF16)
    q_ref[...] = query
    k_ref[...] = key
    v_ref[...] = value
    context = jnp.zeros(query.shape, F32)
    for head in range(query.shape[1] // HD):
        probs = head_probs(query, key, bias_ref[...], head)
        context = context + mul(probs.astype(BF16), head_only(value, head))
    context = context.astype(BF16)
    c_ref[...] = context
    half = own_ref.shape[0]
    for tile in range(D // TILE):
        at = pl.ds(tile * TILE, TILE)
        w_out = jnp.concatenate([w_ref[3, 0, at, :], w_ref[3, 1, at, :]], axis=-1)
        mixed = mul_bt(context, w_out)
        mine_ref[:, at] = mixed[:half]
        theirs_ref[:, at] = mixed[half:].astype(BF16)


def attn_backward_kernel(
    own_ref, other_ref, w_ref, bias_ref, cos_ref, sin_ref, q_ref, k_ref, v_ref,
    dq_ref, dk_ref, dv_ref, mine_ref, theirs_ref,
):
    rows = pair_rows(own_ref, other_ref)
    query, key, value = q_ref[...], k_ref[...], v_ref[...]
    d_context = mul(rows, side_by_side(w_ref, 3)).astype(BF16)
    d_query = jnp.zeros(query.shape, F32)
    d_key = jnp.zeros(query.shape, F32)
    d_value = jnp.zeros(query.shape, F32)
    for head in range(query.shape[1] // HD):
        probs = head_probs(query, key, bias_ref[...], head)
        d_here = head_only(d_context, head)
        d_value = d_value + mul_at(probs.astype(BF16), d_here)
        d_probs = mul_bt(d_here, value)
        inner = jnp.sum(probs * d_probs, axis=-1, keepdims=True)
        d_scores = (probs * (d_probs - inner)).astype(BF16)
        d_query = d_query + mul(d_scores, head_only(key, head))
        d_key = d_key + mul_at(d_scores, head_only(query, head))
    cosine, sine = cos_ref[...], sin_ref[...]
    d_query = d_query * SCORE_SCALE
    d_key = d_key * SCORE_SCALE
    d_query = (d_query * cosine - swap_halves(d_query) * sine).astype(BF16)
    d_key = (d_key * cosine - swap_halves(d_key) * sine).astype(BF16)
    d_value = d_value.astype(BF16)
    dq_ref[...] = d_query
    dk_ref[...] = d_key
    dv_ref[...] = d_value
    half = own_ref.shape[0]
    for tile in range(D // TILE):
        at = pl.ds(tile * TILE, TILE)
        total = jnp.zeros((2 * half, TILE), F32)
        for matrix, columns in ((0, d_query), (1, d_key), (2, d_value)):
            w_here = jnp.concatenate([w_ref[matrix, 0, at, :], w_ref[matrix, 1, at, :]], axis=-1)
            total = total + mul_bt(columns, w_here)
        mine_ref[:, at] = total[:half]
        theirs_ref[:, at] = total[half:].astype(BF16)


def mlp_kernel(
    own_ref, other_ref, d_own_ref, d_other_ref, gate_even, gate_odd, up_even, up_odd, down_even, down_odd,
    hid_ref, dgate_ref, dup_ref, dn_mine_ref, dn_theirs_ref, out_mine_ref, out_theirs_ref, dn_acc, out_acc,
):
    step = pl.program_id(0)
    rows = pair_rows(own_ref, other_ref)
    d_rows = pair_rows(d_own_ref, d_other_ref)
    w_gate = jnp.concatenate([gate_even[...], gate_odd[...]], axis=-1)
    w_up = jnp.concatenate([up_even[...], up_odd[...]], axis=-1)
    w_down = jnp.concatenate([down_even[...], down_odd[...]], axis=-1)
    gate = mul(rows, w_gate)
    up = mul(rows, w_up)
    d_hidden = mul(d_rows, w_down)
    sigmoid = 1.0 / (1.0 + jnp.exp(-gate))
    silu = gate * sigmoid
    hidden = (silu * up).astype(BF16)
    d_gate = (d_hidden * up * sigmoid * (1.0 + gate * (1.0 - sigmoid))).astype(BF16)
    d_up = (d_hidden * silu).astype(BF16)
    hid_ref[...] = hidden
    dgate_ref[...] = d_gate
    dup_ref[...] = d_up

    @pl.when(step == 0)
    def _():
        dn_acc[...] = jnp.zeros_like(dn_acc)
        out_acc[...] = jnp.zeros_like(out_acc)

    dn_acc[...] += mul_bt(d_gate, w_gate) + mul_bt(d_up, w_up)
    out_acc[...] += mul_bt(hidden, w_down)

    @pl.when(step == pl.num_programs(0) - 1)
    def _():
        half = own_ref.shape[0]
        dn_mine_ref[...] = dn_acc[:half]
        dn_theirs_ref[...] = dn_acc[half:].astype(BF16)
        out_mine_ref[...] = out_acc[:half]
        out_theirs_ref[...] = out_acc[half:].astype(BF16)


def grads_kernel(sources, *refs):
    first, second = refs[:8], refs[8:16]
    columns = refs[16:-2]
    outs = refs[-2:]
    row_sets = [jnp.concatenate([ref[...] for ref in part], axis=0) for part in (first, second)]
    for index, source in enumerate(sources):
        stacked = jnp.concatenate([ref[...] for ref in columns[4 * index : 4 * index + 4]], axis=0)
        grad = mul_at(row_sets[source], stacked).astype(BF16)
        for block in range(grad.shape[1] // BW):
            outs[block % 2][block // 2, index] = grad[:, block * BW : (block + 1) * BW]


def split(values):
    high = values.astype(BF16)
    return high, (values - high.astype(F32)).astype(BF16)


def mul_split(a, b):
    return mul(a[0], b[0]) + (mul(a[0], b[1]) + mul(a[1], b[0]))


def muon_kernel(grad_ref, momentum_ref, weight_ref, wg_ref, nm_ref, nw_ref, held, mixers):
    step = pl.program_id(0)
    count = held.shape[0]

    @pl.when(step < count)
    def _():
        grad = grad_ref[...].astype(F32)
        wg_ref[...] = grad
        block = MOMENTUM_DECAY * momentum_ref[...] + grad
        nm_ref[...] = block
        block = block * (1.0 / (jnp.sqrt(jnp.sum(block * block)) + 1e-07))
        held[step] = block
        high, low = split(block)
        cross = mul_at(high, low)
        mixers[step] = mul_at(high, high) + (cross + cross.T)

    @pl.when(step == count - 1)
    def _():
        row = lax.broadcasted_iota(jnp.int32, (BW, BW), 0)
        column = lax.broadcasted_iota(jnp.int32, (BW, BW), 1)
        eye = jnp.where(row == column, COEFF_A, 0.0).astype(F32)
        grams = [mixers[index] for index in range(count)]
        totals = [None] * count
        for turn in range(NS_ITERS):
            for index in range(count):
                pair = split(grams[index])
                mixer = eye + COEFF_B * grams[index] + COEFF_C * mul_split(pair, pair)
                mixed = split(mixer)
                if turn == 0:
                    totals[index] = mixer
                else:
                    totals[index] = mul_split(split(totals[index]), mixed)
                if turn < NS_ITERS - 1:
                    grams[index] = mul_split(split(mul_split(mixed, pair)), mixed)
        for index in range(count):
            mixers[index] = totals[index]

    @pl.when(step >= count)
    def _():
        at = step - count
        ortho = mul_split(split(held[at]), split(mixers[at]))
        nw_ref[...] = weight_ref[...].astype(F32) - (MUON_RATE * math.sqrt(D / BW)) * ortho


def deferred(kernel, inputs, unread):
    return lambda *refs: kernel(*refs[:inputs], *refs[inputs + unread :])


def unread_specs(after):
    return [pl.BlockSpec(memory_space=pl.ANY) for _ in after]


def params(mebibytes):
    return pltpu.CompilerParams(vmem_limit_bytes=mebibytes * 1024 * 1024)


def whole_specs(arrays):
    return [pl.BlockSpec(memory_space=pltpu.VMEM) for _ in arrays]


def shaped(shape, dtype):
    return jax.ShapeDtypeStruct(shape, dtype)


def attn_forward(own, other, w_attn, bias, cosine, sine, after=()):
    half = own.shape[0]
    span = w_attn.shape[1] * w_attn.shape[3]
    square = shaped((2 * half, span), BF16)
    args = (own, other, w_attn, bias, cosine, sine)
    return pl.pallas_call(
        deferred(attn_forward_kernel, len(args), len(after)),
        out_shape=(square,) * 4 + (shaped((half, D), F32), shaped((half, D), BF16)),
        in_specs=whole_specs(args) + unread_specs(after),
        out_specs=tuple(whole_specs(range(6))),
        compiler_params=params(40),
        cost_estimate=pl.CostEstimate(flops=1_300_000_000, bytes_accessed=9_000_000, transcendentals=262_144),
        name="attn_forward",
    )(*args, *after)


def attn_backward(own, other, w_attn, bias, cosine, sine, query, key, value):
    half = own.shape[0]
    square = shaped(query.shape, BF16)
    args = (own, other, w_attn, bias, cosine, sine, query, key, value)
    return pl.pallas_call(
        attn_backward_kernel,
        out_shape=(square,) * 3 + (shaped((half, D), F32), shaped((half, D), BF16)),
        in_specs=whole_specs(args),
        out_specs=tuple(whole_specs(range(5))),
        compiler_params=params(40),
        cost_estimate=pl.CostEstimate(flops=1_600_000_000, bytes_accessed=9_000_000, transcendentals=262_144),
        name="attn_backward",
    )(*args)


def mlp_piece(own, other, d_own, d_other, w_even, w_odd, after=()):
    half = own.shape[0]
    chunks = w_even.shape[0]
    wide = 2 * BW
    keep = pl.BlockSpec((half, D), lambda j: (0, 0))
    weights = [
        pl.BlockSpec((None, None, D, BW), lambda j, kind=kind: (j, kind, 0, 0)) for kind in (0, 0, 1, 1, 2, 2)
    ]
    column = pl.BlockSpec((2 * half, wide), lambda j: (0, j))
    columns = shaped((2 * half, chunks * wide), BF16)
    return pl.pallas_call(
        deferred(mlp_kernel, 10, len(after)),
        grid=(chunks,),
        out_shape=(columns,) * 3 + (shaped((half, D), F32), shaped((half, D), BF16)) * 2,
        in_specs=[keep] * 4 + weights + unread_specs(after),
        out_specs=(column,) * 3 + (keep,) * 4,
        scratch_shapes=[pltpu.VMEM((2 * half, D), F32)] * 2,
        compiler_params=params(40),
        cost_estimate=pl.CostEstimate(flops=6_400_000_000, bytes_accessed=20_000_000, transcendentals=262_144),
        name="mlp_piece",
    )(own, other, d_own, d_other, w_even, w_odd, w_even, w_odd, w_even, w_odd, *after)


def weight_products(first, second, column_sets, sources, name, after=()):
    half = first[0].shape[0]
    span = column_sets[0][0].shape[1]
    pairs = span // (2 * BW)
    row_spec = pl.BlockSpec((half, TILE), lambda i: (0, i))
    column_spec = pl.BlockSpec((2 * half, span), lambda i: (0, 0))
    flat = [piece for pieces in column_sets for piece in pieces]
    return pl.pallas_call(
        deferred(functools.partial(grads_kernel, sources), 16 + len(flat), len(after)),
        grid=(D // TILE,),
        out_shape=(shaped((pairs, len(sources), D, BW), BF16),) * 2,
        in_specs=[row_spec] * 16 + [column_spec] * len(flat) + unread_specs(after),
        out_specs=(pl.BlockSpec((pairs, len(sources), TILE, BW), lambda i: (0, 0, i, 0)),) * 2,
        compiler_params=params(40),
        cost_estimate=pl.CostEstimate(
            flops=2 * 8 * half * D * span * len(sources), bytes_accessed=20_000_000, transcendentals=0
        ),
        name=name,
    )(*first, *second, *flat, *after)


def muon(grads, momentum, weights, offset, stride, begun=(), after=()):
    count = grads.shape[0]
    now = lambda i: jnp.minimum(i, count - 1)
    then = lambda i: jnp.maximum(i - count, 0)
    block = (None, D, BW)
    compact = pl.BlockSpec(block, lambda i: (now(i), 0, 0))
    early = pl.BlockSpec(block, lambda i: (stride * now(i) + offset, 0, 0))
    late = pl.BlockSpec(block, lambda i: (stride * then(i) + offset, 0, 0))
    return pl.pallas_call(
        deferred(muon_kernel, 3, len(begun) + len(after)),
        grid=(2 * count,),
        out_shape=(shaped(momentum.shape, F32),) * 3,
        in_specs=[compact, early, late] + unread_specs(begun) + unread_specs(after),
        out_specs=(early, early, late),
        input_output_aliases={3 + index: index for index in range(len(begun))},
        scratch_shapes=[pltpu.VMEM((count, D, BW), F32), pltpu.VMEM((count, BW, BW), F32)],
        compiler_params=params(40),
        cost_estimate=pl.CostEstimate(flops=1_000_000_000 * count, bytes_accessed=5_500_000 * count, transcendentals=0),
        name="muon",
    )(grads, momentum, weights, *begun, *after)


def mirror(step):
    return [(place, place ^ step) for place in range(4)]


def ring(value, step=1):
    return lax.ppermute(value, "z", [(place, (place + step) % 4) for place in range(4)])


def swap(value):
    return lax.ppermute(value, "tensor", SWAP)


def nothing(value):
    first = value[(0,) * value.ndim].astype(F32)
    return (first * 0.0).astype(jnp.int32)


def hold(value, *others):
    zero = sum((nothing(other) for other in others), jnp.int32(0))
    return value + zero.astype(value.dtype)


def gather_rows(rows):
    mine = [rows]
    for _ in range(3):
        mine.append(ring(mine[-1]))
    return mine, [swap(part) for part in mine]


def scatter_rows(pieces):
    scatter = Scatter()
    for step in (1, 2, 3, 0):
        scatter.add(step, *pieces[step])
    return scatter.result


def gather_rows_at_once(rows):
    plane = lax.axis_index("z")
    mine = lax.all_gather(rows, "z", axis=0, tiled=False)
    other = swap(mine)
    pick = lambda stack, s: lax.dynamic_index_in_dim(stack, (plane + 4 - s) % 4, 0, keepdims=False)
    return [pick(mine, s) for s in range(4)], [pick(other, s) for s in range(4)]


def gather_rows_direct(rows):
    mine = [rows] + [ring(rows, shift) for shift in (1, 2, 3)]
    return mine, [swap(part) for part in mine]


class Scatter:
    def __init__(self):
        self.moving = self.result = None
        self.payloads = []

    def add(self, step, mine, theirs):
        total = mine + swap(theirs).astype(F32)
        if self.moving is not None:
            total = total + self.moving.astype(F32)
        if step:
            self.payloads.append(total.astype(BF16))
            self.moving = ring(self.payloads[-1])
        else:
            self.result = total


def everywhere(value):
    value = value + swap(value)
    for axis in ("m", "z"):
        for step in (1, 2):
            value = value + lax.ppermute(value, axis, mirror(step))
    if lax.axis_size("r") > 1:
        value = lax.psum(value, "r")
    return value


def join(parts):
    if parts.shape[0] == 4:
        return parts
    width = parts.shape[3]
    parts = parts.reshape(4, 2, -1, D, width).transpose(0, 1, 3, 2, 4)
    return parts.reshape(4, 2, D, BW)


def unjoin(grads, width):
    if width == BW:
        return grads
    grads = grads.reshape(4, 2, D, -1, width).transpose(0, 1, 3, 2, 4)
    return grads.reshape(-1, 1, D, width)


def gather_plane(parts):
    return lax.all_gather(jnp.stack(parts), ("m", "r"), axis=0, tiled=False)


def gather_part_direct(part, index, result):
    chip = lax.axis_index("m")
    result = lax.dynamic_update_slice(result, part[None, None], (chip, index, 0, 0))
    for step in (1, 2, 3):
        got = lax.ppermute(part, "m", mirror(step))
        result = lax.dynamic_update_slice(result, got[None, None], (chip ^ step, index, 0, 0))
    return result


def scatter_plane(grads):
    share = lax.psum_scatter(
        grads.reshape(grads.shape[0], -1, grads.shape[3]), ("m", "r"), scatter_dimension=0, tiled=False
    )
    return share.reshape(grads.shape[1:])


def scatter_plane_direct(grads, *others):
    chip = lax.axis_index("m")
    zero = sum((nothing(other) for other in others), jnp.int32(0)).astype(F32)

    def share_for(step):
        return lax.dynamic_index_in_dim(grads, chip ^ step, 0, keepdims=False)

    total = share_for(0).astype(F32) + zero
    for step in (1, 2, 3):
        total = total + lax.ppermute(share_for(step), "m", mirror(step)).astype(F32)
    return total.astype(BF16)


def interleave(mine, other):
    return [rows for pair in zip(mine, other) for rows in pair]


def local(tokens, segments, weights, momentum, gains, gain_first, gain_second, cotangent):
    plane = lax.axis_index("z")
    core = lax.axis_index("tensor")
    block_count = weights.shape[0]

    if block_count == 8:
        shards = weights.reshape(4, 2, D, BW)
    else:
        width = block_count * BW // 4
        shards = weights.reshape(block_count, D, -1, width).transpose(0, 2, 1, 3).reshape(4, 1, D, width)
    parts, width = shards.shape[1], shards.shape[3]

    def shard(shift, part, *others):
        at = sum((nothing(other) for other in others), plane + shift)
        return lax.dynamic_slice(shards, (at % 4, part, 0, 0), (1, 1, D, width))[0, 0]

    rows_in = tokens.astype(F32)
    one_mine, one_other = gather_rows_at_once(rms_norm(rows_in, gains[0]).astype(BF16))

    moved = []
    for part in range(parts):
        others = [moved[0][1]] if part else []
        moved.append([shard(0, part)] + [ring(shard(shift, part, *others), shift) for shift in (1, 2, 3)])

    def kind_part(source, part, *others):
        at = sum((nothing(other) for other in others), plane)
        return lax.select_n(at, *(moved[part][(here - source) % 4] for here in range(4)))

    if parts == 2:
        mlp_parts = [[kind_part(kind, 0) for kind in (1, 2, 3)]]
        w_attn = gather_part_direct(kind_part(0, 0), 0, jnp.zeros((4, 2, D, BW), BF16))
        w_attn_even = w_attn
        waits = (w_attn, mlp_parts[0][0], one_mine[1])
        w_attn = gather_part_direct(kind_part(0, 1, *waits), 1, w_attn)
        mlp_parts.append([kind_part(kind, 1, w_attn_even) for kind in (1, 2, 3)])
        begun = [mlp_parts[1][0]]
        w_mlp = [gather_plane(kinds) for kinds in mlp_parts]
    else:
        w_attn = join(gather_plane([kind_part(0, 0)]))
        w_mlp = gather_plane([kind_part(kind, 0) for kind in (1, 2, 3)])
        w_mlp = jnp.stack([join(w_mlp[:, kind : kind + 1]) for kind in range(3)], axis=1)
        w_mlp = [w_mlp[:, :, 0], w_mlp[:, :, 1]]
        begun = []
    d_mine, d_other = gather_rows_direct(hold(cotangent, *begun))

    segment_parts = [segments] + [ring(segments, shift) for shift in (1, 2, 3)]
    segment_rows = jnp.concatenate(segment_parts, axis=0)
    length = segment_rows.shape[1]
    half = length // 2
    place = jnp.arange(length)
    place = jnp.where(core == 0, place, (place + half) % length)
    segment_rows = jnp.where(core == 0, segment_rows, jnp.roll(segment_rows, half, axis=1))
    allowed = (place[None, None, :] <= place[None, :, None]) & (
        segment_rows[:, None, :] == segment_rows[:, :, None]
    )
    bias = jnp.where(allowed, 0.0, NEG_LARGE).astype(F32)
    cosine, sine = rope_tables(place)

    query, key, value, context = ([None] * 4 for _ in range(4))
    mixed = Scatter()
    for s in (1, 2, 3, 0):
        query[s], key[s], value[s], context[s], *both = attn_forward(
            one_mine[s], one_other[s], w_attn, bias[s], cosine, sine, mixed.payloads[:1] if s == 3 else begun + d_mine[1:] if s == 1 else ()
        )
        mixed.add(s, *both)
    middle = rows_in + mixed.result
    two_mine, two_other = gather_rows(rms_norm(middle, gains[1]).astype(BF16))

    hidden, d_gate, d_up, d_two, outward = ([None] * 4 for _ in range(5))
    d_normed = Scatter()
    for s in range(4):
        hidden[s], d_gate[s], d_up[s], *both = mlp_piece(
            two_mine[s], two_other[s], d_mine[s], d_other[s], *w_mlp, d_normed.payloads[:1] if s == 3 else ()
        )
        d_two[s], outward[s] = both[:2], both[2:]
        if s:
            d_normed.add(s, *d_two[s])
    mlp_grads = weight_products(
        interleave(two_mine, two_other),
        interleave(d_mine, d_other),
        (d_gate, d_up, hidden),
        (0, 0, 1),
        "mlp_products",
        d_normed.payloads[-1:],
    )
    d_normed.add(0, *d_two[0])
    d_normed_two = d_normed.result
    d_output = cotangent.astype(F32)
    d_middle_norm, d_gain_two = rms_norm_back(middle, gains[1], d_normed_two)
    d_middle = d_output + d_middle_norm
    e_mine, e_other = gather_rows(d_middle.astype(BF16))
    d_query, d_key, d_value, d_one = ([None] * 4 for _ in range(4))
    for s in range(4):
        d_query[s], d_key[s], d_value[s], *both = attn_backward(
            e_mine[s], e_other[s], w_attn, bias[s], cosine, sine, query[s], key[s], value[s]
        )
        d_one[s] = both
    attn_grads = weight_products(
        interleave(one_mine, one_other),
        interleave(e_mine, e_other),
        (d_query, d_key, d_value, context),
        (0, 0, 0, 1),
        "attn_products",
    )
    if parts == 2:
        attn_share = [scatter_plane_direct(grads[0]) for grads in attn_grads]
        mlp_share = [scatter_plane(mlp_grads[0]), scatter_plane_direct(mlp_grads[1], attn_grads[0])]
    else:
        attn_share = [scatter_plane(unjoin(jnp.stack([grads[0] for grads in attn_grads], axis=1), width))[0]]
        mlp_grads = jnp.stack(mlp_grads, axis=2)
        mlp_share = [
            jnp.concatenate([scatter_plane(unjoin(mlp_grads[:, kind], width)) for kind in range(3)])
        ]

    d_normed_one = scatter_rows(d_one)
    d_rows_norm, d_gain_one = rms_norm_back(rows_in, gains[0], d_normed_one)
    input_grad = d_middle + d_rows_norm
    late = [(hold(mine, e_other[3]), hold(theirs, e_other[3])) for mine, theirs in outward]
    output = (middle + scatter_rows(late)).astype(BF16)
    gain_grads = everywhere(jnp.stack([d_gain_one, d_gain_two]))

    results = ()
    for part in range(parts):
        shares = jnp.concatenate([attn_share[part][None], mlp_share[part]])
        at = plane + nothing(output) if part == 0 else plane

        def share_of(shift):
            return lax.dynamic_index_in_dim(shares, (at + shift) % 4, 0, keepdims=False)

        back = [share_of(0)] + [ring(share_of(shift), shift) for shift in (1, 2, 3)]
        here = plane + nothing(results[1]) if part else plane
        summed = jnp.stack(
            [lax.select_n(here, *(back[(z - source) % 4] for z in range(4))) for source in range(4)]
        )
        if parts == 1:
            summed = summed.reshape(block_count, -1, D, width).transpose(0, 2, 1, 3).reshape(block_count, D, BW)
        results = muon(summed, momentum, weights, part, parts, results, (gain_grads,) if part == 0 else ())
    weight_grads, new_momentum, new_weights = results

    new_gain_first = BETA_FIRST * gain_first + (1.0 - BETA_FIRST) * gain_grads
    new_gain_second = BETA_SECOND * gain_second + (1.0 - BETA_SECOND) * gain_grads * gain_grads
    first_hat = new_gain_first / (1.0 - BETA_FIRST**STEP)
    second_hat = new_gain_second / (1.0 - BETA_SECOND**STEP)
    new_gains = gains - ADAM_RATE * first_hat / (jnp.sqrt(second_hat) + ADAM_EPS)
    return (
        output,
        input_grad,
        weight_grads,
        new_momentum,
        new_weights,
        new_gain_first,
        new_gain_second,
        new_gains,
    )


def solution(mesh):
    count = mesh.shape["dp"]
    fine = Mesh(
        np.asarray(mesh.devices).reshape(4, 4, count // 16, mesh.shape["tensor"]),
        ("z",) + PLANE,
    )
    every = ("z",) + PLANE
    in_specs = (
        P(every, None),
        P(every[:3], None),
        P(every, None, None),
        P(every, None, None),
        P(),
        P(),
        P(),
        P(every, None),
    )
    out_specs = (
        P(every, None),
        P(every, None),
        P(every, None, None),
        P(every, None, None),
        P(every, None, None),
        P(),
        P(),
        P(),
    )
    return jax.shard_map(local, mesh=fine, in_specs=in_specs, out_specs=out_specs, check_vma=False)
```

```python
import functools
import math

import jax
import jax.numpy as jnp
import numpy as np
from jax import lax
from jax.experimental import pallas as pl
from jax.experimental.pallas import tpu as pltpu
from jax.sharding import Mesh
from jax.sharding import PartitionSpec as P

D = 2048
FF = 8192
HD = 64
BW = 128
NS_ITERS = 5
STEP = 10

HIGHEST = lax.Precision.HIGHEST
ROPE_BASE = 130000.0
NORM_EPS = 1e-05
NEG_LARGE = -1e30
MOMENTUM_DECAY = 0.95
MUON_RATE = 0.25
COEFF_A = 3.4445
COEFF_B = -4.775
COEFF_C = 2.0315
BETA_FIRST = 0.9
BETA_SECOND = 0.95
ADAM_RATE = 1.0
ADAM_EPS = 1e-08

F32 = jnp.float32
BF16 = jnp.bfloat16
PLANE = ("m", "r", "tensor")
SWAP = [(0, 1), (1, 0)]
TILE = 256
SCORE_SCALE = 1.0 / math.sqrt(HD)


def rms_norm(values, gain):
    return values * lax.rsqrt(jnp.mean(values * values, axis=-1, keepdims=True) + NORM_EPS) * gain


def rms_norm_back(values, gain, grad):
    scale = lax.rsqrt(jnp.mean(values * values, axis=-1, keepdims=True) + NORM_EPS)
    scaled = gain * grad
    inner = jnp.mean(scaled * values, axis=-1, keepdims=True)
    gain_grad = jnp.sum(grad * values * scale, axis=0)
    return scale * scaled - values * (scale * scale * scale * inner), gain_grad


def rope_tables(place):
    exponent = jnp.arange(HD // 2).astype(F32) * (2.0 / HD)
    inverse = jnp.exp(-exponent * math.log(ROPE_BASE))
    angle = place.astype(F32)[:, None] * inverse[None, :]
    cosine, sine = jnp.cos(angle), jnp.sin(angle)
    heads = 2 * BW // HD
    return (
        jnp.tile(jnp.concatenate([cosine, cosine], axis=1), (1, heads)),
        jnp.tile(jnp.concatenate([-sine, sine], axis=1), (1, heads)),
    )


def dims(lhs, rhs):
    return (((lhs,), (rhs,)), ((), ()))


def mul(a, b):
    return lax.dot_general(a, b, dims(1, 0), preferred_element_type=F32)


def mul_bt(a, b):
    return lax.dot_general(a, b, dims(1, 1), preferred_element_type=F32)


def mul_at(a, b):
    return lax.dot_general(a, b, dims(0, 0), preferred_element_type=F32)


def side_by_side(ref, *index):
    return jnp.concatenate([ref[index + (0,)], ref[index + (1,)]], axis=-1)


def pair_rows(own_ref, other_ref):
    return jnp.concatenate([own_ref[...], other_ref[...]], axis=0)


def swap_halves(values):
    lane = lax.broadcasted_iota(jnp.int32, values.shape, 1)
    span = values.shape[1]
    ahead = pltpu.roll(values, span - HD // 2, 1)
    behind = pltpu.roll(values, HD // 2, 1)
    return jnp.where(lane % HD < HD // 2, ahead, behind)


def head_only(values, head):
    lane = lax.broadcasted_iota(jnp.int32, values.shape, 1)
    return jnp.where((lane >= head * HD) & (lane < (head + 1) * HD), values, jnp.zeros_like(values))


def head_probs(query, key, bias, head):
    scores = mul_bt(head_only(query, head), key) * SCORE_SCALE + bias
    weights = jnp.exp(scores - jnp.max(scores, axis=-1, keepdims=True))
    return weights / jnp.sum(weights, axis=-1, keepdims=True)


def attn_forward_kernel(
    own_ref, other_ref, w_ref, bias_ref, cos_ref, sin_ref, q_ref, k_ref, v_ref, c_ref, mine_ref, theirs_ref
):
    rows = pair_rows(own_ref, other_ref)
    cosine, sine = cos_ref[...], sin_ref[...]
    lin = mul(rows, side_by_side(w_ref, 0))
    query = (lin * cosine + swap_halves(lin) * sine).astype(BF16)
    lin = mul(rows, side_by_side(w_ref, 1))
    key = (lin * cosine + swap_halves(lin) * sine).astype(BF16)
    value = mul(rows, side_by_side(w_ref, 2)).astype(BF16)
    q_ref[...] = query
    k_ref[...] = key
    v_ref[...] = value
    context = jnp.zeros(query.shape, F32)
    for head in range(query.shape[1] // HD):
        probs = head_probs(query, key, bias_ref[...], head)
        context = context + mul(probs.astype(BF16), head_only(value, head))
    context = context.astype(BF16)
    c_ref[...] = context
    half = own_ref.shape[0]
    for tile in range(D // TILE):
        at = pl.ds(tile * TILE, TILE)
        w_out = jnp.concatenate([w_ref[3, 0, at, :], w_ref[3, 1, at, :]], axis=-1)
        mixed = mul_bt(context, w_out)
        mine_ref[:, at] = mixed[:half]
        theirs_ref[:, at] = mixed[half:].astype(BF16)


def attn_backward_kernel(
    own_ref, other_ref, w_ref, bias_ref, cos_ref, sin_ref, q_ref, k_ref, v_ref,
    dq_ref, dk_ref, dv_ref, mine_ref, theirs_ref,
):
    rows = pair_rows(own_ref, other_ref)
    query, key, value = q_ref[...], k_ref[...], v_ref[...]
    d_context = mul(rows, side_by_side(w_ref, 3)).astype(BF16)
    d_query = jnp.zeros(query.shape, F32)
    d_key = jnp.zeros(query.shape, F32)
    d_value = jnp.zeros(query.shape, F32)
    for head in range(query.shape[1] // HD):
        probs = head_probs(query, key, bias_ref[...], head)
        d_here = head_only(d_context, head)
        d_value = d_value + mul_at(probs.astype(BF16), d_here)
        d_probs = mul_bt(d_here, value)
        inner = jnp.sum(probs * d_probs, axis=-1, keepdims=True)
        d_scores = (probs * (d_probs - inner)).astype(BF16)
        d_query = d_query + mul(d_scores, head_only(key, head))
        d_key = d_key + mul_at(d_scores, head_only(query, head))
    cosine, sine = cos_ref[...], sin_ref[...]
    d_query = d_query * SCORE_SCALE
    d_key = d_key * SCORE_SCALE
    d_query = (d_query * cosine - swap_halves(d_query) * sine).astype(BF16)
    d_key = (d_key * cosine - swap_halves(d_key) * sine).astype(BF16)
    d_value = d_value.astype(BF16)
    dq_ref[...] = d_query
    dk_ref[...] = d_key
    dv_ref[...] = d_value
    half = own_ref.shape[0]
    for tile in range(D // TILE):
        at = pl.ds(tile * TILE, TILE)
        total = jnp.zeros((2 * half, TILE), F32)
        for matrix, columns in ((0, d_query), (1, d_key), (2, d_value)):
            w_here = jnp.concatenate([w_ref[matrix, 0, at, :], w_ref[matrix, 1, at, :]], axis=-1)
            total = total + mul_bt(columns, w_here)
        mine_ref[:, at] = total[:half]
        theirs_ref[:, at] = total[half:].astype(BF16)


def mlp_kernel(
    own_ref, other_ref, d_own_ref, d_other_ref, gate_even, gate_odd, up_even, up_odd, down_even, down_odd,
    hid_ref, dgate_ref, dup_ref, dn_mine_ref, dn_theirs_ref, out_mine_ref, out_theirs_ref, dn_acc, out_acc,
):
    step = pl.program_id(0)
    rows = pair_rows(own_ref, other_ref)
    d_rows = pair_rows(d_own_ref, d_other_ref)
    w_gate = jnp.concatenate([gate_even[...], gate_odd[...]], axis=-1)
    w_up = jnp.concatenate([up_even[...], up_odd[...]], axis=-1)
    w_down = jnp.concatenate([down_even[...], down_odd[...]], axis=-1)
    gate = mul(rows, w_gate)
    up = mul(rows, w_up)
    d_hidden = mul(d_rows, w_down)
    sigmoid = 1.0 / (1.0 + jnp.exp(-gate))
    silu = gate * sigmoid
    hidden = (silu * up).astype(BF16)
    d_gate = (d_hidden * up * sigmoid * (1.0 + gate * (1.0 - sigmoid))).astype(BF16)
    d_up = (d_hidden * silu).astype(BF16)
    hid_ref[...] = hidden
    dgate_ref[...] = d_gate
    dup_ref[...] = d_up

    @pl.when(step == 0)
    def _():
        dn_acc[...] = jnp.zeros_like(dn_acc)
        out_acc[...] = jnp.zeros_like(out_acc)

    dn_acc[...] += mul_bt(d_gate, w_gate) + mul_bt(d_up, w_up)
    out_acc[...] += mul_bt(hidden, w_down)

    @pl.when(step == pl.num_programs(0) - 1)
    def _():
        half = own_ref.shape[0]
        dn_mine_ref[...] = dn_acc[:half]
        dn_theirs_ref[...] = dn_acc[half:].astype(BF16)
        out_mine_ref[...] = out_acc[:half]
        out_theirs_ref[...] = out_acc[half:].astype(BF16)


def grads_kernel(sources, *refs):
    first, second = refs[:8], refs[8:16]
    columns = refs[16:-2]
    outs = refs[-2:]
    row_sets = [jnp.concatenate([ref[...] for ref in part], axis=0) for part in (first, second)]
    for index, source in enumerate(sources):
        stacked = jnp.concatenate([ref[...] for ref in columns[4 * index : 4 * index + 4]], axis=0)
        grad = mul_at(row_sets[source], stacked).astype(BF16)
        for block in range(grad.shape[1] // BW):
            outs[block % 2][block // 2, index] = grad[:, block * BW : (block + 1) * BW]


def split(values):
    high = values.astype(BF16)
    return high, (values - high.astype(F32)).astype(BF16)


def mul_split(a, b):
    return mul(a[0], b[0]) + (mul(a[0], b[1]) + mul(a[1], b[0]))


def muon_kernel(grad_ref, momentum_ref, weight_ref, wg_ref, nm_ref, nw_ref, held, mixers):
    step = pl.program_id(0)
    count = held.shape[0]

    @pl.when(step < count)
    def _():
        grad = grad_ref[...].astype(F32)
        wg_ref[...] = grad
        block = MOMENTUM_DECAY * momentum_ref[...] + grad
        nm_ref[...] = block
        block = block * (1.0 / (jnp.sqrt(jnp.sum(block * block)) + 1e-07))
        held[step] = block
        high, low = split(block)
        cross = mul_at(high, low)
        mixers[step] = mul_at(high, high) + (cross + cross.T)

    @pl.when(step == count - 1)
    def _():
        row = lax.broadcasted_iota(jnp.int32, (BW, BW), 0)
        column = lax.broadcasted_iota(jnp.int32, (BW, BW), 1)
        eye = jnp.where(row == column, COEFF_A, 0.0).astype(F32)
        grams = [mixers[index] for index in range(count)]
        totals = [None] * count
        for turn in range(NS_ITERS):
            for index in range(count):
                pair = split(grams[index])
                mixer = eye + COEFF_B * grams[index] + COEFF_C * mul_split(pair, pair)
                mixed = split(mixer)
                if turn == 0:
                    totals[index] = mixer
                else:
                    totals[index] = mul_split(split(totals[index]), mixed)
                if turn < NS_ITERS - 1:
                    grams[index] = mul_split(split(mul_split(mixed, pair)), mixed)
        for index in range(count):
            mixers[index] = totals[index]

    @pl.when(step >= count)
    def _():
        at = step - count
        ortho = mul_split(split(held[at]), split(mixers[at]))
        nw_ref[...] = weight_ref[...].astype(F32) - (MUON_RATE * math.sqrt(D / BW)) * ortho


def deferred(kernel, inputs, unread):
    return lambda *refs: kernel(*refs[:inputs], *refs[inputs + unread :])


def unread_specs(after):
    return [pl.BlockSpec(memory_space=pl.ANY) for _ in after]


def params(mebibytes):
    return pltpu.CompilerParams(vmem_limit_bytes=mebibytes * 1024 * 1024)


def whole_specs(arrays):
    return [pl.BlockSpec(memory_space=pltpu.VMEM) for _ in arrays]


def shaped(shape, dtype):
    return jax.ShapeDtypeStruct(shape, dtype)


def attn_forward(own, other, w_attn, bias, cosine, sine, after=()):
    half = own.shape[0]
    span = w_attn.shape[1] * w_attn.shape[3]
    square = shaped((2 * half, span), BF16)
    args = (own, other, w_attn, bias, cosine, sine)
    return pl.pallas_call(
        deferred(attn_forward_kernel, len(args), len(after)),
        out_shape=(square,) * 4 + (shaped((half, D), F32), shaped((half, D), BF16)),
        in_specs=whole_specs(args) + unread_specs(after),
        out_specs=tuple(whole_specs(range(6))),
        compiler_params=params(40),
        cost_estimate=pl.CostEstimate(flops=1_300_000_000, bytes_accessed=9_000_000, transcendentals=262_144),
        name="attn_forward",
    )(*args, *after)


def attn_backward(own, other, w_attn, bias, cosine, sine, query, key, value):
    half = own.shape[0]
    square = shaped(query.shape, BF16)
    args = (own, other, w_attn, bias, cosine, sine, query, key, value)
    return pl.pallas_call(
        attn_backward_kernel,
        out_shape=(square,) * 3 + (shaped((half, D), F32), shaped((half, D), BF16)),
        in_specs=whole_specs(args),
        out_specs=tuple(whole_specs(range(5))),
        compiler_params=params(40),
        cost_estimate=pl.CostEstimate(flops=1_600_000_000, bytes_accessed=9_000_000, transcendentals=262_144),
        name="attn_backward",
    )(*args)


def mlp_piece(own, other, d_own, d_other, w_even, w_odd, after=()):
    half = own.shape[0]
    chunks = w_even.shape[0]
    wide = 2 * BW
    keep = pl.BlockSpec((half, D), lambda j: (0, 0))
    weights = [
        pl.BlockSpec((None, None, D, BW), lambda j, kind=kind: (j, kind, 0, 0)) for kind in (0, 0, 1, 1, 2, 2)
    ]
    column = pl.BlockSpec((2 * half, wide), lambda j: (0, j))
    columns = shaped((2 * half, chunks * wide), BF16)
    return pl.pallas_call(
        deferred(mlp_kernel, 10, len(after)),
        grid=(chunks,),
        out_shape=(columns,) * 3 + (shaped((half, D), F32), shaped((half, D), BF16)) * 2,
        in_specs=[keep] * 4 + weights + unread_specs(after),
        out_specs=(column,) * 3 + (keep,) * 4,
        scratch_shapes=[pltpu.VMEM((2 * half, D), F32)] * 2,
        compiler_params=params(40),
        cost_estimate=pl.CostEstimate(flops=6_400_000_000, bytes_accessed=20_000_000, transcendentals=262_144),
        name="mlp_piece",
    )(own, other, d_own, d_other, w_even, w_odd, w_even, w_odd, w_even, w_odd, *after)


def weight_products(first, second, column_sets, sources, name, after=()):
    half = first[0].shape[0]
    span = column_sets[0][0].shape[1]
    pairs = span // (2 * BW)
    row_spec = pl.BlockSpec((half, TILE), lambda i: (0, i))
    column_spec = pl.BlockSpec((2 * half, span), lambda i: (0, 0))
    flat = [piece for pieces in column_sets for piece in pieces]
    return pl.pallas_call(
        deferred(functools.partial(grads_kernel, sources), 16 + len(flat), len(after)),
        grid=(D // TILE,),
        out_shape=(shaped((pairs, len(sources), D, BW), BF16),) * 2,
        in_specs=[row_spec] * 16 + [column_spec] * len(flat) + unread_specs(after),
        out_specs=(pl.BlockSpec((pairs, len(sources), TILE, BW), lambda i: (0, 0, i, 0)),) * 2,
        compiler_params=params(40),
        cost_estimate=pl.CostEstimate(
            flops=2 * 8 * half * D * span * len(sources), bytes_accessed=20_000_000, transcendentals=0
        ),
        name=name,
    )(*first, *second, *flat, *after)


def muon(grads, momentum, weights, offset, stride, begun=(), after=()):
    count = grads.shape[0]
    now = lambda i: jnp.minimum(i, count - 1)
    then = lambda i: jnp.maximum(i - count, 0)
    block = (None, D, BW)
    compact = pl.BlockSpec(block, lambda i: (now(i), 0, 0))
    early = pl.BlockSpec(block, lambda i: (stride * now(i) + offset, 0, 0))
    late = pl.BlockSpec(block, lambda i: (stride * then(i) + offset, 0, 0))
    return pl.pallas_call(
        deferred(muon_kernel, 3, len(begun) + len(after)),
        grid=(2 * count,),
        out_shape=(shaped(momentum.shape, F32),) * 3,
        in_specs=[compact, early, late] + unread_specs(begun) + unread_specs(after),
        out_specs=(early, early, late),
        input_output_aliases={3 + index: index for index in range(len(begun))},
        scratch_shapes=[pltpu.VMEM((count, D, BW), F32), pltpu.VMEM((count, BW, BW), F32)],
        compiler_params=params(40),
        cost_estimate=pl.CostEstimate(flops=1_000_000_000 * count, bytes_accessed=5_500_000 * count, transcendentals=0),
        name="muon",
    )(grads, momentum, weights, *begun, *after)


def mirror(step):
    return [(place, place ^ step) for place in range(4)]


def ring(value, step=1):
    return lax.ppermute(value, "z", [(place, (place + step) % 4) for place in range(4)])


def swap(value):
    return lax.ppermute(value, "tensor", SWAP)


def nothing(value):
    first = value[(0,) * value.ndim].astype(F32)
    return (first * 0.0).astype(jnp.int32)


def hold(value, *others):
    zero = sum((nothing(other) for other in others), jnp.int32(0))
    return value + zero.astype(value.dtype)


def gather_rows(rows):
    mine = [rows]
    for _ in range(3):
        mine.append(ring(mine[-1]))
    return mine, [swap(part) for part in mine]


def scatter_rows(pieces):
    scatter = Scatter()
    for step in (1, 2, 3, 0):
        scatter.add(step, *pieces[step])
    return scatter.result


def exchange(value, axis):
    return lax.all_to_all(value, axis, 0, 0, tiled=False)


def pick_rows(mine, other):
    plane = lax.axis_index("z")
    pick = lambda stack, s: lax.dynamic_index_in_dim(stack, (plane + 4 - s) % 4, 0, keepdims=False)
    return [pick(mine, s) for s in range(4)], [pick(other, s) for s in range(4)]


class Scatter:
    def __init__(self):
        self.moving = self.result = None
        self.payloads = []

    def add(self, step, mine, theirs):
        total = mine + swap(theirs).astype(F32)
        if self.moving is not None:
            total = total + self.moving.astype(F32)
        if step:
            self.payloads.append(total.astype(BF16))
            self.moving = ring(self.payloads[-1])
        else:
            self.result = total


def everywhere(value):
    value = value + swap(value)
    for axis in ("m", "z"):
        for step in (1, 2):
            value = value + lax.ppermute(value, axis, mirror(step))
    if lax.axis_size("r") > 1:
        value = lax.psum(value, "r")
    return value


def join(parts):
    if parts.shape[0] == 4:
        return parts
    width = parts.shape[3]
    parts = parts.reshape(4, 2, -1, D, width).transpose(0, 1, 3, 2, 4)
    return parts.reshape(4, 2, D, BW)


def unjoin(grads, width):
    if width == BW:
        return grads
    grads = grads.reshape(4, 2, D, -1, width).transpose(0, 1, 3, 2, 4)
    return grads.reshape(-1, 1, D, width)


def gather_plane(parts):
    return lax.all_gather(jnp.stack(parts), ("m", "r"), axis=0, tiled=False)


def scatter_plane(grads):
    share = lax.psum_scatter(
        grads.reshape(grads.shape[0], -1, grads.shape[3]), ("m", "r"), scatter_dimension=0, tiled=False
    )
    return share.reshape(grads.shape[1:])


def scatter_plane_direct(grads, *others):
    zero = sum((nothing(other) for other in others), jnp.int32(0)).astype(F32)
    arrived = exchange(grads, "m")
    total = zero + arrived[0].astype(F32)
    for chip in (1, 2, 3):
        total = total + arrived[chip].astype(F32)
    return total.astype(BF16)


def interleave(mine, other):
    return [rows for pair in zip(mine, other) for rows in pair]


def local(tokens, segments, weights, momentum, gains, gain_first, gain_second, cotangent):
    plane = lax.axis_index("z")
    core = lax.axis_index("tensor")
    block_count = weights.shape[0]

    if block_count == 8:
        shards = weights.reshape(4, 2, D, BW)
    else:
        width = block_count * BW // 4
        shards = weights.reshape(block_count, D, -1, width).transpose(0, 2, 1, 3).reshape(4, 1, D, width)
    parts, width = shards.shape[1], shards.shape[3]

    rows_in = tokens.astype(F32)
    one_mine = lax.all_gather(rms_norm(rows_in, gains[0]).astype(BF16), "z", axis=0, tiled=False)
    one_mine, one_other = pick_rows(one_mine, swap(one_mine))

    if parts == 2:
        even = exchange(shards[:, 0], "z")
        odd = exchange(hold(shards[:, 1], even), "z")
        w_mlp = [lax.all_gather(kinds[1:], "m", axis=0, tiled=False) for kinds in (even, odd)]
        attn_even = exchange(jnp.broadcast_to(even[:1], even.shape), "m")
        attn_odd = exchange(jnp.broadcast_to(hold(odd[:1], attn_even, one_mine[1]), odd.shape), "m")
        w_attn = jnp.stack([attn_even, attn_odd], axis=1)
        begun = [odd]
    else:
        kinds = exchange(shards, "z")
        w_attn = join(gather_plane([kinds[0, 0]]))
        w_mlp = gather_plane([kinds[kind, 0] for kind in (1, 2, 3)])
        w_mlp = jnp.stack([join(w_mlp[:, kind : kind + 1]) for kind in range(3)], axis=1)
        w_mlp = [w_mlp[:, :, 0], w_mlp[:, :, 1]]
        begun = []
    d_mine = exchange(jnp.broadcast_to(hold(cotangent, *begun)[None], (4,) + cotangent.shape), "z")
    d_mine, d_other = pick_rows(d_mine, swap(d_mine))

    segment_parts = [segments] + [ring(segments, shift) for shift in (1, 2, 3)]
    segment_rows = jnp.concatenate(segment_parts, axis=0)
    length = segment_rows.shape[1]
    half = length // 2
    place = jnp.arange(length)
    place = jnp.where(core == 0, place, (place + half) % length)
    segment_rows = jnp.where(core == 0, segment_rows, jnp.roll(segment_rows, half, axis=1))
    allowed = (place[None, None, :] <= place[None, :, None]) & (
        segment_rows[:, None, :] == segment_rows[:, :, None]
    )
    bias = jnp.where(allowed, 0.0, NEG_LARGE).astype(F32)
    cosine, sine = rope_tables(place)

    query, key, value, context = ([None] * 4 for _ in range(4))
    mixed = Scatter()
    for s in (1, 2, 3, 0):
        query[s], key[s], value[s], context[s], *both = attn_forward(
            one_mine[s], one_other[s], w_attn, bias[s], cosine, sine, mixed.payloads[:1] if s == 3 else d_mine[1:2] if s == 0 else ()
        )
        mixed.add(s, *both)
    middle = rows_in + mixed.result
    two_mine, two_other = gather_rows(rms_norm(middle, gains[1]).astype(BF16))

    hidden, d_gate, d_up, d_two, outward = ([None] * 4 for _ in range(5))
    d_normed = Scatter()
    for s in range(4):
        hidden[s], d_gate[s], d_up[s], *both = mlp_piece(
            two_mine[s], two_other[s], d_mine[s], d_other[s], *w_mlp, d_normed.payloads[:1] if s == 3 else ()
        )
        d_two[s], outward[s] = both[:2], both[2:]
        if s:
            d_normed.add(s, *d_two[s])
    mlp_grads = weight_products(
        interleave(two_mine, two_other),
        interleave(d_mine, d_other),
        (d_gate, d_up, hidden),
        (0, 0, 1),
        "mlp_products",
        d_normed.payloads[-1:],
    )
    d_normed.add(0, *d_two[0])
    d_normed_two = d_normed.result
    d_output = cotangent.astype(F32)
    d_middle_norm, d_gain_two = rms_norm_back(middle, gains[1], d_normed_two)
    d_middle = d_output + d_middle_norm
    e_mine, e_other = gather_rows(d_middle.astype(BF16))
    d_query, d_key, d_value, d_one = ([None] * 4 for _ in range(4))
    for s in range(4):
        d_query[s], d_key[s], d_value[s], *both = attn_backward(
            e_mine[s], e_other[s], w_attn, bias[s], cosine, sine, query[s], key[s], value[s]
        )
        d_one[s] = both
    attn_grads = weight_products(
        interleave(one_mine, one_other),
        interleave(e_mine, e_other),
        (d_query, d_key, d_value, context),
        (0, 0, 0, 1),
        "attn_products",
    )
    d_normed_one = scatter_rows(d_one)
    d_rows_norm, d_gain_one = rms_norm_back(rows_in, gains[0], d_normed_one)
    input_grad = d_middle + d_rows_norm
    late = [(hold(mine, e_other[3]), hold(theirs, e_other[3])) for mine, theirs in outward]
    output = (middle + scatter_rows(late)).astype(BF16)
    gain_grads = everywhere(jnp.stack([d_gain_one, d_gain_two]))

    if parts == 2:
        attn_share = [scatter_plane_direct(attn_grads[0][0]), scatter_plane_direct(attn_grads[1][0], output)]
        mlp_share = [scatter_plane(mlp_grads[0]), scatter_plane_direct(mlp_grads[1], attn_grads[0])]
    else:
        attn_share = [scatter_plane(unjoin(jnp.stack([grads[0] for grads in attn_grads], axis=1), width))[0]]
        mlp_grads = jnp.stack(mlp_grads, axis=2)
        mlp_share = [
            jnp.concatenate([scatter_plane(unjoin(mlp_grads[:, kind], width)) for kind in range(3)])
        ]

    results = ()
    for part in range(parts):
        summed = exchange(jnp.concatenate([attn_share[part][None], mlp_share[part]]), "z")
        if parts == 1:
            summed = summed.reshape(block_count, -1, D, width).transpose(0, 2, 1, 3).reshape(block_count, D, BW)
        results = muon(summed, momentum, weights, part, parts, results, (gain_grads,) if part == 0 else ())
    weight_grads, new_momentum, new_weights = results

    new_gain_first = BETA_FIRST * gain_first + (1.0 - BETA_FIRST) * gain_grads
    new_gain_second = BETA_SECOND * gain_second + (1.0 - BETA_SECOND) * gain_grads * gain_grads
    first_hat = new_gain_first / (1.0 - BETA_FIRST**STEP)
    second_hat = new_gain_second / (1.0 - BETA_SECOND**STEP)
    new_gains = gains - ADAM_RATE * first_hat / (jnp.sqrt(second_hat) + ADAM_EPS)
    return (
        output,
        input_grad,
        weight_grads,
        new_momentum,
        new_weights,
        new_gain_first,
        new_gain_second,
        new_gains,
    )


def solution(mesh):
    count = mesh.shape["dp"]
    fine = Mesh(
        np.asarray(mesh.devices).reshape(4, 4, count // 16, mesh.shape["tensor"]),
        ("z",) + PLANE,
    )
    every = ("z",) + PLANE
    in_specs = (
        P(every, None),
        P(every[:3], None),
        P(every, None, None),
        P(every, None, None),
        P(),
        P(),
        P(),
        P(every, None),
    )
    out_specs = (
        P(every, None),
        P(every, None),
        P(every, None, None),
        P(every, None, None),
        P(every, None, None),
        P(),
        P(),
        P(),
    )
    return jax.shard_map(local, mesh=fine, in_specs=in_specs, out_specs=out_specs, check_vma=False)
```

```python
import functools
import math

import jax
import jax.numpy as jnp
import numpy as np
from jax import lax
from jax.experimental import pallas as pl
from jax.experimental.pallas import tpu as pltpu
from jax.sharding import Mesh
from jax.sharding import PartitionSpec as P

D = 2048
FF = 8192
HD = 64
BW = 128
NS_ITERS = 5
STEP = 10

HIGHEST = lax.Precision.HIGHEST
ROPE_BASE = 130000.0
NORM_EPS = 1e-05
NEG_LARGE = -1e30
MOMENTUM_DECAY = 0.95
MUON_RATE = 0.25
COEFF_A = 3.4445
COEFF_B = -4.775
COEFF_C = 2.0315
BETA_FIRST = 0.9
BETA_SECOND = 0.95
ADAM_RATE = 1.0
ADAM_EPS = 1e-08

F32 = jnp.float32
BF16 = jnp.bfloat16
PLANE = ("m", "r", "tensor")
SWAP = [(0, 1), (1, 0)]
TILE = 256
SCORE_SCALE = 1.0 / math.sqrt(HD)


def rms_norm(values, gain):
    return values * lax.rsqrt(jnp.mean(values * values, axis=-1, keepdims=True) + NORM_EPS) * gain


def rms_norm_back(values, gain, grad):
    scale = lax.rsqrt(jnp.mean(values * values, axis=-1, keepdims=True) + NORM_EPS)
    scaled = gain * grad
    inner = jnp.mean(scaled * values, axis=-1, keepdims=True)
    gain_grad = jnp.sum(grad * values * scale, axis=0)
    return scale * scaled - values * (scale * scale * scale * inner), gain_grad


def rope_tables(place):
    exponent = jnp.arange(HD // 2).astype(F32) * (2.0 / HD)
    inverse = jnp.exp(-exponent * math.log(ROPE_BASE))
    angle = place.astype(F32)[:, None] * inverse[None, :]
    cosine, sine = jnp.cos(angle), jnp.sin(angle)
    heads = 2 * BW // HD
    return (
        jnp.tile(jnp.concatenate([cosine, cosine], axis=1), (1, heads)),
        jnp.tile(jnp.concatenate([-sine, sine], axis=1), (1, heads)),
    )


def dims(lhs, rhs):
    return (((lhs,), (rhs,)), ((), ()))


def mul(a, b):
    return lax.dot_general(a, b, dims(1, 0), preferred_element_type=F32)


def mul_bt(a, b):
    return lax.dot_general(a, b, dims(1, 1), preferred_element_type=F32)


def mul_at(a, b):
    return lax.dot_general(a, b, dims(0, 0), preferred_element_type=F32)


def side_by_side(ref, *index):
    return jnp.concatenate([ref[index + (0,)], ref[index + (1,)]], axis=-1)


def pair_rows(own_ref, other_ref):
    return jnp.concatenate([own_ref[...], other_ref[...]], axis=0)


def swap_halves(values):
    lane = lax.broadcasted_iota(jnp.int32, values.shape, 1)
    span = values.shape[1]
    ahead = pltpu.roll(values, span - HD // 2, 1)
    behind = pltpu.roll(values, HD // 2, 1)
    return jnp.where(lane % HD < HD // 2, ahead, behind)


def head_only(values, head):
    lane = lax.broadcasted_iota(jnp.int32, values.shape, 1)
    return jnp.where((lane >= head * HD) & (lane < (head + 1) * HD), values, jnp.zeros_like(values))


def head_probs(query, key, bias, head):
    scores = mul_bt(head_only(query, head), key) * SCORE_SCALE + bias
    weights = jnp.exp(scores - jnp.max(scores, axis=-1, keepdims=True))
    return weights / jnp.sum(weights, axis=-1, keepdims=True)


def attn_forward_kernel(
    own_ref, other_ref, w_ref, bias_ref, cos_ref, sin_ref, q_ref, k_ref, v_ref, c_ref, mine_ref, theirs_ref
):
    rows = pair_rows(own_ref, other_ref)
    cosine, sine = cos_ref[...], sin_ref[...]
    lin = mul(rows, side_by_side(w_ref, 0))
    query = (lin * cosine + swap_halves(lin) * sine).astype(BF16)
    lin = mul(rows, side_by_side(w_ref, 1))
    key = (lin * cosine + swap_halves(lin) * sine).astype(BF16)
    value = mul(rows, side_by_side(w_ref, 2)).astype(BF16)
    q_ref[...] = query
    k_ref[...] = key
    v_ref[...] = value
    context = jnp.zeros(query.shape, F32)
    for head in range(query.shape[1] // HD):
        probs = head_probs(query, key, bias_ref[...], head)
        context = context + mul(probs.astype(BF16), head_only(value, head))
    context = context.astype(BF16)
    c_ref[...] = context
    half = own_ref.shape[0]
    for tile in range(D // TILE):
        at = pl.ds(tile * TILE, TILE)
        w_out = jnp.concatenate([w_ref[3, 0, at, :], w_ref[3, 1, at, :]], axis=-1)
        mixed = mul_bt(context, w_out)
        mine_ref[:, at] = mixed[:half]
        theirs_ref[:, at] = mixed[half:].astype(BF16)


def attn_backward_kernel(
    own_ref, other_ref, w_ref, bias_ref, cos_ref, sin_ref, q_ref, k_ref, v_ref,
    dq_ref, dk_ref, dv_ref, mine_ref, theirs_ref,
):
    rows = pair_rows(own_ref, other_ref)
    query, key, value = q_ref[...], k_ref[...], v_ref[...]
    d_context = mul(rows, side_by_side(w_ref, 3)).astype(BF16)
    d_query = jnp.zeros(query.shape, F32)
    d_key = jnp.zeros(query.shape, F32)
    d_value = jnp.zeros(query.shape, F32)
    for head in range(query.shape[1] // HD):
        probs = head_probs(query, key, bias_ref[...], head)
        d_here = head_only(d_context, head)
        d_value = d_value + mul_at(probs.astype(BF16), d_here)
        d_probs = mul_bt(d_here, value)
        inner = jnp.sum(probs * d_probs, axis=-1, keepdims=True)
        d_scores = (probs * (d_probs - inner)).astype(BF16)
        d_query = d_query + mul(d_scores, head_only(key, head))
        d_key = d_key + mul_at(d_scores, head_only(query, head))
    cosine, sine = cos_ref[...], sin_ref[...]
    d_query = d_query * SCORE_SCALE
    d_key = d_key * SCORE_SCALE
    d_query = (d_query * cosine - swap_halves(d_query) * sine).astype(BF16)
    d_key = (d_key * cosine - swap_halves(d_key) * sine).astype(BF16)
    d_value = d_value.astype(BF16)
    dq_ref[...] = d_query
    dk_ref[...] = d_key
    dv_ref[...] = d_value
    half = own_ref.shape[0]
    for tile in range(D // TILE):
        at = pl.ds(tile * TILE, TILE)
        total = jnp.zeros((2 * half, TILE), F32)
        for matrix, columns in ((0, d_query), (1, d_key), (2, d_value)):
            w_here = jnp.concatenate([w_ref[matrix, 0, at, :], w_ref[matrix, 1, at, :]], axis=-1)
            total = total + mul_bt(columns, w_here)
        mine_ref[:, at] = total[:half]
        theirs_ref[:, at] = total[half:].astype(BF16)


def mlp_kernel(
    own_ref, other_ref, d_own_ref, d_other_ref, gate_even, gate_odd, up_even, up_odd, down_even, down_odd,
    hid_ref, dgate_ref, dup_ref, dn_mine_ref, dn_theirs_ref, out_mine_ref, out_theirs_ref, dn_acc, out_acc,
):
    step = pl.program_id(0)
    rows = pair_rows(own_ref, other_ref)
    d_rows = pair_rows(d_own_ref, d_other_ref)
    w_gate = jnp.concatenate([gate_even[...], gate_odd[...]], axis=-1)
    w_up = jnp.concatenate([up_even[...], up_odd[...]], axis=-1)
    w_down = jnp.concatenate([down_even[...], down_odd[...]], axis=-1)
    gate = mul(rows, w_gate)
    up = mul(rows, w_up)
    d_hidden = mul(d_rows, w_down)
    sigmoid = 1.0 / (1.0 + jnp.exp(-gate))
    silu = gate * sigmoid
    hidden = (silu * up).astype(BF16)
    d_gate = (d_hidden * up * sigmoid * (1.0 + gate * (1.0 - sigmoid))).astype(BF16)
    d_up = (d_hidden * silu).astype(BF16)
    hid_ref[...] = hidden
    dgate_ref[...] = d_gate
    dup_ref[...] = d_up

    @pl.when(step == 0)
    def _():
        dn_acc[...] = jnp.zeros_like(dn_acc)
        out_acc[...] = jnp.zeros_like(out_acc)

    dn_acc[...] += mul_bt(d_gate, w_gate) + mul_bt(d_up, w_up)
    out_acc[...] += mul_bt(hidden, w_down)

    @pl.when(step == pl.num_programs(0) - 1)
    def _():
        half = own_ref.shape[0]
        dn_mine_ref[...] = dn_acc[:half]
        dn_theirs_ref[...] = dn_acc[half:].astype(BF16)
        out_mine_ref[...] = out_acc[:half]
        out_theirs_ref[...] = out_acc[half:].astype(BF16)


def grads_kernel(sources, *refs):
    first, second = refs[:8], refs[8:16]
    columns = refs[16:-2]
    outs = refs[-2:]
    row_sets = [jnp.concatenate([ref[...] for ref in part], axis=0) for part in (first, second)]
    for index, source in enumerate(sources):
        stacked = jnp.concatenate([ref[...] for ref in columns[4 * index : 4 * index + 4]], axis=0)
        grad = mul_at(row_sets[source], stacked).astype(BF16)
        for block in range(grad.shape[1] // BW):
            outs[block % 2][block // 2, index] = grad[:, block * BW : (block + 1) * BW]


def split(values):
    high = values.astype(BF16)
    return high, (values - high.astype(F32)).astype(BF16)


def mul_split(a, b):
    return mul(a[0], b[0]) + (mul(a[0], b[1]) + mul(a[1], b[0]))


def muon_kernel(grad_ref, momentum_ref, weight_ref, wg_ref, nm_ref, nw_ref, held, mixers):
    step = pl.program_id(0)
    count = held.shape[0]

    @pl.when(step < count)
    def _():
        grad = grad_ref[...].astype(F32)
        wg_ref[...] = grad
        block = MOMENTUM_DECAY * momentum_ref[...] + grad
        nm_ref[...] = block
        block = block * (1.0 / (jnp.sqrt(jnp.sum(block * block)) + 1e-07))
        held[step] = block
        high, low = split(block)
        cross = mul_at(high, low)
        mixers[step] = mul_at(high, high) + (cross + cross.T)

    @pl.when(step == count - 1)
    def _():
        row = lax.broadcasted_iota(jnp.int32, (BW, BW), 0)
        column = lax.broadcasted_iota(jnp.int32, (BW, BW), 1)
        eye = jnp.where(row == column, COEFF_A, 0.0).astype(F32)
        grams = [mixers[index] for index in range(count)]
        totals = [None] * count
        for turn in range(NS_ITERS):
            for index in range(count):
                pair = split(grams[index])
                mixer = eye + COEFF_B * grams[index] + COEFF_C * mul_split(pair, pair)
                mixed = split(mixer)
                if turn == 0:
                    totals[index] = mixer
                else:
                    totals[index] = mul_split(split(totals[index]), mixed)
                if turn < NS_ITERS - 1:
                    grams[index] = mul_split(split(mul_split(mixed, pair)), mixed)
        for index in range(count):
            mixers[index] = totals[index]

    @pl.when(step >= count)
    def _():
        at = step - count
        ortho = mul_split(split(held[at]), split(mixers[at]))
        nw_ref[...] = weight_ref[...].astype(F32) - (MUON_RATE * math.sqrt(D / BW)) * ortho


def deferred(kernel, inputs, unread):
    return lambda *refs: kernel(*refs[:inputs], *refs[inputs + unread :])


def unread_specs(after):
    return [pl.BlockSpec(memory_space=pl.ANY) for _ in after]


def cost(flops, accessed):
    return pl.CostEstimate(flops=flops // 6, bytes_accessed=accessed // 6, transcendentals=0)


def params(mebibytes):
    return pltpu.CompilerParams(vmem_limit_bytes=mebibytes * 1024 * 1024)


def whole_specs(arrays):
    return [pl.BlockSpec(memory_space=pltpu.VMEM) for _ in arrays]


def shaped(shape, dtype):
    return jax.ShapeDtypeStruct(shape, dtype)


def attn_forward(own, other, w_attn, bias, cosine, sine, after=()):
    half = own.shape[0]
    span = w_attn.shape[1] * w_attn.shape[3]
    square = shaped((2 * half, span), BF16)
    args = (own, other, w_attn, bias, cosine, sine)
    return pl.pallas_call(
        deferred(attn_forward_kernel, len(args), len(after)),
        out_shape=(square,) * 4 + (shaped((half, D), F32), shaped((half, D), BF16)),
        in_specs=whole_specs(args) + unread_specs(after),
        out_specs=tuple(whole_specs(range(6))),
        compiler_params=params(40),
        cost_estimate=cost(1_300_000_000, 9_000_000),
        name="attn_forward",
    )(*args, *after)


def attn_backward(own, other, w_attn, bias, cosine, sine, query, key, value):
    half = own.shape[0]
    square = shaped(query.shape, BF16)
    args = (own, other, w_attn, bias, cosine, sine, query, key, value)
    return pl.pallas_call(
        attn_backward_kernel,
        out_shape=(square,) * 3 + (shaped((half, D), F32), shaped((half, D), BF16)),
        in_specs=whole_specs(args),
        out_specs=tuple(whole_specs(range(5))),
        compiler_params=params(40),
        cost_estimate=cost(1_600_000_000, 9_000_000),
        name="attn_backward",
    )(*args)


def mlp_piece(own, other, d_own, d_other, w_even, w_odd, after=()):
    half = own.shape[0]
    chunks = w_even.shape[0]
    wide = 2 * BW
    keep = pl.BlockSpec((half, D), lambda j: (0, 0))
    weights = [
        pl.BlockSpec((None, None, D, BW), lambda j, kind=kind: (j, kind, 0, 0)) for kind in (0, 0, 1, 1, 2, 2)
    ]
    column = pl.BlockSpec((2 * half, wide), lambda j: (0, j))
    columns = shaped((2 * half, chunks * wide), BF16)
    return pl.pallas_call(
        deferred(mlp_kernel, 10, len(after)),
        grid=(chunks,),
        out_shape=(columns,) * 3 + (shaped((half, D), F32), shaped((half, D), BF16)) * 2,
        in_specs=[keep] * 4 + weights + unread_specs(after),
        out_specs=(column,) * 3 + (keep,) * 4,
        scratch_shapes=[pltpu.VMEM((2 * half, D), F32)] * 2,
        compiler_params=params(40),
        cost_estimate=cost(6_400_000_000, 20_000_000),
        name="mlp_piece",
    )(own, other, d_own, d_other, w_even, w_odd, w_even, w_odd, w_even, w_odd, *after)


def weight_products(first, second, column_sets, sources, name, after=()):
    half = first[0].shape[0]
    span = column_sets[0][0].shape[1]
    pairs = span // (2 * BW)
    row_spec = pl.BlockSpec((half, TILE), lambda i: (0, i))
    column_spec = pl.BlockSpec((2 * half, span), lambda i: (0, 0))
    flat = [piece for pieces in column_sets for piece in pieces]
    return pl.pallas_call(
        deferred(functools.partial(grads_kernel, sources), 16 + len(flat), len(after)),
        grid=(D // TILE,),
        out_shape=(shaped((pairs, len(sources), D, BW), BF16),) * 2,
        in_specs=[row_spec] * 16 + [column_spec] * len(flat) + unread_specs(after),
        out_specs=(pl.BlockSpec((pairs, len(sources), TILE, BW), lambda i: (0, 0, i, 0)),) * 2,
        compiler_params=params(40),
        cost_estimate=cost(2 * 8 * half * D * span * len(sources), 20_000_000),
        name=name,
    )(*first, *second, *flat, *after)


def muon(grads, momentum, weights, offset, stride, begun=(), after=()):
    count = grads.shape[0]
    now = lambda i: jnp.minimum(i, count - 1)
    then = lambda i: jnp.maximum(i - count, 0)
    block = (None, D, BW)
    compact = pl.BlockSpec(block, lambda i: (now(i), 0, 0))
    early = pl.BlockSpec(block, lambda i: (stride * now(i) + offset, 0, 0))
    late = pl.BlockSpec(block, lambda i: (stride * then(i) + offset, 0, 0))
    return pl.pallas_call(
        deferred(muon_kernel, 3, len(begun) + len(after)),
        grid=(2 * count,),
        out_shape=(shaped(momentum.shape, F32),) * 3,
        in_specs=[compact, early, late] + unread_specs(begun) + unread_specs(after),
        out_specs=(early, early, late),
        input_output_aliases={3 + index: index for index in range(len(begun))},
        scratch_shapes=[pltpu.VMEM((count, D, BW), F32), pltpu.VMEM((count, BW, BW), F32)],
        compiler_params=params(40),
        cost_estimate=cost(1_000_000_000 * count, 5_500_000 * count),
        name="muon",
    )(grads, momentum, weights, *begun, *after)


def mirror(step):
    return [(place, place ^ step) for place in range(4)]


def ring(value, step=1):
    return lax.ppermute(value, "z", [(place, (place + step) % 4) for place in range(4)])


def swap(value):
    return lax.ppermute(value, "tensor", SWAP)


def nothing(value):
    first = value[(0,) * value.ndim].astype(F32)
    return (first * 0.0).astype(jnp.int32)


def hold(value, *others):
    zero = sum((nothing(other) for other in others), jnp.int32(0))
    return value + zero.astype(value.dtype)


def gather_rows(rows):
    mine = [rows]
    for _ in range(3):
        mine.append(ring(mine[-1]))
    return mine, [swap(part) for part in mine]


def scatter_rows(pieces):
    scatter = Scatter()
    for step in (1, 2, 3, 0):
        scatter.add(step, *pieces[step])
    return scatter.result


def gather_rows_at_once(rows):
    plane = lax.axis_index("z")
    mine = lax.all_gather(rows, "z", axis=0, tiled=False)
    other = swap(mine)
    pick = lambda stack, s: lax.dynamic_index_in_dim(stack, (plane + 4 - s) % 4, 0, keepdims=False)
    return [pick(mine, s) for s in range(4)], [pick(other, s) for s in range(4)]


def gather_rows_direct(rows):
    mine = [rows] + [ring(rows, shift) for shift in (1, 2, 3)]
    return mine, [swap(part) for part in mine]


class Scatter:
    def __init__(self):
        self.moving = self.result = None
        self.payloads = []

    def add(self, step, mine, theirs):
        total = mine + swap(theirs).astype(F32)
        if self.moving is not None:
            total = total + self.moving.astype(F32)
        if step:
            self.payloads.append(total.astype(BF16))
            self.moving = ring(self.payloads[-1])
        else:
            self.result = total


def everywhere(value):
    value = value + swap(value)
    for axis in ("m", "z"):
        for step in (1, 2):
            value = value + lax.ppermute(value, axis, mirror(step))
    if lax.axis_size("r") > 1:
        value = lax.psum(value, "r")
    return value


def join(parts):
    if parts.shape[0] == 4:
        return parts
    width = parts.shape[3]
    parts = parts.reshape(4, 2, -1, D, width).transpose(0, 1, 3, 2, 4)
    return parts.reshape(4, 2, D, BW)


def unjoin(grads, width):
    if width == BW:
        return grads
    grads = grads.reshape(4, 2, D, -1, width).transpose(0, 1, 3, 2, 4)
    return grads.reshape(-1, 1, D, width)


def gather_plane(parts):
    return lax.all_gather(jnp.stack(parts), ("m", "r"), axis=0, tiled=False)


def gather_part_direct(part, index, result):
    chip = lax.axis_index("m")
    result = lax.dynamic_update_slice(result, part[None, None], (chip, index, 0, 0))
    for step in (1, 2, 3):
        got = lax.ppermute(part, "m", mirror(step))
        result = lax.dynamic_update_slice(result, got[None, None], (chip ^ step, index, 0, 0))
    return result


def scatter_plane(grads):
    share = lax.psum_scatter(
        grads.reshape(grads.shape[0], -1, grads.shape[3]), ("m", "r"), scatter_dimension=0, tiled=False
    )
    return share.reshape(grads.shape[1:])


def scatter_plane_direct(grads, *others):
    chip = lax.axis_index("m")
    zero = sum((nothing(other) for other in others), jnp.int32(0)).astype(F32)

    def share_for(step):
        return lax.dynamic_index_in_dim(grads, chip ^ step, 0, keepdims=False)

    total = share_for(0).astype(F32) + zero
    for step in (1, 2, 3):
        total = total + lax.ppermute(share_for(step), "m", mirror(step)).astype(F32)
    return total.astype(BF16)


def interleave(mine, other):
    return [rows for pair in zip(mine, other) for rows in pair]


def local(tokens, segments, weights, momentum, gains, gain_first, gain_second, cotangent):
    plane = lax.axis_index("z")
    core = lax.axis_index("tensor")
    block_count = weights.shape[0]

    if block_count == 8:
        shards = weights.reshape(4, 2, D, BW)
    else:
        width = block_count * BW // 4
        shards = weights.reshape(block_count, D, -1, width).transpose(0, 2, 1, 3).reshape(4, 1, D, width)
    parts, width = shards.shape[1], shards.shape[3]

    def shard(shift, part, *others):
        at = sum((nothing(other) for other in others), plane + shift)
        return lax.dynamic_slice(shards, (at % 4, part, 0, 0), (1, 1, D, width))[0, 0]

    rows_in = tokens.astype(F32)
    one_mine, one_other = gather_rows_at_once(rms_norm(rows_in, gains[0]).astype(BF16))

    moved = []
    for part in range(parts):
        others = moved[0][1:] if part else []
        moved.append([shard(0, part)] + [ring(shard(shift, part, *others), shift) for shift in (1, 2, 3)])

    def kind_part(source, part, *others):
        at = sum((nothing(other) for other in others), plane)
        return lax.select_n(at, *(moved[part][(here - source) % 4] for here in range(4)))

    if parts == 2:
        mlp_parts = [[kind_part(kind, 0) for kind in (1, 2, 3)]]
        w_attn = gather_part_direct(kind_part(0, 0), 0, jnp.zeros((4, 2, D, BW), BF16))
        w_attn_even = w_attn
        waits = (w_attn, mlp_parts[0][0], one_mine[1])
        w_attn = gather_part_direct(kind_part(0, 1, *waits), 1, w_attn)
        mlp_parts.append([kind_part(kind, 1, w_attn_even) for kind in (1, 2, 3)])
        begun = [mlp_parts[1][0]]
        w_mlp = [gather_plane(kinds) for kinds in mlp_parts]
    else:
        w_attn = join(gather_plane([kind_part(0, 0)]))
        w_mlp = gather_plane([kind_part(kind, 0) for kind in (1, 2, 3)])
        w_mlp = jnp.stack([join(w_mlp[:, kind : kind + 1]) for kind in range(3)], axis=1)
        w_mlp = [w_mlp[:, :, 0], w_mlp[:, :, 1]]
        begun = []
    d_mine, d_other = gather_rows_direct(hold(cotangent, *begun))

    segment_parts = [segments] + [ring(segments, shift) for shift in (1, 2, 3)]
    segment_rows = jnp.concatenate(segment_parts, axis=0)
    length = segment_rows.shape[1]
    half = length // 2
    place = jnp.arange(length)
    place = jnp.where(core == 0, place, (place + half) % length)
    segment_rows = jnp.where(core == 0, segment_rows, jnp.roll(segment_rows, half, axis=1))
    allowed = (place[None, None, :] <= place[None, :, None]) & (
        segment_rows[:, None, :] == segment_rows[:, :, None]
    )
    bias = jnp.where(allowed, 0.0, NEG_LARGE).astype(F32)
    cosine, sine = rope_tables(place)

    query, key, value, context = ([None] * 4 for _ in range(4))
    mixed = Scatter()
    for s in (1, 2, 3, 0):
        query[s], key[s], value[s], context[s], *both = attn_forward(
            one_mine[s], one_other[s], w_attn, bias[s], cosine, sine, mixed.payloads[:1] if s == 3 else begun + d_mine[1:] if s == 1 else ()
        )
        mixed.add(s, *both)
    middle = rows_in + mixed.result
    two_mine, two_other = gather_rows(rms_norm(middle, gains[1]).astype(BF16))

    hidden, d_gate, d_up, d_two, outward = ([None] * 4 for _ in range(5))
    d_normed = Scatter()
    for s in range(4):
        hidden[s], d_gate[s], d_up[s], *both = mlp_piece(
            two_mine[s], two_other[s], d_mine[s], d_other[s], *w_mlp, d_normed.payloads[:1] if s == 3 else ()
        )
        d_two[s], outward[s] = both[:2], both[2:]
        if s:
            d_normed.add(s, *d_two[s])
    mlp_grads = weight_products(
        interleave(two_mine, two_other),
        interleave(d_mine, d_other),
        (d_gate, d_up, hidden),
        (0, 0, 1),
        "mlp_products",
        d_normed.payloads[-1:],
    )
    d_normed.add(0, *d_two[0])
    d_normed_two = d_normed.result
    d_output = cotangent.astype(F32)
    d_middle_norm, d_gain_two = rms_norm_back(middle, gains[1], d_normed_two)
    d_middle = d_output + d_middle_norm
    e_mine, e_other = gather_rows(d_middle.astype(BF16))
    d_query, d_key, d_value, d_one = ([None] * 4 for _ in range(4))
    for s in range(4):
        d_query[s], d_key[s], d_value[s], *both = attn_backward(
            e_mine[s], e_other[s], w_attn, bias[s], cosine, sine, query[s], key[s], value[s]
        )
        d_one[s] = both
    attn_grads = weight_products(
        interleave(one_mine, one_other),
        interleave(e_mine, e_other),
        (d_query, d_key, d_value, context),
        (0, 0, 0, 1),
        "attn_products",
    )
    if parts == 2:
        attn_share = [scatter_plane_direct(grads[0]) for grads in attn_grads]
        mlp_share = [scatter_plane(mlp_grads[0]), scatter_plane_direct(mlp_grads[1], attn_grads[0])]
    else:
        attn_share = [scatter_plane(unjoin(jnp.stack([grads[0] for grads in attn_grads], axis=1), width))[0]]
        mlp_grads = jnp.stack(mlp_grads, axis=2)
        mlp_share = [
            jnp.concatenate([scatter_plane(unjoin(mlp_grads[:, kind], width)) for kind in range(3)])
        ]

    d_normed_one = scatter_rows(d_one)
    d_rows_norm, d_gain_one = rms_norm_back(rows_in, gains[0], d_normed_one)
    input_grad = d_middle + d_rows_norm
    late = [(hold(mine, e_other[3]), hold(theirs, e_other[3])) for mine, theirs in outward]
    output = (middle + scatter_rows(late)).astype(BF16)
    gain_grads = everywhere(jnp.stack([d_gain_one, d_gain_two]))

    results = ()
    for part in range(parts):
        shares = jnp.concatenate([attn_share[part][None], mlp_share[part]])
        at = plane + nothing(output) if part == 0 else plane

        def share_of(shift):
            return lax.dynamic_index_in_dim(shares, (at + shift) % 4, 0, keepdims=False)

        back = [share_of(0)] + [ring(share_of(shift), shift) for shift in (1, 2, 3)]
        here = plane + nothing(results[1]) if part else plane
        summed = jnp.stack(
            [lax.select_n(here, *(back[(z - source) % 4] for z in range(4))) for source in range(4)]
        )
        if parts == 1:
            summed = summed.reshape(block_count, -1, D, width).transpose(0, 2, 1, 3).reshape(block_count, D, BW)
        results = muon(summed, momentum, weights, part, parts, results, (gain_grads,) if part == 0 else ())
    weight_grads, new_momentum, new_weights = results

    new_gain_first = BETA_FIRST * gain_first + (1.0 - BETA_FIRST) * gain_grads
    new_gain_second = BETA_SECOND * gain_second + (1.0 - BETA_SECOND) * gain_grads * gain_grads
    first_hat = new_gain_first / (1.0 - BETA_FIRST**STEP)
    second_hat = new_gain_second / (1.0 - BETA_SECOND**STEP)
    new_gains = gains - ADAM_RATE * first_hat / (jnp.sqrt(second_hat) + ADAM_EPS)
    return (
        output,
        input_grad,
        weight_grads,
        new_momentum,
        new_weights,
        new_gain_first,
        new_gain_second,
        new_gains,
    )


def solution(mesh):
    count = mesh.shape["dp"]
    fine = Mesh(
        np.asarray(mesh.devices).reshape(4, 4, count // 16, mesh.shape["tensor"]),
        ("z",) + PLANE,
    )
    every = ("z",) + PLANE
    in_specs = (
        P(every, None),
        P(every[:3], None),
        P(every, None, None),
        P(every, None, None),
        P(),
        P(),
        P(),
        P(every, None),
    )
    out_specs = (
        P(every, None),
        P(every, None),
        P(every, None, None),
        P(every, None, None),
        P(every, None, None),
        P(),
        P(),
        P(),
    )
    return jax.shard_map(local, mesh=fine, in_specs=in_specs, out_specs=out_specs, check_vma=False)
```

```python
import functools
import math

import jax
import jax.numpy as jnp
import numpy as np
from jax import lax
from jax.experimental import pallas as pl
from jax.experimental.pallas import tpu as pltpu
from jax.sharding import Mesh
from jax.sharding import PartitionSpec as P

D = 2048
FF = 8192
HD = 64
BW = 128
NS_ITERS = 5
STEP = 10

HIGHEST = lax.Precision.HIGHEST
ROPE_BASE = 130000.0
NORM_EPS = 1e-05
NEG_LARGE = -1e30
MOMENTUM_DECAY = 0.95
MUON_RATE = 0.25
COEFF_A = 3.4445
COEFF_B = -4.775
COEFF_C = 2.0315
BETA_FIRST = 0.9
BETA_SECOND = 0.95
ADAM_RATE = 1.0
ADAM_EPS = 1e-08

F32 = jnp.float32
BF16 = jnp.bfloat16
PLANE = ("m", "r", "tensor")
SWAP = [(0, 1), (1, 0)]
TILE = 256
SCORE_SCALE = 1.0 / math.sqrt(HD)


def rms_norm(values, gain):
    return values * lax.rsqrt(jnp.mean(values * values, axis=-1, keepdims=True) + NORM_EPS) * gain


def rms_norm_back(values, gain, grad):
    scale = lax.rsqrt(jnp.mean(values * values, axis=-1, keepdims=True) + NORM_EPS)
    scaled = gain * grad
    inner = jnp.mean(scaled * values, axis=-1, keepdims=True)
    gain_grad = jnp.sum(grad * values * scale, axis=0)
    return scale * scaled - values * (scale * scale * scale * inner), gain_grad


def rope_tables(place):
    exponent = jnp.arange(HD // 2).astype(F32) * (2.0 / HD)
    inverse = jnp.exp(-exponent * math.log(ROPE_BASE))
    angle = place.astype(F32)[:, None] * inverse[None, :]
    cosine, sine = jnp.cos(angle), jnp.sin(angle)
    heads = 2 * BW // HD
    return (
        jnp.tile(jnp.concatenate([cosine, cosine], axis=1), (1, heads)),
        jnp.tile(jnp.concatenate([-sine, sine], axis=1), (1, heads)),
    )


def dims(lhs, rhs):
    return (((lhs,), (rhs,)), ((), ()))


def mul(a, b):
    return lax.dot_general(a, b, dims(1, 0), preferred_element_type=F32)


def mul_bt(a, b):
    return lax.dot_general(a, b, dims(1, 1), preferred_element_type=F32)


def mul_at(a, b):
    return lax.dot_general(a, b, dims(0, 0), preferred_element_type=F32)


def side_by_side(ref, *index):
    return jnp.concatenate([ref[index + (0,)], ref[index + (1,)]], axis=-1)


def pair_rows(own_ref, other_ref):
    return jnp.concatenate([own_ref[...], other_ref[...]], axis=0)


def swap_halves(values):
    lane = lax.broadcasted_iota(jnp.int32, values.shape, 1)
    span = values.shape[1]
    ahead = pltpu.roll(values, span - HD // 2, 1)
    behind = pltpu.roll(values, HD // 2, 1)
    return jnp.where(lane % HD < HD // 2, ahead, behind)


def head_only(values, head):
    lane = lax.broadcasted_iota(jnp.int32, values.shape, 1)
    return jnp.where((lane >= head * HD) & (lane < (head + 1) * HD), values, jnp.zeros_like(values))


def head_probs(query, key, bias, head):
    scores = mul_bt(head_only(query, head), key) * SCORE_SCALE + bias
    weights = jnp.exp(scores - jnp.max(scores, axis=-1, keepdims=True))
    return weights / jnp.sum(weights, axis=-1, keepdims=True)


def attn_forward_kernel(
    own_ref, other_ref, w_ref, bias_ref, cos_ref, sin_ref, q_ref, k_ref, v_ref, c_ref, mine_ref, theirs_ref
):
    rows = pair_rows(own_ref, other_ref)
    cosine, sine = cos_ref[...], sin_ref[...]
    lin = mul(rows, side_by_side(w_ref, 0))
    query = (lin * cosine + swap_halves(lin) * sine).astype(BF16)
    lin = mul(rows, side_by_side(w_ref, 1))
    key = (lin * cosine + swap_halves(lin) * sine).astype(BF16)
    value = mul(rows, side_by_side(w_ref, 2)).astype(BF16)
    q_ref[...] = query
    k_ref[...] = key
    v_ref[...] = value
    context = jnp.zeros(query.shape, F32)
    for head in range(query.shape[1] // HD):
        probs = head_probs(query, key, bias_ref[...], head)
        context = context + mul(probs.astype(BF16), head_only(value, head))
    context = context.astype(BF16)
    c_ref[...] = context
    half = own_ref.shape[0]
    for tile in range(D // TILE):
        at = pl.ds(tile * TILE, TILE)
        w_out = jnp.concatenate([w_ref[3, 0, at, :], w_ref[3, 1, at, :]], axis=-1)
        mixed = mul_bt(context, w_out)
        mine_ref[:, at] = mixed[:half]
        theirs_ref[:, at] = mixed[half:].astype(BF16)


def attn_backward_kernel(
    own_ref, other_ref, w_ref, bias_ref, cos_ref, sin_ref, q_ref, k_ref, v_ref,
    dq_ref, dk_ref, dv_ref, mine_ref, theirs_ref,
):
    rows = pair_rows(own_ref, other_ref)
    query, key, value = q_ref[...], k_ref[...], v_ref[...]
    d_context = mul(rows, side_by_side(w_ref, 3)).astype(BF16)
    d_query = jnp.zeros(query.shape, F32)
    d_key = jnp.zeros(query.shape, F32)
    d_value = jnp.zeros(query.shape, F32)
    for head in range(query.shape[1] // HD):
        probs = head_probs(query, key, bias_ref[...], head)
        d_here = head_only(d_context, head)
        d_value = d_value + mul_at(probs.astype(BF16), d_here)
        d_probs = mul_bt(d_here, value)
        inner = jnp.sum(probs * d_probs, axis=-1, keepdims=True)
        d_scores = (probs * (d_probs - inner)).astype(BF16)
        d_query = d_query + mul(d_scores, head_only(key, head))
        d_key = d_key + mul_at(d_scores, head_only(query, head))
    cosine, sine = cos_ref[...], sin_ref[...]
    d_query = d_query * SCORE_SCALE
    d_key = d_key * SCORE_SCALE
    d_query = (d_query * cosine - swap_halves(d_query) * sine).astype(BF16)
    d_key = (d_key * cosine - swap_halves(d_key) * sine).astype(BF16)
    d_value = d_value.astype(BF16)
    dq_ref[...] = d_query
    dk_ref[...] = d_key
    dv_ref[...] = d_value
    half = own_ref.shape[0]
    for tile in range(D // TILE):
        at = pl.ds(tile * TILE, TILE)
        total = jnp.zeros((2 * half, TILE), F32)
        for matrix, columns in ((0, d_query), (1, d_key), (2, d_value)):
            w_here = jnp.concatenate([w_ref[matrix, 0, at, :], w_ref[matrix, 1, at, :]], axis=-1)
            total = total + mul_bt(columns, w_here)
        mine_ref[:, at] = total[:half]
        theirs_ref[:, at] = total[half:].astype(BF16)


def mlp_half_kernel(*refs):
    rows, d_rows = refs[:8], refs[8:16]
    w_ref, hid_ref, dgate_ref, dup_ref, grad_ref = refs[16:]
    w_gate, w_up, w_down = (
        jnp.concatenate([w_ref[0, kind], w_ref[1, kind]], axis=-1) for kind in range(3)
    )
    for piece in range(4):
        here = pair_rows(rows[2 * piece], rows[2 * piece + 1])
        gate = mul(here, w_gate)
        up = mul(here, w_up)
        d_hidden = mul(pair_rows(d_rows[2 * piece], d_rows[2 * piece + 1]), w_down)
        sigmoid = 1.0 / (1.0 + jnp.exp(-gate))
        silu = gate * sigmoid
        at = pl.ds(piece * here.shape[0], here.shape[0])
        hid_ref[at, :] = (silu * up).astype(BF16)
        dgate_ref[at, :] = (d_hidden * up * sigmoid * (1.0 + gate * (1.0 - sigmoid))).astype(BF16)
        dup_ref[at, :] = (d_hidden * silu).astype(BF16)
    for tile in range(D // TILE):
        at = pl.ds(tile * TILE, TILE)
        across = jnp.concatenate([ref[:, at] for ref in rows], axis=0)
        d_across = jnp.concatenate([ref[:, at] for ref in d_rows], axis=0)
        for kind, left, right in ((0, across, dgate_ref), (1, across, dup_ref), (2, d_across, hid_ref)):
            grad = mul_at(left, right[...]).astype(BF16)
            for chip in range(2):
                grad_ref[chip, kind, at, :] = grad[:, chip * BW : (chip + 1) * BW]


def mlp_back_kernel(
    hid_even, hid_odd, dgate_even, dgate_odd, dup_even, dup_odd, w_even, w_odd,
    dn_mine_ref, dn_theirs_ref, out_mine_ref, out_theirs_ref,
):
    def whole(kind):
        return jnp.concatenate([ref[chip, kind] for ref in (w_even, w_odd) for chip in range(4)], axis=-1)

    def columns(even, odd):
        return jnp.concatenate([even[...], odd[...]], axis=-1)

    half = dn_mine_ref.shape[0]
    total = mul_bt(columns(dgate_even, dgate_odd), whole(0)) + mul_bt(columns(dup_even, dup_odd), whole(1))
    dn_mine_ref[...] = total[:half]
    dn_theirs_ref[...] = total[half:].astype(BF16)
    total = mul_bt(columns(hid_even, hid_odd), whole(2))
    out_mine_ref[...] = total[:half]
    out_theirs_ref[...] = total[half:].astype(BF16)


def grads_kernel(sources, *refs):
    first, second = refs[:8], refs[8:16]
    columns = refs[16:-2]
    outs = refs[-2:]
    row_sets = [jnp.concatenate([ref[...] for ref in part], axis=0) for part in (first, second)]
    for index, source in enumerate(sources):
        stacked = jnp.concatenate([ref[...] for ref in columns[4 * index : 4 * index + 4]], axis=0)
        grad = mul_at(row_sets[source], stacked).astype(BF16)
        for block in range(grad.shape[1] // BW):
            outs[block % 2][block // 2, index] = grad[:, block * BW : (block + 1) * BW]


def split(values):
    high = values.astype(BF16)
    return high, (values - high.astype(F32)).astype(BF16)


def mul_split(a, b):
    return mul(a[0], b[0]) + (mul(a[0], b[1]) + mul(a[1], b[0]))


def muon_kernel(grad_ref, momentum_ref, weight_ref, wg_ref, nm_ref, nw_ref, held, mixers):
    step = pl.program_id(0)
    count = held.shape[0]

    @pl.when(step < count)
    def _():
        grad = grad_ref[...].astype(F32)
        wg_ref[...] = grad
        block = MOMENTUM_DECAY * momentum_ref[...] + grad
        nm_ref[...] = block
        block = block * (1.0 / (jnp.sqrt(jnp.sum(block * block)) + 1e-07))
        held[step] = block
        high, low = split(block)
        cross = mul_at(high, low)
        mixers[step] = mul_at(high, high) + (cross + cross.T)

    @pl.when(step == count - 1)
    def _():
        row = lax.broadcasted_iota(jnp.int32, (BW, BW), 0)
        column = lax.broadcasted_iota(jnp.int32, (BW, BW), 1)
        eye = jnp.where(row == column, COEFF_A, 0.0).astype(F32)
        grams = [mixers[index] for index in range(count)]
        totals = [None] * count
        for turn in range(NS_ITERS):
            for index in range(count):
                pair = split(grams[index])
                mixer = eye + COEFF_B * grams[index] + COEFF_C * mul_split(pair, pair)
                mixed = split(mixer)
                if turn == 0:
                    totals[index] = mixer
                else:
                    totals[index] = mul_split(split(totals[index]), mixed)
                if turn < NS_ITERS - 1:
                    grams[index] = mul_split(split(mul_split(mixed, pair)), mixed)
        for index in range(count):
            mixers[index] = totals[index]

    @pl.when(step >= count)
    def _():
        at = step - count
        ortho = mul_split(split(held[at]), split(mixers[at]))
        nw_ref[...] = weight_ref[...].astype(F32) - (MUON_RATE * math.sqrt(D / BW)) * ortho


def deferred(kernel, inputs, unread):
    return lambda *refs: kernel(*refs[:inputs], *refs[inputs + unread :])


def unread_specs(after):
    return [pl.BlockSpec(memory_space=pl.ANY) for _ in after]


def cost(flops, accessed):
    return pl.CostEstimate(flops=flops // 6, bytes_accessed=accessed // 6, transcendentals=0)


def params(mebibytes):
    return pltpu.CompilerParams(vmem_limit_bytes=mebibytes * 1024 * 1024)


def whole_specs(arrays):
    return [pl.BlockSpec(memory_space=pltpu.VMEM) for _ in arrays]


def shaped(shape, dtype):
    return jax.ShapeDtypeStruct(shape, dtype)


def attn_forward(own, other, w_attn, bias, cosine, sine, after=()):
    half = own.shape[0]
    span = w_attn.shape[1] * w_attn.shape[3]
    square = shaped((2 * half, span), BF16)
    args = (own, other, w_attn, bias, cosine, sine)
    return pl.pallas_call(
        deferred(attn_forward_kernel, len(args), len(after)),
        out_shape=(square,) * 4 + (shaped((half, D), F32), shaped((half, D), BF16)),
        in_specs=whole_specs(args) + unread_specs(after),
        out_specs=tuple(whole_specs(range(6))),
        compiler_params=params(40),
        cost_estimate=cost(1_300_000_000, 9_000_000),
        name="attn_forward",
    )(*args, *after)


def attn_backward(own, other, w_attn, bias, cosine, sine, query, key, value):
    half = own.shape[0]
    square = shaped(query.shape, BF16)
    args = (own, other, w_attn, bias, cosine, sine, query, key, value)
    return pl.pallas_call(
        attn_backward_kernel,
        out_shape=(square,) * 3 + (shaped((half, D), F32), shaped((half, D), BF16)),
        in_specs=whole_specs(args),
        out_specs=tuple(whole_specs(range(5))),
        compiler_params=params(40),
        cost_estimate=cost(1_600_000_000, 9_000_000),
        name="attn_backward",
    )(*args)


def mlp_half(rows, d_rows, w_half):
    half = rows[0].shape[0]
    columns = shaped((8 * half, 4 * BW), BF16)
    blocks = pl.BlockSpec((2, 3, D, BW), lambda j: (j, 0, 0, 0))
    return pl.pallas_call(
        mlp_half_kernel,
        grid=(2,),
        out_shape=(columns,) * 3 + (shaped(w_half.shape, BF16),),
        in_specs=[pl.BlockSpec((half, D), lambda j: (0, 0)) for _ in range(16)]
        + [blocks],
        out_specs=(pl.BlockSpec((8 * half, 2 * BW), lambda j: (0, j)),) * 3 + (blocks,),
        compiler_params=params(48),
        cost_estimate=cost(13_000_000_000, 20_000_000),
        name="mlp_half",
    )(*rows, *d_rows, w_half)


def mlp_back(piece, halves, w_even, w_odd):
    rows = halves[0][0].shape[0] // 4
    wide = 2 * TILE
    args = [half[index] for index in range(3) for half in halves]
    tile = pl.BlockSpec((rows // 2, wide), lambda i: (0, i))
    weight = pl.BlockSpec((4, 3, wide, BW), lambda i: (0, 0, i, 0))
    return pl.pallas_call(
        mlp_back_kernel,
        grid=(D // wide,),
        out_shape=(shaped((rows // 2, D), F32), shaped((rows // 2, D), BF16)) * 2,
        in_specs=[pl.BlockSpec((rows, 4 * BW), lambda i: (piece, 0)) for _ in args] + [weight] * 2,
        out_specs=(tile,) * 4,
        compiler_params=params(40),
        cost_estimate=cost(3_200_000_000, 16_000_000),
        name="mlp_back",
    )(*args, w_even, w_odd)


def weight_products(first, second, column_sets, sources, name, after=()):
    half = first[0].shape[0]
    span = column_sets[0][0].shape[1]
    pairs = span // (2 * BW)
    row_spec = pl.BlockSpec((half, TILE), lambda i: (0, i))
    column_spec = pl.BlockSpec((2 * half, span), lambda i: (0, 0))
    flat = [piece for pieces in column_sets for piece in pieces]
    return pl.pallas_call(
        deferred(functools.partial(grads_kernel, sources), 16 + len(flat), len(after)),
        grid=(D // TILE,),
        out_shape=(shaped((pairs, len(sources), D, BW), BF16),) * 2,
        in_specs=[row_spec] * 16 + [column_spec] * len(flat) + unread_specs(after),
        out_specs=(pl.BlockSpec((pairs, len(sources), TILE, BW), lambda i: (0, 0, i, 0)),) * 2,
        compiler_params=params(40),
        cost_estimate=cost(2 * 8 * half * D * span * len(sources), 20_000_000),
        name=name,
    )(*first, *second, *flat, *after)


def muon(grads, momentum, weights, offset, stride, begun=(), after=()):
    count = grads.shape[0]
    now = lambda i: jnp.minimum(i, count - 1)
    then = lambda i: jnp.maximum(i - count, 0)
    block = (None, D, BW)
    compact = pl.BlockSpec(block, lambda i: (now(i), 0, 0))
    early = pl.BlockSpec(block, lambda i: (stride * now(i) + offset, 0, 0))
    late = pl.BlockSpec(block, lambda i: (stride * then(i) + offset, 0, 0))
    return pl.pallas_call(
        deferred(muon_kernel, 3, len(begun) + len(after)),
        grid=(2 * count,),
        out_shape=(shaped(momentum.shape, F32),) * 3,
        in_specs=[compact, early, late] + unread_specs(begun) + unread_specs(after),
        out_specs=(early, early, late),
        input_output_aliases={3 + index: index for index in range(len(begun))},
        scratch_shapes=[pltpu.VMEM((count, D, BW), F32), pltpu.VMEM((count, BW, BW), F32)],
        compiler_params=params(40),
        cost_estimate=cost(1_000_000_000 * count, 5_500_000 * count),
        name="muon",
    )(grads, momentum, weights, *begun, *after)


def mirror(step):
    return [(place, place ^ step) for place in range(4)]


def ring(value, step=1):
    return lax.ppermute(value, "z", [(place, (place + step) % 4) for place in range(4)])


def swap(value):
    return lax.ppermute(value, "tensor", SWAP)


def nothing(value):
    first = value[(0,) * value.ndim].astype(F32)
    return (first * 0.0).astype(jnp.int32)


def hold(value, *others):
    zero = sum((nothing(other) for other in others), jnp.int32(0))
    return value + zero.astype(value.dtype)


def gather_rows(rows):
    mine = [rows]
    for _ in range(3):
        mine.append(ring(mine[-1]))
    return mine, [swap(part) for part in mine]


def scatter_rows(pieces):
    scatter = Scatter()
    for step in (1, 2, 3, 0):
        scatter.add(step, *pieces[step])
    return scatter.result


def gather_rows_at_once(rows):
    plane = lax.axis_index("z")
    mine = lax.all_gather(rows, "z", axis=0, tiled=False)
    other = swap(mine)
    pick = lambda stack, s: lax.dynamic_index_in_dim(stack, (plane + 4 - s) % 4, 0, keepdims=False)
    return [pick(mine, s) for s in range(4)], [pick(other, s) for s in range(4)]


def gather_rows_direct(rows):
    mine = [rows] + [ring(rows, shift) for shift in (1, 2, 3)]
    return mine, [swap(part) for part in mine]


class Scatter:
    def __init__(self):
        self.moving = self.result = None
        self.payloads = []

    def add(self, step, mine, theirs):
        total = mine + swap(theirs).astype(F32)
        if self.moving is not None:
            total = total + self.moving.astype(F32)
        if step:
            self.payloads.append(total.astype(BF16))
            self.moving = ring(self.payloads[-1])
        else:
            self.result = total


def everywhere(value):
    value = value + swap(value)
    for axis in ("m", "z"):
        for step in (1, 2):
            value = value + lax.ppermute(value, axis, mirror(step))
    if lax.axis_size("r") > 1:
        value = lax.psum(value, "r")
    return value


def join(parts):
    if parts.shape[0] == 4:
        return parts
    width = parts.shape[3]
    parts = parts.reshape(4, 2, -1, D, width).transpose(0, 1, 3, 2, 4)
    return parts.reshape(4, 2, D, BW)


def unjoin(grads, width):
    if width == BW:
        return grads
    grads = grads.reshape(4, 2, D, -1, width).transpose(0, 1, 3, 2, 4)
    return grads.reshape(-1, 1, D, width)


def gather_plane(parts):
    return lax.all_gather(jnp.stack(parts), ("m", "r"), axis=0, tiled=False)


def gather_part_direct(part, index, result):
    chip = lax.axis_index("m")
    result = lax.dynamic_update_slice(result, part[None, None], (chip, index, 0, 0))
    for step in (1, 2, 3):
        got = lax.ppermute(part, "m", mirror(step))
        result = lax.dynamic_update_slice(result, got[None, None], (chip ^ step, index, 0, 0))
    return result


def scatter_plane(grads):
    share = lax.psum_scatter(
        grads.reshape(grads.shape[0], -1, grads.shape[3]), ("m", "r"), scatter_dimension=0, tiled=False
    )
    return share.reshape(grads.shape[1:])


def scatter_plane_direct(grads, *others):
    chip = lax.axis_index("m")
    zero = sum((nothing(other) for other in others), jnp.int32(0)).astype(F32)

    def share_for(step):
        return lax.dynamic_index_in_dim(grads, chip ^ step, 0, keepdims=False)

    total = share_for(0).astype(F32) + zero
    for step in (1, 2, 3):
        total = total + lax.ppermute(share_for(step), "m", mirror(step)).astype(F32)
    return total.astype(BF16)


def interleave(mine, other):
    return [rows for pair in zip(mine, other) for rows in pair]


def local(tokens, segments, weights, momentum, gains, gain_first, gain_second, cotangent):
    plane = lax.axis_index("z")
    core = lax.axis_index("tensor")
    block_count = weights.shape[0]

    if block_count == 8:
        shards = weights.reshape(4, 2, D, BW)
    else:
        width = block_count * BW // 4
        shards = weights.reshape(block_count, D, -1, width).transpose(0, 2, 1, 3).reshape(4, 1, D, width)
    parts, width = shards.shape[1], shards.shape[3]

    def shard(shift, part, *others):
        at = sum((nothing(other) for other in others), plane + shift)
        return lax.dynamic_slice(shards, (at % 4, part, 0, 0), (1, 1, D, width))[0, 0]

    rows_in = tokens.astype(F32)
    one_mine, one_other = gather_rows_at_once(rms_norm(rows_in, gains[0]).astype(BF16))

    moved = []
    for part in range(parts):
        others = moved[0][1:] if part else []
        moved.append([shard(0, part)] + [ring(shard(shift, part, *others), shift) for shift in (1, 2, 3)])

    def kind_part(source, part, *others):
        at = sum((nothing(other) for other in others), plane)
        return lax.select_n(at, *(moved[part][(here - source) % 4] for here in range(4)))

    if parts == 2:
        mlp_parts = [[kind_part(kind, 0) for kind in (1, 2, 3)]]
        w_attn = gather_part_direct(kind_part(0, 0), 0, jnp.zeros((4, 2, D, BW), BF16))
        w_attn_even = w_attn
        waits = (w_attn, mlp_parts[0][0], one_mine[1])
        w_attn = gather_part_direct(kind_part(0, 1, *waits), 1, w_attn)
        mlp_parts.append([kind_part(kind, 1, w_attn_even) for kind in (1, 2, 3)])
        begun = [mlp_parts[1][0]]
        w_mlp = [gather_plane(kinds) for kinds in mlp_parts]
    else:
        w_attn = join(gather_plane([kind_part(0, 0)]))
        w_mlp = gather_plane([kind_part(kind, 0) for kind in (1, 2, 3)])
        w_mlp = jnp.stack([join(w_mlp[:, kind : kind + 1]) for kind in range(3)], axis=1)
        w_mlp = [w_mlp[:, :, 0], w_mlp[:, :, 1]]
        begun = []
    d_mine, d_other = gather_rows(hold(cotangent, *begun))

    segment_parts = [segments] + [ring(segments, shift) for shift in (1, 2, 3)]
    segment_rows = jnp.concatenate(segment_parts, axis=0)
    length = segment_rows.shape[1]
    half = length // 2
    place = jnp.arange(length)
    place = jnp.where(core == 0, place, (place + half) % length)
    segment_rows = jnp.where(core == 0, segment_rows, jnp.roll(segment_rows, half, axis=1))
    allowed = (place[None, None, :] <= place[None, :, None]) & (
        segment_rows[:, None, :] == segment_rows[:, :, None]
    )
    bias = jnp.where(allowed, 0.0, NEG_LARGE).astype(F32)
    cosine, sine = rope_tables(place)

    query, key, value, context = ([None] * 4 for _ in range(4))
    mixed = Scatter()
    for s in (1, 2, 3, 0):
        query[s], key[s], value[s], context[s], *both = attn_forward(
            one_mine[s], one_other[s], w_attn, bias[s], cosine, sine, mixed.payloads[:1] if s == 3 else begun if s == 1 else d_mine[2:3] if s == 0 else ()
        )
        mixed.add(s, *both)
    middle = rows_in + mixed.result
    two_mine, two_other = gather_rows(rms_norm(middle, gains[1]).astype(BF16))

    two_rows, d_rows = interleave(two_mine, two_other), interleave(d_mine, d_other)
    *even_half, mlp_even = mlp_half(two_rows, d_rows, w_mlp[0])
    *odd_half, mlp_odd = mlp_half(two_rows, d_rows, w_mlp[1])
    outward = [None] * 4
    d_normed = Scatter()
    for s in (1, 2, 3, 0):
        *d_two, out_mine, out_theirs = mlp_back(s, (even_half, odd_half), *w_mlp)
        outward[s] = (out_mine, out_theirs)
        d_normed.add(s, *d_two)
    d_normed_two = d_normed.result

    d_output = cotangent.astype(F32)
    d_middle_norm, d_gain_two = rms_norm_back(middle, gains[1], d_normed_two)
    d_middle = d_output + d_middle_norm
    e_mine, e_other = gather_rows(d_middle.astype(BF16))
    d_query, d_key, d_value, d_one = ([None] * 4 for _ in range(4))
    for s in range(4):
        d_query[s], d_key[s], d_value[s], *both = attn_backward(
            e_mine[s], e_other[s], w_attn, bias[s], cosine, sine, query[s], key[s], value[s]
        )
        d_one[s] = both
    attn_grads = weight_products(
        interleave(one_mine, one_other),
        interleave(e_mine, e_other),
        (d_query, d_key, d_value, context),
        (0, 0, 0, 1),
        "attn_products",
    )
    if parts == 2:
        attn_share = [scatter_plane_direct(grads[0]) for grads in attn_grads]
        mlp_share = [
            scatter_plane(mlp_even),
            scatter_plane(mlp_odd),
        ]
    else:
        attn_share = [scatter_plane(unjoin(jnp.stack([grads[0] for grads in attn_grads], axis=1), width))[0]]
        mlp_grads = jnp.stack([mlp_even, mlp_odd], axis=2)
        mlp_share = [
            jnp.concatenate([scatter_plane(unjoin(mlp_grads[:, kind], width)) for kind in range(3)])
        ]

    d_normed_one = scatter_rows(d_one)
    d_rows_norm, d_gain_one = rms_norm_back(rows_in, gains[0], d_normed_one)
    input_grad = d_middle + d_rows_norm
    late = [(hold(mine, e_other[3]), hold(theirs, e_other[3])) for mine, theirs in outward]
    output = (middle + scatter_rows(late)).astype(BF16)
    gain_grads = everywhere(jnp.stack([d_gain_one, d_gain_two]))

    results = ()
    for part in range(parts):
        shares = jnp.concatenate([attn_share[part][None], mlp_share[part]])
        at = plane + nothing(output) if part == 0 else plane

        def share_of(shift):
            return lax.dynamic_index_in_dim(shares, (at + shift) % 4, 0, keepdims=False)

        back = [share_of(0)] + [ring(share_of(shift), shift) for shift in (1, 2, 3)]
        here = plane + nothing(results[1]) if part else plane
        summed = jnp.stack(
            [lax.select_n(here, *(back[(z - source) % 4] for z in range(4))) for source in range(4)]
        )
        if parts == 1:
            summed = summed.reshape(block_count, -1, D, width).transpose(0, 2, 1, 3).reshape(block_count, D, BW)
        results = muon(summed, momentum, weights, part, parts, results, (gain_grads,) if part == 0 else ())
    weight_grads, new_momentum, new_weights = results

    new_gain_first = BETA_FIRST * gain_first + (1.0 - BETA_FIRST) * gain_grads
    new_gain_second = BETA_SECOND * gain_second + (1.0 - BETA_SECOND) * gain_grads * gain_grads
    first_hat = new_gain_first / (1.0 - BETA_FIRST**STEP)
    second_hat = new_gain_second / (1.0 - BETA_SECOND**STEP)
    new_gains = gains - ADAM_RATE * first_hat / (jnp.sqrt(second_hat) + ADAM_EPS)
    return (
        output,
        input_grad,
        weight_grads,
        new_momentum,
        new_weights,
        new_gain_first,
        new_gain_second,
        new_gains,
    )


def solution(mesh):
    count = mesh.shape["dp"]
    fine = Mesh(
        np.asarray(mesh.devices).reshape(4, 4, count // 16, mesh.shape["tensor"]),
        ("z",) + PLANE,
    )
    every = ("z",) + PLANE
    in_specs = (
        P(every, None),
        P(every[:3], None),
        P(every, None, None),
        P(every, None, None),
        P(),
        P(),
        P(),
        P(every, None),
    )
    out_specs = (
        P(every, None),
        P(every, None),
        P(every, None, None),
        P(every, None, None),
        P(every, None, None),
        P(),
        P(),
        P(),
    )
    return jax.shard_map(local, mesh=fine, in_specs=in_specs, out_specs=out_specs, check_vma=False)
```

```python
import functools
import math

import jax
import jax.numpy as jnp
import numpy as np
from jax import lax
from jax.experimental import pallas as pl
from jax.experimental.pallas import tpu as pltpu
from jax.sharding import Mesh
from jax.sharding import PartitionSpec as P

D = 2048
FF = 8192
HD = 64
BW = 128
NS_ITERS = 5
STEP = 10

HIGHEST = lax.Precision.HIGHEST
ROPE_BASE = 130000.0
NORM_EPS = 1e-05
NEG_LARGE = -1e30
MOMENTUM_DECAY = 0.95
MUON_RATE = 0.25
COEFF_A = 3.4445
COEFF_B = -4.775
COEFF_C = 2.0315
BETA_FIRST = 0.9
BETA_SECOND = 0.95
ADAM_RATE = 1.0
ADAM_EPS = 1e-08

F32 = jnp.float32
BF16 = jnp.bfloat16
PLANE = ("m", "r", "tensor")
SWAP = [(0, 1), (1, 0)]
TILE = 256
SCORE_SCALE = 1.0 / math.sqrt(HD)


def rms_norm(values, gain):
    return values * lax.rsqrt(jnp.mean(values * values, axis=-1, keepdims=True) + NORM_EPS) * gain


def rms_norm_back(values, gain, grad):
    scale = lax.rsqrt(jnp.mean(values * values, axis=-1, keepdims=True) + NORM_EPS)
    scaled = gain * grad
    inner = jnp.mean(scaled * values, axis=-1, keepdims=True)
    gain_grad = jnp.sum(grad * values * scale, axis=0)
    return scale * scaled - values * (scale * scale * scale * inner), gain_grad


def rope_tables(place):
    exponent = jnp.arange(HD // 2).astype(F32) * (2.0 / HD)
    inverse = jnp.exp(-exponent * math.log(ROPE_BASE))
    angle = place.astype(F32)[:, None] * inverse[None, :]
    cosine, sine = jnp.cos(angle), jnp.sin(angle)
    heads = 2 * BW // HD
    return (
        jnp.tile(jnp.concatenate([cosine, cosine], axis=1), (1, heads)),
        jnp.tile(jnp.concatenate([-sine, sine], axis=1), (1, heads)),
    )


def dims(lhs, rhs):
    return (((lhs,), (rhs,)), ((), ()))


def mul(a, b):
    return lax.dot_general(a, b, dims(1, 0), preferred_element_type=F32)


def mul_bt(a, b):
    return lax.dot_general(a, b, dims(1, 1), preferred_element_type=F32)


def mul_at(a, b):
    return lax.dot_general(a, b, dims(0, 0), preferred_element_type=F32)


def side_by_side(ref, *index):
    return jnp.concatenate([ref[index + (0,)], ref[index + (1,)]], axis=-1)


def pair_rows(own_ref, other_ref):
    return jnp.concatenate([own_ref[...], other_ref[...]], axis=0)


def swap_halves(values):
    lane = lax.broadcasted_iota(jnp.int32, values.shape, 1)
    span = values.shape[1]
    ahead = pltpu.roll(values, span - HD // 2, 1)
    behind = pltpu.roll(values, HD // 2, 1)
    return jnp.where(lane % HD < HD // 2, ahead, behind)


def head_only(values, head):
    lane = lax.broadcasted_iota(jnp.int32, values.shape, 1)
    return jnp.where((lane >= head * HD) & (lane < (head + 1) * HD), values, jnp.zeros_like(values))


def head_probs(query, key, bias, head):
    scores = mul_bt(head_only(query, head), key) * SCORE_SCALE + bias
    weights = jnp.exp(scores - jnp.max(scores, axis=-1, keepdims=True))
    return weights / jnp.sum(weights, axis=-1, keepdims=True)


def attn_forward_kernel(
    own_ref, other_ref, w_ref, bias_ref, cos_ref, sin_ref, q_ref, k_ref, v_ref, c_ref, mine_ref, theirs_ref
):
    rows = pair_rows(own_ref, other_ref)
    cosine, sine = cos_ref[...], sin_ref[...]
    lin = mul(rows, side_by_side(w_ref, 0))
    query = (lin * cosine + swap_halves(lin) * sine).astype(BF16)
    lin = mul(rows, side_by_side(w_ref, 1))
    key = (lin * cosine + swap_halves(lin) * sine).astype(BF16)
    value = mul(rows, side_by_side(w_ref, 2)).astype(BF16)
    q_ref[...] = query
    k_ref[...] = key
    v_ref[...] = value
    context = jnp.zeros(query.shape, F32)
    for head in range(query.shape[1] // HD):
        probs = head_probs(query, key, bias_ref[...], head)
        context = context + mul(probs.astype(BF16), head_only(value, head))
    context = context.astype(BF16)
    c_ref[...] = context
    half = own_ref.shape[0]
    for tile in range(D // TILE):
        at = pl.ds(tile * TILE, TILE)
        w_out = jnp.concatenate([w_ref[3, 0, at, :], w_ref[3, 1, at, :]], axis=-1)
        mixed = mul_bt(context, w_out)
        mine_ref[:, at] = mixed[:half]
        theirs_ref[:, at] = mixed[half:].astype(BF16)


def attn_backward_kernel(
    own_ref, other_ref, w_ref, bias_ref, cos_ref, sin_ref, q_ref, k_ref, v_ref,
    dq_ref, dk_ref, dv_ref, mine_ref, theirs_ref,
):
    rows = pair_rows(own_ref, other_ref)
    query, key, value = q_ref[...], k_ref[...], v_ref[...]
    d_context = mul(rows, side_by_side(w_ref, 3)).astype(BF16)
    d_query = jnp.zeros(query.shape, F32)
    d_key = jnp.zeros(query.shape, F32)
    d_value = jnp.zeros(query.shape, F32)
    for head in range(query.shape[1] // HD):
        probs = head_probs(query, key, bias_ref[...], head)
        d_here = head_only(d_context, head)
        d_value = d_value + mul_at(probs.astype(BF16), d_here)
        d_probs = mul_bt(d_here, value)
        inner = jnp.sum(probs * d_probs, axis=-1, keepdims=True)
        d_scores = (probs * (d_probs - inner)).astype(BF16)
        d_query = d_query + mul(d_scores, head_only(key, head))
        d_key = d_key + mul_at(d_scores, head_only(query, head))
    cosine, sine = cos_ref[...], sin_ref[...]
    d_query = d_query * SCORE_SCALE
    d_key = d_key * SCORE_SCALE
    d_query = (d_query * cosine - swap_halves(d_query) * sine).astype(BF16)
    d_key = (d_key * cosine - swap_halves(d_key) * sine).astype(BF16)
    d_value = d_value.astype(BF16)
    dq_ref[...] = d_query
    dk_ref[...] = d_key
    dv_ref[...] = d_value
    half = own_ref.shape[0]
    for tile in range(D // TILE):
        at = pl.ds(tile * TILE, TILE)
        total = jnp.zeros((2 * half, TILE), F32)
        for matrix, columns in ((0, d_query), (1, d_key), (2, d_value)):
            w_here = jnp.concatenate([w_ref[matrix, 0, at, :], w_ref[matrix, 1, at, :]], axis=-1)
            total = total + mul_bt(columns, w_here)
        mine_ref[:, at] = total[:half]
        theirs_ref[:, at] = total[half:].astype(BF16)


def mlp_half_kernel(*refs):
    rows, d_rows = refs[:8], refs[8:16]
    w_ref, hid_ref, dgate_ref, dup_ref, grad_ref = refs[16:]
    w_gate, w_up, w_down = (
        jnp.concatenate([w_ref[0, kind], w_ref[1, kind]], axis=-1) for kind in range(3)
    )
    for piece in range(4):
        here = pair_rows(rows[2 * piece], rows[2 * piece + 1])
        gate = mul(here, w_gate)
        up = mul(here, w_up)
        d_hidden = mul(pair_rows(d_rows[2 * piece], d_rows[2 * piece + 1]), w_down)
        sigmoid = 1.0 / (1.0 + jnp.exp(-gate))
        silu = gate * sigmoid
        at = pl.ds(piece * here.shape[0], here.shape[0])
        hid_ref[at, :] = (silu * up).astype(BF16)
        dgate_ref[at, :] = (d_hidden * up * sigmoid * (1.0 + gate * (1.0 - sigmoid))).astype(BF16)
        dup_ref[at, :] = (d_hidden * silu).astype(BF16)
    for tile in range(D // TILE):
        at = pl.ds(tile * TILE, TILE)
        across = jnp.concatenate([ref[:, at] for ref in rows], axis=0)
        d_across = jnp.concatenate([ref[:, at] for ref in d_rows], axis=0)
        for kind, left, right in ((0, across, dgate_ref), (1, across, dup_ref), (2, d_across, hid_ref)):
            grad = mul_at(left, right[...]).astype(BF16)
            for chip in range(2):
                grad_ref[chip, kind, at, :] = grad[:, chip * BW : (chip + 1) * BW]


def mlp_back_kernel(
    hid_even, hid_odd, dgate_even, dgate_odd, dup_even, dup_odd, w_even, w_odd,
    dn_mine_ref, dn_theirs_ref, out_mine_ref, out_theirs_ref,
):
    def whole(kind):
        return jnp.concatenate([ref[chip, kind] for ref in (w_even, w_odd) for chip in range(4)], axis=-1)

    def columns(even, odd):
        return jnp.concatenate([even[...], odd[...]], axis=-1)

    half = dn_mine_ref.shape[0]
    total = mul_bt(columns(dgate_even, dgate_odd), whole(0)) + mul_bt(columns(dup_even, dup_odd), whole(1))
    dn_mine_ref[...] = total[:half]
    dn_theirs_ref[...] = total[half:].astype(BF16)
    total = mul_bt(columns(hid_even, hid_odd), whole(2))
    out_mine_ref[...] = total[:half]
    out_theirs_ref[...] = total[half:].astype(BF16)


def grads_kernel(sources, *refs):
    first, second = refs[:8], refs[8:16]
    columns = refs[16:-1]
    out_ref = refs[-1]
    row_sets = [jnp.concatenate([ref[...] for ref in part], axis=0) for part in (first, second)]
    for index, source in enumerate(sources):
        stacked = jnp.concatenate([ref[...] for ref in columns[4 * index : 4 * index + 4]], axis=0)
        grad = mul_at(row_sets[source], stacked).astype(BF16)
        for block in range(grad.shape[1] // BW):
            out_ref[index, block] = grad[:, block * BW : (block + 1) * BW]


def split(values):
    high = values.astype(BF16)
    return high, (values - high.astype(F32)).astype(BF16)


def mul_split(a, b):
    return mul(a[0], b[0]) + (mul(a[0], b[1]) + mul(a[1], b[0]))


def muon_kernel(grad_ref, momentum_ref, weight_ref, wg_ref, nm_ref, nw_ref, held, mixers):
    step = pl.program_id(0)
    count = held.shape[0]

    @pl.when(step < count)
    def _():
        grad = grad_ref[...].astype(F32)
        wg_ref[...] = grad
        block = MOMENTUM_DECAY * momentum_ref[...] + grad
        nm_ref[...] = block
        block = block * (1.0 / (jnp.sqrt(jnp.sum(block * block)) + 1e-07))
        held[step] = block
        high, low = split(block)
        cross = mul_at(high, low)
        mixers[step] = mul_at(high, high) + (cross + cross.T)

    @pl.when(step == count - 1)
    def _():
        row = lax.broadcasted_iota(jnp.int32, (BW, BW), 0)
        column = lax.broadcasted_iota(jnp.int32, (BW, BW), 1)
        eye = jnp.where(row == column, COEFF_A, 0.0).astype(F32)
        grams = [mixers[index] for index in range(count)]
        totals = [None] * count
        for turn in range(NS_ITERS):
            for index in range(count):
                pair = split(grams[index])
                mixer = eye + COEFF_B * grams[index] + COEFF_C * mul_split(pair, pair)
                mixed = split(mixer)
                if turn == 0:
                    totals[index] = mixer
                else:
                    totals[index] = mul_split(split(totals[index]), mixed)
                if turn < NS_ITERS - 1:
                    grams[index] = mul_split(split(mul_split(mixed, pair)), mixed)
        for index in range(count):
            mixers[index] = totals[index]

    @pl.when(step >= count)
    def _():
        at = step - count
        ortho = mul_split(split(held[at]), split(mixers[at]))
        nw_ref[...] = weight_ref[...].astype(F32) - (MUON_RATE * math.sqrt(D / BW)) * ortho


def deferred(kernel, inputs, unread):
    return lambda *refs: kernel(*refs[:inputs], *refs[inputs + unread :])


def unread_specs(after):
    return [pl.BlockSpec(memory_space=pl.ANY) for _ in after]


def cost(flops, accessed):
    return pl.CostEstimate(flops=flops // 6, bytes_accessed=accessed // 6, transcendentals=0)


def params(mebibytes):
    return pltpu.CompilerParams(vmem_limit_bytes=mebibytes * 1024 * 1024)


def whole_specs(arrays):
    return [pl.BlockSpec(memory_space=pltpu.VMEM) for _ in arrays]


def shaped(shape, dtype):
    return jax.ShapeDtypeStruct(shape, dtype)


def attn_forward(own, other, w_attn, bias, cosine, sine, after=()):
    half = own.shape[0]
    span = w_attn.shape[1] * w_attn.shape[3]
    square = shaped((2 * half, span), BF16)
    args = (own, other, w_attn, bias, cosine, sine)
    return pl.pallas_call(
        deferred(attn_forward_kernel, len(args), len(after)),
        out_shape=(square,) * 4 + (shaped((half, D), F32), shaped((half, D), BF16)),
        in_specs=whole_specs(args) + unread_specs(after),
        out_specs=tuple(whole_specs(range(6))),
        compiler_params=params(40),
        cost_estimate=cost(1_300_000_000, 9_000_000),
        name="attn_forward",
    )(*args, *after)


def attn_backward(own, other, w_attn, bias, cosine, sine, query, key, value):
    half = own.shape[0]
    square = shaped(query.shape, BF16)
    args = (own, other, w_attn, bias, cosine, sine, query, key, value)
    return pl.pallas_call(
        attn_backward_kernel,
        out_shape=(square,) * 3 + (shaped((half, D), F32), shaped((half, D), BF16)),
        in_specs=whole_specs(args),
        out_specs=tuple(whole_specs(range(5))),
        compiler_params=params(40),
        cost_estimate=cost(1_600_000_000, 9_000_000),
        name="attn_backward",
    )(*args)


def mlp_half(rows, d_rows, w_half):
    half = rows[0].shape[0]
    columns = shaped((8 * half, 4 * BW), BF16)
    blocks = pl.BlockSpec((2, 3, D, BW), lambda j: (j, 0, 0, 0))
    return pl.pallas_call(
        mlp_half_kernel,
        grid=(2,),
        out_shape=(columns,) * 3 + (shaped(w_half.shape, BF16),),
        in_specs=[pl.BlockSpec((half, D), lambda j: (0, 0)) for _ in range(16)]
        + [blocks],
        out_specs=(pl.BlockSpec((8 * half, 2 * BW), lambda j: (0, j)),) * 3 + (blocks,),
        compiler_params=params(58),
        cost_estimate=cost(13_000_000_000, 20_000_000),
        name="mlp_half",
    )(*rows, *d_rows, w_half)


def mlp_back(piece, halves, w_even, w_odd):
    rows = halves[0][0].shape[0] // 4
    wide = 2 * TILE
    args = [half[index] for index in range(3) for half in halves]
    tile = pl.BlockSpec((rows // 2, wide), lambda i: (0, i))
    weight = pl.BlockSpec((4, 3, wide, BW), lambda i: (0, 0, i, 0))
    return pl.pallas_call(
        mlp_back_kernel,
        grid=(D // wide,),
        out_shape=(shaped((rows // 2, D), F32), shaped((rows // 2, D), BF16)) * 2,
        in_specs=[pl.BlockSpec((rows, 4 * BW), lambda i: (piece, 0)) for _ in args] + [weight] * 2,
        out_specs=(tile,) * 4,
        compiler_params=params(58),
        cost_estimate=cost(3_200_000_000, 16_000_000),
        name="mlp_back",
    )(*args, w_even, w_odd)


def weight_products(first, second, column_sets, sources, name, after=()):
    half = first[0].shape[0]
    span = column_sets[0][0].shape[1]
    row_spec = pl.BlockSpec((half, TILE), lambda i: (0, i))
    column_spec = pl.BlockSpec((2 * half, span), lambda i: (0, 0))
    flat = [piece for pieces in column_sets for piece in pieces]
    return pl.pallas_call(
        deferred(functools.partial(grads_kernel, sources), 16 + len(flat), len(after)),
        grid=(D // TILE,),
        out_shape=shaped((len(sources), span // BW, D, BW), BF16),
        in_specs=[row_spec] * 16 + [column_spec] * len(flat) + unread_specs(after),
        out_specs=pl.BlockSpec((len(sources), span // BW, TILE, BW), lambda i: (0, 0, i, 0)),
        compiler_params=params(40),
        cost_estimate=cost(2 * 8 * half * D * span * len(sources), 20_000_000),
        name=name,
    )(*first, *second, *flat, *after)


def muon(grads, momentum, weights, offset, stride, begun=(), after=()):
    count = grads.shape[0]
    now = lambda i: jnp.minimum(i, count - 1)
    then = lambda i: jnp.maximum(i - count, 0)
    block = (None, D, BW)
    compact = pl.BlockSpec(block, lambda i: (now(i), 0, 0))
    early = pl.BlockSpec(block, lambda i: (stride * now(i) + offset, 0, 0))
    late = pl.BlockSpec(block, lambda i: (stride * then(i) + offset, 0, 0))
    return pl.pallas_call(
        deferred(muon_kernel, 3, len(begun) + len(after)),
        grid=(2 * count,),
        out_shape=(shaped(momentum.shape, F32),) * 3,
        in_specs=[compact, early, late] + unread_specs(begun) + unread_specs(after),
        out_specs=(early, early, late),
        input_output_aliases={3 + index: index for index in range(len(begun))},
        scratch_shapes=[pltpu.VMEM((count, D, BW), F32), pltpu.VMEM((count, BW, BW), F32)],
        compiler_params=params(40),
        cost_estimate=cost(1_000_000_000 * count, 5_500_000 * count),
        name="muon",
    )(grads, momentum, weights, *begun, *after)


def mirror(step):
    return [(place, place ^ step) for place in range(4)]


def ring(value, step=1):
    return lax.ppermute(value, "z", [(place, (place + step) % 4) for place in range(4)])


def swap(value):
    return lax.ppermute(value, "tensor", SWAP)


def nothing(value):
    first = value[(0,) * value.ndim].astype(F32)
    return (first * 0.0).astype(jnp.int32)


def hold(value, *others):
    zero = sum((nothing(other) for other in others), jnp.int32(0))
    return value + zero.astype(value.dtype)


def gather_rows(rows):
    mine = [rows]
    for _ in range(3):
        mine.append(ring(mine[-1]))
    return mine, [swap(part) for part in mine]


def gather_rows_at_once(rows):
    plane = lax.axis_index("z")
    mine = lax.all_gather(rows, "z", axis=0, tiled=False)
    other = swap(mine)
    pick = lambda stack, s: lax.dynamic_index_in_dim(stack, (plane + 4 - s) % 4, 0, keepdims=False)
    return [pick(mine, s) for s in range(4)], [pick(other, s) for s in range(4)]


def gather_rows_direct(rows):
    mine = [rows] + [ring(rows, shift) for shift in (1, 2, 3)]
    return mine, [swap(part) for part in mine]


class Scatter:
    def __init__(self):
        self.moving = self.result = None
        self.payloads = []

    def add(self, step, mine, theirs):
        total = mine + swap(theirs).astype(F32)
        if self.moving is not None:
            total = total + self.moving.astype(F32)
        if step:
            self.payloads.append(total.astype(BF16))
            self.moving = ring(self.payloads[-1])
        else:
            self.result = total


def everywhere(value):
    value = value + swap(value)
    for axis in ("m", "z"):
        for step in (1, 2):
            value = value + lax.ppermute(value, axis, mirror(step))
    if lax.axis_size("r") > 1:
        value = lax.psum(value, "r")
    return value


def join(parts):
    if parts.shape[0] == 4:
        return parts
    width = parts.shape[3]
    parts = parts.reshape(4, 2, -1, D, width).transpose(0, 1, 3, 2, 4)
    return parts.reshape(4, 2, D, BW)


def unjoin(grads, width):
    if width == BW:
        return grads
    grads = grads.reshape(4, 2, D, -1, width).transpose(0, 1, 3, 2, 4)
    return grads.reshape(-1, 1, D, width)


def gather_plane(parts):
    return lax.all_gather(jnp.stack(parts), ("m", "r"), axis=0, tiled=False)


def gather_part_direct(part, index, result):
    chip = lax.axis_index("m")
    result = lax.dynamic_update_slice(result, part[None, None], (chip, index, 0, 0))
    for step in (1, 2, 3):
        got = lax.ppermute(part, "m", mirror(step))
        result = lax.dynamic_update_slice(result, got[None, None], (chip ^ step, index, 0, 0))
    return result


def scatter_plane(grads):
    share = lax.psum_scatter(
        grads.reshape(grads.shape[0], -1, grads.shape[3]), ("m", "r"), scatter_dimension=0, tiled=False
    )
    return share.reshape(grads.shape[1:])


def scatter_plane_direct(grads, *others):
    chip = lax.axis_index("m")
    zero = sum((nothing(other) for other in others), jnp.int32(0)).astype(F32)

    def share_for(step):
        return lax.dynamic_index_in_dim(grads, chip ^ step, 0, keepdims=False)

    total = share_for(0).astype(F32) + zero
    for step in (1, 2, 3):
        total = total + lax.ppermute(share_for(step), "m", mirror(step)).astype(F32)
    return total.astype(BF16)


def interleave(mine, other):
    return [rows for pair in zip(mine, other) for rows in pair]


def local(tokens, segments, weights, momentum, gains, gain_first, gain_second, cotangent):
    plane = lax.axis_index("z")
    core = lax.axis_index("tensor")
    block_count = weights.shape[0]

    if block_count == 8:
        shards = weights.reshape(4, 2, D, BW)
    else:
        width = block_count * BW // 4
        shards = weights.reshape(block_count, D, -1, width).transpose(0, 2, 1, 3).reshape(4, 1, D, width)
    parts, width = shards.shape[1], shards.shape[3]

    def shard(shift, part, *others):
        at = sum((nothing(other) for other in others), plane + shift)
        return lax.dynamic_slice(shards, (at % 4, part, 0, 0), (1, 1, D, width))[0, 0]

    rows_in = tokens.astype(F32)
    one_mine, one_other = gather_rows_at_once(rms_norm(rows_in, gains[0]).astype(BF16))

    moved = []
    for part in range(parts):
        others = moved[0][1:] if part else []
        moved.append([shard(0, part)] + [ring(shard(shift, part, *others), shift) for shift in (1, 2, 3)])

    def kind_part(source, part, *others):
        at = sum((nothing(other) for other in others), plane)
        return lax.select_n(at, *(moved[part][(here - source) % 4] for here in range(4)))

    if parts == 2:
        mlp_parts = [[kind_part(kind, 0) for kind in (1, 2, 3)]]
        w_attn = gather_part_direct(kind_part(0, 0), 0, jnp.zeros((4, 2, D, BW), BF16))
        w_attn_even = w_attn
        waits = (w_attn, mlp_parts[0][0], one_mine[1])
        w_attn = gather_part_direct(kind_part(0, 1, *waits), 1, w_attn)
        mlp_parts.append([kind_part(kind, 1, w_attn_even) for kind in (1, 2, 3)])
        begun = [mlp_parts[1][0]]
        w_mlp = [gather_plane(kinds) for kinds in mlp_parts]
    else:
        w_attn = join(gather_plane([kind_part(0, 0)]))
        w_mlp = gather_plane([kind_part(kind, 0) for kind in (1, 2, 3)])
        w_mlp = jnp.stack([join(w_mlp[:, kind : kind + 1]) for kind in range(3)], axis=1)
        w_mlp = [w_mlp[:, :, 0], w_mlp[:, :, 1]]
        begun = []
    d_mine, d_other = gather_rows(hold(cotangent, w_attn))

    segment_parts = [segments] + [ring(segments, shift) for shift in (1, 2, 3)]
    segment_rows = jnp.concatenate(segment_parts, axis=0)
    length = segment_rows.shape[1]
    half = length // 2
    place = jnp.arange(length)
    place = jnp.where(core == 0, place, (place + half) % length)
    segment_rows = jnp.where(core == 0, segment_rows, jnp.roll(segment_rows, half, axis=1))
    allowed = (place[None, None, :] <= place[None, :, None]) & (
        segment_rows[:, None, :] == segment_rows[:, :, None]
    )
    bias = jnp.where(allowed, 0.0, NEG_LARGE).astype(F32)
    cosine, sine = rope_tables(place)

    query, key, value, context = ([None] * 4 for _ in range(4))
    mixed = Scatter()
    for s in (1, 2, 3, 0):
        query[s], key[s], value[s], context[s], *both = attn_forward(
            one_mine[s], one_other[s], w_attn, bias[s], cosine, sine, mixed.payloads[:1] if s == 3 else begun if s == 1 else d_mine[2:3] if s == 0 else ()
        )
        mixed.add(s, *both)
    middle = rows_in + mixed.result
    two_mine, two_other = gather_rows(rms_norm(middle, gains[1]).astype(BF16))

    two_rows, d_rows = interleave(two_mine, two_other), interleave(d_mine, d_other)
    *even_half, mlp_even = mlp_half(two_rows, d_rows, w_mlp[0])
    *odd_half, mlp_odd = mlp_half(two_rows, d_rows, w_mlp[1])
    outward = [None] * 4
    d_normed = Scatter()
    for s in (1, 2, 3, 0):
        *d_two, out_mine, out_theirs = mlp_back(s, (even_half, odd_half), *w_mlp)
        outward[s] = (out_mine, out_theirs)
        d_normed.add(s, *d_two)
    d_normed_two = d_normed.result

    d_output = cotangent.astype(F32)
    d_middle_norm, d_gain_two = rms_norm_back(middle, gains[1], d_normed_two)
    d_middle = d_output + d_middle_norm
    e_mine, e_other = gather_rows(d_middle.astype(BF16))
    d_query, d_key, d_value, d_one = ([None] * 4 for _ in range(4))
    for s in range(4):
        d_query[s], d_key[s], d_value[s], *both = attn_backward(
            e_mine[s], e_other[s], w_attn, bias[s], cosine, sine, query[s], key[s], value[s]
        )
        d_one[s] = both
    attn_grads = weight_products(
        interleave(one_mine, one_other),
        interleave(e_mine, e_other),
        (d_query, d_key, d_value, context),
        (0, 0, 0, 1),
        "attn_products",
    )
    if parts == 2:
        attn_share = scatter_plane_direct(attn_grads)
        mlp_share = [
            scatter_plane(mlp_even),
            scatter_plane(mlp_odd),
        ]
    else:
        attn_share = scatter_plane(unjoin(attn_grads, width))
        mlp_grads = jnp.stack([mlp_even, mlp_odd], axis=2)
        mlp_share = [
            jnp.concatenate([scatter_plane(unjoin(mlp_grads[:, kind], width)) for kind in range(3)])
        ]

    last = Scatter()
    for s in (1, 2, 3, 0):
        mine, theirs = (jnp.stack([a, b]) for a, b in zip(d_one[s], outward[s]))
        last.add(s, mine, theirs)
    d_normed_one, outward_sum = last.result
    d_rows_norm, d_gain_one = rms_norm_back(rows_in, gains[0], d_normed_one)
    input_grad = d_middle + d_rows_norm
    output = (middle + outward_sum).astype(BF16)
    gain_grads = everywhere(jnp.stack([d_gain_one, d_gain_two]))

    results = ()
    for part in range(parts):
        shares = jnp.concatenate([attn_share[part][None], mlp_share[part]])
        at = plane + nothing(output) if part == 0 else plane

        def share_of(shift):
            return lax.dynamic_index_in_dim(shares, (at + shift) % 4, 0, keepdims=False)

        back = [share_of(0)] + [ring(share_of(shift), shift) for shift in (1, 2, 3)]
        here = plane + nothing(results[1]) if part else plane
        summed = jnp.stack(
            [lax.select_n(here, *(back[(z - source) % 4] for z in range(4))) for source in range(4)]
        )
        if parts == 1:
            summed = summed.reshape(block_count, -1, D, width).transpose(0, 2, 1, 3).reshape(block_count, D, BW)
        results = muon(summed, momentum, weights, part, parts, results, (gain_grads,) if part == 0 else ())
    weight_grads, new_momentum, new_weights = results

    new_gain_first = BETA_FIRST * gain_first + (1.0 - BETA_FIRST) * gain_grads
    new_gain_second = BETA_SECOND * gain_second + (1.0 - BETA_SECOND) * gain_grads * gain_grads
    first_hat = new_gain_first / (1.0 - BETA_FIRST**STEP)
    second_hat = new_gain_second / (1.0 - BETA_SECOND**STEP)
    new_gains = gains - ADAM_RATE * first_hat / (jnp.sqrt(second_hat) + ADAM_EPS)
    return (
        output,
        input_grad,
        weight_grads,
        new_momentum,
        new_weights,
        new_gain_first,
        new_gain_second,
        new_gains,
    )


def solution(mesh):
    count = mesh.shape["dp"]
    fine = Mesh(
        np.asarray(mesh.devices).reshape(4, 4, count // 16, mesh.shape["tensor"]),
        ("z",) + PLANE,
    )
    every = ("z",) + PLANE
    in_specs = (
        P(every, None),
        P(every[:3], None),
        P(every, None, None),
        P(every, None, None),
        P(),
        P(),
        P(),
        P(every, None),
    )
    out_specs = (
        P(every, None),
        P(every, None),
        P(every, None, None),
        P(every, None, None),
        P(every, None, None),
        P(),
        P(),
        P(),
    )
    return jax.shard_map(local, mesh=fine, in_specs=in_specs, out_specs=out_specs, check_vma=False)
```

```python
import functools
import math

import jax
import jax.numpy as jnp
import numpy as np
from jax import lax
from jax.experimental import pallas as pl
from jax.experimental.pallas import tpu as pltpu
from jax.sharding import Mesh
from jax.sharding import PartitionSpec as P

D = 2048
FF = 8192
HD = 64
BW = 128
NS_ITERS = 5
STEP = 10

HIGHEST = lax.Precision.HIGHEST
ROPE_BASE = 130000.0
NORM_EPS = 1e-05
NEG_LARGE = -1e30
MOMENTUM_DECAY = 0.95
MUON_RATE = 0.25
COEFF_A = 3.4445
COEFF_B = -4.775
COEFF_C = 2.0315
BETA_FIRST = 0.9
BETA_SECOND = 0.95
ADAM_RATE = 1.0
ADAM_EPS = 1e-08

F32 = jnp.float32
BF16 = jnp.bfloat16
PLANE = ("m", "r", "tensor")
SWAP = [(0, 1), (1, 0)]
TILE = 256
SCORE_SCALE = 1.0 / math.sqrt(HD)


def rms_norm(values, gain):
    return values * lax.rsqrt(jnp.mean(values * values, axis=-1, keepdims=True) + NORM_EPS) * gain


def rms_norm_back(values, gain, grad):
    scale = lax.rsqrt(jnp.mean(values * values, axis=-1, keepdims=True) + NORM_EPS)
    scaled = gain * grad
    inner = jnp.mean(scaled * values, axis=-1, keepdims=True)
    gain_grad = jnp.sum(grad * values * scale, axis=0)
    return scale * scaled - values * (scale * scale * scale * inner), gain_grad


def rope_tables(place):
    exponent = jnp.arange(HD // 2).astype(F32) * (2.0 / HD)
    inverse = jnp.exp(-exponent * math.log(ROPE_BASE))
    angle = place.astype(F32)[:, None] * inverse[None, :]
    cosine, sine = jnp.cos(angle), jnp.sin(angle)
    heads = 2 * BW // HD
    return (
        jnp.tile(jnp.concatenate([cosine, cosine], axis=1), (1, heads)),
        jnp.tile(jnp.concatenate([-sine, sine], axis=1), (1, heads)),
    )


def dims(lhs, rhs):
    return (((lhs,), (rhs,)), ((), ()))


def mul(a, b):
    return lax.dot_general(a, b, dims(1, 0), preferred_element_type=F32)


def mul_bt(a, b):
    return lax.dot_general(a, b, dims(1, 1), preferred_element_type=F32)


def mul_at(a, b):
    return lax.dot_general(a, b, dims(0, 0), preferred_element_type=F32)


def side_by_side(ref, *index):
    return jnp.concatenate([ref[index + (0,)], ref[index + (1,)]], axis=-1)


def pair_rows(own_ref, other_ref):
    return jnp.concatenate([own_ref[...], other_ref[...]], axis=0)


def swap_halves(values):
    lane = lax.broadcasted_iota(jnp.int32, values.shape, 1)
    span = values.shape[1]
    ahead = pltpu.roll(values, span - HD // 2, 1)
    behind = pltpu.roll(values, HD // 2, 1)
    return jnp.where(lane % HD < HD // 2, ahead, behind)


def head_only(values, head):
    lane = lax.broadcasted_iota(jnp.int32, values.shape, 1)
    return jnp.where((lane >= head * HD) & (lane < (head + 1) * HD), values, jnp.zeros_like(values))


def head_probs(query, key, bias, head):
    scores = mul_bt(head_only(query, head), key) * SCORE_SCALE + bias
    weights = jnp.exp(scores - jnp.max(scores, axis=-1, keepdims=True))
    return weights / jnp.sum(weights, axis=-1, keepdims=True)


def attn_forward_kernel(
    own_ref, other_ref, w_ref, bias_ref, cos_ref, sin_ref, q_ref, k_ref, v_ref, c_ref, mine_ref, theirs_ref
):
    rows = pair_rows(own_ref, other_ref)
    cosine, sine = cos_ref[...], sin_ref[...]
    lin = mul(rows, side_by_side(w_ref, 0))
    query = (lin * cosine + swap_halves(lin) * sine).astype(BF16)
    lin = mul(rows, side_by_side(w_ref, 1))
    key = (lin * cosine + swap_halves(lin) * sine).astype(BF16)
    value = mul(rows, side_by_side(w_ref, 2)).astype(BF16)
    q_ref[...] = query
    k_ref[...] = key
    v_ref[...] = value
    context = jnp.zeros(query.shape, F32)
    for head in range(query.shape[1] // HD):
        probs = head_probs(query, key, bias_ref[...], head)
        context = context + mul(probs.astype(BF16), head_only(value, head))
    context = context.astype(BF16)
    c_ref[...] = context
    half = own_ref.shape[0]
    for tile in range(D // TILE):
        at = pl.ds(tile * TILE, TILE)
        w_out = jnp.concatenate([w_ref[3, 0, at, :], w_ref[3, 1, at, :]], axis=-1)
        mixed = mul_bt(context, w_out)
        mine_ref[:, at] = mixed[:half]
        theirs_ref[:, at] = mixed[half:].astype(BF16)


def attn_backward_kernel(
    own_ref, other_ref, w_ref, bias_ref, cos_ref, sin_ref, q_ref, k_ref, v_ref,
    dq_ref, dk_ref, dv_ref, mine_ref, theirs_ref,
):
    rows = pair_rows(own_ref, other_ref)
    query, key, value = q_ref[...], k_ref[...], v_ref[...]
    d_context = mul(rows, side_by_side(w_ref, 3)).astype(BF16)
    d_query = jnp.zeros(query.shape, F32)
    d_key = jnp.zeros(query.shape, F32)
    d_value = jnp.zeros(query.shape, F32)
    for head in range(query.shape[1] // HD):
        probs = head_probs(query, key, bias_ref[...], head)
        d_here = head_only(d_context, head)
        d_value = d_value + mul_at(probs.astype(BF16), d_here)
        d_probs = mul_bt(d_here, value)
        inner = jnp.sum(probs * d_probs, axis=-1, keepdims=True)
        d_scores = (probs * (d_probs - inner)).astype(BF16)
        d_query = d_query + mul(d_scores, head_only(key, head))
        d_key = d_key + mul_at(d_scores, head_only(query, head))
    cosine, sine = cos_ref[...], sin_ref[...]
    d_query = d_query * SCORE_SCALE
    d_key = d_key * SCORE_SCALE
    d_query = (d_query * cosine - swap_halves(d_query) * sine).astype(BF16)
    d_key = (d_key * cosine - swap_halves(d_key) * sine).astype(BF16)
    d_value = d_value.astype(BF16)
    dq_ref[...] = d_query
    dk_ref[...] = d_key
    dv_ref[...] = d_value
    half = own_ref.shape[0]
    for tile in range(D // TILE):
        at = pl.ds(tile * TILE, TILE)
        total = jnp.zeros((2 * half, TILE), F32)
        for matrix, columns in ((0, d_query), (1, d_key), (2, d_value)):
            w_here = jnp.concatenate([w_ref[matrix, 0, at, :], w_ref[matrix, 1, at, :]], axis=-1)
            total = total + mul_bt(columns, w_here)
        mine_ref[:, at] = total[:half]
        theirs_ref[:, at] = total[half:].astype(BF16)


def mlp_half_kernel(*refs):
    rows, d_rows = refs[:8], refs[8:16]
    w_ref, hid_ref, dgate_ref, dup_ref, grad_ref = refs[16:]
    w_gate, w_up, w_down = (
        jnp.concatenate([w_ref[0, kind], w_ref[1, kind]], axis=-1) for kind in range(3)
    )
    for piece in range(4):
        here = pair_rows(rows[2 * piece], rows[2 * piece + 1])
        gate = mul(here, w_gate)
        up = mul(here, w_up)
        d_hidden = mul(pair_rows(d_rows[2 * piece], d_rows[2 * piece + 1]), w_down)
        sigmoid = 1.0 / (1.0 + jnp.exp(-gate))
        silu = gate * sigmoid
        at = pl.ds(piece * here.shape[0], here.shape[0])
        hid_ref[at, :] = (silu * up).astype(BF16)
        dgate_ref[at, :] = (d_hidden * up * sigmoid * (1.0 + gate * (1.0 - sigmoid))).astype(BF16)
        dup_ref[at, :] = (d_hidden * silu).astype(BF16)
    for tile in range(D // TILE):
        at = pl.ds(tile * TILE, TILE)
        across = jnp.concatenate([ref[:, at] for ref in rows], axis=0)
        d_across = jnp.concatenate([ref[:, at] for ref in d_rows], axis=0)
        for kind, left, right in ((0, across, dgate_ref), (1, across, dup_ref), (2, d_across, hid_ref)):
            grad = mul_at(left, right[...]).astype(BF16)
            for chip in range(2):
                grad_ref[chip, kind, at, :] = grad[:, chip * BW : (chip + 1) * BW]


def mlp_back_kernel(
    hid_even, hid_odd, dgate_even, dgate_odd, dup_even, dup_odd, w_even, w_odd,
    dn_mine_ref, dn_theirs_ref, out_mine_ref, out_theirs_ref,
):
    def whole(kind):
        return jnp.concatenate([ref[chip, kind] for ref in (w_even, w_odd) for chip in range(4)], axis=-1)

    def columns(even, odd):
        return jnp.concatenate([even[...], odd[...]], axis=-1)

    half = dn_mine_ref.shape[0]
    total = mul_bt(columns(dgate_even, dgate_odd), whole(0)) + mul_bt(columns(dup_even, dup_odd), whole(1))
    dn_mine_ref[...] = total[:half]
    dn_theirs_ref[...] = total[half:].astype(BF16)
    total = mul_bt(columns(hid_even, hid_odd), whole(2))
    out_mine_ref[...] = total[:half]
    out_theirs_ref[...] = total[half:].astype(BF16)


def grads_kernel(sources, *refs):
    first, second = refs[:8], refs[8:16]
    columns = refs[16:-1]
    out_ref = refs[-1]
    row_sets = [jnp.concatenate([ref[...] for ref in part], axis=0) for part in (first, second)]
    for index, source in enumerate(sources):
        stacked = jnp.concatenate([ref[...] for ref in columns[4 * index : 4 * index + 4]], axis=0)
        grad = mul_at(row_sets[source], stacked).astype(BF16)
        for block in range(grad.shape[1] // BW):
            out_ref[index, block] = grad[:, block * BW : (block + 1) * BW]


def split(values):
    high = values.astype(BF16)
    return high, (values - high.astype(F32)).astype(BF16)


def mul_split(a, b):
    return mul(a[0], b[0]) + (mul(a[0], b[1]) + mul(a[1], b[0]))


def muon_kernel(grad_ref, momentum_ref, weight_ref, wg_ref, nm_ref, nw_ref, held, mixers):
    step = pl.program_id(0)
    count = held.shape[0]

    @pl.when(step < count)
    def _():
        grad = grad_ref[...].astype(F32)
        wg_ref[...] = grad
        block = MOMENTUM_DECAY * momentum_ref[...] + grad
        nm_ref[...] = block
        block = block * (1.0 / (jnp.sqrt(jnp.sum(block * block)) + 1e-07))
        held[step] = block
        high, low = split(block)
        cross = mul_at(high, low)
        mixers[step] = mul_at(high, high) + (cross + cross.T)

    @pl.when(step == count - 1)
    def _():
        row = lax.broadcasted_iota(jnp.int32, (BW, BW), 0)
        column = lax.broadcasted_iota(jnp.int32, (BW, BW), 1)
        eye = jnp.where(row == column, COEFF_A, 0.0).astype(F32)
        grams = [mixers[index] for index in range(count)]
        totals = [None] * count
        for turn in range(NS_ITERS):
            for index in range(count):
                pair = split(grams[index])
                mixer = eye + COEFF_B * grams[index] + COEFF_C * mul_split(pair, pair)
                mixed = split(mixer)
                if turn == 0:
                    totals[index] = mixer
                else:
                    totals[index] = mul_split(split(totals[index]), mixed)
                if turn < NS_ITERS - 1:
                    grams[index] = mul_split(split(mul_split(mixed, pair)), mixed)
        for index in range(count):
            mixers[index] = totals[index]

    @pl.when(step >= count)
    def _():
        at = step - count
        ortho = mul_split(split(held[at]), split(mixers[at]))
        nw_ref[...] = weight_ref[...].astype(F32) - (MUON_RATE * math.sqrt(D / BW)) * ortho


def deferred(kernel, inputs, unread):
    return lambda *refs: kernel(*refs[:inputs], *refs[inputs + unread :])


def unread_specs(after):
    return [pl.BlockSpec(memory_space=pl.ANY) for _ in after]


def cost(flops, accessed):
    return pl.CostEstimate(flops=flops // 6, bytes_accessed=accessed // 6, transcendentals=0)


def params(mebibytes):
    return pltpu.CompilerParams(vmem_limit_bytes=mebibytes * 1024 * 1024)


def whole_specs(arrays):
    return [pl.BlockSpec(memory_space=pltpu.VMEM) for _ in arrays]


def shaped(shape, dtype):
    return jax.ShapeDtypeStruct(shape, dtype)


def attn_forward(own, other, w_attn, bias, cosine, sine, after=()):
    half = own.shape[0]
    span = w_attn.shape[1] * w_attn.shape[3]
    square = shaped((2 * half, span), BF16)
    args = (own, other, w_attn, bias, cosine, sine)
    return pl.pallas_call(
        deferred(attn_forward_kernel, len(args), len(after)),
        out_shape=(square,) * 4 + (shaped((half, D), F32), shaped((half, D), BF16)),
        in_specs=whole_specs(args) + unread_specs(after),
        out_specs=tuple(whole_specs(range(6))),
        compiler_params=params(40),
        cost_estimate=cost(1_300_000_000, 9_000_000),
        name="attn_forward",
    )(*args, *after)


def attn_backward(own, other, w_attn, bias, cosine, sine, query, key, value):
    half = own.shape[0]
    square = shaped(query.shape, BF16)
    args = (own, other, w_attn, bias, cosine, sine, query, key, value)
    return pl.pallas_call(
        attn_backward_kernel,
        out_shape=(square,) * 3 + (shaped((half, D), F32), shaped((half, D), BF16)),
        in_specs=whole_specs(args),
        out_specs=tuple(whole_specs(range(5))),
        compiler_params=params(40),
        cost_estimate=cost(1_600_000_000, 9_000_000),
        name="attn_backward",
    )(*args)


def mlp_half(rows, d_rows, w_half):
    half = rows[0].shape[0]
    columns = shaped((8 * half, 4 * BW), BF16)
    blocks = pl.BlockSpec((2, 3, D, BW), lambda j: (j, 0, 0, 0))
    return pl.pallas_call(
        mlp_half_kernel,
        grid=(2,),
        out_shape=(columns,) * 3 + (shaped(w_half.shape, BF16),),
        in_specs=[pl.BlockSpec((half, D), lambda j: (0, 0)) for _ in range(16)]
        + [blocks],
        out_specs=(pl.BlockSpec((8 * half, 2 * BW), lambda j: (0, j)),) * 3 + (blocks,),
        compiler_params=params(58),
        cost_estimate=cost(13_000_000_000, 20_000_000),
        name="mlp_half",
    )(*rows, *d_rows, w_half)


def mlp_back(piece, halves, w_even, w_odd):
    rows = halves[0][0].shape[0] // 4
    wide = 2 * TILE
    args = [half[index] for index in range(3) for half in halves]
    tile = pl.BlockSpec((rows // 2, wide), lambda i: (0, i))
    weight = pl.BlockSpec((4, 3, wide, BW), lambda i: (0, 0, i, 0))
    return pl.pallas_call(
        mlp_back_kernel,
        grid=(D // wide,),
        out_shape=(shaped((rows // 2, D), F32), shaped((rows // 2, D), BF16)) * 2,
        in_specs=[pl.BlockSpec((rows, 4 * BW), lambda i: (piece, 0)) for _ in args] + [weight] * 2,
        out_specs=(tile,) * 4,
        compiler_params=params(58),
        cost_estimate=cost(3_200_000_000, 16_000_000),
        name="mlp_back",
    )(*args, w_even, w_odd)


def weight_products(first, second, column_sets, sources, name, after=()):
    half = first[0].shape[0]
    span = column_sets[0][0].shape[1]
    row_spec = pl.BlockSpec((half, TILE), lambda i: (0, i))
    column_spec = pl.BlockSpec((2 * half, span), lambda i: (0, 0))
    flat = [piece for pieces in column_sets for piece in pieces]
    return pl.pallas_call(
        deferred(functools.partial(grads_kernel, sources), 16 + len(flat), len(after)),
        grid=(D // TILE,),
        out_shape=shaped((len(sources), span // BW, D, BW), BF16),
        in_specs=[row_spec] * 16 + [column_spec] * len(flat) + unread_specs(after),
        out_specs=pl.BlockSpec((len(sources), span // BW, TILE, BW), lambda i: (0, 0, i, 0)),
        compiler_params=params(40),
        cost_estimate=cost(2 * 8 * half * D * span * len(sources), 20_000_000),
        name=name,
    )(*first, *second, *flat, *after)


def muon(grads, momentum, weights, offset, stride, begun=(), after=()):
    count = grads.shape[0]
    now = lambda i: jnp.minimum(i, count - 1)
    then = lambda i: jnp.maximum(i - count, 0)
    block = (None, D, BW)
    compact = pl.BlockSpec(block, lambda i: (now(i), 0, 0))
    early = pl.BlockSpec(block, lambda i: (stride * now(i) + offset, 0, 0))
    late = pl.BlockSpec(block, lambda i: (stride * then(i) + offset, 0, 0))
    return pl.pallas_call(
        deferred(muon_kernel, 3, len(begun) + len(after)),
        grid=(2 * count,),
        out_shape=(shaped(momentum.shape, F32),) * 3,
        in_specs=[compact, early, late] + unread_specs(begun) + unread_specs(after),
        out_specs=(early, early, late),
        input_output_aliases={3 + index: index for index in range(len(begun))},
        scratch_shapes=[pltpu.VMEM((count, D, BW), F32), pltpu.VMEM((count, BW, BW), F32)],
        compiler_params=params(40),
        cost_estimate=cost(1_000_000_000 * count, 5_500_000 * count),
        name="muon",
    )(grads, momentum, weights, *begun, *after)


def mirror(step):
    return [(place, place ^ step) for place in range(4)]


def ring(value, step=1):
    return lax.ppermute(value, "z", [(place, (place + step) % 4) for place in range(4)])


def swap(value):
    return lax.ppermute(value, "tensor", SWAP)


def nothing(value):
    first = value[(0,) * value.ndim].astype(F32)
    return (first * 0.0).astype(jnp.int32)


def hold(value, *others):
    zero = sum((nothing(other) for other in others), jnp.int32(0))
    return value + zero.astype(value.dtype)


def gather_rows(rows):
    mine = [rows]
    for _ in range(3):
        mine.append(ring(mine[-1]))
    return mine, [swap(part) for part in mine]


def gather_rows_at_once(rows):
    plane = lax.axis_index("z")
    mine = lax.all_gather(rows, "z", axis=0, tiled=False)
    other = swap(mine)
    pick = lambda stack, s: lax.dynamic_index_in_dim(stack, (plane + 4 - s) % 4, 0, keepdims=False)
    return [pick(mine, s) for s in range(4)], [pick(other, s) for s in range(4)]


def gather_rows_direct(rows):
    mine = [rows] + [ring(rows, shift) for shift in (1, 2, 3)]
    return mine, [swap(part) for part in mine]


class Scatter:
    def __init__(self):
        self.moving = self.result = None
        self.payloads = []

    def add(self, step, mine, theirs):
        total = mine + swap(theirs).astype(F32)
        if self.moving is not None:
            total = total + self.moving.astype(F32)
        if step:
            self.payloads.append(total.astype(BF16))
            self.moving = ring(self.payloads[-1])
        else:
            self.result = total


def everywhere(value):
    value = value + swap(value)
    for axis in ("m", "z"):
        for step in (1, 2):
            value = value + lax.ppermute(value, axis, mirror(step))
    if lax.axis_size("r") > 1:
        value = lax.psum(value, "r")
    return value


def join(parts):
    if parts.shape[0] == 4:
        return parts
    width = parts.shape[3]
    parts = parts.reshape(4, 2, -1, D, width).transpose(0, 1, 3, 2, 4)
    return parts.reshape(4, 2, D, BW)


def unjoin(grads, width):
    if width == BW:
        return grads
    grads = grads.reshape(4, 2, D, -1, width).transpose(0, 1, 3, 2, 4)
    return grads.reshape(-1, 1, D, width)


def gather_plane(parts):
    return lax.all_gather(jnp.stack(parts), ("m", "r"), axis=0, tiled=False)


def gather_part_direct(part, index, result):
    chip = lax.axis_index("m")
    result = lax.dynamic_update_slice(result, part[None, None], (chip, index, 0, 0))
    for step in (1, 2, 3):
        got = lax.ppermute(part, "m", mirror(step))
        result = lax.dynamic_update_slice(result, got[None, None], (chip ^ step, index, 0, 0))
    return result


def scatter_plane(grads):
    share = lax.psum_scatter(
        grads.reshape(grads.shape[0], -1, grads.shape[3]), ("m", "r"), scatter_dimension=0, tiled=False
    )
    return share.reshape(grads.shape[1:])


def scatter_plane_direct(grads, *others):
    chip = lax.axis_index("m")
    zero = sum((nothing(other) for other in others), jnp.int32(0)).astype(F32)

    def share_for(step):
        return lax.dynamic_index_in_dim(grads, chip ^ step, 0, keepdims=False)

    total = share_for(0).astype(F32) + zero
    for step in (1, 2, 3):
        total = total + lax.ppermute(share_for(step), "m", mirror(step)).astype(F32)
    return total.astype(BF16)


def interleave(mine, other):
    return [rows for pair in zip(mine, other) for rows in pair]


def local(tokens, segments, weights, momentum, gains, gain_first, gain_second, cotangent):
    plane = lax.axis_index("z")
    core = lax.axis_index("tensor")
    block_count = weights.shape[0]

    if block_count == 8:
        shards = weights.reshape(4, 2, D, BW)
    else:
        width = block_count * BW // 4
        shards = weights.reshape(block_count, D, -1, width).transpose(0, 2, 1, 3).reshape(4, 1, D, width)
    parts, width = shards.shape[1], shards.shape[3]

    def shard(shift, part, *others):
        at = sum((nothing(other) for other in others), plane + shift)
        return lax.dynamic_slice(shards, (at % 4, part, 0, 0), (1, 1, D, width))[0, 0]

    rows_in = tokens.astype(F32)
    one_mine, one_other = gather_rows_at_once(rms_norm(rows_in, gains[0]).astype(BF16))

    segment_parts = [segments] + [ring(segments, shift) for shift in (1, 2, 3)]
    segment_rows = jnp.concatenate(segment_parts, axis=0)
    moved = []
    for part in range(parts):
        others = [moved[0][1], moved[0][3]] if part else []
        moved.append([shard(0, part)] + [ring(shard(shift, part, *others), shift) for shift in (1, 2, 3)])

    def kind_part(source, part, *others):
        at = sum((nothing(other) for other in others), plane)
        return lax.select_n(at, *(moved[part][(here - source) % 4] for here in range(4)))

    if parts == 2:
        mlp_parts = [[kind_part(kind, 0) for kind in (1, 2, 3)]]
        w_attn = gather_part_direct(kind_part(0, 0, segment_rows), 0, jnp.zeros((4, 2, D, BW), BF16))
        w_attn_even = w_attn
        waits = (w_attn, mlp_parts[0][0])
        w_attn = gather_part_direct(kind_part(0, 1, *waits), 1, w_attn)
        mlp_parts.append([kind_part(kind, 1, w_attn_even) for kind in (1, 2, 3)])
        begun = [mlp_parts[1][0]]
        w_mlp = [gather_plane(kinds) for kinds in mlp_parts]
    else:
        w_attn = join(gather_plane([kind_part(0, 0)]))
        w_mlp = gather_plane([kind_part(kind, 0) for kind in (1, 2, 3)])
        w_mlp = jnp.stack([join(w_mlp[:, kind : kind + 1]) for kind in range(3)], axis=1)
        w_mlp = [w_mlp[:, :, 0], w_mlp[:, :, 1]]
        begun = []
    d_mine, d_other = gather_rows(hold(cotangent, w_attn))

    length = segment_rows.shape[1]
    half = length // 2
    place = jnp.arange(length)
    place = jnp.where(core == 0, place, (place + half) % length)
    segment_rows = jnp.where(core == 0, segment_rows, jnp.roll(segment_rows, half, axis=1))
    allowed = (place[None, None, :] <= place[None, :, None]) & (
        segment_rows[:, None, :] == segment_rows[:, :, None]
    )
    bias = jnp.where(allowed, 0.0, NEG_LARGE).astype(F32)
    cosine, sine = rope_tables(place)

    query, key, value, context = ([None] * 4 for _ in range(4))
    mixed = Scatter()
    for s in (1, 2, 3, 0):
        query[s], key[s], value[s], context[s], *both = attn_forward(
            one_mine[s], one_other[s], w_attn, bias[s], cosine, sine, mixed.payloads[:1] if s == 3 else begun if s == 1 else d_mine[2:3] if s == 0 else ()
        )
        mixed.add(s, *both)
    middle = rows_in + mixed.result
    two_mine, two_other = gather_rows(rms_norm(middle, gains[1]).astype(BF16))

    two_rows, d_rows = interleave(two_mine, two_other), interleave(d_mine, d_other)
    *even_half, mlp_even = mlp_half(two_rows, d_rows, w_mlp[0])
    *odd_half, mlp_odd = mlp_half(two_rows, d_rows, w_mlp[1])
    outward = [None] * 4
    d_normed = Scatter()
    for s in (1, 2, 3, 0):
        *d_two, out_mine, out_theirs = mlp_back(s, (even_half, odd_half), *w_mlp)
        outward[s] = (out_mine, out_theirs)
        d_normed.add(s, *d_two)
    d_normed_two = d_normed.result

    d_output = cotangent.astype(F32)
    d_middle_norm, d_gain_two = rms_norm_back(middle, gains[1], d_normed_two)
    d_middle = d_output + d_middle_norm
    e_mine, e_other = gather_rows(d_middle.astype(BF16))
    d_query, d_key, d_value, d_one = ([None] * 4 for _ in range(4))
    for s in range(4):
        d_query[s], d_key[s], d_value[s], *both = attn_backward(
            e_mine[s], e_other[s], w_attn, bias[s], cosine, sine, query[s], key[s], value[s]
        )
        d_one[s] = both
    attn_grads = weight_products(
        interleave(one_mine, one_other),
        interleave(e_mine, e_other),
        (d_query, d_key, d_value, context),
        (0, 0, 0, 1),
        "attn_products",
    )
    if parts == 2:
        attn_share = scatter_plane_direct(attn_grads)
        mlp_share = [
            scatter_plane(mlp_even),
            scatter_plane(mlp_odd),
        ]
    else:
        attn_share = scatter_plane(unjoin(attn_grads, width))
        mlp_grads = jnp.stack([mlp_even, mlp_odd], axis=2)
        mlp_share = [
            jnp.concatenate([scatter_plane(unjoin(mlp_grads[:, kind], width)) for kind in range(3)])
        ]

    last = Scatter()
    for s in (1, 2, 3, 0):
        mine, theirs = (jnp.stack([a, b]) for a, b in zip(d_one[s], outward[s]))
        if s == 2:
            mine = hold(mine, attn_grads)
        last.add(s, mine, theirs)
    d_normed_one, outward_sum = last.result
    d_rows_norm, d_gain_one = rms_norm_back(rows_in, gains[0], d_normed_one)
    input_grad = d_middle + d_rows_norm
    output = (middle + outward_sum).astype(BF16)
    gain_grads = everywhere(jnp.stack([d_gain_one, d_gain_two]))

    results = ()
    for part in range(parts):
        shares = jnp.concatenate([attn_share[part][None], mlp_share[part]])

        def share_of(shift):
            return lax.dynamic_index_in_dim(shares, (plane + shift) % 4, 0, keepdims=False)

        back = [share_of(0)] + [ring(share_of(shift), shift) for shift in (1, 2, 3)]
        here = plane + nothing(results[1]) if part else plane
        summed = jnp.stack(
            [lax.select_n(here, *(back[(z - source) % 4] for z in range(4))) for source in range(4)]
        )
        if parts == 1:
            summed = summed.reshape(block_count, -1, D, width).transpose(0, 2, 1, 3).reshape(block_count, D, BW)
        results = muon(summed, momentum, weights, part, parts, results, (gain_grads,) if part else ())
    weight_grads, new_momentum, new_weights = results

    new_gain_first = BETA_FIRST * gain_first + (1.0 - BETA_FIRST) * gain_grads
    new_gain_second = BETA_SECOND * gain_second + (1.0 - BETA_SECOND) * gain_grads * gain_grads
    first_hat = new_gain_first / (1.0 - BETA_FIRST**STEP)
    second_hat = new_gain_second / (1.0 - BETA_SECOND**STEP)
    new_gains = gains - ADAM_RATE * first_hat / (jnp.sqrt(second_hat) + ADAM_EPS)
    return (
        output,
        input_grad,
        weight_grads,
        new_momentum,
        new_weights,
        new_gain_first,
        new_gain_second,
        new_gains,
    )


def solution(mesh):
    count = mesh.shape["dp"]
    fine = Mesh(
        np.asarray(mesh.devices).reshape(4, 4, count // 16, mesh.shape["tensor"]),
        ("z",) + PLANE,
    )
    every = ("z",) + PLANE
    in_specs = (
        P(every, None),
        P(every[:3], None),
        P(every, None, None),
        P(every, None, None),
        P(),
        P(),
        P(),
        P(every, None),
    )
    out_specs = (
        P(every, None),
        P(every, None),
        P(every, None, None),
        P(every, None, None),
        P(every, None, None),
        P(),
        P(),
        P(),
    )
    return jax.shard_map(local, mesh=fine, in_specs=in_specs, out_specs=out_specs, check_vma=False)
```

```python
import functools
import math

import jax
import jax.numpy as jnp
import numpy as np
from jax import lax
from jax.experimental import pallas as pl
from jax.experimental.pallas import tpu as pltpu
from jax.sharding import Mesh
from jax.sharding import PartitionSpec as P

D = 2048
FF = 8192
HD = 64
BW = 128
NS_ITERS = 5
STEP = 10

HIGHEST = lax.Precision.HIGHEST
ROPE_BASE = 130000.0
NORM_EPS = 1e-05
NEG_LARGE = -1e30
MOMENTUM_DECAY = 0.95
MUON_RATE = 0.25
COEFF_A = 3.4445
COEFF_B = -4.775
COEFF_C = 2.0315
BETA_FIRST = 0.9
BETA_SECOND = 0.95
ADAM_RATE = 1.0
ADAM_EPS = 1e-08

F32 = jnp.float32
BF16 = jnp.bfloat16
PLANE = ("m", "r", "tensor")
SWAP = [(0, 1), (1, 0)]
TILE = 256
SCORE_SCALE = 1.0 / math.sqrt(HD)


def rms_norm(values, gain):
    return values * lax.rsqrt(jnp.mean(values * values, axis=-1, keepdims=True) + NORM_EPS) * gain


def rms_norm_back(values, gain, grad):
    scale = lax.rsqrt(jnp.mean(values * values, axis=-1, keepdims=True) + NORM_EPS)
    scaled = gain * grad
    inner = jnp.mean(scaled * values, axis=-1, keepdims=True)
    gain_grad = jnp.sum(grad * values * scale, axis=0)
    return scale * scaled - values * (scale * scale * scale * inner), gain_grad


def rope_tables(place):
    exponent = jnp.arange(HD // 2).astype(F32) * (2.0 / HD)
    inverse = jnp.exp(-exponent * math.log(ROPE_BASE))
    angle = place.astype(F32)[:, None] * inverse[None, :]
    cosine, sine = jnp.cos(angle), jnp.sin(angle)
    heads = 2 * BW // HD
    return (
        jnp.tile(jnp.concatenate([cosine, cosine], axis=1), (1, heads)),
        jnp.tile(jnp.concatenate([-sine, sine], axis=1), (1, heads)),
    )


def dims(lhs, rhs):
    return (((lhs,), (rhs,)), ((), ()))


def mul(a, b):
    return lax.dot_general(a, b, dims(1, 0), preferred_element_type=F32)


def mul_bt(a, b):
    return lax.dot_general(a, b, dims(1, 1), preferred_element_type=F32)


def mul_at(a, b):
    return lax.dot_general(a, b, dims(0, 0), preferred_element_type=F32)


def side_by_side(ref, *index):
    return jnp.concatenate([ref[index + (0,)], ref[index + (1,)]], axis=-1)


def pair_rows(own_ref, other_ref):
    return jnp.concatenate([own_ref[...], other_ref[...]], axis=0)


def swap_halves(values):
    lane = lax.broadcasted_iota(jnp.int32, values.shape, 1)
    span = values.shape[1]
    ahead = pltpu.roll(values, span - HD // 2, 1)
    behind = pltpu.roll(values, HD // 2, 1)
    return jnp.where(lane % HD < HD // 2, ahead, behind)


def head_only(values, head):
    lane = lax.broadcasted_iota(jnp.int32, values.shape, 1)
    return jnp.where((lane >= head * HD) & (lane < (head + 1) * HD), values, jnp.zeros_like(values))


def head_probs(query, key, bias, head):
    scores = mul_bt(head_only(query, head), key) * SCORE_SCALE + bias
    weights = jnp.exp(scores - jnp.max(scores, axis=-1, keepdims=True))
    return weights / jnp.sum(weights, axis=-1, keepdims=True)


def attn_forward_kernel(
    own_ref, other_ref, w_ref, bias_ref, cos_ref, sin_ref, q_ref, k_ref, v_ref, c_ref, mine_ref, theirs_ref
):
    rows = pair_rows(own_ref, other_ref)
    cosine, sine = cos_ref[...], sin_ref[...]
    lin = mul(rows, side_by_side(w_ref, 0))
    query = (lin * cosine + swap_halves(lin) * sine).astype(BF16)
    lin = mul(rows, side_by_side(w_ref, 1))
    key = (lin * cosine + swap_halves(lin) * sine).astype(BF16)
    value = mul(rows, side_by_side(w_ref, 2)).astype(BF16)
    q_ref[...] = query
    k_ref[...] = key
    v_ref[...] = value
    context = jnp.zeros(query.shape, F32)
    for head in range(query.shape[1] // HD):
        probs = head_probs(query, key, bias_ref[...], head)
        context = context + mul(probs.astype(BF16), head_only(value, head))
    context = context.astype(BF16)
    c_ref[...] = context
    half = own_ref.shape[0]
    for tile in range(D // TILE):
        at = pl.ds(tile * TILE, TILE)
        w_out = jnp.concatenate([w_ref[3, 0, at, :], w_ref[3, 1, at, :]], axis=-1)
        mixed = mul_bt(context, w_out)
        mine_ref[:, at] = mixed[:half]
        theirs_ref[:, at] = mixed[half:].astype(BF16)


def attn_backward_kernel(
    own_ref, other_ref, w_ref, bias_ref, cos_ref, sin_ref, q_ref, k_ref, v_ref,
    dq_ref, dk_ref, dv_ref, mine_ref, theirs_ref,
):
    rows = pair_rows(own_ref, other_ref)
    query, key, value = q_ref[...], k_ref[...], v_ref[...]
    d_context = mul(rows, side_by_side(w_ref, 3)).astype(BF16)
    d_query = jnp.zeros(query.shape, F32)
    d_key = jnp.zeros(query.shape, F32)
    d_value = jnp.zeros(query.shape, F32)
    for head in range(query.shape[1] // HD):
        probs = head_probs(query, key, bias_ref[...], head)
        d_here = head_only(d_context, head)
        d_value = d_value + mul_at(probs.astype(BF16), d_here)
        d_probs = mul_bt(d_here, value)
        inner = jnp.sum(probs * d_probs, axis=-1, keepdims=True)
        d_scores = (probs * (d_probs - inner)).astype(BF16)
        d_query = d_query + mul(d_scores, head_only(key, head))
        d_key = d_key + mul_at(d_scores, head_only(query, head))
    cosine, sine = cos_ref[...], sin_ref[...]
    d_query = d_query * SCORE_SCALE
    d_key = d_key * SCORE_SCALE
    d_query = (d_query * cosine - swap_halves(d_query) * sine).astype(BF16)
    d_key = (d_key * cosine - swap_halves(d_key) * sine).astype(BF16)
    d_value = d_value.astype(BF16)
    dq_ref[...] = d_query
    dk_ref[...] = d_key
    dv_ref[...] = d_value
    half = own_ref.shape[0]
    for tile in range(D // TILE):
        at = pl.ds(tile * TILE, TILE)
        total = jnp.zeros((2 * half, TILE), F32)
        for matrix, columns in ((0, d_query), (1, d_key), (2, d_value)):
            w_here = jnp.concatenate([w_ref[matrix, 0, at, :], w_ref[matrix, 1, at, :]], axis=-1)
            total = total + mul_bt(columns, w_here)
        mine_ref[:, at] = total[:half]
        theirs_ref[:, at] = total[half:].astype(BF16)


def mlp_half_kernel(*refs):
    rows, d_rows = refs[:8], refs[8:16]
    w_ref, hid_ref, dgate_ref, dup_ref, grad_ref = refs[16:]
    w_gate, w_up, w_down = (
        jnp.concatenate([w_ref[0, kind], w_ref[1, kind]], axis=-1) for kind in range(3)
    )
    for piece in range(4):
        here = pair_rows(rows[2 * piece], rows[2 * piece + 1])
        gate = mul(here, w_gate)
        up = mul(here, w_up)
        d_hidden = mul(pair_rows(d_rows[2 * piece], d_rows[2 * piece + 1]), w_down)
        sigmoid = 1.0 / (1.0 + jnp.exp(-gate))
        silu = gate * sigmoid
        at = pl.ds(piece * here.shape[0], here.shape[0])
        hid_ref[at, :] = (silu * up).astype(BF16)
        dgate_ref[at, :] = (d_hidden * up * sigmoid * (1.0 + gate * (1.0 - sigmoid))).astype(BF16)
        dup_ref[at, :] = (d_hidden * silu).astype(BF16)
    for tile in range(D // TILE):
        at = pl.ds(tile * TILE, TILE)
        across = jnp.concatenate([ref[:, at] for ref in rows], axis=0)
        d_across = jnp.concatenate([ref[:, at] for ref in d_rows], axis=0)
        for kind, left, right in ((0, across, dgate_ref), (1, across, dup_ref), (2, d_across, hid_ref)):
            grad = mul_at(left, right[...]).astype(BF16)
            for chip in range(2):
                grad_ref[chip, kind, at, :] = grad[:, chip * BW : (chip + 1) * BW]


def all_columns(kind, w_even, w_odd):
    return jnp.concatenate([ref[chip, kind] for ref in (w_even, w_odd) for chip in range(4)], axis=-1)


def both_columns(even, odd):
    return jnp.concatenate([even[...], odd[...]], axis=-1)


def mlp_back_kernel(dgate_even, dgate_odd, dup_even, dup_odd, w_even, w_odd, mine_ref, theirs_ref):
    total = mul_bt(both_columns(dgate_even, dgate_odd), all_columns(0, w_even, w_odd))
    total = total + mul_bt(both_columns(dup_even, dup_odd), all_columns(1, w_even, w_odd))
    half = mine_ref.shape[0]
    mine_ref[...] = total[:half]
    theirs_ref[...] = total[half:].astype(BF16)


def mlp_out_kernel(hid_even, hid_odd, w_even, w_odd, mine_ref, theirs_ref):
    total = mul_bt(both_columns(hid_even, hid_odd), all_columns(0, w_even, w_odd))
    half = mine_ref.shape[1]
    for piece in range(4):
        mine_ref[piece] = total[2 * piece * half : (2 * piece + 1) * half]
        theirs_ref[piece] = total[(2 * piece + 1) * half : 2 * (piece + 1) * half].astype(BF16)


def grads_kernel(sources, *refs):
    first, second = refs[:8], refs[8:16]
    columns = refs[16:-1]
    out_ref = refs[-1]
    row_sets = [jnp.concatenate([ref[...] for ref in part], axis=0) for part in (first, second)]
    for index, source in enumerate(sources):
        stacked = jnp.concatenate([ref[...] for ref in columns[4 * index : 4 * index + 4]], axis=0)
        grad = mul_at(row_sets[source], stacked).astype(BF16)
        for block in range(grad.shape[1] // BW):
            out_ref[index, block] = grad[:, block * BW : (block + 1) * BW]


def split(values):
    high = values.astype(BF16)
    return high, (values - high.astype(F32)).astype(BF16)


def mul_split(a, b):
    return mul(a[0], b[0]) + (mul(a[0], b[1]) + mul(a[1], b[0]))


def muon_kernel(grad_ref, momentum_ref, weight_ref, wg_ref, nm_ref, nw_ref, held, mixers):
    step = pl.program_id(0)
    count = held.shape[0]

    @pl.when(step < count)
    def _():
        grad = grad_ref[...].astype(F32)
        wg_ref[...] = grad
        block = MOMENTUM_DECAY * momentum_ref[...] + grad
        nm_ref[...] = block
        block = block * (1.0 / (jnp.sqrt(jnp.sum(block * block)) + 1e-07))
        held[step] = block
        high, low = split(block)
        cross = mul_at(high, low)
        mixers[step] = mul_at(high, high) + (cross + cross.T)

    @pl.when(step == count - 1)
    def _():
        row = lax.broadcasted_iota(jnp.int32, (BW, BW), 0)
        column = lax.broadcasted_iota(jnp.int32, (BW, BW), 1)
        eye = jnp.where(row == column, COEFF_A, 0.0).astype(F32)
        grams = [mixers[index] for index in range(count)]
        totals = [None] * count
        for turn in range(NS_ITERS):
            for index in range(count):
                pair = split(grams[index])
                mixer = eye + COEFF_B * grams[index] + COEFF_C * mul_split(pair, pair)
                mixed = split(mixer)
                if turn == 0:
                    totals[index] = mixer
                else:
                    totals[index] = mul_split(split(totals[index]), mixed)
                if turn < NS_ITERS - 1:
                    grams[index] = mul_split(split(mul_split(mixed, pair)), mixed)
        for index in range(count):
            mixers[index] = totals[index]

    @pl.when(step >= count)
    def _():
        at = step - count
        ortho = mul_split(split(held[at]), split(mixers[at]))
        nw_ref[...] = weight_ref[...].astype(F32) - (MUON_RATE * math.sqrt(D / BW)) * ortho


def deferred(kernel, inputs, unread):
    return lambda *refs: kernel(*refs[:inputs], *refs[inputs + unread :])


def unread_specs(after):
    return [pl.BlockSpec(memory_space=pl.ANY) for _ in after]


def cost(flops, accessed):
    return pl.CostEstimate(flops=flops // 6, bytes_accessed=accessed // 6, transcendentals=0)


def params(mebibytes):
    return pltpu.CompilerParams(vmem_limit_bytes=mebibytes * 1024 * 1024)


def whole_specs(arrays):
    return [pl.BlockSpec(memory_space=pltpu.VMEM) for _ in arrays]


def shaped(shape, dtype):
    return jax.ShapeDtypeStruct(shape, dtype)


def attn_forward(own, other, w_attn, bias, cosine, sine, after=()):
    half = own.shape[0]
    span = w_attn.shape[1] * w_attn.shape[3]
    square = shaped((2 * half, span), BF16)
    args = (own, other, w_attn, bias, cosine, sine)
    return pl.pallas_call(
        deferred(attn_forward_kernel, len(args), len(after)),
        out_shape=(square,) * 4 + (shaped((half, D), F32), shaped((half, D), BF16)),
        in_specs=whole_specs(args) + unread_specs(after),
        out_specs=tuple(whole_specs(range(6))),
        compiler_params=params(40),
        cost_estimate=cost(1_300_000_000, 9_000_000),
        name="attn_forward",
    )(*args, *after)


def attn_backward(own, other, w_attn, bias, cosine, sine, query, key, value):
    half = own.shape[0]
    square = shaped(query.shape, BF16)
    args = (own, other, w_attn, bias, cosine, sine, query, key, value)
    return pl.pallas_call(
        attn_backward_kernel,
        out_shape=(square,) * 3 + (shaped((half, D), F32), shaped((half, D), BF16)),
        in_specs=whole_specs(args),
        out_specs=tuple(whole_specs(range(5))),
        compiler_params=params(40),
        cost_estimate=cost(1_600_000_000, 9_000_000),
        name="attn_backward",
    )(*args)


def mlp_half(rows, d_rows, w_half):
    half = rows[0].shape[0]
    columns = shaped((8 * half, 4 * BW), BF16)
    blocks = pl.BlockSpec((2, 3, D, BW), lambda j: (j, 0, 0, 0))
    return pl.pallas_call(
        mlp_half_kernel,
        grid=(2,),
        out_shape=(columns,) * 3 + (shaped(w_half.shape, BF16),),
        in_specs=[pl.BlockSpec((half, D), lambda j: (0, 0)) for _ in range(16)]
        + [blocks],
        out_specs=(pl.BlockSpec((8 * half, 2 * BW), lambda j: (0, j)),) * 3 + (blocks,),
        compiler_params=params(58),
        cost_estimate=cost(13_000_000_000, 20_000_000),
        name="mlp_half",
    )(*rows, *d_rows, w_half)


def mlp_back(piece, halves, w_even, w_odd):
    rows = halves[0][0].shape[0] // 4
    wide = 2 * TILE
    args = [half[index] for index in (1, 2) for half in halves]
    tile = pl.BlockSpec((rows // 2, wide), lambda i: (0, i))
    weight = pl.BlockSpec((4, 2, wide, BW), lambda i: (0, 0, i, 0))
    return pl.pallas_call(
        mlp_back_kernel,
        grid=(D // wide,),
        out_shape=(shaped((rows // 2, D), F32), shaped((rows // 2, D), BF16)),
        in_specs=[pl.BlockSpec((rows, 4 * BW), lambda i: (piece, 0)) for _ in args] + [weight] * 2,
        out_specs=(tile,) * 2,
        compiler_params=params(58),
        cost_estimate=cost(2_200_000_000, 11_000_000),
        name="mlp_back",
    )(*args, w_even, w_odd)


def mlp_out(halves, w_even, w_odd, after):
    count = halves[0][0].shape[0]
    args = [half[0] for half in halves]
    wide = 2 * TILE
    tile = pl.BlockSpec((4, count // 8, wide), lambda i: (0, 0, i))
    weight = pl.BlockSpec((4, 1, wide, BW), lambda i: (0, 2, i, 0))
    return pl.pallas_call(
        deferred(mlp_out_kernel, 4, len(after)),
        grid=(D // wide,),
        out_shape=(shaped((4, count // 8, D), F32), shaped((4, count // 8, D), BF16)),
        in_specs=[pl.BlockSpec((count, 4 * BW), lambda i: (0, 0)) for _ in args] + [weight] * 2 + unread_specs(after),
        out_specs=(tile,) * 2,
        compiler_params=params(58),
        cost_estimate=cost(4_300_000_000, 18_000_000),
        name="mlp_out",
    )(*args, w_even, w_odd, *after)


def weight_products(first, second, column_sets, sources, name, after=()):
    half = first[0].shape[0]
    span = column_sets[0][0].shape[1]
    row_spec = pl.BlockSpec((half, TILE), lambda i: (0, i))
    column_spec = pl.BlockSpec((2 * half, span), lambda i: (0, 0))
    flat = [piece for pieces in column_sets for piece in pieces]
    return pl.pallas_call(
        deferred(functools.partial(grads_kernel, sources), 16 + len(flat), len(after)),
        grid=(D // TILE,),
        out_shape=shaped((len(sources), span // BW, D, BW), BF16),
        in_specs=[row_spec] * 16 + [column_spec] * len(flat) + unread_specs(after),
        out_specs=pl.BlockSpec((len(sources), span // BW, TILE, BW), lambda i: (0, 0, i, 0)),
        compiler_params=params(40),
        cost_estimate=cost(2 * 8 * half * D * span * len(sources), 20_000_000),
        name=name,
    )(*first, *second, *flat, *after)


def muon(grads, momentum, weights, offset, stride, begun=(), after=()):
    count = grads.shape[0]
    now = lambda i: jnp.minimum(i, count - 1)
    then = lambda i: jnp.maximum(i - count, 0)
    block = (None, D, BW)
    compact = pl.BlockSpec(block, lambda i: (now(i), 0, 0))
    early = pl.BlockSpec(block, lambda i: (stride * now(i) + offset, 0, 0))
    late = pl.BlockSpec(block, lambda i: (stride * then(i) + offset, 0, 0))
    return pl.pallas_call(
        deferred(muon_kernel, 3, len(begun) + len(after)),
        grid=(2 * count,),
        out_shape=(shaped(momentum.shape, F32),) * 3,
        in_specs=[compact, early, late] + unread_specs(begun) + unread_specs(after),
        out_specs=(early, early, late),
        input_output_aliases={3 + index: index for index in range(len(begun))},
        scratch_shapes=[pltpu.VMEM((count, D, BW), F32), pltpu.VMEM((count, BW, BW), F32)],
        compiler_params=params(40),
        cost_estimate=cost(1_000_000_000 * count, 5_500_000 * count),
        name="muon",
    )(grads, momentum, weights, *begun, *after)


def mirror(step):
    return [(place, place ^ step) for place in range(4)]


def ring(value, step=1):
    return lax.ppermute(value, "z", [(place, (place + step) % 4) for place in range(4)])


def swap(value):
    return lax.ppermute(value, "tensor", SWAP)


def nothing(value):
    first = value[(0,) * value.ndim].astype(F32)
    return (first * 0.0).astype(jnp.int32)


def hold(value, *others):
    zero = sum((nothing(other) for other in others), jnp.int32(0))
    return value + zero.astype(value.dtype)


def gather_rows(rows):
    mine = [rows]
    for _ in range(3):
        mine.append(ring(mine[-1]))
    return mine, [swap(part) for part in mine]


class Scatter:
    def __init__(self):
        self.moving = self.result = None
        self.payloads = []

    def add(self, step, mine, theirs):
        total = mine + swap(theirs).astype(F32)
        if self.moving is not None:
            total = total + self.moving.astype(F32)
        if step:
            self.payloads.append(total.astype(BF16))
            self.moving = ring(self.payloads[-1])
        else:
            self.result = total


def everywhere(value):
    value = value + swap(value)
    for axis in ("m", "z"):
        one, two, three = (lax.ppermute(value, axis, mirror(step)) for step in (1, 2, 3))
        value = (value + one) + (two + three)
    if lax.axis_size("r") > 1:
        value = lax.psum(value, "r")
    return value


def join(parts):
    if parts.shape[0] == 4:
        return parts
    width = parts.shape[3]
    parts = parts.reshape(4, 2, -1, D, width).transpose(0, 1, 3, 2, 4)
    return parts.reshape(4, 2, D, BW)


def unjoin(grads, width):
    if width == BW:
        return grads
    grads = grads.reshape(4, 2, D, -1, width).transpose(0, 1, 3, 2, 4)
    return grads.reshape(-1, 1, D, width)


def gather_plane(parts):
    return lax.all_gather(jnp.stack(parts), ("m", "r"), axis=0, tiled=False)


def gather_part_direct(part, index, result):
    chip = lax.axis_index("m")
    result = lax.dynamic_update_slice(result, part[None, None], (chip, index, 0, 0))
    for step in (1, 2, 3):
        got = lax.ppermute(part, "m", mirror(step))
        result = lax.dynamic_update_slice(result, got[None, None], (chip ^ step, index, 0, 0))
    return result


def scatter_plane(grads):
    share = lax.psum_scatter(
        grads.reshape(grads.shape[0], -1, grads.shape[3]), ("m", "r"), scatter_dimension=0, tiled=False
    )
    return share.reshape(grads.shape[1:])


def scatter_plane_direct(grads, *others):
    chip = lax.axis_index("m")
    zero = sum((nothing(other) for other in others), jnp.int32(0)).astype(F32)

    def share_for(step):
        return lax.dynamic_index_in_dim(grads, chip ^ step, 0, keepdims=False)

    total = share_for(0).astype(F32) + zero
    for step in (1, 2, 3):
        total = total + lax.ppermute(share_for(step), "m", mirror(step)).astype(F32)
    return total.astype(BF16)


def interleave(mine, other):
    return [rows for pair in zip(mine, other) for rows in pair]


def local(tokens, segments, weights, momentum, gains, gain_first, gain_second, cotangent):
    plane = lax.axis_index("z")
    core = lax.axis_index("tensor")
    block_count = weights.shape[0]

    if block_count == 8:
        shards = weights.reshape(4, 2, D, BW)
    else:
        width = block_count * BW // 4
        shards = weights.reshape(block_count, D, -1, width).transpose(0, 2, 1, 3).reshape(4, 1, D, width)
    parts, width = shards.shape[1], shards.shape[3]

    def shard(shift, part, *others):
        at = sum((nothing(other) for other in others), plane + shift)
        return lax.dynamic_slice(shards, (at % 4, part, 0, 0), (1, 1, D, width))[0, 0]

    rows_in = tokens.astype(F32)
    segment_parts = [segments] + [ring(segments, shift) for shift in (1, 2, 3)]
    segment_rows = jnp.concatenate(segment_parts, axis=0)
    moved = []
    for part in range(parts):
        others = [moved[0][1], moved[0][3]] if part else []
        moved.append([shard(0, part)] + [ring(shard(shift, part, *others), shift) for shift in (1, 2, 3)])

    def kind_part(source, part, *others):
        at = sum((nothing(other) for other in others), plane)
        return lax.select_n(at, *(moved[part][(here - source) % 4] for here in range(4)))

    if parts == 2:
        mlp_parts = [[kind_part(kind, 0) for kind in (1, 2, 3)]]
        one_mine, one_other = gather_rows(hold(rms_norm(rows_in, gains[0]), mlp_parts[0][0]).astype(BF16))
        w_attn = gather_part_direct(kind_part(0, 0, segment_rows), 0, jnp.zeros((4, 2, D, BW), BF16))
        w_attn_even = w_attn
        waits = (w_attn, mlp_parts[0][0])
        w_attn = gather_part_direct(kind_part(0, 1, *waits), 1, w_attn)
        mlp_parts.append([kind_part(kind, 1, w_attn_even) for kind in (1, 2, 3)])
        begun = [mlp_parts[1][0]]
        w_mlp = [gather_plane(kinds) for kinds in mlp_parts]
    else:
        w_attn = join(gather_plane([kind_part(0, 0)]))
        w_mlp = gather_plane([kind_part(kind, 0) for kind in (1, 2, 3)])
        w_mlp = jnp.stack([join(w_mlp[:, kind : kind + 1]) for kind in range(3)], axis=1)
        w_mlp = [w_mlp[:, :, 0], w_mlp[:, :, 1]]
        one_mine, one_other = gather_rows(rms_norm(rows_in, gains[0]).astype(BF16))
        begun = []
    d_mine, d_other = gather_rows(hold(cotangent, *begun))

    length = segment_rows.shape[1]
    half = length // 2
    place = jnp.arange(length)
    place = jnp.where(core == 0, place, (place + half) % length)
    segment_rows = jnp.where(core == 0, segment_rows, jnp.roll(segment_rows, half, axis=1))
    allowed = (place[None, None, :] <= place[None, :, None]) & (
        segment_rows[:, None, :] == segment_rows[:, :, None]
    )
    bias = jnp.where(allowed, 0.0, NEG_LARGE).astype(F32)
    cosine, sine = rope_tables(place)

    query, key, value, context = ([None] * 4 for _ in range(4))
    mixed = Scatter()
    for s in (1, 2, 3, 0):
        query[s], key[s], value[s], context[s], *both = attn_forward(
            one_mine[s], one_other[s], w_attn, bias[s], cosine, sine, mixed.payloads[:1] if s == 3 else begun if s == 1 else ()
        )
        mixed.add(s, *both)
    middle = rows_in + mixed.result
    two_mine, two_other = gather_rows(rms_norm(middle, gains[1]).astype(BF16))

    two_rows, d_rows = interleave(two_mine, two_other), interleave(d_mine, d_other)
    *even_half, mlp_even = mlp_half(two_rows, d_rows, w_mlp[0])
    *odd_half, mlp_odd = mlp_half(two_rows, d_rows, w_mlp[1])
    d_normed = Scatter()
    for s in (1, 2, 3, 0):
        d_normed.add(s, *mlp_back(s, (even_half, odd_half), *w_mlp))
    d_normed_two = d_normed.result

    d_output = cotangent.astype(F32)
    d_middle_norm, d_gain_two = rms_norm_back(middle, gains[1], d_normed_two)
    d_middle = d_output + d_middle_norm
    e_mine, e_other = gather_rows(d_middle.astype(BF16))
    outward = mlp_out((even_half, odd_half), *w_mlp, e_mine[:1])
    d_query, d_key, d_value, d_one = ([None] * 4 for _ in range(4))
    for s in range(4):
        d_query[s], d_key[s], d_value[s], *both = attn_backward(
            e_mine[s], e_other[s], w_attn, bias[s], cosine, sine, query[s], key[s], value[s]
        )
        d_one[s] = both
    attn_grads = weight_products(
        interleave(one_mine, one_other),
        interleave(e_mine, e_other),
        (d_query, d_key, d_value, context),
        (0, 0, 0, 1),
        "attn_products",
    )
    if parts == 2:
        attn_share = scatter_plane_direct(attn_grads)
        mlp_share = [
            scatter_plane(mlp_even),
            scatter_plane(mlp_odd),
        ]
    else:
        attn_share = scatter_plane(unjoin(attn_grads, width))
        mlp_grads = jnp.stack([mlp_even, mlp_odd], axis=2)
        mlp_share = [
            jnp.concatenate([scatter_plane(unjoin(mlp_grads[:, kind], width)) for kind in range(3)])
        ]

    last = Scatter()
    for s in (1, 2, 3, 0):
        mine, theirs = (jnp.stack([a, b[s]]) for a, b in zip(d_one[s], outward))
        if s == 2:
            mine = hold(mine, attn_grads)
        last.add(s, mine, theirs)
    d_normed_one, outward_sum = last.result
    d_rows_norm, d_gain_one = rms_norm_back(rows_in, gains[0], d_normed_one)
    input_grad = d_middle + d_rows_norm
    output = (middle + outward_sum).astype(BF16)
    gain_grads = everywhere(jnp.stack([d_gain_one, d_gain_two]))

    results = ()
    for part in range(parts):
        shares = jnp.concatenate([attn_share[part][None], mlp_share[part]])

        def share_of(shift):
            return lax.dynamic_index_in_dim(shares, (plane + shift) % 4, 0, keepdims=False)

        back = [share_of(0)] + [ring(share_of(shift), shift) for shift in (1, 2, 3)]
        here = plane + nothing(results[1]) if part else plane
        summed = jnp.stack(
            [lax.select_n(here, *(back[(z - source) % 4] for z in range(4))) for source in range(4)]
        )
        if parts == 1:
            summed = summed.reshape(block_count, -1, D, width).transpose(0, 2, 1, 3).reshape(block_count, D, BW)
        results = muon(summed, momentum, weights, part, parts, results)
    weight_grads, new_momentum, new_weights = results

    new_gain_first = BETA_FIRST * gain_first + (1.0 - BETA_FIRST) * gain_grads
    new_gain_second = BETA_SECOND * gain_second + (1.0 - BETA_SECOND) * gain_grads * gain_grads
    first_hat = new_gain_first / (1.0 - BETA_FIRST**STEP)
    second_hat = new_gain_second / (1.0 - BETA_SECOND**STEP)
    new_gains = gains - ADAM_RATE * first_hat / (jnp.sqrt(second_hat) + ADAM_EPS)
    return (
        output,
        input_grad,
        weight_grads,
        new_momentum,
        new_weights,
        new_gain_first,
        new_gain_second,
        new_gains,
    )


def solution(mesh):
    count = mesh.shape["dp"]
    fine = Mesh(
        np.asarray(mesh.devices).reshape(4, 4, count // 16, mesh.shape["tensor"]),
        ("z",) + PLANE,
    )
    every = ("z",) + PLANE
    in_specs = (
        P(every, None),
        P(every[:3], None),
        P(every, None, None),
        P(every, None, None),
        P(),
        P(),
        P(),
        P(every, None),
    )
    out_specs = (
        P(every, None),
        P(every, None),
        P(every, None, None),
        P(every, None, None),
        P(every, None, None),
        P(),
        P(),
        P(),
    )
    return jax.shard_map(local, mesh=fine, in_specs=in_specs, out_specs=out_specs, check_vma=False)
```

```python
import functools
import math

import jax
import jax.numpy as jnp
import numpy as np
from jax import lax
from jax.experimental import pallas as pl
from jax.experimental.pallas import tpu as pltpu
from jax.sharding import Mesh
from jax.sharding import PartitionSpec as P

D = 2048
FF = 8192
HD = 64
BW = 128
NS_ITERS = 5
STEP = 10

HIGHEST = lax.Precision.HIGHEST
ROPE_BASE = 130000.0
NORM_EPS = 1e-05
NEG_LARGE = -1e30
MOMENTUM_DECAY = 0.95
MUON_RATE = 0.25
COEFF_A = 3.4445
COEFF_B = -4.775
COEFF_C = 2.0315
BETA_FIRST = 0.9
BETA_SECOND = 0.95
ADAM_RATE = 1.0
ADAM_EPS = 1e-08

F32 = jnp.float32
BF16 = jnp.bfloat16
PLANE = ("m", "r", "tensor")
SWAP = [(0, 1), (1, 0)]
TILE = 256
SCORE_SCALE = 1.0 / math.sqrt(HD)


def rms_norm(values, gain):
    return values * lax.rsqrt(jnp.mean(values * values, axis=-1, keepdims=True) + NORM_EPS) * gain


def rms_norm_back(values, gain, grad):
    scale = lax.rsqrt(jnp.mean(values * values, axis=-1, keepdims=True) + NORM_EPS)
    scaled = gain * grad
    inner = jnp.mean(scaled * values, axis=-1, keepdims=True)
    gain_grad = jnp.sum(grad * values * scale, axis=0)
    return scale * scaled - values * (scale * scale * scale * inner), gain_grad


def rope_tables(place):
    exponent = jnp.arange(HD // 2).astype(F32) * (2.0 / HD)
    inverse = jnp.exp(-exponent * math.log(ROPE_BASE))
    angle = place.astype(F32)[:, None] * inverse[None, :]
    cosine, sine = jnp.cos(angle), jnp.sin(angle)
    heads = 2 * BW // HD
    return (
        jnp.tile(jnp.concatenate([cosine, cosine], axis=1), (1, heads)),
        jnp.tile(jnp.concatenate([-sine, sine], axis=1), (1, heads)),
    )


def dims(lhs, rhs):
    return (((lhs,), (rhs,)), ((), ()))


def mul(a, b):
    return lax.dot_general(a, b, dims(1, 0), preferred_element_type=F32)


def mul_bt(a, b):
    return lax.dot_general(a, b, dims(1, 1), preferred_element_type=F32)


def mul_at(a, b):
    return lax.dot_general(a, b, dims(0, 0), preferred_element_type=F32)


def side_by_side(ref, *index):
    return jnp.concatenate([ref[index + (0,)], ref[index + (1,)]], axis=-1)


def pair_rows(own_ref, other_ref):
    return jnp.concatenate([own_ref[...], other_ref[...]], axis=0)


def swap_halves(values):
    lane = lax.broadcasted_iota(jnp.int32, values.shape, 1)
    span = values.shape[1]
    ahead = pltpu.roll(values, span - HD // 2, 1)
    behind = pltpu.roll(values, HD // 2, 1)
    return jnp.where(lane % HD < HD // 2, ahead, behind)


def head_only(values, head):
    lane = lax.broadcasted_iota(jnp.int32, values.shape, 1)
    return jnp.where((lane >= head * HD) & (lane < (head + 1) * HD), values, jnp.zeros_like(values))


def head_probs(query, key, bias, head):
    scores = mul_bt(head_only(query, head), key) * SCORE_SCALE + bias
    weights = jnp.exp(scores - jnp.max(scores, axis=-1, keepdims=True))
    return weights / jnp.sum(weights, axis=-1, keepdims=True)


def attn_forward_kernel(
    own_ref, other_ref, w_ref, bias_ref, cos_ref, sin_ref, q_ref, k_ref, v_ref, c_ref, mine_ref, theirs_ref
):
    rows = pair_rows(own_ref, other_ref)
    cosine, sine = cos_ref[...], sin_ref[...]
    lin = mul(rows, side_by_side(w_ref, 0))
    query = (lin * cosine + swap_halves(lin) * sine).astype(BF16)
    lin = mul(rows, side_by_side(w_ref, 1))
    key = (lin * cosine + swap_halves(lin) * sine).astype(BF16)
    value = mul(rows, side_by_side(w_ref, 2)).astype(BF16)
    q_ref[...] = query
    k_ref[...] = key
    v_ref[...] = value
    context = jnp.zeros(query.shape, F32)
    for head in range(query.shape[1] // HD):
        probs = head_probs(query, key, bias_ref[...], head)
        context = context + mul(probs.astype(BF16), head_only(value, head))
    context = context.astype(BF16)
    c_ref[...] = context
    half = own_ref.shape[0]
    for tile in range(D // TILE):
        at = pl.ds(tile * TILE, TILE)
        w_out = jnp.concatenate([w_ref[3, 0, at, :], w_ref[3, 1, at, :]], axis=-1)
        mixed = mul_bt(context, w_out)
        mine_ref[:, at] = mixed[:half]
        theirs_ref[:, at] = mixed[half:].astype(BF16)


def attn_backward_kernel(
    own_ref, other_ref, w_ref, bias_ref, cos_ref, sin_ref, q_ref, k_ref, v_ref,
    dq_ref, dk_ref, dv_ref, mine_ref, theirs_ref,
):
    rows = pair_rows(own_ref, other_ref)
    query, key, value = q_ref[...], k_ref[...], v_ref[...]
    d_context = mul(rows, side_by_side(w_ref, 3)).astype(BF16)
    d_query = jnp.zeros(query.shape, F32)
    d_key = jnp.zeros(query.shape, F32)
    d_value = jnp.zeros(query.shape, F32)
    for head in range(query.shape[1] // HD):
        probs = head_probs(query, key, bias_ref[...], head)
        d_here = head_only(d_context, head)
        d_value = d_value + mul_at(probs.astype(BF16), d_here)
        d_probs = mul_bt(d_here, value)
        inner = jnp.sum(probs * d_probs, axis=-1, keepdims=True)
        d_scores = (probs * (d_probs - inner)).astype(BF16)
        d_query = d_query + mul(d_scores, head_only(key, head))
        d_key = d_key + mul_at(d_scores, head_only(query, head))
    cosine, sine = cos_ref[...], sin_ref[...]
    d_query = d_query * SCORE_SCALE
    d_key = d_key * SCORE_SCALE
    d_query = (d_query * cosine - swap_halves(d_query) * sine).astype(BF16)
    d_key = (d_key * cosine - swap_halves(d_key) * sine).astype(BF16)
    d_value = d_value.astype(BF16)
    dq_ref[...] = d_query
    dk_ref[...] = d_key
    dv_ref[...] = d_value
    half = own_ref.shape[0]
    for tile in range(D // TILE):
        at = pl.ds(tile * TILE, TILE)
        total = jnp.zeros((2 * half, TILE), F32)
        for matrix, columns in ((0, d_query), (1, d_key), (2, d_value)):
            w_here = jnp.concatenate([w_ref[matrix, 0, at, :], w_ref[matrix, 1, at, :]], axis=-1)
            total = total + mul_bt(columns, w_here)
        mine_ref[:, at] = total[:half]
        theirs_ref[:, at] = total[half:].astype(BF16)


def mlp_half_kernel(*refs):
    rows, d_rows = refs[:8], refs[8:16]
    w_ref, hid_ref, dgate_ref, dup_ref, grad_ref = refs[16:]
    w_gate, w_up, w_down = (
        jnp.concatenate([w_ref[0, kind], w_ref[1, kind]], axis=-1) for kind in range(3)
    )
    for piece in range(4):
        here = pair_rows(rows[2 * piece], rows[2 * piece + 1])
        gate = mul(here, w_gate)
        up = mul(here, w_up)
        d_hidden = mul(pair_rows(d_rows[2 * piece], d_rows[2 * piece + 1]), w_down)
        sigmoid = 1.0 / (1.0 + jnp.exp(-gate))
        silu = gate * sigmoid
        at = pl.ds(piece * here.shape[0], here.shape[0])
        hid_ref[at, :] = (silu * up).astype(BF16)
        dgate_ref[at, :] = (d_hidden * up * sigmoid * (1.0 + gate * (1.0 - sigmoid))).astype(BF16)
        dup_ref[at, :] = (d_hidden * silu).astype(BF16)
    for tile in range(D // TILE):
        at = pl.ds(tile * TILE, TILE)
        across = jnp.concatenate([ref[:, at] for ref in rows], axis=0)
        d_across = jnp.concatenate([ref[:, at] for ref in d_rows], axis=0)
        for kind, left, right in ((0, across, dgate_ref), (1, across, dup_ref), (2, d_across, hid_ref)):
            grad = mul_at(left, right[...]).astype(BF16)
            for chip in range(2):
                grad_ref[chip, kind, at, :] = grad[:, chip * BW : (chip + 1) * BW]


def all_columns(kind, w_even, w_odd):
    return jnp.concatenate([ref[chip, kind] for ref in (w_even, w_odd) for chip in range(4)], axis=-1)


def both_columns(even, odd):
    return jnp.concatenate([even[...], odd[...]], axis=-1)


def mlp_back_kernel(dgate_even, dgate_odd, dup_even, dup_odd, w_even, w_odd, mine_ref, theirs_ref):
    total = mul_bt(both_columns(dgate_even, dgate_odd), all_columns(0, w_even, w_odd))
    total = total + mul_bt(both_columns(dup_even, dup_odd), all_columns(1, w_even, w_odd))
    half = mine_ref.shape[0]
    mine_ref[...] = total[:half]
    theirs_ref[...] = total[half:].astype(BF16)


def mlp_out_kernel(hid_even, hid_odd, w_even, w_odd, mine_ref, theirs_ref):
    total = mul_bt(both_columns(hid_even, hid_odd), all_columns(0, w_even, w_odd))
    half = mine_ref.shape[1]
    for piece in range(4):
        mine_ref[piece] = total[2 * piece * half : (2 * piece + 1) * half]
        theirs_ref[piece] = total[(2 * piece + 1) * half : 2 * (piece + 1) * half].astype(BF16)


def grads_kernel(sources, *refs):
    first, second = refs[:8], refs[8:16]
    columns = refs[16:-1]
    out_ref = refs[-1]
    row_sets = [jnp.concatenate([ref[...] for ref in part], axis=0) for part in (first, second)]
    for index, source in enumerate(sources):
        stacked = jnp.concatenate([ref[...] for ref in columns[4 * index : 4 * index + 4]], axis=0)
        grad = mul_at(row_sets[source], stacked).astype(BF16)
        for block in range(grad.shape[1] // BW):
            out_ref[index, block] = grad[:, block * BW : (block + 1) * BW]


def split(values):
    high = values.astype(BF16)
    return high, (values - high.astype(F32)).astype(BF16)


def mul_split(a, b):
    return mul(a[0], b[0]) + (mul(a[0], b[1]) + mul(a[1], b[0]))


def muon_kernel(grad_ref, momentum_ref, weight_ref, wg_ref, nm_ref, nw_ref, held, mixers):
    step = pl.program_id(0)
    count = held.shape[0]

    @pl.when(step < count)
    def _():
        grad = grad_ref[...].astype(F32)
        wg_ref[...] = grad
        block = MOMENTUM_DECAY * momentum_ref[...] + grad
        nm_ref[...] = block
        block = block * (1.0 / (jnp.sqrt(jnp.sum(block * block)) + 1e-07))
        held[step] = block
        high, low = split(block)
        cross = mul_at(high, low)
        mixers[step] = mul_at(high, high) + (cross + cross.T)

    @pl.when(step == count - 1)
    def _():
        row = lax.broadcasted_iota(jnp.int32, (BW, BW), 0)
        column = lax.broadcasted_iota(jnp.int32, (BW, BW), 1)
        eye = jnp.where(row == column, COEFF_A, 0.0).astype(F32)
        grams = [mixers[index] for index in range(count)]
        totals = [None] * count
        for turn in range(NS_ITERS):
            for index in range(count):
                pair = split(grams[index])
                mixer = eye + COEFF_B * grams[index] + COEFF_C * mul_split(pair, pair)
                mixed = split(mixer)
                if turn == 0:
                    totals[index] = mixer
                else:
                    totals[index] = mul_split(split(totals[index]), mixed)
                if turn < NS_ITERS - 1:
                    grams[index] = mul_split(split(mul_split(mixed, pair)), mixed)
        for index in range(count):
            mixers[index] = totals[index]

    @pl.when(step >= count)
    def _():
        at = step - count
        ortho = mul_split(split(held[at]), split(mixers[at]))
        nw_ref[...] = weight_ref[...].astype(F32) - (MUON_RATE * math.sqrt(D / BW)) * ortho


def deferred(kernel, inputs, unread):
    return lambda *refs: kernel(*refs[:inputs], *refs[inputs + unread :])


def unread_specs(after):
    return [pl.BlockSpec(memory_space=pl.ANY) for _ in after]


def cost(flops, accessed):
    return pl.CostEstimate(flops=flops // 6, bytes_accessed=accessed // 6, transcendentals=0)


def sort_kernel(plane_ref, *refs):
    moved, attn_ref, mlp_ref = refs[:4], refs[4], refs[5]
    for here in range(4):

        @pl.when(plane_ref[0] == here)
        def _():
            attn_ref[...] = moved[here][...]
            for kind in (1, 2, 3):
                mlp_ref[kind - 1] = moved[(here - kind) % 4][...]


def sort_kinds(plane, moved, after):
    shape = moved[0].shape
    return pl.pallas_call(
        deferred(sort_kernel, 5, len(after)),
        out_shape=(shaped(shape, BF16), shaped((3,) + shape, BF16)),
        in_specs=[pl.BlockSpec(memory_space=pltpu.SMEM)] + whole_specs(moved) + unread_specs(after),
        out_specs=tuple(whole_specs(range(2))),
        compiler_params=params(32),
        cost_estimate=cost(0, 4_000_000),
        name="sort_kinds",
    )(plane.astype(jnp.int32).reshape(1), *moved, *after)


def params(mebibytes):
    return pltpu.CompilerParams(vmem_limit_bytes=mebibytes * 1024 * 1024)


def whole_specs(arrays):
    return [pl.BlockSpec(memory_space=pltpu.VMEM) for _ in arrays]


def shaped(shape, dtype):
    return jax.ShapeDtypeStruct(shape, dtype)


def attn_forward(own, other, w_attn, bias, cosine, sine, after=()):
    half = own.shape[1]
    rows = pl.BlockSpec((None, half, D), lambda i: (0, 0, 0))
    span = w_attn.shape[1] * w_attn.shape[3]
    square = shaped((2 * half, span), BF16)
    args = (own, other, w_attn, bias, cosine, sine)
    return pl.pallas_call(
        deferred(attn_forward_kernel, len(args), len(after)),
        grid=(1,),
        out_shape=(square,) * 4 + (shaped((half, D), F32), shaped((half, D), BF16)),
        in_specs=[rows, rows] + whole_specs(args[2:]) + unread_specs(after),
        out_specs=tuple(whole_specs(range(6))),
        compiler_params=params(40),
        cost_estimate=cost(1_300_000_000, 9_000_000),
        name="attn_forward",
    )(*args, *after)


def attn_backward(own, other, w_attn, bias, cosine, sine, query, key, value):
    half = own.shape[0]
    square = shaped(query.shape, BF16)
    args = (own, other, w_attn, bias, cosine, sine, query, key, value)
    return pl.pallas_call(
        attn_backward_kernel,
        out_shape=(square,) * 3 + (shaped((half, D), F32), shaped((half, D), BF16)),
        in_specs=whole_specs(args),
        out_specs=tuple(whole_specs(range(5))),
        compiler_params=params(40),
        cost_estimate=cost(1_600_000_000, 9_000_000),
        name="attn_backward",
    )(*args)


def mlp_half(rows, pairs, w_half):
    half = rows[0].shape[0]
    columns = shaped((8 * half, 4 * BW), BF16)
    blocks = pl.BlockSpec((2, 3, D, BW), lambda j: (j, 0, 0, 0))
    return pl.pallas_call(
        mlp_half_kernel,
        grid=(2,),
        out_shape=(columns,) * 3 + (shaped(w_half.shape, BF16),),
        in_specs=[pl.BlockSpec((half, D), lambda j: (0, 0)) for _ in range(8)]
        + [pl.BlockSpec((None, half, D), lambda j: (1, 0, 0)) for _ in range(8)]
        + [blocks],
        out_specs=(pl.BlockSpec((8 * half, 2 * BW), lambda j: (0, j)),) * 3 + (blocks,),
        compiler_params=params(58),
        cost_estimate=cost(13_000_000_000, 20_000_000),
        name="mlp_half",
    )(*rows, *pairs, w_half)


def mlp_back(piece, halves, w_even, w_odd):
    rows = halves[0][0].shape[0] // 4
    wide = 2 * TILE
    args = [half[index] for index in (1, 2) for half in halves]
    tile = pl.BlockSpec((rows // 2, wide), lambda i: (0, i))
    weight = pl.BlockSpec((4, 2, wide, BW), lambda i: (0, 0, i, 0))
    return pl.pallas_call(
        mlp_back_kernel,
        grid=(D // wide,),
        out_shape=(shaped((rows // 2, D), F32), shaped((rows // 2, D), BF16)),
        in_specs=[pl.BlockSpec((rows, 4 * BW), lambda i: (piece, 0)) for _ in args] + [weight] * 2,
        out_specs=(tile,) * 2,
        compiler_params=params(58),
        cost_estimate=cost(2_200_000_000, 11_000_000),
        name="mlp_back",
    )(*args, w_even, w_odd)


def mlp_out(halves, w_even, w_odd, after):
    count = halves[0][0].shape[0]
    args = [half[0] for half in halves]
    wide = 2 * TILE
    tile = pl.BlockSpec((4, count // 8, wide), lambda i: (0, 0, i))
    weight = pl.BlockSpec((4, 1, wide, BW), lambda i: (0, 2, i, 0))
    return pl.pallas_call(
        deferred(mlp_out_kernel, 4, len(after)),
        grid=(D // wide,),
        out_shape=(shaped((4, count // 8, D), F32), shaped((4, count // 8, D), BF16)),
        in_specs=[pl.BlockSpec((count, 4 * BW), lambda i: (0, 0)) for _ in args] + [weight] * 2 + unread_specs(after),
        out_specs=(tile,) * 2,
        compiler_params=params(58),
        cost_estimate=cost(4_300_000_000, 18_000_000),
        name="mlp_out",
    )(*args, w_even, w_odd, *after)


def weight_products(pairs, rows, column_sets, sources, name):
    half = rows[0].shape[0]
    span = column_sets[0][0].shape[1]
    pair_spec = pl.BlockSpec((None, half, TILE), lambda i: (0, 0, i))
    row_spec = pl.BlockSpec((half, TILE), lambda i: (0, i))
    column_spec = pl.BlockSpec((2 * half, span), lambda i: (0, 0))
    flat = [piece for pieces in column_sets for piece in pieces]
    return pl.pallas_call(
        functools.partial(grads_kernel, sources),
        grid=(D // TILE,),
        out_shape=shaped((len(sources), span // BW, D, BW), BF16),
        in_specs=[pair_spec] * 8 + [row_spec] * 8 + [column_spec] * len(flat),
        out_specs=pl.BlockSpec((len(sources), span // BW, TILE, BW), lambda i: (0, 0, i, 0)),
        compiler_params=params(40),
        cost_estimate=cost(2 * 8 * half * D * span * len(sources), 20_000_000),
        name=name,
    )(*pairs, *rows, *flat)


def muon(grads, momentum, weights, offset, stride, begun=(), after=()):
    count = grads.shape[0]
    now = lambda i: jnp.minimum(i, count - 1)
    then = lambda i: jnp.maximum(i - count, 0)
    block = (None, D, BW)
    compact = pl.BlockSpec(block, lambda i: (now(i), 0, 0))
    early = pl.BlockSpec(block, lambda i: (stride * now(i) + offset, 0, 0))
    late = pl.BlockSpec(block, lambda i: (stride * then(i) + offset, 0, 0))
    return pl.pallas_call(
        deferred(muon_kernel, 3, len(begun) + len(after)),
        grid=(2 * count,),
        out_shape=(shaped(momentum.shape, F32),) * 3,
        in_specs=[compact, early, late] + unread_specs(begun) + unread_specs(after),
        out_specs=(early, early, late),
        input_output_aliases={3 + index: index for index in range(len(begun))},
        scratch_shapes=[pltpu.VMEM((count, D, BW), F32), pltpu.VMEM((count, BW, BW), F32)],
        compiler_params=params(40),
        cost_estimate=cost(1_000_000_000 * count, 5_500_000 * count),
        name="muon",
    )(grads, momentum, weights, *begun, *after)


def mirror(step):
    return [(place, place ^ step) for place in range(4)]


def ring(value, step=1):
    return lax.ppermute(value, "z", [(place, (place + step) % 4) for place in range(4)])


def swap(value):
    return lax.ppermute(value, "tensor", SWAP)


def nothing(value):
    first = value[(0,) * value.ndim].astype(F32)
    return (first * 0.0).astype(jnp.int32)


def hold(value, *others):
    zero = sum((nothing(other) for other in others), jnp.int32(0))
    return value + zero.astype(value.dtype)


def gather_rows(rows):
    mine = [rows]
    for _ in range(3):
        mine.append(ring(mine[-1]))
    return mine, [swap(part) for part in mine]


class Scatter:
    def __init__(self):
        self.moving = self.result = None
        self.payloads = []

    def add(self, step, mine, theirs):
        total = mine + swap(theirs).astype(F32)
        if self.moving is not None:
            total = total + self.moving.astype(F32)
        if step:
            self.payloads.append(total.astype(BF16))
            self.moving = ring(self.payloads[-1])
        else:
            self.result = total


def everywhere(value):
    value = value + swap(value)
    for axis in ("m", "z"):
        one, two, three = (lax.ppermute(value, axis, mirror(step)) for step in (1, 2, 3))
        value = (value + one) + (two + three)
    if lax.axis_size("r") > 1:
        value = lax.psum(value, "r")
    return value


def join(parts):
    if parts.shape[0] == 4:
        return parts
    width = parts.shape[3]
    parts = parts.reshape(4, 2, -1, D, width).transpose(0, 1, 3, 2, 4)
    return parts.reshape(4, 2, D, BW)


def unjoin(grads, width):
    if width == BW:
        return grads
    grads = grads.reshape(4, 2, D, -1, width).transpose(0, 1, 3, 2, 4)
    return grads.reshape(-1, 1, D, width)


def gather_plane(parts):
    return lax.all_gather(parts, ("m", "r"), axis=0, tiled=False)


def gather_part_direct(part, index, result):
    chip = lax.axis_index("m")
    result = lax.dynamic_update_slice(result, part[None, None], (chip, index, 0, 0))
    for step in (1, 2, 3):
        got = lax.ppermute(part, "m", mirror(step))
        result = lax.dynamic_update_slice(result, got[None, None], (chip ^ step, index, 0, 0))
    return result


def scatter_plane(grads):
    share = lax.psum_scatter(
        grads.reshape(grads.shape[0], -1, grads.shape[3]), ("m", "r"), scatter_dimension=0, tiled=False
    )
    return share.reshape(grads.shape[1:])


def scatter_plane_direct(grads):
    chip = lax.axis_index("m")
    shares = []
    for part in range(2):
        at = chip + sum((nothing(share) for share in shares), jnp.int32(0))

        def share_for(step):
            return lax.dynamic_slice(grads, (at ^ step, part, 0, 0), (1, 1) + grads.shape[2:])[0, 0]

        total = share_for(0).astype(F32)
        arrived = []
        for step in (1, 2, 3):
            arrived.append(lax.ppermute(share_for(step), "m", mirror(step)))
            total = total + arrived[-1].astype(F32)
        shares.append(total.astype(BF16))
    return shares


def interleave(mine, other):
    return [rows for pair in zip(mine, other) for rows in pair]


def local(tokens, segments, weights, momentum, gains, gain_first, gain_second, cotangent):
    plane = lax.axis_index("z")
    core = lax.axis_index("tensor")
    block_count = weights.shape[0]

    if block_count == 8:
        shards = weights.reshape(4, 2, D, BW)
    else:
        width = block_count * BW // 4
        shards = weights.reshape(block_count, D, -1, width).transpose(0, 2, 1, 3).reshape(4, 1, D, width)
    parts, width = shards.shape[1], shards.shape[3]

    def shard(shift, part, *others):
        at = sum((nothing(other) for other in others), plane + shift)
        return lax.dynamic_slice(shards, (at % 4, part, 0, 0), (1, 1, D, width))[0, 0]

    rows_in = tokens.astype(F32)
    segment_own = segments.astype(F32)
    segment_parts = [segment_own] + [ring(segment_own, shift) for shift in (1, 2, 3)]
    segment_rows = jnp.concatenate(segment_parts, axis=0)
    moved = []
    for part in range(parts):
        others = [moved[0][1], moved[0][3]] if part else []
        moved.append([shard(0, part)] + [ring(shard(shift, part, *others), shift) for shift in (1, 2, 3)])

    def kind_part(source):
        return lax.select_n(plane, *(moved[0][(here - source) % 4] for here in range(4)))

    row_pair = lambda *others: jnp.stack([hold(rms_norm(rows_in, gains[0]), *others).astype(BF16), cotangent])
    if parts == 2:
        attn_even, mlp_even = sort_kinds(plane, moved[0], [segment_rows])
        w_attn = gather_part_direct(attn_even, 0, jnp.zeros((4, 2, D, BW), BF16))
        attn_odd, mlp_odd = sort_kinds(plane, moved[1], [w_attn])
        w_attn = gather_part_direct(attn_odd, 1, w_attn)
        w_mlp = [gather_plane(mlp_even), gather_plane(mlp_odd)]
        begun = [mlp_odd]
        first_mine, first_other = gather_rows(row_pair(attn_even))
    else:
        w_attn = join(gather_plane(kind_part(0)[None]))
        w_mlp = gather_plane(jnp.stack([kind_part(kind) for kind in (1, 2, 3)]))
        w_mlp = jnp.stack([join(w_mlp[:, kind : kind + 1]) for kind in range(3)], axis=1)
        w_mlp = [w_mlp[:, :, 0], w_mlp[:, :, 1]]
        begun = []
        first_mine, first_other = gather_rows(row_pair())
    first_rows = interleave(first_mine, first_other)

    length = segment_rows.shape[1]
    half = length // 2
    place = jnp.arange(length)
    place = jnp.where(core == 0, place, (place + half) % length)
    segment_rows = jnp.where(core == 0, segment_rows, jnp.roll(segment_rows, half, axis=1))
    allowed = (place[None, None, :] <= place[None, :, None]) & (
        segment_rows[:, None, :] == segment_rows[:, :, None]
    )
    bias = jnp.where(allowed, 0.0, NEG_LARGE).astype(F32)
    cosine, sine = rope_tables(place)

    query, key, value, context = ([None] * 4 for _ in range(4))
    mixed = Scatter()
    for s in (1, 2, 3, 0):
        query[s], key[s], value[s], context[s], *both = attn_forward(
            first_mine[s], first_other[s], w_attn, bias[s], cosine, sine, mixed.payloads[:1] if s == 3 else begun if s == 1 else ()
        )
        mixed.add(s, *both)
    middle = rows_in + mixed.result
    two_mine, two_other = gather_rows(rms_norm(middle, gains[1]).astype(BF16))

    two_rows = interleave(two_mine, two_other)
    *even_half, grads_even = mlp_half(two_rows, first_rows, w_mlp[0])
    *odd_half, grads_odd = mlp_half(two_rows, first_rows, w_mlp[1])
    d_normed = Scatter()
    for s in (1, 2, 3, 0):
        d_normed.add(s, *mlp_back(s, (even_half, odd_half), *w_mlp))
    outward = mlp_out((even_half, odd_half), *w_mlp, d_normed.payloads[-1:])
    d_normed_two = hold(d_normed.result, outward[1])

    d_output = cotangent.astype(F32)
    d_middle_norm, d_gain_two = rms_norm_back(middle, gains[1], d_normed_two)
    d_middle = d_output + d_middle_norm
    e_mine, e_other = gather_rows(d_middle.astype(BF16))
    d_query, d_key, d_value, d_one = ([None] * 4 for _ in range(4))
    for s in range(4):
        d_query[s], d_key[s], d_value[s], *both = attn_backward(
            e_mine[s], e_other[s], w_attn, bias[s], cosine, sine, query[s], key[s], value[s]
        )
        d_one[s] = both
    attn_grads = weight_products(
        first_rows,
        interleave(e_mine, e_other),
        (d_query, d_key, d_value, context),
        (0, 0, 0, 1),
        "attn_products",
    )
    if parts == 2:
        attn_share = scatter_plane_direct(attn_grads)
        mlp_share = [
            scatter_plane(grads_even),
            scatter_plane(grads_odd),
        ]
    else:
        attn_share = scatter_plane(unjoin(attn_grads, width))
        mlp_grads = jnp.stack([grads_even, grads_odd], axis=2)
        mlp_share = [
            jnp.concatenate([scatter_plane(unjoin(mlp_grads[:, kind], width)) for kind in range(3)])
        ]

    last = Scatter()
    for s in (1, 2, 3, 0):
        mine, theirs = (jnp.stack([a, b[s]]) for a, b in zip(d_one[s], outward))
        if s == 2:
            mine = hold(mine, attn_grads)
        last.add(s, mine, theirs)
    d_normed_one, outward_sum = last.result
    d_rows_norm, d_gain_one = rms_norm_back(rows_in, gains[0], d_normed_one)
    input_grad = d_middle + d_rows_norm
    output = (middle + outward_sum).astype(BF16)
    gain_grads = everywhere(jnp.stack([d_gain_one, d_gain_two]))

    results = ()
    for part in range(parts):
        shares = jnp.concatenate([attn_share[part][None], mlp_share[part]])

        def share_of(shift):
            return lax.dynamic_index_in_dim(shares, (plane + shift) % 4, 0, keepdims=False)

        back = [share_of(0)] + [ring(share_of(shift), shift) for shift in (1, 2, 3)]
        here = plane + nothing(results[1]) if part else plane
        summed = jnp.stack(
            [lax.select_n(here, *(back[(z - source) % 4] for z in range(4))) for source in range(4)]
        )
        if parts == 1:
            summed = summed.reshape(block_count, -1, D, width).transpose(0, 2, 1, 3).reshape(block_count, D, BW)
        results = muon(summed, momentum, weights, part, parts, results)
    weight_grads, new_momentum, new_weights = results

    new_gain_first = BETA_FIRST * gain_first + (1.0 - BETA_FIRST) * gain_grads
    new_gain_second = BETA_SECOND * gain_second + (1.0 - BETA_SECOND) * gain_grads * gain_grads
    first_hat = new_gain_first / (1.0 - BETA_FIRST**STEP)
    second_hat = new_gain_second / (1.0 - BETA_SECOND**STEP)
    new_gains = gains - ADAM_RATE * first_hat / (jnp.sqrt(second_hat) + ADAM_EPS)
    return (
        output,
        input_grad,
        weight_grads,
        new_momentum,
        new_weights,
        new_gain_first,
        new_gain_second,
        new_gains,
    )


def solution(mesh):
    count = mesh.shape["dp"]
    fine = Mesh(
        np.asarray(mesh.devices).reshape(4, 4, count // 16, mesh.shape["tensor"]),
        ("z",) + PLANE,
    )
    every = ("z",) + PLANE
    in_specs = (
        P(every, None),
        P(every[:3], None),
        P(every, None, None),
        P(every, None, None),
        P(),
        P(),
        P(),
        P(every, None),
    )
    out_specs = (
        P(every, None),
        P(every, None),
        P(every, None, None),
        P(every, None, None),
        P(every, None, None),
        P(),
        P(),
        P(),
    )
    return jax.shard_map(local, mesh=fine, in_specs=in_specs, out_specs=out_specs, check_vma=False)
```

```python
import functools
import math

import jax
import jax.numpy as jnp
import numpy as np
from jax import lax
from jax.experimental import pallas as pl
from jax.experimental.pallas import tpu as pltpu
from jax.sharding import Mesh
from jax.sharding import PartitionSpec as P

D = 2048
FF = 8192
HD = 64
BW = 128
NS_ITERS = 5
STEP = 10

HIGHEST = lax.Precision.HIGHEST
ROPE_BASE = 130000.0
NORM_EPS = 1e-05
NEG_LARGE = -1e30
MOMENTUM_DECAY = 0.95
MUON_RATE = 0.25
COEFF_A = 3.4445
COEFF_B = -4.775
COEFF_C = 2.0315
BETA_FIRST = 0.9
BETA_SECOND = 0.95
ADAM_RATE = 1.0
ADAM_EPS = 1e-08

F32 = jnp.float32
BF16 = jnp.bfloat16
PLANE = ("m", "r", "tensor")
SWAP = [(0, 1), (1, 0)]
TILE = 256
SCORE_SCALE = 1.0 / math.sqrt(HD)


def rms_norm(values, gain):
    return values * lax.rsqrt(jnp.mean(values * values, axis=-1, keepdims=True) + NORM_EPS) * gain


def rms_norm_back(values, gain, grad):
    scale = lax.rsqrt(jnp.mean(values * values, axis=-1, keepdims=True) + NORM_EPS)
    scaled = gain * grad
    inner = jnp.mean(scaled * values, axis=-1, keepdims=True)
    gain_grad = jnp.sum(grad * values * scale, axis=0)
    return scale * scaled - values * (scale * scale * scale * inner), gain_grad


def rope_tables(place):
    exponent = jnp.arange(HD // 2).astype(F32) * (2.0 / HD)
    inverse = jnp.exp(-exponent * math.log(ROPE_BASE))
    angle = place.astype(F32)[:, None] * inverse[None, :]
    cosine, sine = jnp.cos(angle), jnp.sin(angle)
    heads = 2 * BW // HD
    return (
        jnp.tile(jnp.concatenate([cosine, cosine], axis=1), (1, heads)),
        jnp.tile(jnp.concatenate([-sine, sine], axis=1), (1, heads)),
    )


def dims(lhs, rhs):
    return (((lhs,), (rhs,)), ((), ()))


def mul(a, b):
    return lax.dot_general(a, b, dims(1, 0), preferred_element_type=F32)


def mul_bt(a, b):
    return lax.dot_general(a, b, dims(1, 1), preferred_element_type=F32)


def mul_at(a, b):
    return lax.dot_general(a, b, dims(0, 0), preferred_element_type=F32)


def side_by_side(ref, *index):
    return jnp.concatenate([ref[index + (0,)], ref[index + (1,)]], axis=-1)


def pair_rows(own_ref, other_ref):
    return jnp.concatenate([own_ref[...], other_ref[...]], axis=0)


def swap_halves(values):
    lane = lax.broadcasted_iota(jnp.int32, values.shape, 1)
    span = values.shape[1]
    ahead = pltpu.roll(values, span - HD // 2, 1)
    behind = pltpu.roll(values, HD // 2, 1)
    return jnp.where(lane % HD < HD // 2, ahead, behind)


def head_only(values, head):
    lane = lax.broadcasted_iota(jnp.int32, values.shape, 1)
    return jnp.where((lane >= head * HD) & (lane < (head + 1) * HD), values, jnp.zeros_like(values))


def head_probs(query, key, bias, head):
    scores = mul_bt(head_only(query, head), key) * SCORE_SCALE + bias
    weights = jnp.exp(scores - jnp.max(scores, axis=-1, keepdims=True))
    return weights / jnp.sum(weights, axis=-1, keepdims=True)


def attn_forward_kernel(
    own_ref, other_ref, w_ref, bias_ref, cos_ref, sin_ref, q_ref, k_ref, v_ref, c_ref, mine_ref, theirs_ref
):
    rows = pair_rows(own_ref, other_ref)
    cosine, sine = cos_ref[...], sin_ref[...]
    lin = mul(rows, side_by_side(w_ref, 0))
    query = (lin * cosine + swap_halves(lin) * sine).astype(BF16)
    lin = mul(rows, side_by_side(w_ref, 1))
    key = (lin * cosine + swap_halves(lin) * sine).astype(BF16)
    value = mul(rows, side_by_side(w_ref, 2)).astype(BF16)
    q_ref[...] = query
    k_ref[...] = key
    v_ref[...] = value
    context = jnp.zeros(query.shape, F32)
    for head in range(query.shape[1] // HD):
        probs = head_probs(query, key, bias_ref[...], head)
        context = context + mul(probs.astype(BF16), head_only(value, head))
    context = context.astype(BF16)
    c_ref[...] = context
    half = own_ref.shape[0]
    for tile in range(D // TILE):
        at = pl.ds(tile * TILE, TILE)
        w_out = jnp.concatenate([w_ref[3, 0, at, :], w_ref[3, 1, at, :]], axis=-1)
        mixed = mul_bt(context, w_out)
        mine_ref[:, at] = mixed[:half]
        theirs_ref[:, at] = mixed[half:].astype(BF16)


def attn_backward_kernel(
    own_ref, other_ref, w_ref, bias_ref, cos_ref, sin_ref, q_ref, k_ref, v_ref,
    dq_ref, dk_ref, dv_ref, mine_ref, theirs_ref,
):
    rows = pair_rows(own_ref, other_ref)
    query, key, value = q_ref[...], k_ref[...], v_ref[...]
    d_context = mul(rows, side_by_side(w_ref, 3)).astype(BF16)
    d_query = jnp.zeros(query.shape, F32)
    d_key = jnp.zeros(query.shape, F32)
    d_value = jnp.zeros(query.shape, F32)
    for head in range(query.shape[1] // HD):
        probs = head_probs(query, key, bias_ref[...], head)
        d_here = head_only(d_context, head)
        d_value = d_value + mul_at(probs.astype(BF16), d_here)
        d_probs = mul_bt(d_here, value)
        inner = jnp.sum(probs * d_probs, axis=-1, keepdims=True)
        d_scores = (probs * (d_probs - inner)).astype(BF16)
        d_query = d_query + mul(d_scores, head_only(key, head))
        d_key = d_key + mul_at(d_scores, head_only(query, head))
    cosine, sine = cos_ref[...], sin_ref[...]
    d_query = d_query * SCORE_SCALE
    d_key = d_key * SCORE_SCALE
    d_query = (d_query * cosine - swap_halves(d_query) * sine).astype(BF16)
    d_key = (d_key * cosine - swap_halves(d_key) * sine).astype(BF16)
    d_value = d_value.astype(BF16)
    dq_ref[...] = d_query
    dk_ref[...] = d_key
    dv_ref[...] = d_value
    half = own_ref.shape[0]
    for tile in range(D // TILE):
        at = pl.ds(tile * TILE, TILE)
        total = jnp.zeros((2 * half, TILE), F32)
        for matrix, columns in ((0, d_query), (1, d_key), (2, d_value)):
            w_here = jnp.concatenate([w_ref[matrix, 0, at, :], w_ref[matrix, 1, at, :]], axis=-1)
            total = total + mul_bt(columns, w_here)
        mine_ref[:, at] = total[:half]
        theirs_ref[:, at] = total[half:].astype(BF16)


def mlp_half_kernel(*refs):
    rows, d_rows = refs[:8], refs[8:16]
    w_ref, hid_ref, dgate_ref, dup_ref, grad_ref = refs[16:]
    w_gate, w_up, w_down = (
        jnp.concatenate([w_ref[0, kind], w_ref[1, kind]], axis=-1) for kind in range(3)
    )
    for piece in range(4):
        here = pair_rows(rows[2 * piece], rows[2 * piece + 1])
        gate = mul(here, w_gate)
        up = mul(here, w_up)
        d_hidden = mul(pair_rows(d_rows[2 * piece], d_rows[2 * piece + 1]), w_down)
        sigmoid = 1.0 / (1.0 + jnp.exp(-gate))
        silu = gate * sigmoid
        at = pl.ds(piece * here.shape[0], here.shape[0])
        hid_ref[at, :] = (silu * up).astype(BF16)
        dgate_ref[at, :] = (d_hidden * up * sigmoid * (1.0 + gate * (1.0 - sigmoid))).astype(BF16)
        dup_ref[at, :] = (d_hidden * silu).astype(BF16)
    for tile in range(D // TILE):
        at = pl.ds(tile * TILE, TILE)
        across = jnp.concatenate([ref[:, at] for ref in rows], axis=0)
        d_across = jnp.concatenate([ref[:, at] for ref in d_rows], axis=0)
        for kind, left, right in ((0, across, dgate_ref), (1, across, dup_ref), (2, d_across, hid_ref)):
            grad = mul_at(left, right[...]).astype(BF16)
            for chip in range(2):
                grad_ref[chip, kind, at, :] = grad[:, chip * BW : (chip + 1) * BW]


def all_columns(kind, w_even, w_odd):
    return jnp.concatenate([ref[chip, kind] for ref in (w_even, w_odd) for chip in range(4)], axis=-1)


def both_columns(even, odd):
    return jnp.concatenate([even[...], odd[...]], axis=-1)


def mlp_back_kernel(dgate_even, dgate_odd, dup_even, dup_odd, w_even, w_odd, mine_ref, theirs_ref):
    total = mul_bt(both_columns(dgate_even, dgate_odd), all_columns(0, w_even, w_odd))
    total = total + mul_bt(both_columns(dup_even, dup_odd), all_columns(1, w_even, w_odd))
    half = mine_ref.shape[0]
    mine_ref[...] = total[:half]
    theirs_ref[...] = total[half:].astype(BF16)


def mlp_out_kernel(hid_even, hid_odd, w_even, w_odd, mine_ref, theirs_ref):
    total = mul_bt(both_columns(hid_even, hid_odd), all_columns(0, w_even, w_odd))
    half = mine_ref.shape[1]
    for piece in range(4):
        mine_ref[piece] = total[2 * piece * half : (2 * piece + 1) * half]
        theirs_ref[piece] = total[(2 * piece + 1) * half : 2 * (piece + 1) * half].astype(BF16)


def grads_kernel(sources, *refs):
    first, second = refs[:8], refs[8:16]
    columns = refs[16:-1]
    out_ref = refs[-1]
    row_sets = [jnp.concatenate([ref[...] for ref in part], axis=0) for part in (first, second)]
    for index, source in enumerate(sources):
        stacked = jnp.concatenate([ref[...] for ref in columns[4 * index : 4 * index + 4]], axis=0)
        grad = mul_at(row_sets[source], stacked).astype(BF16)
        for block in range(grad.shape[1] // BW):
            out_ref[index, block] = grad[:, block * BW : (block + 1) * BW]


def split(values):
    high = values.astype(BF16)
    return high, (values - high.astype(F32)).astype(BF16)


def mul_split(a, b):
    return mul(a[0], b[0]) + (mul(a[0], b[1]) + mul(a[1], b[0]))


def muon_kernel(grad_ref, momentum_ref, weight_ref, wg_ref, nm_ref, nw_ref, held, mixers):
    step = pl.program_id(0)
    count = held.shape[0]

    @pl.when(step < count)
    def _():
        grad = grad_ref[...].astype(F32)
        wg_ref[...] = grad
        block = MOMENTUM_DECAY * momentum_ref[...] + grad
        nm_ref[...] = block
        block = block * (1.0 / (jnp.sqrt(jnp.sum(block * block)) + 1e-07))
        held[step] = block
        high, low = split(block)
        cross = mul_at(high, low)
        mixers[step] = mul_at(high, high) + (cross + cross.T)

    @pl.when(step == count - 1)
    def _():
        row = lax.broadcasted_iota(jnp.int32, (BW, BW), 0)
        column = lax.broadcasted_iota(jnp.int32, (BW, BW), 1)
        eye = jnp.where(row == column, COEFF_A, 0.0).astype(F32)
        grams = [mixers[index] for index in range(count)]
        totals = [None] * count
        for turn in range(NS_ITERS):
            for index in range(count):
                pair = split(grams[index])
                mixer = eye + COEFF_B * grams[index] + COEFF_C * mul_split(pair, pair)
                mixed = split(mixer)
                if turn == 0:
                    totals[index] = mixer
                else:
                    totals[index] = mul_split(split(totals[index]), mixed)
                if turn < NS_ITERS - 1:
                    grams[index] = mul_split(split(mul_split(mixed, pair)), mixed)
        for index in range(count):
            mixers[index] = totals[index]

    @pl.when(step >= count)
    def _():
        at = step - count
        ortho = mul_split(split(held[at]), split(mixers[at]))
        nw_ref[...] = weight_ref[...].astype(F32) - (MUON_RATE * math.sqrt(D / BW)) * ortho


def deferred(kernel, inputs, unread):
    return lambda *refs: kernel(*refs[:inputs], *refs[inputs + unread :])


def unread_specs(after):
    return [pl.BlockSpec(memory_space=pl.ANY) for _ in after]


def cost(flops, accessed):
    return pl.CostEstimate(flops=flops // 6, bytes_accessed=accessed // 6, transcendentals=0)


def sort_kernel(plane_ref, *refs):
    moved, attn_ref, mlp_ref = refs[:4], refs[4], refs[5]
    for here in range(4):

        @pl.when(plane_ref[0] == here)
        def _():
            attn_ref[...] = moved[here][...]
            for kind in (1, 2, 3):
                mlp_ref[kind - 1] = moved[(here - kind) % 4][...]


def sort_kinds(plane, moved, after):
    shape = moved[0].shape
    return pl.pallas_call(
        deferred(sort_kernel, 5, len(after)),
        out_shape=(shaped(shape, BF16), shaped((3,) + shape, BF16)),
        in_specs=[pl.BlockSpec(memory_space=pltpu.SMEM)] + whole_specs(moved) + unread_specs(after),
        out_specs=tuple(whole_specs(range(2))),
        compiler_params=params(32),
        cost_estimate=cost(0, 4_000_000),
        name="sort_kinds",
    )(plane.astype(jnp.int32).reshape(1), *moved, *after)


def params(mebibytes):
    return pltpu.CompilerParams(vmem_limit_bytes=mebibytes * 1024 * 1024)


def whole_specs(arrays):
    return [pl.BlockSpec(memory_space=pltpu.VMEM) for _ in arrays]


def shaped(shape, dtype):
    return jax.ShapeDtypeStruct(shape, dtype)


def attn_forward(own, other, w_attn, bias, cosine, sine, after=()):
    half = own.shape[1]
    rows = pl.BlockSpec((None, half, D), lambda i: (0, 0, 0))
    span = w_attn.shape[1] * w_attn.shape[3]
    square = shaped((2 * half, span), BF16)
    args = (own, other, w_attn, bias, cosine, sine)
    return pl.pallas_call(
        deferred(attn_forward_kernel, len(args), len(after)),
        grid=(1,),
        out_shape=(square,) * 4 + (shaped((half, D), F32), shaped((half, D), BF16)),
        in_specs=[rows, rows] + whole_specs(args[2:]) + unread_specs(after),
        out_specs=tuple(whole_specs(range(6))),
        compiler_params=params(40),
        cost_estimate=cost(1_300_000_000, 9_000_000),
        name="attn_forward",
    )(*args, *after)


def attn_backward(own, other, w_attn, bias, cosine, sine, query, key, value):
    half = own.shape[0]
    square = shaped(query.shape, BF16)
    args = (own, other, w_attn, bias, cosine, sine, query, key, value)
    return pl.pallas_call(
        attn_backward_kernel,
        out_shape=(square,) * 3 + (shaped((half, D), F32), shaped((half, D), BF16)),
        in_specs=whole_specs(args),
        out_specs=tuple(whole_specs(range(5))),
        compiler_params=params(40),
        cost_estimate=cost(1_600_000_000, 9_000_000),
        name="attn_backward",
    )(*args)


def mlp_half(rows, pairs, w_half):
    half = rows[0].shape[0]
    columns = shaped((8 * half, 4 * BW), BF16)
    blocks = pl.BlockSpec((2, 3, D, BW), lambda j: (j, 0, 0, 0))
    return pl.pallas_call(
        mlp_half_kernel,
        grid=(2,),
        out_shape=(columns,) * 3 + (shaped(w_half.shape, BF16),),
        in_specs=[pl.BlockSpec((half, D), lambda j: (0, 0)) for _ in range(8)]
        + [pl.BlockSpec((None, half, D), lambda j: (1, 0, 0)) for _ in range(8)]
        + [blocks],
        out_specs=(pl.BlockSpec((8 * half, 2 * BW), lambda j: (0, j)),) * 3 + (blocks,),
        compiler_params=params(58),
        cost_estimate=cost(13_000_000_000, 20_000_000),
        name="mlp_half",
    )(*rows, *pairs, w_half)


def mlp_back(piece, halves, w_even, w_odd):
    rows = halves[0][0].shape[0] // 4
    wide = 2 * TILE
    args = [half[index] for index in (1, 2) for half in halves]
    tile = pl.BlockSpec((rows // 2, wide), lambda i: (0, i))
    weight = pl.BlockSpec((4, 2, wide, BW), lambda i: (0, 0, i, 0))
    return pl.pallas_call(
        mlp_back_kernel,
        grid=(D // wide,),
        out_shape=(shaped((rows // 2, D), F32), shaped((rows // 2, D), BF16)),
        in_specs=[pl.BlockSpec((rows, 4 * BW), lambda i: (piece, 0)) for _ in args] + [weight] * 2,
        out_specs=(tile,) * 2,
        compiler_params=params(58),
        cost_estimate=cost(2_200_000_000, 11_000_000),
        name="mlp_back",
    )(*args, w_even, w_odd)


def mlp_out(halves, w_even, w_odd, after):
    count = halves[0][0].shape[0]
    args = [half[0] for half in halves]
    wide = 2 * TILE
    tile = pl.BlockSpec((4, count // 8, wide), lambda i: (0, 0, i))
    weight = pl.BlockSpec((4, 1, wide, BW), lambda i: (0, 2, i, 0))
    return pl.pallas_call(
        deferred(mlp_out_kernel, 4, len(after)),
        grid=(D // wide,),
        out_shape=(shaped((4, count // 8, D), F32), shaped((4, count // 8, D), BF16)),
        in_specs=[pl.BlockSpec((count, 4 * BW), lambda i: (0, 0)) for _ in args] + [weight] * 2 + unread_specs(after),
        out_specs=(tile,) * 2,
        compiler_params=params(58),
        cost_estimate=cost(4_300_000_000, 18_000_000),
        name="mlp_out",
    )(*args, w_even, w_odd, *after)


def weight_products(pairs, rows, column_sets, sources, name, after=()):
    half = rows[0].shape[0]
    span = column_sets[0][0].shape[1]
    pair_spec = pl.BlockSpec((None, half, TILE), lambda i: (0, 0, i))
    row_spec = pl.BlockSpec((half, TILE), lambda i: (0, i))
    column_spec = pl.BlockSpec((2 * half, span), lambda i: (0, 0))
    flat = [piece for pieces in column_sets for piece in pieces]
    return pl.pallas_call(
        deferred(functools.partial(grads_kernel, sources), 16 + len(flat), len(after)),
        grid=(D // TILE,),
        out_shape=shaped((len(sources), span // BW, D, BW), BF16),
        in_specs=[pair_spec] * 8 + [row_spec] * 8 + [column_spec] * len(flat) + unread_specs(after),
        out_specs=pl.BlockSpec((len(sources), span // BW, TILE, BW), lambda i: (0, 0, i, 0)),
        compiler_params=params(40),
        cost_estimate=cost(2 * 8 * half * D * span * len(sources), 20_000_000),
        name=name,
    )(*pairs, *rows, *flat, *after)


def muon(grads, momentum, weights, offset, stride, begun=(), after=()):
    count = grads.shape[0]
    now = lambda i: jnp.minimum(i, count - 1)
    then = lambda i: jnp.maximum(i - count, 0)
    block = (None, D, BW)
    compact = pl.BlockSpec(block, lambda i: (now(i), 0, 0))
    early = pl.BlockSpec(block, lambda i: (stride * now(i) + offset, 0, 0))
    late = pl.BlockSpec(block, lambda i: (stride * then(i) + offset, 0, 0))
    return pl.pallas_call(
        deferred(muon_kernel, 3, len(begun) + len(after)),
        grid=(2 * count,),
        out_shape=(shaped(momentum.shape, F32),) * 3,
        in_specs=[compact, early, late] + unread_specs(begun) + unread_specs(after),
        out_specs=(early, early, late),
        input_output_aliases={3 + index: index for index in range(len(begun))},
        scratch_shapes=[pltpu.VMEM((count, D, BW), F32), pltpu.VMEM((count, BW, BW), F32)],
        compiler_params=params(40),
        cost_estimate=cost(1_000_000_000 * count, 5_500_000 * count),
        name="muon",
    )(grads, momentum, weights, *begun, *after)


def mirror(step):
    return [(place, place ^ step) for place in range(4)]


def ring(value, step=1):
    return lax.ppermute(value, "z", [(place, (place + step) % 4) for place in range(4)])


def swap(value):
    return lax.ppermute(value, "tensor", SWAP)


def nothing(value):
    first = value[(0,) * value.ndim].astype(F32)
    return (first * 0.0).astype(jnp.int32)


def hold(value, *others):
    zero = sum((nothing(other) for other in others), jnp.int32(0))
    return value + zero.astype(value.dtype)


def gather_rows(rows):
    mine = [rows]
    for _ in range(3):
        mine.append(ring(mine[-1]))
    return mine, [swap(part) for part in mine]


class Scatter:
    def __init__(self):
        self.moving = self.result = None
        self.payloads = []

    def add(self, step, mine, theirs):
        total = mine + swap(theirs).astype(F32)
        if self.moving is not None:
            total = total + self.moving.astype(F32)
        if step:
            self.payloads.append(total.astype(BF16))
            self.moving = ring(self.payloads[-1])
        else:
            self.result = total


def everywhere(value):
    value = value + swap(value)
    for axis in ("m", "z"):
        one, two, three = (lax.ppermute(value, axis, mirror(step)) for step in (1, 2, 3))
        value = (value + one) + (two + three)
    if lax.axis_size("r") > 1:
        value = lax.psum(value, "r")
    return value


def join(parts):
    if parts.shape[0] == 4:
        return parts
    width = parts.shape[3]
    parts = parts.reshape(4, 2, -1, D, width).transpose(0, 1, 3, 2, 4)
    return parts.reshape(4, 2, D, BW)


def unjoin(grads, width):
    if width == BW:
        return grads
    grads = grads.reshape(4, 2, D, -1, width).transpose(0, 1, 3, 2, 4)
    return grads.reshape(-1, 1, D, width)


def gather_plane(parts):
    return lax.all_gather(parts, ("m", "r"), axis=0, tiled=False)


def gather_part_direct(part, index, result):
    chip = lax.axis_index("m")
    result = lax.dynamic_update_slice(result, part[None, None], (chip, index, 0, 0))
    for step in (1, 2, 3):
        got = lax.ppermute(part, "m", mirror(step))
        result = lax.dynamic_update_slice(result, got[None, None], (chip ^ step, index, 0, 0))
    return result


def scatter_plane(grads):
    share = lax.psum_scatter(
        grads.reshape(grads.shape[0], -1, grads.shape[3]), ("m", "r"), scatter_dimension=0, tiled=False
    )
    return share.reshape(grads.shape[1:])


def scatter_plane_direct(grads, late):
    chip = lax.axis_index("m")
    shares = []
    for part in range(2):
        at = chip + sum((nothing(other) for other in shares + [late] * part), jnp.int32(0))

        def share_for(step):
            return lax.dynamic_slice(grads, (at ^ step, part, 0, 0), (1, 1) + grads.shape[2:])[0, 0]

        total = share_for(0).astype(F32)
        arrived = []
        for step in (1, 2, 3):
            arrived.append(lax.ppermute(share_for(step), "m", mirror(step)))
            total = total + arrived[-1].astype(F32)
        shares.append(total.astype(BF16))
    return shares


def interleave(mine, other):
    return [rows for pair in zip(mine, other) for rows in pair]


def local(tokens, segments, weights, momentum, gains, gain_first, gain_second, cotangent):
    plane = lax.axis_index("z")
    core = lax.axis_index("tensor")
    block_count = weights.shape[0]

    if block_count == 8:
        shards = weights.reshape(4, 2, D, BW)
    else:
        width = block_count * BW // 4
        shards = weights.reshape(block_count, D, -1, width).transpose(0, 2, 1, 3).reshape(4, 1, D, width)
    parts, width = shards.shape[1], shards.shape[3]

    def shard(shift, part, *others):
        at = sum((nothing(other) for other in others), plane + shift)
        return lax.dynamic_slice(shards, (at % 4, part, 0, 0), (1, 1, D, width))[0, 0]

    rows_in = tokens.astype(F32)
    segment_own = segments.astype(F32)
    segment_parts = [segment_own] + [ring(segment_own, shift) for shift in (1, 2, 3)]
    segment_rows = jnp.concatenate(segment_parts, axis=0)
    def move(part, *others):
        return [shard(0, part)] + [ring(shard(shift, part, *others), shift) for shift in (1, 2, 3)]

    moved_even = move(0)

    def kind_part(source):
        return lax.select_n(plane, *(moved_even[(here - source) % 4] for here in range(4)))

    row_pair = lambda *others: jnp.stack([hold(rms_norm(rows_in, gains[0]), *others).astype(BF16), cotangent])
    if parts == 2:
        attn_even, mlp_even = sort_kinds(plane, moved_even, [segment_rows])
        w_attn = gather_part_direct(attn_even, 0, jnp.zeros((4, 2, D, BW), BF16))
        attn_odd, mlp_odd = sort_kinds(plane, move(1, attn_even), [w_attn])
        w_attn = gather_part_direct(attn_odd, 1, w_attn)
        w_mlp = [gather_plane(mlp_even), gather_plane(mlp_odd)]
        begun = [mlp_odd]
        first_mine, first_other = gather_rows(row_pair(attn_odd))
    else:
        w_attn = join(gather_plane(kind_part(0)[None]))
        w_mlp = gather_plane(jnp.stack([kind_part(kind) for kind in (1, 2, 3)]))
        w_mlp = jnp.stack([join(w_mlp[:, kind : kind + 1]) for kind in range(3)], axis=1)
        w_mlp = [w_mlp[:, :, 0], w_mlp[:, :, 1]]
        begun = []
        first_mine, first_other = gather_rows(row_pair())
    first_rows = interleave(first_mine, first_other)

    length = segment_rows.shape[1]
    half = length // 2
    place = jnp.arange(length)
    place = jnp.where(core == 0, place, (place + half) % length)
    segment_rows = jnp.where(core == 0, segment_rows, jnp.roll(segment_rows, half, axis=1))
    allowed = (place[None, None, :] <= place[None, :, None]) & (
        segment_rows[:, None, :] == segment_rows[:, :, None]
    )
    bias = jnp.where(allowed, 0.0, NEG_LARGE).astype(F32)
    cosine, sine = rope_tables(place)

    query, key, value, context = ([None] * 4 for _ in range(4))
    mixed = Scatter()
    for s in (1, 2, 3, 0):
        query[s], key[s], value[s], context[s], *both = attn_forward(
            first_mine[s], first_other[s], w_attn, bias[s], cosine, sine, mixed.payloads[:1] if s == 3 else begun if s == 1 else ()
        )
        mixed.add(s, *both)
    middle = rows_in + mixed.result
    two_mine, two_other = gather_rows(rms_norm(middle, gains[1]).astype(BF16))

    two_rows = interleave(two_mine, two_other)
    *even_half, grads_even = mlp_half(two_rows, first_rows, w_mlp[0])
    *odd_half, grads_odd = mlp_half(two_rows, first_rows, w_mlp[1])
    if parts == 2:
        mlp_share = [scatter_plane(grads_even), scatter_plane(grads_odd)]
    else:
        mlp_grads = jnp.stack([grads_even, grads_odd], axis=2)
        mlp_share = [
            jnp.concatenate([scatter_plane(unjoin(mlp_grads[:, kind], width)) for kind in range(3)])
        ]
    d_normed = Scatter()
    for s in (1, 2, 3, 0):
        d_normed.add(s, *mlp_back(s, (even_half, odd_half), *w_mlp))
    outward = mlp_out((even_half, odd_half), *w_mlp, d_normed.payloads[-1:])
    d_normed_two = hold(d_normed.result, outward[1])

    d_output = cotangent.astype(F32)
    d_middle_norm, d_gain_two = rms_norm_back(middle, gains[1], d_normed_two)
    d_middle = d_output + d_middle_norm
    e_mine, e_other = gather_rows(d_middle.astype(BF16))
    d_query, d_key, d_value, d_one = ([None] * 4 for _ in range(4))
    for s in range(4):
        d_query[s], d_key[s], d_value[s], *both = attn_backward(
            e_mine[s], e_other[s], w_attn, bias[s], cosine, sine, query[s], key[s], value[s]
        )
        d_one[s] = both
    attn_grads = weight_products(
        first_rows,
        interleave(e_mine, e_other),
        (d_query, d_key, d_value, context),
        (0, 0, 0, 1),
        "attn_products",
        mlp_share[:1],
    )
    if parts == 2:
        attn_share = scatter_plane_direct(attn_grads, mlp_share[1])
    else:
        attn_share = scatter_plane(unjoin(attn_grads, width))

    last = Scatter()
    for s in (1, 2, 3, 0):
        mine, theirs = (jnp.stack([a, b[s]]) for a, b in zip(d_one[s], outward))
        if s == 2:
            mine = hold(mine, d_query[0])
        last.add(s, mine, theirs)
    d_normed_one, outward_sum = last.result
    d_rows_norm, d_gain_one = rms_norm_back(rows_in, gains[0], d_normed_one)
    input_grad = d_middle + d_rows_norm
    output = (middle + outward_sum).astype(BF16)
    gain_grads = everywhere(jnp.stack([d_gain_one, d_gain_two]))

    results = ()
    for part in range(parts):
        shares = jnp.concatenate([attn_share[part][None], mlp_share[part]])

        def share_of(shift):
            return lax.dynamic_index_in_dim(shares, (plane + shift) % 4, 0, keepdims=False)

        back = [share_of(0)] + [ring(share_of(shift), shift) for shift in (1, 2, 3)]
        here = plane + nothing(results[1]) if part else plane
        summed = jnp.stack(
            [lax.select_n(here, *(back[(z - source) % 4] for z in range(4))) for source in range(4)]
        )
        if parts == 1:
            summed = summed.reshape(block_count, -1, D, width).transpose(0, 2, 1, 3).reshape(block_count, D, BW)
        results = muon(summed, momentum, weights, part, parts, results)
    weight_grads, new_momentum, new_weights = results

    new_gain_first = BETA_FIRST * gain_first + (1.0 - BETA_FIRST) * gain_grads
    new_gain_second = BETA_SECOND * gain_second + (1.0 - BETA_SECOND) * gain_grads * gain_grads
    first_hat = new_gain_first / (1.0 - BETA_FIRST**STEP)
    second_hat = new_gain_second / (1.0 - BETA_SECOND**STEP)
    new_gains = gains - ADAM_RATE * first_hat / (jnp.sqrt(second_hat) + ADAM_EPS)
    return (
        output,
        input_grad,
        weight_grads,
        new_momentum,
        new_weights,
        new_gain_first,
        new_gain_second,
        new_gains,
    )


def solution(mesh):
    count = mesh.shape["dp"]
    fine = Mesh(
        np.asarray(mesh.devices).reshape(4, 4, count // 16, mesh.shape["tensor"]),
        ("z",) + PLANE,
    )
    every = ("z",) + PLANE
    in_specs = (
        P(every, None),
        P(every[:3], None),
        P(every, None, None),
        P(every, None, None),
        P(),
        P(),
        P(),
        P(every, None),
    )
    out_specs = (
        P(every, None),
        P(every, None),
        P(every, None, None),
        P(every, None, None),
        P(every, None, None),
        P(),
        P(),
        P(),
    )
    return jax.shard_map(local, mesh=fine, in_specs=in_specs, out_specs=out_specs, check_vma=False)
```

```python
import functools
import math

import jax
import jax.numpy as jnp
import numpy as np
from jax import lax
from jax.experimental import pallas as pl
from jax.experimental.pallas import tpu as pltpu
from jax.sharding import Mesh
from jax.sharding import PartitionSpec as P

D = 2048
FF = 8192
HD = 64
BW = 128
NS_ITERS = 5
STEP = 10

HIGHEST = lax.Precision.HIGHEST
ROPE_BASE = 130000.0
NORM_EPS = 1e-05
NEG_LARGE = -1e30
MOMENTUM_DECAY = 0.95
MUON_RATE = 0.25
COEFF_A = 3.4445
COEFF_B = -4.775
COEFF_C = 2.0315
BETA_FIRST = 0.9
BETA_SECOND = 0.95
ADAM_RATE = 1.0
ADAM_EPS = 1e-08

F32 = jnp.float32
BF16 = jnp.bfloat16
PLANE = ("m", "r", "tensor")
SWAP = [(0, 1), (1, 0)]
TILE = 256
SCORE_SCALE = 1.0 / math.sqrt(HD)


def rms_norm(values, gain):
    return values * lax.rsqrt(jnp.mean(values * values, axis=-1, keepdims=True) + NORM_EPS) * gain


def rms_norm_back(values, gain, grad):
    scale = lax.rsqrt(jnp.mean(values * values, axis=-1, keepdims=True) + NORM_EPS)
    scaled = gain * grad
    inner = jnp.mean(scaled * values, axis=-1, keepdims=True)
    gain_grad = jnp.sum(grad * values * scale, axis=0)
    return scale * scaled - values * (scale * scale * scale * inner), gain_grad


def rope_tables(place):
    exponent = jnp.arange(HD // 2).astype(F32) * (2.0 / HD)
    inverse = jnp.exp(-exponent * math.log(ROPE_BASE))
    angle = place.astype(F32)[:, None] * inverse[None, :]
    cosine, sine = jnp.cos(angle), jnp.sin(angle)
    heads = 2 * BW // HD
    return (
        jnp.tile(jnp.concatenate([cosine, cosine], axis=1), (1, heads)),
        jnp.tile(jnp.concatenate([-sine, sine], axis=1), (1, heads)),
    )


def dims(lhs, rhs):
    return (((lhs,), (rhs,)), ((), ()))


def mul(a, b):
    return lax.dot_general(a, b, dims(1, 0), preferred_element_type=F32)


def mul_bt(a, b):
    return lax.dot_general(a, b, dims(1, 1), preferred_element_type=F32)


def mul_at(a, b):
    return lax.dot_general(a, b, dims(0, 0), preferred_element_type=F32)


def side_by_side(ref, *index):
    return jnp.concatenate([ref[index + (0,)], ref[index + (1,)]], axis=-1)


def pair_rows(own_ref, other_ref):
    return jnp.concatenate([own_ref[...], other_ref[...]], axis=0)


def swap_halves(values):
    lane = lax.broadcasted_iota(jnp.int32, values.shape, 1)
    span = values.shape[1]
    ahead = pltpu.roll(values, span - HD // 2, 1)
    behind = pltpu.roll(values, HD // 2, 1)
    return jnp.where(lane % HD < HD // 2, ahead, behind)


def head_only(values, head):
    lane = lax.broadcasted_iota(jnp.int32, values.shape, 1)
    return jnp.where((lane >= head * HD) & (lane < (head + 1) * HD), values, jnp.zeros_like(values))


def head_probs(query, key, bias, head):
    scores = mul_bt(head_only(query, head), key) * SCORE_SCALE + bias
    weights = jnp.exp(scores - jnp.max(scores, axis=-1, keepdims=True))
    return weights / jnp.sum(weights, axis=-1, keepdims=True)


def attn_forward_kernel(
    own_ref, other_ref, w_ref, bias_ref, cos_ref, sin_ref, q_ref, k_ref, v_ref, c_ref, mine_ref, theirs_ref
):
    rows = pair_rows(own_ref, other_ref)
    cosine, sine = cos_ref[...], sin_ref[...]
    lin = mul(rows, side_by_side(w_ref, 0))
    query = (lin * cosine + swap_halves(lin) * sine).astype(BF16)
    lin = mul(rows, side_by_side(w_ref, 1))
    key = (lin * cosine + swap_halves(lin) * sine).astype(BF16)
    value = mul(rows, side_by_side(w_ref, 2)).astype(BF16)
    q_ref[...] = query
    k_ref[...] = key
    v_ref[...] = value
    context = jnp.zeros(query.shape, F32)
    for head in range(query.shape[1] // HD):
        probs = head_probs(query, key, bias_ref[...], head)
        context = context + mul(probs.astype(BF16), head_only(value, head))
    context = context.astype(BF16)
    c_ref[...] = context
    half = own_ref.shape[0]
    for tile in range(D // TILE):
        at = pl.ds(tile * TILE, TILE)
        w_out = jnp.concatenate([w_ref[3, 0, at, :], w_ref[3, 1, at, :]], axis=-1)
        mixed = mul_bt(context, w_out)
        mine_ref[:, at] = mixed[:half]
        theirs_ref[:, at] = mixed[half:].astype(BF16)


def attn_backward_kernel(
    own_ref, other_ref, w_ref, bias_ref, cos_ref, sin_ref, q_ref, k_ref, v_ref,
    dq_ref, dk_ref, dv_ref, mine_ref, theirs_ref,
):
    rows = pair_rows(own_ref, other_ref)
    query, key, value = q_ref[...], k_ref[...], v_ref[...]
    d_context = mul(rows, side_by_side(w_ref, 3)).astype(BF16)
    d_query = jnp.zeros(query.shape, F32)
    d_key = jnp.zeros(query.shape, F32)
    d_value = jnp.zeros(query.shape, F32)
    for head in range(query.shape[1] // HD):
        probs = head_probs(query, key, bias_ref[...], head)
        d_here = head_only(d_context, head)
        d_value = d_value + mul_at(probs.astype(BF16), d_here)
        d_probs = mul_bt(d_here, value)
        inner = jnp.sum(probs * d_probs, axis=-1, keepdims=True)
        d_scores = (probs * (d_probs - inner)).astype(BF16)
        d_query = d_query + mul(d_scores, head_only(key, head))
        d_key = d_key + mul_at(d_scores, head_only(query, head))
    cosine, sine = cos_ref[...], sin_ref[...]
    d_query = d_query * SCORE_SCALE
    d_key = d_key * SCORE_SCALE
    d_query = (d_query * cosine - swap_halves(d_query) * sine).astype(BF16)
    d_key = (d_key * cosine - swap_halves(d_key) * sine).astype(BF16)
    d_value = d_value.astype(BF16)
    dq_ref[...] = d_query
    dk_ref[...] = d_key
    dv_ref[...] = d_value
    half = own_ref.shape[0]
    for tile in range(D // TILE):
        at = pl.ds(tile * TILE, TILE)
        total = jnp.zeros((2 * half, TILE), F32)
        for matrix, columns in ((0, d_query), (1, d_key), (2, d_value)):
            w_here = jnp.concatenate([w_ref[matrix, 0, at, :], w_ref[matrix, 1, at, :]], axis=-1)
            total = total + mul_bt(columns, w_here)
        mine_ref[:, at] = total[:half]
        theirs_ref[:, at] = total[half:].astype(BF16)


def mlp_half_kernel(*refs):
    rows, d_rows = refs[:8], refs[8:16]
    w_ref, hid_ref, dgate_ref, dup_ref, grad_ref = refs[16:]
    w_gate, w_up, w_down = (
        jnp.concatenate([w_ref[0, kind], w_ref[1, kind]], axis=-1) for kind in range(3)
    )
    for piece in range(4):
        here = pair_rows(rows[2 * piece], rows[2 * piece + 1])
        gate = mul(here, w_gate)
        up = mul(here, w_up)
        d_hidden = mul(pair_rows(d_rows[2 * piece], d_rows[2 * piece + 1]), w_down)
        sigmoid = 1.0 / (1.0 + jnp.exp(-gate))
        silu = gate * sigmoid
        at = pl.ds(piece * here.shape[0], here.shape[0])
        hid_ref[at, :] = (silu * up).astype(BF16)
        dgate_ref[at, :] = (d_hidden * up * sigmoid * (1.0 + gate * (1.0 - sigmoid))).astype(BF16)
        dup_ref[at, :] = (d_hidden * silu).astype(BF16)
    for tile in range(D // TILE):
        at = pl.ds(tile * TILE, TILE)
        across = jnp.concatenate([ref[:, at] for ref in rows], axis=0)
        d_across = jnp.concatenate([ref[:, at] for ref in d_rows], axis=0)
        for kind, left, right in ((0, across, dgate_ref), (1, across, dup_ref), (2, d_across, hid_ref)):
            grad = mul_at(left, right[...]).astype(BF16)
            for chip in range(2):
                grad_ref[chip, kind, at, :] = grad[:, chip * BW : (chip + 1) * BW]


def all_columns(kind, w_even, w_odd):
    return jnp.concatenate([ref[chip, kind] for ref in (w_even, w_odd) for chip in range(4)], axis=-1)


def both_columns(even, odd):
    return jnp.concatenate([even[...], odd[...]], axis=-1)


def mlp_back_kernel(dgate_even, dgate_odd, dup_even, dup_odd, w_even, w_odd, mine_ref, theirs_ref):
    total = mul_bt(both_columns(dgate_even, dgate_odd), all_columns(0, w_even, w_odd))
    total = total + mul_bt(both_columns(dup_even, dup_odd), all_columns(1, w_even, w_odd))
    half = mine_ref.shape[0]
    mine_ref[...] = total[:half]
    theirs_ref[...] = total[half:].astype(BF16)


def mlp_out_kernel(hid_even, hid_odd, w_even, w_odd, mine_ref, theirs_ref):
    total = mul_bt(both_columns(hid_even, hid_odd), all_columns(0, w_even, w_odd))
    half = mine_ref.shape[1]
    for piece in range(4):
        mine_ref[piece] = total[2 * piece * half : (2 * piece + 1) * half]
        theirs_ref[piece] = total[(2 * piece + 1) * half : 2 * (piece + 1) * half].astype(BF16)


def grads_kernel(sources, *refs):
    first, second = refs[:8], refs[8:16]
    columns = refs[16:-1]
    out_ref = refs[-1]
    row_sets = [jnp.concatenate([ref[...] for ref in part], axis=0) for part in (first, second)]
    for index, source in enumerate(sources):
        stacked = jnp.concatenate([ref[...] for ref in columns[4 * index : 4 * index + 4]], axis=0)
        grad = mul_at(row_sets[source], stacked).astype(BF16)
        for block in range(grad.shape[1] // BW):
            out_ref[index, block] = grad[:, block * BW : (block + 1) * BW]


def split(values):
    high = values.astype(BF16)
    return high, (values - high.astype(F32)).astype(BF16)


def mul_split(a, b):
    return mul(a[0], b[0]) + (mul(a[0], b[1]) + mul(a[1], b[0]))


def muon_kernel(grad_ref, momentum_ref, weight_ref, wg_ref, nm_ref, nw_ref, held, mixers):
    step = pl.program_id(0)
    count = held.shape[0]

    @pl.when(step < count)
    def _():
        grad = grad_ref[...].astype(F32)
        wg_ref[...] = grad
        block = MOMENTUM_DECAY * momentum_ref[...] + grad
        nm_ref[...] = block
        block = block * (1.0 / (jnp.sqrt(jnp.sum(block * block)) + 1e-07))
        held[step] = block
        high, low = split(block)
        cross = mul_at(high, low)
        mixers[step] = mul_at(high, high) + (cross + cross.T)

    @pl.when(step == count - 1)
    def _():
        row = lax.broadcasted_iota(jnp.int32, (BW, BW), 0)
        column = lax.broadcasted_iota(jnp.int32, (BW, BW), 1)
        eye = jnp.where(row == column, COEFF_A, 0.0).astype(F32)
        grams = [mixers[index] for index in range(count)]
        totals = [None] * count
        for turn in range(NS_ITERS):
            for index in range(count):
                pair = split(grams[index])
                mixer = eye + COEFF_B * grams[index] + COEFF_C * mul_split(pair, pair)
                mixed = split(mixer)
                if turn == 0:
                    totals[index] = mixer
                else:
                    totals[index] = mul_split(split(totals[index]), mixed)
                if turn < NS_ITERS - 1:
                    grams[index] = mul_split(split(mul_split(mixed, pair)), mixed)
        for index in range(count):
            mixers[index] = totals[index]

    @pl.when(step >= count)
    def _():
        at = step - count
        ortho = mul_split(split(held[at]), split(mixers[at]))
        nw_ref[...] = weight_ref[...].astype(F32) - (MUON_RATE * math.sqrt(D / BW)) * ortho


def deferred(kernel, inputs, unread):
    return lambda *refs: kernel(*refs[:inputs], *refs[inputs + unread :])


def unread_specs(after):
    return [pl.BlockSpec(memory_space=pl.ANY) for _ in after]


def cost(flops, accessed):
    return pl.CostEstimate(flops=flops // 6, bytes_accessed=accessed // 6, transcendentals=0)


def sort_kernel(plane_ref, *refs):
    moved, attn_ref, mlp_ref = refs[:4], refs[4], refs[5]
    for here in range(4):

        @pl.when(plane_ref[0] == here)
        def _():
            attn_ref[...] = moved[here][...]
            for kind in (1, 2, 3):
                mlp_ref[kind - 1] = moved[(here - kind) % 4][...]


def sort_kinds(plane, moved, after):
    shape = moved[0].shape
    return pl.pallas_call(
        deferred(sort_kernel, 5, len(after)),
        out_shape=(shaped(shape, BF16), shaped((3,) + shape, BF16)),
        in_specs=[pl.BlockSpec(memory_space=pltpu.SMEM)] + whole_specs(moved) + unread_specs(after),
        out_specs=tuple(whole_specs(range(2))),
        compiler_params=params(32),
        cost_estimate=cost(0, 4_000_000),
        name="sort_kinds",
    )(plane.astype(jnp.int32).reshape(1), *moved, *after)


def params(mebibytes):
    return pltpu.CompilerParams(vmem_limit_bytes=mebibytes * 1024 * 1024)


def whole_specs(arrays):
    return [pl.BlockSpec(memory_space=pltpu.VMEM) for _ in arrays]


def shaped(shape, dtype):
    return jax.ShapeDtypeStruct(shape, dtype)


def attn_forward(own, other, w_attn, bias, cosine, sine, after=()):
    half = own.shape[1]
    rows = pl.BlockSpec((None, half, D), lambda i: (0, 0, 0))
    span = w_attn.shape[1] * w_attn.shape[3]
    square = shaped((2 * half, span), BF16)
    args = (own, other, w_attn, bias, cosine, sine)
    return pl.pallas_call(
        deferred(attn_forward_kernel, len(args), len(after)),
        grid=(1,),
        out_shape=(square,) * 4 + (shaped((half, D), F32), shaped((half, D), BF16)),
        in_specs=[rows, rows] + whole_specs(args[2:]) + unread_specs(after),
        out_specs=tuple(whole_specs(range(6))),
        compiler_params=params(40),
        cost_estimate=cost(1_300_000_000, 9_000_000),
        name="attn_forward",
    )(*args, *after)


def attn_backward(own, other, w_attn, bias, cosine, sine, query, key, value):
    half = own.shape[0]
    square = shaped(query.shape, BF16)
    args = (own, other, w_attn, bias, cosine, sine, query, key, value)
    return pl.pallas_call(
        attn_backward_kernel,
        out_shape=(square,) * 3 + (shaped((half, D), F32), shaped((half, D), BF16)),
        in_specs=whole_specs(args),
        out_specs=tuple(whole_specs(range(5))),
        compiler_params=params(40),
        cost_estimate=cost(1_600_000_000, 9_000_000),
        name="attn_backward",
    )(*args)


def mlp_half(rows, pairs, w_half):
    half = rows[0].shape[0]
    columns = shaped((8 * half, 4 * BW), BF16)
    blocks = pl.BlockSpec((2, 3, D, BW), lambda j: (j, 0, 0, 0))
    return pl.pallas_call(
        mlp_half_kernel,
        grid=(2,),
        out_shape=(columns,) * 3 + (shaped(w_half.shape, BF16),),
        in_specs=[pl.BlockSpec((half, D), lambda j: (0, 0)) for _ in range(8)]
        + [pl.BlockSpec((None, half, D), lambda j: (1, 0, 0)) for _ in range(8)]
        + [blocks],
        out_specs=(pl.BlockSpec((8 * half, 2 * BW), lambda j: (0, j)),) * 3 + (blocks,),
        compiler_params=params(58),
        cost_estimate=cost(13_000_000_000, 20_000_000),
        name="mlp_half",
    )(*rows, *pairs, w_half)


def mlp_back(piece, halves, w_even, w_odd):
    rows = halves[0][0].shape[0] // 4
    wide = 2 * TILE
    args = [half[index] for index in (1, 2) for half in halves]
    tile = pl.BlockSpec((rows // 2, wide), lambda i: (0, i))
    weight = pl.BlockSpec((4, 2, wide, BW), lambda i: (0, 0, i, 0))
    return pl.pallas_call(
        mlp_back_kernel,
        grid=(D // wide,),
        out_shape=(shaped((rows // 2, D), F32), shaped((rows // 2, D), BF16)),
        in_specs=[pl.BlockSpec((rows, 4 * BW), lambda i: (piece, 0)) for _ in args] + [weight] * 2,
        out_specs=(tile,) * 2,
        compiler_params=params(58),
        cost_estimate=cost(2_200_000_000, 11_000_000),
        name="mlp_back",
    )(*args, w_even, w_odd)


def mlp_out(halves, w_even, w_odd, after):
    count = halves[0][0].shape[0]
    args = [half[0] for half in halves]
    wide = 2 * TILE
    tile = pl.BlockSpec((4, count // 8, wide), lambda i: (0, 0, i))
    weight = pl.BlockSpec((4, 1, wide, BW), lambda i: (0, 2, i, 0))
    return pl.pallas_call(
        deferred(mlp_out_kernel, 4, len(after)),
        grid=(D // wide,),
        out_shape=(shaped((4, count // 8, D), F32), shaped((4, count // 8, D), BF16)),
        in_specs=[pl.BlockSpec((count, 4 * BW), lambda i: (0, 0)) for _ in args] + [weight] * 2 + unread_specs(after),
        out_specs=(tile,) * 2,
        compiler_params=params(58),
        cost_estimate=cost(4_300_000_000, 18_000_000),
        name="mlp_out",
    )(*args, w_even, w_odd, *after)


def weight_products(pairs, rows, column_sets, sources, name, after=()):
    half = rows[0].shape[0]
    span = column_sets[0][0].shape[1]
    pair_spec = pl.BlockSpec((None, half, TILE), lambda i: (0, 0, i))
    row_spec = pl.BlockSpec((half, TILE), lambda i: (0, i))
    column_spec = pl.BlockSpec((2 * half, span), lambda i: (0, 0))
    flat = [piece for pieces in column_sets for piece in pieces]
    return pl.pallas_call(
        deferred(functools.partial(grads_kernel, sources), 16 + len(flat), len(after)),
        grid=(D // TILE,),
        out_shape=shaped((len(sources), span // BW, D, BW), BF16),
        in_specs=[pair_spec] * 8 + [row_spec] * 8 + [column_spec] * len(flat) + unread_specs(after),
        out_specs=pl.BlockSpec((len(sources), span // BW, TILE, BW), lambda i: (0, 0, i, 0)),
        compiler_params=params(60),
        cost_estimate=cost(2 * 8 * half * D * span * len(sources), 20_000_000),
        name=name,
    )(*pairs, *rows, *flat, *after)


def muon(grads, momentum, weights, offset, stride, begun=(), after=()):
    count = grads.shape[0]
    now = lambda i: jnp.minimum(i, count - 1)
    then = lambda i: jnp.maximum(i - count, 0)
    block = (None, D, BW)
    compact = pl.BlockSpec(block, lambda i: (now(i), 0, 0))
    early = pl.BlockSpec(block, lambda i: (stride * now(i) + offset, 0, 0))
    late = pl.BlockSpec(block, lambda i: (stride * then(i) + offset, 0, 0))
    return pl.pallas_call(
        deferred(muon_kernel, 3, len(begun) + len(after)),
        grid=(2 * count,),
        out_shape=(shaped(momentum.shape, F32),) * 3,
        in_specs=[compact, early, late] + unread_specs(begun) + unread_specs(after),
        out_specs=(early, early, late),
        input_output_aliases={3 + index: index for index in range(len(begun))},
        scratch_shapes=[pltpu.VMEM((count, D, BW), F32), pltpu.VMEM((count, BW, BW), F32)],
        compiler_params=params(40),
        cost_estimate=cost(1_000_000_000 * count, 5_500_000 * count),
        name="muon",
    )(grads, momentum, weights, *begun, *after)


def mirror(step):
    return [(place, place ^ step) for place in range(4)]


def ring(value, step=1):
    return lax.ppermute(value, "z", [(place, (place + step) % 4) for place in range(4)])


def swap(value):
    return lax.ppermute(value, "tensor", SWAP)


def nothing(value):
    first = value[(0,) * value.ndim].astype(F32)
    return (first * 0.0).astype(jnp.int32)


def hold(value, *others):
    zero = sum((nothing(other) for other in others), jnp.int32(0))
    return value + zero.astype(value.dtype)


def gather_rows(rows):
    mine = [rows]
    for _ in range(3):
        mine.append(ring(mine[-1]))
    return mine, [swap(part) for part in mine]


class Scatter:
    def __init__(self):
        self.moving = self.result = None
        self.payloads = []

    def add(self, step, mine, theirs):
        total = mine + swap(theirs).astype(F32)
        if self.moving is not None:
            total = total + self.moving.astype(F32)
        if step:
            self.payloads.append(total.astype(BF16))
            self.moving = ring(self.payloads[-1])
        else:
            self.result = total


def everywhere(value):
    value = value + swap(value)
    for axis in ("m", "z"):
        one, two, three = (lax.ppermute(value, axis, mirror(step)) for step in (1, 2, 3))
        value = (value + one) + (two + three)
    if lax.axis_size("r") > 1:
        value = lax.psum(value, "r")
    return value


def join(parts):
    if parts.shape[0] == 4:
        return parts
    width = parts.shape[3]
    parts = parts.reshape(4, 2, -1, D, width).transpose(0, 1, 3, 2, 4)
    return parts.reshape(4, 2, D, BW)


def unjoin(grads, width):
    if width == BW:
        return grads
    grads = grads.reshape(4, 2, D, -1, width).transpose(0, 1, 3, 2, 4)
    return grads.reshape(-1, 1, D, width)


def gather_plane(parts):
    return lax.all_gather(parts, ("m", "r"), axis=0, tiled=False)


def gather_part_direct(part, index, result):
    chip = lax.axis_index("m")
    result = lax.dynamic_update_slice(result, part[None, None], (chip, index, 0, 0))
    for step in (1, 2, 3):
        got = lax.ppermute(part, "m", mirror(step))
        result = lax.dynamic_update_slice(result, got[None, None], (chip ^ step, index, 0, 0))
    return result


def scatter_plane(grads):
    share = lax.psum_scatter(
        grads.reshape(grads.shape[0], -1, grads.shape[3]), ("m", "r"), scatter_dimension=0, tiled=False
    )
    return share.reshape(grads.shape[1:])


def scatter_plane_direct(grads):
    chip = lax.axis_index("m")
    shares = []
    for part in range(2):
        at = chip + sum((nothing(other) for other in shares), jnp.int32(0))

        def share_for(step):
            return lax.dynamic_slice(grads, (at ^ step, part, 0, 0), (1, 1) + grads.shape[2:])[0, 0]

        total = share_for(0).astype(F32)
        arrived = []
        for step in (1, 2, 3):
            arrived.append(lax.ppermute(share_for(step), "m", mirror(step)))
            total = total + arrived[-1].astype(F32)
        shares.append(total.astype(BF16))
    return shares


def interleave(mine, other):
    return [rows for pair in zip(mine, other) for rows in pair]


def local(tokens, segments, weights, momentum, gains, gain_first, gain_second, cotangent):
    plane = lax.axis_index("z")
    core = lax.axis_index("tensor")
    block_count = weights.shape[0]

    if block_count == 8:
        shards = weights.reshape(4, 2, D, BW)
    else:
        width = block_count * BW // 4
        shards = weights.reshape(block_count, D, -1, width).transpose(0, 2, 1, 3).reshape(4, 1, D, width)
    parts, width = shards.shape[1], shards.shape[3]

    def shard(shift, part, *others):
        at = sum((nothing(other) for other in others), plane + shift)
        return lax.dynamic_slice(shards, (at % 4, part, 0, 0), (1, 1, D, width))[0, 0]

    rows_in = tokens.astype(F32)
    segment_own = segments.astype(F32)
    segment_parts = [segment_own] + [ring(segment_own, shift) for shift in (1, 2, 3)]
    segment_rows = jnp.concatenate(segment_parts, axis=0)
    def move(part, *others):
        return [shard(0, part)] + [ring(shard(shift, part, *others), shift) for shift in (1, 2, 3)]

    moved_even = move(0)

    def kind_part(source):
        return lax.select_n(plane, *(moved_even[(here - source) % 4] for here in range(4)))

    row_pair = lambda *others: jnp.stack([hold(rms_norm(rows_in, gains[0]), *others).astype(BF16), cotangent])
    if parts == 2:
        attn_even, mlp_even = sort_kinds(plane, moved_even, [segment_rows])
        moved_odd = move(1, attn_even)
        w_attn = gather_part_direct(hold(attn_even, moved_odd[1]), 0, jnp.zeros((4, 2, D, BW), BF16))
        attn_odd, mlp_odd = sort_kinds(plane, moved_odd, [])
        w_attn = gather_part_direct(attn_odd, 1, w_attn)
        w_mlp = [gather_plane(mlp_even), gather_plane(mlp_odd)]
        begun = [mlp_odd]
        first_mine, first_other = gather_rows(row_pair(attn_odd))
    else:
        w_attn = join(gather_plane(kind_part(0)[None]))
        w_mlp = gather_plane(jnp.stack([kind_part(kind) for kind in (1, 2, 3)]))
        w_mlp = jnp.stack([join(w_mlp[:, kind : kind + 1]) for kind in range(3)], axis=1)
        w_mlp = [w_mlp[:, :, 0], w_mlp[:, :, 1]]
        begun = []
        first_mine, first_other = gather_rows(row_pair())
    first_rows = interleave(first_mine, first_other)

    length = segment_rows.shape[1]
    half = length // 2
    place = jnp.arange(length)
    place = jnp.where(core == 0, place, (place + half) % length)
    segment_rows = jnp.where(core == 0, segment_rows, jnp.roll(segment_rows, half, axis=1))
    allowed = (place[None, None, :] <= place[None, :, None]) & (
        segment_rows[:, None, :] == segment_rows[:, :, None]
    )
    bias = jnp.where(allowed, 0.0, NEG_LARGE).astype(F32)
    cosine, sine = rope_tables(place)

    query, key, value, context = ([None] * 4 for _ in range(4))
    mixed = Scatter()
    for s in (1, 2, 3, 0):
        query[s], key[s], value[s], context[s], *both = attn_forward(
            first_mine[s], first_other[s], w_attn, bias[s], cosine, sine, mixed.payloads[:1] if s == 3 else begun if s == 1 else ()
        )
        mixed.add(s, *both)
    middle = rows_in + mixed.result
    two_mine, two_other = gather_rows(rms_norm(middle, gains[1]).astype(BF16))

    two_rows = interleave(two_mine, two_other)
    *even_half, grads_even = mlp_half(two_rows, first_rows, w_mlp[0])
    *odd_half, grads_odd = mlp_half(two_rows, first_rows, w_mlp[1])
    if parts == 2:
        mlp_share = [scatter_plane(grads_even), scatter_plane(grads_odd)]
    else:
        mlp_grads = jnp.stack([grads_even, grads_odd], axis=2)
        mlp_share = [
            jnp.concatenate([scatter_plane(unjoin(mlp_grads[:, kind], width)) for kind in range(3)])
        ]
    d_normed = Scatter()
    for s in (1, 2, 3, 0):
        d_normed.add(s, *mlp_back(s, (even_half, odd_half), *w_mlp))
    outward = mlp_out((even_half, odd_half), *w_mlp, d_normed.payloads[-1:])
    d_normed_two = hold(d_normed.result, outward[1])

    d_output = cotangent.astype(F32)
    d_middle_norm, d_gain_two = rms_norm_back(middle, gains[1], d_normed_two)
    d_middle = d_output + d_middle_norm
    e_mine, e_other = gather_rows(d_middle.astype(BF16))
    d_query, d_key, d_value, d_one = ([None] * 4 for _ in range(4))
    for s in range(4):
        d_query[s], d_key[s], d_value[s], *both = attn_backward(
            e_mine[s], e_other[s], w_attn, bias[s], cosine, sine, query[s], key[s], value[s]
        )
        d_one[s] = both
    attn_grads = weight_products(
        first_rows,
        interleave(e_mine, e_other),
        (d_query, d_key, d_value, context),
        (0, 0, 0, 1),
        "attn_products",
        mlp_share[:1],
    )
    if parts == 2:
        attn_share = scatter_plane_direct(attn_grads)
    else:
        attn_share = scatter_plane(unjoin(attn_grads, width))

    last = Scatter()
    for s in (1, 2, 3, 0):
        mine, theirs = (jnp.stack([a, b[s]]) for a, b in zip(d_one[s], outward))
        if s == 2:
            mine = hold(mine, attn_grads)
        last.add(s, mine, theirs)
    d_normed_one, outward_sum = last.result
    d_rows_norm, d_gain_one = rms_norm_back(rows_in, gains[0], d_normed_one)
    input_grad = d_middle + d_rows_norm
    output = (middle + outward_sum).astype(BF16)
    gain_grads = everywhere(jnp.stack([d_gain_one, d_gain_two]))

    results = ()
    for part in range(parts):
        shares = jnp.concatenate([attn_share[part][None], mlp_share[part]])

        def share_of(shift):
            return lax.dynamic_index_in_dim(shares, (plane + shift) % 4, 0, keepdims=False)

        back = [share_of(0)] + [ring(share_of(shift), shift) for shift in (1, 2, 3)]
        here = plane + nothing(results[1]) if part else plane
        summed = jnp.stack(
            [lax.select_n(here, *(back[(z - source) % 4] for z in range(4))) for source in range(4)]
        )
        if parts == 1:
            summed = summed.reshape(block_count, -1, D, width).transpose(0, 2, 1, 3).reshape(block_count, D, BW)
        results = muon(summed, momentum, weights, part, parts, results)
    weight_grads, new_momentum, new_weights = results

    new_gain_first = BETA_FIRST * gain_first + (1.0 - BETA_FIRST) * gain_grads
    new_gain_second = BETA_SECOND * gain_second + (1.0 - BETA_SECOND) * gain_grads * gain_grads
    first_hat = new_gain_first / (1.0 - BETA_FIRST**STEP)
    second_hat = new_gain_second / (1.0 - BETA_SECOND**STEP)
    new_gains = gains - ADAM_RATE * first_hat / (jnp.sqrt(second_hat) + ADAM_EPS)
    return (
        output,
        input_grad,
        weight_grads,
        new_momentum,
        new_weights,
        new_gain_first,
        new_gain_second,
        new_gains,
    )


def solution(mesh):
    count = mesh.shape["dp"]
    fine = Mesh(
        np.asarray(mesh.devices).reshape(4, 4, count // 16, mesh.shape["tensor"]),
        ("z",) + PLANE,
    )
    every = ("z",) + PLANE
    in_specs = (
        P(every, None),
        P(every[:3], None),
        P(every, None, None),
        P(every, None, None),
        P(),
        P(),
        P(),
        P(every, None),
    )
    out_specs = (
        P(every, None),
        P(every, None),
        P(every, None, None),
        P(every, None, None),
        P(every, None, None),
        P(),
        P(),
        P(),
    )
    return jax.shard_map(local, mesh=fine, in_specs=in_specs, out_specs=out_specs, check_vma=False)
```

```python
import functools
import math

import jax
import jax.numpy as jnp
import numpy as np
from jax import lax
from jax.experimental import pallas as pl
from jax.experimental.pallas import tpu as pltpu
from jax.sharding import Mesh
from jax.sharding import PartitionSpec as P

D = 2048
FF = 8192
HD = 64
BW = 128
NS_ITERS = 5
STEP = 10

HIGHEST = lax.Precision.HIGHEST
ROPE_BASE = 130000.0
NORM_EPS = 1e-05
NEG_LARGE = -1e30
MOMENTUM_DECAY = 0.95
MUON_RATE = 0.25
COEFF_A = 3.4445
COEFF_B = -4.775
COEFF_C = 2.0315
BETA_FIRST = 0.9
BETA_SECOND = 0.95
ADAM_RATE = 1.0
ADAM_EPS = 1e-08

F32 = jnp.float32
BF16 = jnp.bfloat16
PLANE = ("m", "r", "tensor")
SWAP = [(0, 1), (1, 0)]
TILE = 256
SCORE_SCALE = 1.0 / math.sqrt(HD)


def rms_norm(values, gain):
    return values * lax.rsqrt(jnp.mean(values * values, axis=-1, keepdims=True) + NORM_EPS) * gain


def rms_norm_back(values, gain, grad):
    scale = lax.rsqrt(jnp.mean(values * values, axis=-1, keepdims=True) + NORM_EPS)
    scaled = gain * grad
    inner = jnp.mean(scaled * values, axis=-1, keepdims=True)
    gain_grad = jnp.sum(grad * values * scale, axis=0)
    return scale * scaled - values * (scale * scale * scale * inner), gain_grad


def rope_tables(place):
    exponent = jnp.arange(HD // 2).astype(F32) * (2.0 / HD)
    inverse = jnp.exp(-exponent * math.log(ROPE_BASE))
    angle = place.astype(F32)[:, None] * inverse[None, :]
    cosine, sine = jnp.cos(angle), jnp.sin(angle)
    heads = 2 * BW // HD
    return (
        jnp.tile(jnp.concatenate([cosine, cosine], axis=1), (1, heads)),
        jnp.tile(jnp.concatenate([-sine, sine], axis=1), (1, heads)),
    )


def dims(lhs, rhs):
    return (((lhs,), (rhs,)), ((), ()))


def mul(a, b):
    return lax.dot_general(a, b, dims(1, 0), preferred_element_type=F32)


def mul_bt(a, b):
    return lax.dot_general(a, b, dims(1, 1), preferred_element_type=F32)


def mul_at(a, b):
    return lax.dot_general(a, b, dims(0, 0), preferred_element_type=F32)


def side_by_side(ref, *index):
    return jnp.concatenate([ref[index + (0,)], ref[index + (1,)]], axis=-1)


def pair_rows(own_ref, other_ref):
    return jnp.concatenate([own_ref[...], other_ref[...]], axis=0)


def swap_halves(values):
    lane = lax.broadcasted_iota(jnp.int32, values.shape, 1)
    span = values.shape[1]
    ahead = pltpu.roll(values, span - HD // 2, 1)
    behind = pltpu.roll(values, HD // 2, 1)
    return jnp.where(lane % HD < HD // 2, ahead, behind)


def head_only(values, head):
    lane = lax.broadcasted_iota(jnp.int32, values.shape, 1)
    return jnp.where((lane >= head * HD) & (lane < (head + 1) * HD), values, jnp.zeros_like(values))


def head_probs(query, key, bias, head):
    scores = mul_bt(head_only(query, head), key) * SCORE_SCALE + bias
    weights = jnp.exp(scores - jnp.max(scores, axis=-1, keepdims=True))
    return weights / jnp.sum(weights, axis=-1, keepdims=True)


def attn_forward_kernel(
    own_ref, other_ref, w_ref, bias_ref, cos_ref, sin_ref, q_ref, k_ref, v_ref, c_ref, mine_ref, theirs_ref
):
    rows = pair_rows(own_ref, other_ref)
    cosine, sine = cos_ref[...], sin_ref[...]
    lin = mul(rows, side_by_side(w_ref, 0))
    query = (lin * cosine + swap_halves(lin) * sine).astype(BF16)
    lin = mul(rows, side_by_side(w_ref, 1))
    key = (lin * cosine + swap_halves(lin) * sine).astype(BF16)
    value = mul(rows, side_by_side(w_ref, 2)).astype(BF16)
    q_ref[...] = query
    k_ref[...] = key
    v_ref[...] = value
    context = jnp.zeros(query.shape, F32)
    for head in range(query.shape[1] // HD):
        probs = head_probs(query, key, bias_ref[...], head)
        context = context + mul(probs.astype(BF16), head_only(value, head))
    context = context.astype(BF16)
    c_ref[...] = context
    half = own_ref.shape[0]
    for tile in range(D // TILE):
        at = pl.ds(tile * TILE, TILE)
        w_out = jnp.concatenate([w_ref[3, 0, at, :], w_ref[3, 1, at, :]], axis=-1)
        mixed = mul_bt(context, w_out)
        mine_ref[:, at] = mixed[:half]
        theirs_ref[:, at] = mixed[half:].astype(BF16)


def attn_backward_kernel(
    own_ref, other_ref, w_ref, bias_ref, cos_ref, sin_ref, q_ref, k_ref, v_ref,
    dq_ref, dk_ref, dv_ref, mine_ref, theirs_ref,
):
    rows = pair_rows(own_ref, other_ref)
    query, key, value = q_ref[...], k_ref[...], v_ref[...]
    d_context = mul(rows, side_by_side(w_ref, 3)).astype(BF16)
    d_query = jnp.zeros(query.shape, F32)
    d_key = jnp.zeros(query.shape, F32)
    d_value = jnp.zeros(query.shape, F32)
    for head in range(query.shape[1] // HD):
        probs = head_probs(query, key, bias_ref[...], head)
        d_here = head_only(d_context, head)
        d_value = d_value + mul_at(probs.astype(BF16), d_here)
        d_probs = mul_bt(d_here, value)
        inner = jnp.sum(probs * d_probs, axis=-1, keepdims=True)
        d_scores = (probs * (d_probs - inner)).astype(BF16)
        d_query = d_query + mul(d_scores, head_only(key, head))
        d_key = d_key + mul_at(d_scores, head_only(query, head))
    cosine, sine = cos_ref[...], sin_ref[...]
    d_query = d_query * SCORE_SCALE
    d_key = d_key * SCORE_SCALE
    d_query = (d_query * cosine - swap_halves(d_query) * sine).astype(BF16)
    d_key = (d_key * cosine - swap_halves(d_key) * sine).astype(BF16)
    d_value = d_value.astype(BF16)
    dq_ref[...] = d_query
    dk_ref[...] = d_key
    dv_ref[...] = d_value
    half = own_ref.shape[0]
    for tile in range(D // TILE):
        at = pl.ds(tile * TILE, TILE)
        total = jnp.zeros((2 * half, TILE), F32)
        for matrix, columns in ((0, d_query), (1, d_key), (2, d_value)):
            w_here = jnp.concatenate([w_ref[matrix, 0, at, :], w_ref[matrix, 1, at, :]], axis=-1)
            total = total + mul_bt(columns, w_here)
        mine_ref[:, at] = total[:half]
        theirs_ref[:, at] = total[half:].astype(BF16)


def mlp_half_kernel(*refs):
    rows, d_rows = refs[:8], refs[8:16]
    w_ref, hid_ref, dgate_ref, dup_ref, grad_ref = refs[16:]
    w_gate, w_up, w_down = (
        jnp.concatenate([w_ref[0, kind], w_ref[1, kind]], axis=-1) for kind in range(3)
    )
    for piece in range(4):
        here = pair_rows(rows[2 * piece], rows[2 * piece + 1])
        gate = mul(here, w_gate)
        up = mul(here, w_up)
        d_hidden = mul(pair_rows(d_rows[2 * piece], d_rows[2 * piece + 1]), w_down)
        sigmoid = 1.0 / (1.0 + jnp.exp(-gate))
        silu = gate * sigmoid
        at = pl.ds(piece * here.shape[0], here.shape[0])
        hid_ref[at, :] = (silu * up).astype(BF16)
        dgate_ref[at, :] = (d_hidden * up * sigmoid * (1.0 + gate * (1.0 - sigmoid))).astype(BF16)
        dup_ref[at, :] = (d_hidden * silu).astype(BF16)
    for tile in range(D // TILE):
        at = pl.ds(tile * TILE, TILE)
        across = jnp.concatenate([ref[:, at] for ref in rows], axis=0)
        d_across = jnp.concatenate([ref[:, at] for ref in d_rows], axis=0)
        for kind, left, right in ((0, across, dgate_ref), (1, across, dup_ref), (2, d_across, hid_ref)):
            grad = mul_at(left, right[...]).astype(BF16)
            for chip in range(2):
                grad_ref[chip, kind, at, :] = grad[:, chip * BW : (chip + 1) * BW]


def all_columns(kind, w_even, w_odd):
    return jnp.concatenate([ref[chip, kind] for ref in (w_even, w_odd) for chip in range(4)], axis=-1)


def both_columns(even, odd):
    return jnp.concatenate([even[...], odd[...]], axis=-1)


def mlp_back_kernel(dgate_even, dgate_odd, dup_even, dup_odd, w_even, w_odd, mine_ref, theirs_ref):
    total = mul_bt(both_columns(dgate_even, dgate_odd), all_columns(0, w_even, w_odd))
    total = total + mul_bt(both_columns(dup_even, dup_odd), all_columns(1, w_even, w_odd))
    half = mine_ref.shape[0]
    mine_ref[...] = total[:half]
    theirs_ref[...] = total[half:].astype(BF16)


def mlp_out_kernel(hid_even, hid_odd, w_even, w_odd, mine_ref, theirs_ref):
    total = mul_bt(both_columns(hid_even, hid_odd), all_columns(0, w_even, w_odd))
    half = mine_ref.shape[1]
    for piece in range(4):
        mine_ref[piece] = total[2 * piece * half : (2 * piece + 1) * half]
        theirs_ref[piece] = total[(2 * piece + 1) * half : 2 * (piece + 1) * half].astype(BF16)


def grads_kernel(sources, *refs):
    first, second = refs[:8], refs[8:16]
    columns = refs[16:-1]
    out_ref = refs[-1]
    row_sets = [jnp.concatenate([ref[...] for ref in part], axis=0) for part in (first, second)]
    for index, source in enumerate(sources):
        stacked = jnp.concatenate([ref[...] for ref in columns[4 * index : 4 * index + 4]], axis=0)
        grad = mul_at(row_sets[source], stacked).astype(BF16)
        for block in range(grad.shape[1] // BW):
            out_ref[index, block] = grad[:, block * BW : (block + 1) * BW]


def split(values):
    high = values.astype(BF16)
    return high, (values - high.astype(F32)).astype(BF16)


def mul_split(a, b):
    return mul(a[0], b[0]) + (mul(a[0], b[1]) + mul(a[1], b[0]))


def muon_kernel(grad_ref, momentum_ref, weight_ref, wg_ref, nm_ref, nw_ref, held, mixers):
    step = pl.program_id(0)
    count = held.shape[0]

    @pl.when(step < count)
    def _():
        grad = grad_ref[...].astype(F32)
        wg_ref[...] = grad
        block = MOMENTUM_DECAY * momentum_ref[...] + grad
        nm_ref[...] = block
        block = block * (1.0 / (jnp.sqrt(jnp.sum(block * block)) + 1e-07))
        held[step] = block
        high, low = split(block)
        cross = mul_at(high, low)
        mixers[step] = mul_at(high, high) + (cross + cross.T)

    @pl.when(step == count - 1)
    def _():
        row = lax.broadcasted_iota(jnp.int32, (BW, BW), 0)
        column = lax.broadcasted_iota(jnp.int32, (BW, BW), 1)
        eye = jnp.where(row == column, COEFF_A, 0.0).astype(F32)
        grams = [mixers[index] for index in range(count)]
        totals = [None] * count
        for turn in range(NS_ITERS):
            for index in range(count):
                pair = split(grams[index])
                mixer = eye + COEFF_B * grams[index] + COEFF_C * mul_split(pair, pair)
                mixed = split(mixer)
                if turn == 0:
                    totals[index] = mixer
                else:
                    totals[index] = mul_split(split(totals[index]), mixed)
                if turn < NS_ITERS - 1:
                    grams[index] = mul_split(split(mul_split(mixed, pair)), mixed)
        for index in range(count):
            mixers[index] = totals[index]

    @pl.when(step >= count)
    def _():
        at = step - count
        ortho = mul_split(split(held[at]), split(mixers[at]))
        nw_ref[...] = weight_ref[...].astype(F32) - (MUON_RATE * math.sqrt(D / BW)) * ortho


def deferred(kernel, inputs, unread):
    return lambda *refs: kernel(*refs[:inputs], *refs[inputs + unread :])


def unread_specs(after):
    return [pl.BlockSpec(memory_space=pl.ANY) for _ in after]


def cost(flops, accessed):
    return pl.CostEstimate(flops=flops // 6, bytes_accessed=accessed // 6, transcendentals=0)


def sort_kernel(plane_ref, *refs):
    moved, attn_ref, mlp_ref = refs[:4], refs[4], refs[5]
    for here in range(4):

        @pl.when(plane_ref[0] == here)
        def _():
            attn_ref[...] = moved[here][...]
            for kind in (1, 2, 3):
                mlp_ref[kind - 1] = moved[(here - kind) % 4][...]


def sort_kinds(plane, moved, after):
    shape = moved[0].shape
    return pl.pallas_call(
        deferred(sort_kernel, 5, len(after)),
        out_shape=(shaped(shape, BF16), shaped((3,) + shape, BF16)),
        in_specs=[pl.BlockSpec(memory_space=pltpu.SMEM)] + whole_specs(moved) + unread_specs(after),
        out_specs=tuple(whole_specs(range(2))),
        compiler_params=params(32),
        cost_estimate=cost(0, 4_000_000),
        name="sort_kinds",
    )(plane.astype(jnp.int32).reshape(1), *moved, *after)


def params(mebibytes):
    return pltpu.CompilerParams(vmem_limit_bytes=mebibytes * 1024 * 1024)


def whole_specs(arrays):
    return [pl.BlockSpec(memory_space=pltpu.VMEM) for _ in arrays]


def shaped(shape, dtype):
    return jax.ShapeDtypeStruct(shape, dtype)


def attn_forward(own, other, w_attn, bias, cosine, sine, after=()):
    half = own.shape[1]
    rows = pl.BlockSpec((None, half, D), lambda i: (0, 0, 0))
    span = w_attn.shape[1] * w_attn.shape[3]
    square = shaped((2 * half, span), BF16)
    args = (own, other, w_attn, bias, cosine, sine)
    return pl.pallas_call(
        deferred(attn_forward_kernel, len(args), len(after)),
        grid=(1,),
        out_shape=(square,) * 4 + (shaped((half, D), F32), shaped((half, D), BF16)),
        in_specs=[rows, rows] + whole_specs(args[2:]) + unread_specs(after),
        out_specs=tuple(whole_specs(range(6))),
        compiler_params=params(40),
        cost_estimate=cost(1_300_000_000, 9_000_000),
        name="attn_forward",
    )(*args, *after)


def attn_backward(own, other, w_attn, bias, cosine, sine, query, key, value):
    half = own.shape[0]
    square = shaped(query.shape, BF16)
    args = (own, other, w_attn, bias, cosine, sine, query, key, value)
    return pl.pallas_call(
        attn_backward_kernel,
        out_shape=(square,) * 3 + (shaped((half, D), F32), shaped((half, D), BF16)),
        in_specs=whole_specs(args),
        out_specs=tuple(whole_specs(range(5))),
        compiler_params=params(40),
        cost_estimate=cost(1_600_000_000, 9_000_000),
        name="attn_backward",
    )(*args)


def mlp_half(rows, pairs, w_half):
    half = rows[0].shape[0]
    columns = shaped((8 * half, 4 * BW), BF16)
    blocks = pl.BlockSpec((2, 3, D, BW), lambda j: (j, 0, 0, 0))
    return pl.pallas_call(
        mlp_half_kernel,
        grid=(2,),
        out_shape=(columns,) * 3 + (shaped(w_half.shape, BF16),),
        in_specs=[pl.BlockSpec((half, D), lambda j: (0, 0)) for _ in range(8)]
        + [pl.BlockSpec((None, half, D), lambda j: (1, 0, 0)) for _ in range(8)]
        + [blocks],
        out_specs=(pl.BlockSpec((8 * half, 2 * BW), lambda j: (0, j)),) * 3 + (blocks,),
        compiler_params=params(58),
        cost_estimate=cost(13_000_000_000, 20_000_000),
        name="mlp_half",
    )(*rows, *pairs, w_half)


def mlp_back(piece, halves, w_even, w_odd):
    rows = halves[0][0].shape[0] // 4
    wide = 2 * TILE
    args = [half[index] for index in (1, 2) for half in halves]
    tile = pl.BlockSpec((rows // 2, wide), lambda i: (0, i))
    weight = pl.BlockSpec((4, 2, wide, BW), lambda i: (0, 0, i, 0))
    return pl.pallas_call(
        mlp_back_kernel,
        grid=(D // wide,),
        out_shape=(shaped((rows // 2, D), F32), shaped((rows // 2, D), BF16)),
        in_specs=[pl.BlockSpec((rows, 4 * BW), lambda i: (piece, 0)) for _ in args] + [weight] * 2,
        out_specs=(tile,) * 2,
        compiler_params=params(58),
        cost_estimate=cost(2_200_000_000, 11_000_000),
        name="mlp_back",
    )(*args, w_even, w_odd)


def mlp_out(halves, w_even, w_odd, after):
    count = halves[0][0].shape[0]
    args = [half[0] for half in halves]
    wide = 2 * TILE
    tile = pl.BlockSpec((4, count // 8, wide), lambda i: (0, 0, i))
    weight = pl.BlockSpec((4, 1, wide, BW), lambda i: (0, 2, i, 0))
    return pl.pallas_call(
        deferred(mlp_out_kernel, 4, len(after)),
        grid=(D // wide,),
        out_shape=(shaped((4, count // 8, D), F32), shaped((4, count // 8, D), BF16)),
        in_specs=[pl.BlockSpec((count, 4 * BW), lambda i: (0, 0)) for _ in args] + [weight] * 2 + unread_specs(after),
        out_specs=(tile,) * 2,
        compiler_params=params(58),
        cost_estimate=cost(4_300_000_000, 18_000_000),
        name="mlp_out",
    )(*args, w_even, w_odd, *after)


def weight_products(pairs, rows, column_sets, sources, name, after=()):
    half = rows[0].shape[0]
    span = column_sets[0][0].shape[1]
    pair_spec = pl.BlockSpec((None, half, TILE), lambda i: (0, 0, i))
    row_spec = pl.BlockSpec((half, TILE), lambda i: (0, i))
    column_spec = pl.BlockSpec((2 * half, span), lambda i: (0, 0))
    flat = [piece for pieces in column_sets for piece in pieces]
    return pl.pallas_call(
        deferred(functools.partial(grads_kernel, sources), 16 + len(flat), len(after)),
        grid=(D // TILE,),
        out_shape=shaped((len(sources), span // BW, D, BW), BF16),
        in_specs=[pair_spec] * 8 + [row_spec] * 8 + [column_spec] * len(flat) + unread_specs(after),
        out_specs=pl.BlockSpec((len(sources), span // BW, TILE, BW), lambda i: (0, 0, i, 0)),
        compiler_params=params(60),
        cost_estimate=cost(2 * 8 * half * D * span * len(sources), 20_000_000),
        name=name,
    )(*pairs, *rows, *flat, *after)


def muon(grads, momentum, weights, offset, stride, begun=(), after=()):
    count = grads.shape[0]
    now = lambda i: jnp.minimum(i, count - 1)
    then = lambda i: jnp.maximum(i - count, 0)
    block = (None, D, BW)
    compact = pl.BlockSpec(block, lambda i: (now(i), 0, 0))
    early = pl.BlockSpec(block, lambda i: (stride * now(i) + offset, 0, 0))
    late = pl.BlockSpec(block, lambda i: (stride * then(i) + offset, 0, 0))
    return pl.pallas_call(
        deferred(muon_kernel, 3, len(begun) + len(after)),
        grid=(2 * count,),
        out_shape=(shaped(momentum.shape, F32),) * 3,
        in_specs=[compact, early, late] + unread_specs(begun) + unread_specs(after),
        out_specs=(early, early, late),
        input_output_aliases={3 + index: index for index in range(len(begun))},
        scratch_shapes=[pltpu.VMEM((count, D, BW), F32), pltpu.VMEM((count, BW, BW), F32)],
        compiler_params=params(40),
        cost_estimate=cost(1_000_000_000 * count, 5_500_000 * count),
        name="muon",
    )(grads, momentum, weights, *begun, *after)


def mirror(step):
    return [(place, place ^ step) for place in range(4)]


def ring(value, step=1):
    return lax.ppermute(value, "z", [(place, (place + step) % 4) for place in range(4)])


def swap(value):
    return lax.ppermute(value, "tensor", SWAP)


def nothing(value):
    first = value[(0,) * value.ndim].astype(F32)
    return (first * 0.0).astype(jnp.int32)


def hold(value, *others):
    zero = sum((nothing(other) for other in others), jnp.int32(0))
    return value + zero.astype(value.dtype)


def gather_rows(rows):
    mine = [rows]
    for _ in range(3):
        mine.append(ring(mine[-1]))
    return mine, [swap(part) for part in mine]


class Scatter:
    def __init__(self):
        self.moving = self.result = None
        self.payloads = []

    def add(self, step, mine, theirs):
        total = mine + swap(theirs).astype(F32)
        if self.moving is not None:
            total = total + self.moving.astype(F32)
        if step:
            self.payloads.append(total.astype(BF16))
            self.moving = ring(self.payloads[-1])
        else:
            self.result = total


def everywhere(value):
    value = value + swap(value)
    for axis in ("m", "z"):
        one, two, three = (lax.ppermute(value, axis, mirror(step)) for step in (1, 2, 3))
        value = (value + one) + (two + three)
    if lax.axis_size("r") > 1:
        value = lax.psum(value, "r")
    return value


def join(parts):
    if parts.shape[0] == 4:
        return parts
    width = parts.shape[3]
    parts = parts.reshape(4, 2, -1, D, width).transpose(0, 1, 3, 2, 4)
    return parts.reshape(4, 2, D, BW)


def unjoin(grads, width):
    if width == BW:
        return grads
    grads = grads.reshape(4, 2, D, -1, width).transpose(0, 1, 3, 2, 4)
    return grads.reshape(-1, 1, D, width)


def gather_plane(parts):
    return lax.all_gather(parts, ("m", "r"), axis=0, tiled=False)


def gather_part_direct(part, index, result):
    chip = lax.axis_index("m")
    result = lax.dynamic_update_slice(result, part[None, None], (chip, index, 0, 0))
    for step in (1, 2, 3):
        got = lax.ppermute(part, "m", mirror(step))
        result = lax.dynamic_update_slice(result, got[None, None], (chip ^ step, index, 0, 0))
    return result


def scatter_plane(grads):
    share = lax.psum_scatter(
        grads.reshape(grads.shape[0], -1, grads.shape[3]), ("m", "r"), scatter_dimension=0, tiled=False
    )
    return share.reshape(grads.shape[1:])


def scatter_plane_direct(grads):
    chip = lax.axis_index("m")

    def share_for(step):
        return lax.dynamic_index_in_dim(grads, chip ^ step, 0, keepdims=False)

    total = share_for(0).astype(F32)
    for step in (1, 2, 3):
        total = total + lax.ppermute(share_for(step), "m", mirror(step)).astype(F32)
    return total.astype(BF16)


def interleave(mine, other):
    return [rows for pair in zip(mine, other) for rows in pair]


def local(tokens, segments, weights, momentum, gains, gain_first, gain_second, cotangent):
    plane = lax.axis_index("z")
    core = lax.axis_index("tensor")
    block_count = weights.shape[0]

    if block_count == 8:
        shards = weights.reshape(4, 2, D, BW)
    else:
        width = block_count * BW // 4
        shards = weights.reshape(block_count, D, -1, width).transpose(0, 2, 1, 3).reshape(4, 1, D, width)
    parts, width = shards.shape[1], shards.shape[3]

    def shard(shift, part, *others):
        at = sum((nothing(other) for other in others), plane + shift)
        return lax.dynamic_slice(shards, (at % 4, part, 0, 0), (1, 1, D, width))[0, 0]

    rows_in = tokens.astype(F32)
    segment_own = segments.astype(F32)
    segment_parts = [segment_own] + [ring(segment_own, shift) for shift in (1, 2, 3)]
    segment_rows = jnp.concatenate(segment_parts, axis=0)
    def move(part, *others):
        return [shard(0, part)] + [ring(shard(shift, part, *others), shift) for shift in (1, 2, 3)]

    moved_even = move(0)

    def kind_part(source):
        return lax.select_n(plane, *(moved_even[(here - source) % 4] for here in range(4)))

    row_pair = lambda *others: jnp.stack([hold(rms_norm(rows_in, gains[0]), *others).astype(BF16), cotangent])
    if parts == 2:
        attn_even, mlp_even = sort_kinds(plane, moved_even, [segment_rows])
        w_attn = gather_part_direct(attn_even, 0, jnp.zeros((4, 2, D, BW), BF16))
        attn_odd, mlp_odd = sort_kinds(plane, move(1, *moved_even[1:]), [w_attn])
        w_attn = gather_part_direct(attn_odd, 1, w_attn)
        w_mlp = [gather_plane(mlp_even), gather_plane(mlp_odd)]
        begun = [mlp_odd]
        first_mine, first_other = gather_rows(row_pair(attn_odd))
    else:
        w_attn = join(gather_plane(kind_part(0)[None]))
        w_mlp = gather_plane(jnp.stack([kind_part(kind) for kind in (1, 2, 3)]))
        w_mlp = jnp.stack([join(w_mlp[:, kind : kind + 1]) for kind in range(3)], axis=1)
        w_mlp = [w_mlp[:, :, 0], w_mlp[:, :, 1]]
        begun = []
        first_mine, first_other = gather_rows(row_pair())
    first_rows = interleave(first_mine, first_other)

    length = segment_rows.shape[1]
    half = length // 2
    place = jnp.arange(length)
    place = jnp.where(core == 0, place, (place + half) % length)
    segment_rows = jnp.where(core == 0, segment_rows, jnp.roll(segment_rows, half, axis=1))
    allowed = (place[None, None, :] <= place[None, :, None]) & (
        segment_rows[:, None, :] == segment_rows[:, :, None]
    )
    bias = jnp.where(allowed, 0.0, NEG_LARGE).astype(F32)
    cosine, sine = rope_tables(place)

    query, key, value, context = ([None] * 4 for _ in range(4))
    mixed = Scatter()
    for s in (1, 2, 3, 0):
        query[s], key[s], value[s], context[s], *both = attn_forward(
            first_mine[s], first_other[s], w_attn, bias[s], cosine, sine, mixed.payloads[:1] if s == 3 else begun if s == 1 else ()
        )
        mixed.add(s, *both)
    middle = rows_in + mixed.result
    two_mine, two_other = gather_rows(rms_norm(middle, gains[1]).astype(BF16))

    two_rows = interleave(two_mine, two_other)
    *even_half, grads_even = mlp_half(two_rows, first_rows, w_mlp[0])
    *odd_half, grads_odd = mlp_half(two_rows, first_rows, w_mlp[1])
    if parts == 2:
        mlp_share = [scatter_plane(grads_even), scatter_plane(grads_odd)]
    else:
        mlp_grads = jnp.stack([grads_even, grads_odd], axis=2)
        mlp_share = [
            jnp.concatenate([scatter_plane(unjoin(mlp_grads[:, kind], width)) for kind in range(3)])
        ]
    d_normed = Scatter()
    for s in (1, 2, 3, 0):
        d_normed.add(s, *mlp_back(s, (even_half, odd_half), *w_mlp))
    outward = mlp_out((even_half, odd_half), *w_mlp, d_normed.payloads[-1:])
    d_normed_two = hold(d_normed.result, outward[1])

    d_output = cotangent.astype(F32)
    d_middle_norm, d_gain_two = rms_norm_back(middle, gains[1], d_normed_two)
    d_middle = d_output + d_middle_norm
    e_mine, e_other = gather_rows(d_middle.astype(BF16))
    d_query, d_key, d_value, d_one = ([None] * 4 for _ in range(4))
    for s in range(4):
        d_query[s], d_key[s], d_value[s], *both = attn_backward(
            e_mine[s], e_other[s], w_attn, bias[s], cosine, sine, query[s], key[s], value[s]
        )
        d_one[s] = both
    attn_grads = weight_products(
        first_rows,
        interleave(e_mine, e_other),
        (d_query, d_key, d_value, context),
        (0, 0, 0, 1),
        "attn_products",
        mlp_share[:1],
    )
    if parts == 2:
        attn_share = scatter_plane_direct(attn_grads)
    else:
        attn_share = scatter_plane(unjoin(attn_grads, width))

    last = Scatter()
    for s in (1, 2, 3, 0):
        mine, theirs = (jnp.stack([a, b[s]]) for a, b in zip(d_one[s], outward))
        if s == 2:
            mine = hold(mine, attn_grads)
        last.add(s, mine, theirs)
    d_normed_one, outward_sum = last.result
    d_rows_norm, d_gain_one = rms_norm_back(rows_in, gains[0], d_normed_one)
    input_grad = d_middle + d_rows_norm
    output = (middle + outward_sum).astype(BF16)
    gain_grads = everywhere(jnp.stack([d_gain_one, d_gain_two]))

    results = ()
    for part in range(parts):
        shares = jnp.concatenate([attn_share[part][None], mlp_share[part]])

        def share_of(shift):
            return lax.dynamic_index_in_dim(shares, (plane + shift) % 4, 0, keepdims=False)

        back = [share_of(0)] + [ring(share_of(shift), shift) for shift in (1, 2, 3)]
        here = plane + nothing(results[1]) if part else plane
        summed = jnp.stack(
            [lax.select_n(here, *(back[(z - source) % 4] for z in range(4))) for source in range(4)]
        )
        if parts == 1:
            summed = summed.reshape(block_count, -1, D, width).transpose(0, 2, 1, 3).reshape(block_count, D, BW)
        results = muon(summed, momentum, weights, part, parts, results)
    weight_grads, new_momentum, new_weights = results

    new_gain_first = BETA_FIRST * gain_first + (1.0 - BETA_FIRST) * gain_grads
    new_gain_second = BETA_SECOND * gain_second + (1.0 - BETA_SECOND) * gain_grads * gain_grads
    first_hat = new_gain_first / (1.0 - BETA_FIRST**STEP)
    second_hat = new_gain_second / (1.0 - BETA_SECOND**STEP)
    new_gains = gains - ADAM_RATE * first_hat / (jnp.sqrt(second_hat) + ADAM_EPS)
    return (
        output,
        input_grad,
        weight_grads,
        new_momentum,
        new_weights,
        new_gain_first,
        new_gain_second,
        new_gains,
    )


def solution(mesh):
    count = mesh.shape["dp"]
    fine = Mesh(
        np.asarray(mesh.devices).reshape(4, 4, count // 16, mesh.shape["tensor"]),
        ("z",) + PLANE,
    )
    every = ("z",) + PLANE
    in_specs = (
        P(every, None),
        P(every[:3], None),
        P(every, None, None),
        P(every, None, None),
        P(),
        P(),
        P(),
        P(every, None),
    )
    out_specs = (
        P(every, None),
        P(every, None),
        P(every, None, None),
        P(every, None, None),
        P(every, None, None),
        P(),
        P(),
        P(),
    )
    return jax.shard_map(local, mesh=fine, in_specs=in_specs, out_specs=out_specs, check_vma=False)
```

```python
import functools
import math

import jax
import jax.numpy as jnp
import numpy as np
from jax import lax
from jax.experimental import pallas as pl
from jax.experimental.pallas import tpu as pltpu
from jax.sharding import Mesh
from jax.sharding import PartitionSpec as P

D = 2048
FF = 8192
HD = 64
BW = 128
NS_ITERS = 5
STEP = 10

HIGHEST = lax.Precision.HIGHEST
ROPE_BASE = 130000.0
NORM_EPS = 1e-05
NEG_LARGE = -1e30
MOMENTUM_DECAY = 0.95
MUON_RATE = 0.25
COEFF_A = 3.4445
COEFF_B = -4.775
COEFF_C = 2.0315
BETA_FIRST = 0.9
BETA_SECOND = 0.95
ADAM_RATE = 1.0
ADAM_EPS = 1e-08

F32 = jnp.float32
BF16 = jnp.bfloat16
PLANE = ("m", "r", "tensor")
SWAP = [(0, 1), (1, 0)]
TILE = 256
SCORE_SCALE = 1.0 / math.sqrt(HD)


def rms_norm(values, gain):
    return values * lax.rsqrt(jnp.mean(values * values, axis=-1, keepdims=True) + NORM_EPS) * gain


def rms_norm_back(values, gain, grad):
    scale = lax.rsqrt(jnp.mean(values * values, axis=-1, keepdims=True) + NORM_EPS)
    scaled = gain * grad
    inner = jnp.mean(scaled * values, axis=-1, keepdims=True)
    gain_grad = jnp.sum(grad * values * scale, axis=0)
    return scale * scaled - values * (scale * scale * scale * inner), gain_grad


def rope_tables(place):
    exponent = jnp.arange(HD // 2).astype(F32) * (2.0 / HD)
    inverse = jnp.exp(-exponent * math.log(ROPE_BASE))
    angle = place.astype(F32)[:, None] * inverse[None, :]
    cosine, sine = jnp.cos(angle), jnp.sin(angle)
    heads = 2 * BW // HD
    return (
        jnp.tile(jnp.concatenate([cosine, cosine], axis=1), (1, heads)),
        jnp.tile(jnp.concatenate([-sine, sine], axis=1), (1, heads)),
    )


def dims(lhs, rhs):
    return (((lhs,), (rhs,)), ((), ()))


def mul(a, b):
    return lax.dot_general(a, b, dims(1, 0), preferred_element_type=F32)


def mul_bt(a, b):
    return lax.dot_general(a, b, dims(1, 1), preferred_element_type=F32)


def mul_at(a, b):
    return lax.dot_general(a, b, dims(0, 0), preferred_element_type=F32)


def side_by_side(ref, *index):
    return jnp.concatenate([ref[index + (0,)], ref[index + (1,)]], axis=-1)


def pair_rows(own_ref, other_ref):
    return jnp.concatenate([own_ref[...], other_ref[...]], axis=0)


def swap_halves(values):
    lane = lax.broadcasted_iota(jnp.int32, values.shape, 1)
    span = values.shape[1]
    ahead = pltpu.roll(values, span - HD // 2, 1)
    behind = pltpu.roll(values, HD // 2, 1)
    return jnp.where(lane % HD < HD // 2, ahead, behind)


def head_only(values, head):
    lane = lax.broadcasted_iota(jnp.int32, values.shape, 1)
    return jnp.where((lane >= head * HD) & (lane < (head + 1) * HD), values, jnp.zeros_like(values))


def head_probs(query, key, bias, head):
    scores = mul_bt(head_only(query, head), key) * SCORE_SCALE + bias
    weights = jnp.exp(scores - jnp.max(scores, axis=-1, keepdims=True))
    return weights / jnp.sum(weights, axis=-1, keepdims=True)


def attn_forward_kernel(
    own_ref, other_ref, w_ref, bias_ref, cos_ref, sin_ref, q_ref, k_ref, v_ref, c_ref, mine_ref, theirs_ref
):
    rows = pair_rows(own_ref, other_ref)
    cosine, sine = cos_ref[...], sin_ref[...]
    lin = mul(rows, side_by_side(w_ref, 0))
    query = (lin * cosine + swap_halves(lin) * sine).astype(BF16)
    lin = mul(rows, side_by_side(w_ref, 1))
    key = (lin * cosine + swap_halves(lin) * sine).astype(BF16)
    value = mul(rows, side_by_side(w_ref, 2)).astype(BF16)
    q_ref[...] = query
    k_ref[...] = key
    v_ref[...] = value
    context = jnp.zeros(query.shape, F32)
    for head in range(query.shape[1] // HD):
        probs = head_probs(query, key, bias_ref[...], head)
        context = context + mul(probs.astype(BF16), head_only(value, head))
    context = context.astype(BF16)
    c_ref[...] = context
    half = own_ref.shape[0]
    for tile in range(D // TILE):
        at = pl.ds(tile * TILE, TILE)
        w_out = jnp.concatenate([w_ref[3, 0, at, :], w_ref[3, 1, at, :]], axis=-1)
        mixed = mul_bt(context, w_out)
        mine_ref[:, at] = mixed[:half]
        theirs_ref[:, at] = mixed[half:].astype(BF16)


def attn_backward_kernel(
    own_ref, other_ref, w_ref, bias_ref, cos_ref, sin_ref, q_ref, k_ref, v_ref,
    dq_ref, dk_ref, dv_ref, mine_ref, theirs_ref,
):
    rows = pair_rows(own_ref, other_ref)
    query, key, value = q_ref[...], k_ref[...], v_ref[...]
    d_context = mul(rows, side_by_side(w_ref, 3)).astype(BF16)
    d_query = jnp.zeros(query.shape, F32)
    d_key = jnp.zeros(query.shape, F32)
    d_value = jnp.zeros(query.shape, F32)
    for head in range(query.shape[1] // HD):
        probs = head_probs(query, key, bias_ref[...], head)
        d_here = head_only(d_context, head)
        d_value = d_value + mul_at(probs.astype(BF16), d_here)
        d_probs = mul_bt(d_here, value)
        inner = jnp.sum(probs * d_probs, axis=-1, keepdims=True)
        d_scores = (probs * (d_probs - inner)).astype(BF16)
        d_query = d_query + mul(d_scores, head_only(key, head))
        d_key = d_key + mul_at(d_scores, head_only(query, head))
    cosine, sine = cos_ref[...], sin_ref[...]
    d_query = d_query * SCORE_SCALE
    d_key = d_key * SCORE_SCALE
    d_query = (d_query * cosine - swap_halves(d_query) * sine).astype(BF16)
    d_key = (d_key * cosine - swap_halves(d_key) * sine).astype(BF16)
    d_value = d_value.astype(BF16)
    dq_ref[...] = d_query
    dk_ref[...] = d_key
    dv_ref[...] = d_value
    half = own_ref.shape[0]
    for tile in range(D // TILE):
        at = pl.ds(tile * TILE, TILE)
        total = jnp.zeros((2 * half, TILE), F32)
        for matrix, columns in ((0, d_query), (1, d_key), (2, d_value)):
            w_here = jnp.concatenate([w_ref[matrix, 0, at, :], w_ref[matrix, 1, at, :]], axis=-1)
            total = total + mul_bt(columns, w_here)
        mine_ref[:, at] = total[:half]
        theirs_ref[:, at] = total[half:].astype(BF16)


def mlp_half_kernel(*refs):
    rows, d_rows = refs[:8], refs[8:16]
    w_ref, hid_ref, dgate_ref, dup_ref, grad_ref = refs[16:]
    w_gate, w_up, w_down = (
        jnp.concatenate([w_ref[0, kind], w_ref[1, kind]], axis=-1) for kind in range(3)
    )
    for piece in range(4):
        here = pair_rows(rows[2 * piece], rows[2 * piece + 1])
        gate = mul(here, w_gate)
        up = mul(here, w_up)
        d_hidden = mul(pair_rows(d_rows[2 * piece], d_rows[2 * piece + 1]), w_down)
        sigmoid = 1.0 / (1.0 + jnp.exp(-gate))
        silu = gate * sigmoid
        at = pl.ds(piece * here.shape[0], here.shape[0])
        hid_ref[at, :] = (silu * up).astype(BF16)
        dgate_ref[at, :] = (d_hidden * up * sigmoid * (1.0 + gate * (1.0 - sigmoid))).astype(BF16)
        dup_ref[at, :] = (d_hidden * silu).astype(BF16)
    for tile in range(D // TILE):
        at = pl.ds(tile * TILE, TILE)
        across = jnp.concatenate([ref[:, at] for ref in rows], axis=0)
        d_across = jnp.concatenate([ref[:, at] for ref in d_rows], axis=0)
        for kind, left, right in ((0, across, dgate_ref), (1, across, dup_ref), (2, d_across, hid_ref)):
            grad = mul_at(left, right[...]).astype(BF16)
            for chip in range(2):
                grad_ref[chip, kind, at, :] = grad[:, chip * BW : (chip + 1) * BW]


def all_columns(kind, w_even, w_odd):
    return jnp.concatenate([ref[chip, kind] for ref in (w_even, w_odd) for chip in range(4)], axis=-1)


def both_columns(even, odd):
    return jnp.concatenate([even[...], odd[...]], axis=-1)


def mlp_back_kernel(dgate_even, dgate_odd, dup_even, dup_odd, w_even, w_odd, mine_ref, theirs_ref):
    total = mul_bt(both_columns(dgate_even, dgate_odd), all_columns(0, w_even, w_odd))
    total = total + mul_bt(both_columns(dup_even, dup_odd), all_columns(1, w_even, w_odd))
    half = mine_ref.shape[0]
    mine_ref[...] = total[:half]
    theirs_ref[...] = total[half:].astype(BF16)


def mlp_out_kernel(hid_even, hid_odd, w_even, w_odd, mine_ref, theirs_ref):
    total = mul_bt(both_columns(hid_even, hid_odd), all_columns(0, w_even, w_odd))
    half = mine_ref.shape[1]
    for piece in range(4):
        mine_ref[piece] = total[2 * piece * half : (2 * piece + 1) * half]
        theirs_ref[piece] = total[(2 * piece + 1) * half : 2 * (piece + 1) * half].astype(BF16)


def grads_kernel(sources, *refs):
    first, second = refs[:8], refs[8:16]
    columns = refs[16:-1]
    out_ref = refs[-1]
    row_sets = [jnp.concatenate([ref[...] for ref in part], axis=0) for part in (first, second)]
    for index, source in enumerate(sources):
        stacked = jnp.concatenate([ref[...] for ref in columns[4 * index : 4 * index + 4]], axis=0)
        grad = mul_at(row_sets[source], stacked).astype(BF16)
        for block in range(grad.shape[1] // BW):
            out_ref[index, block] = grad[:, block * BW : (block + 1) * BW]


def split(values):
    high = values.astype(BF16)
    return high, (values - high.astype(F32)).astype(BF16)


def mul_split(a, b):
    return mul(a[0], b[0]) + (mul(a[0], b[1]) + mul(a[1], b[0]))


def muon_kernel(grad_ref, momentum_ref, weight_ref, wg_ref, nm_ref, nw_ref, held, mixers):
    step = pl.program_id(0)
    count = held.shape[0]

    @pl.when(step < count)
    def _():
        grad = grad_ref[...].astype(F32)
        wg_ref[...] = grad
        block = MOMENTUM_DECAY * momentum_ref[...] + grad
        nm_ref[...] = block
        block = block * (1.0 / (jnp.sqrt(jnp.sum(block * block)) + 1e-07))
        held[step] = block
        high, low = split(block)
        cross = mul_at(high, low)
        mixers[step] = mul_at(high, high) + (cross + cross.T)

    @pl.when(step == count - 1)
    def _():
        row = lax.broadcasted_iota(jnp.int32, (BW, BW), 0)
        column = lax.broadcasted_iota(jnp.int32, (BW, BW), 1)
        eye = jnp.where(row == column, COEFF_A, 0.0).astype(F32)
        grams = [mixers[index] for index in range(count)]
        totals = [None] * count
        for turn in range(NS_ITERS):
            for index in range(count):
                pair = split(grams[index])
                mixer = eye + COEFF_B * grams[index] + COEFF_C * mul_split(pair, pair)
                mixed = split(mixer)
                if turn == 0:
                    totals[index] = mixer
                else:
                    totals[index] = mul_split(split(totals[index]), mixed)
                if turn < NS_ITERS - 1:
                    grams[index] = mul_split(split(mul_split(mixed, pair)), mixed)
        for index in range(count):
            mixers[index] = totals[index]

    @pl.when(step >= count)
    def _():
        at = step - count
        ortho = mul_split(split(held[at]), split(mixers[at]))
        nw_ref[...] = weight_ref[...].astype(F32) - (MUON_RATE * math.sqrt(D / BW)) * ortho


def deferred(kernel, inputs, unread):
    return lambda *refs: kernel(*refs[:inputs], *refs[inputs + unread :])


def unread_specs(after):
    return [pl.BlockSpec(memory_space=pl.ANY) for _ in after]


def cost(flops, accessed):
    return pl.CostEstimate(flops=flops // 6, bytes_accessed=accessed // 6, transcendentals=0)


def sort_kernel(plane_ref, *refs):
    moved, attn_ref, mlp_ref = refs[:4], refs[4], refs[5]
    for here in range(4):

        @pl.when(plane_ref[0] == here)
        def _():
            attn_ref[...] = moved[here][...]
            for kind in (1, 2, 3):
                mlp_ref[kind - 1] = moved[(here - kind) % 4][...]


def sort_kinds(plane, moved, after):
    shape = moved[0].shape
    return pl.pallas_call(
        deferred(sort_kernel, 5, len(after)),
        out_shape=(shaped(shape, BF16), shaped((3,) + shape, BF16)),
        in_specs=[pl.BlockSpec(memory_space=pltpu.SMEM)] + whole_specs(moved) + unread_specs(after),
        out_specs=tuple(whole_specs(range(2))),
        compiler_params=params(32),
        cost_estimate=cost(0, 4_000_000),
        name="sort_kinds",
    )(plane.astype(jnp.int32).reshape(1), *moved, *after)


def params(mebibytes):
    return pltpu.CompilerParams(vmem_limit_bytes=mebibytes * 1024 * 1024)


def whole_specs(arrays):
    return [pl.BlockSpec(memory_space=pltpu.VMEM) for _ in arrays]


def shaped(shape, dtype):
    return jax.ShapeDtypeStruct(shape, dtype)


def attn_forward(own, other, w_attn, bias, cosine, sine, after=()):
    half = own.shape[1]
    rows = pl.BlockSpec((None, half, D), lambda i: (0, 0, 0))
    span = w_attn.shape[1] * w_attn.shape[3]
    square = shaped((2 * half, span), BF16)
    args = (own, other, w_attn, bias, cosine, sine)
    return pl.pallas_call(
        deferred(attn_forward_kernel, len(args), len(after)),
        grid=(1,),
        out_shape=(square,) * 4 + (shaped((half, D), F32), shaped((half, D), BF16)),
        in_specs=[rows, rows] + whole_specs(args[2:]) + unread_specs(after),
        out_specs=tuple(whole_specs(range(6))),
        compiler_params=params(40),
        cost_estimate=cost(1_300_000_000, 9_000_000),
        name="attn_forward",
    )(*args, *after)


def attn_backward(own, other, w_attn, bias, cosine, sine, query, key, value):
    half = own.shape[0]
    square = shaped(query.shape, BF16)
    args = (own, other, w_attn, bias, cosine, sine, query, key, value)
    return pl.pallas_call(
        attn_backward_kernel,
        out_shape=(square,) * 3 + (shaped((half, D), F32), shaped((half, D), BF16)),
        in_specs=whole_specs(args),
        out_specs=tuple(whole_specs(range(5))),
        compiler_params=params(40),
        cost_estimate=cost(1_600_000_000, 9_000_000),
        name="attn_backward",
    )(*args)


def mlp_half(rows, pairs, w_half):
    half = rows[0].shape[0]
    columns = shaped((8 * half, 4 * BW), BF16)
    blocks = pl.BlockSpec((2, 3, D, BW), lambda j: (j, 0, 0, 0))
    return pl.pallas_call(
        mlp_half_kernel,
        grid=(2,),
        out_shape=(columns,) * 3 + (shaped(w_half.shape, BF16),),
        in_specs=[pl.BlockSpec((half, D), lambda j: (0, 0)) for _ in range(8)]
        + [pl.BlockSpec((None, half, D), lambda j: (1, 0, 0)) for _ in range(8)]
        + [blocks],
        out_specs=(pl.BlockSpec((8 * half, 2 * BW), lambda j: (0, j)),) * 3 + (blocks,),
        compiler_params=params(58),
        cost_estimate=cost(13_000_000_000, 20_000_000),
        name="mlp_half",
    )(*rows, *pairs, w_half)


def mlp_back(piece, halves, w_even, w_odd):
    rows = halves[0][0].shape[0] // 4
    wide = 2 * TILE
    args = [half[index] for index in (1, 2) for half in halves]
    tile = pl.BlockSpec((rows // 2, wide), lambda i: (0, i))
    weight = pl.BlockSpec((4, 2, wide, BW), lambda i: (0, 0, i, 0))
    return pl.pallas_call(
        mlp_back_kernel,
        grid=(D // wide,),
        out_shape=(shaped((rows // 2, D), F32), shaped((rows // 2, D), BF16)),
        in_specs=[pl.BlockSpec((rows, 4 * BW), lambda i: (piece, 0)) for _ in args] + [weight] * 2,
        out_specs=(tile,) * 2,
        compiler_params=params(58),
        cost_estimate=cost(2_200_000_000, 11_000_000),
        name="mlp_back",
    )(*args, w_even, w_odd)


def mlp_out(halves, w_even, w_odd, after):
    count = halves[0][0].shape[0]
    args = [half[0] for half in halves]
    wide = 2 * TILE
    tile = pl.BlockSpec((4, count // 8, wide), lambda i: (0, 0, i))
    weight = pl.BlockSpec((4, 1, wide, BW), lambda i: (0, 2, i, 0))
    return pl.pallas_call(
        deferred(mlp_out_kernel, 4, len(after)),
        grid=(D // wide,),
        out_shape=(shaped((4, count // 8, D), F32), shaped((4, count // 8, D), BF16)),
        in_specs=[pl.BlockSpec((count, 4 * BW), lambda i: (0, 0)) for _ in args] + [weight] * 2 + unread_specs(after),
        out_specs=(tile,) * 2,
        compiler_params=params(58),
        cost_estimate=cost(4_300_000_000, 18_000_000),
        name="mlp_out",
    )(*args, w_even, w_odd, *after)


def weight_products(pairs, rows, column_sets, sources, name, after=()):
    half = rows[0].shape[0]
    span = column_sets[0][0].shape[1]
    pair_spec = pl.BlockSpec((None, half, TILE), lambda i: (0, 0, i))
    row_spec = pl.BlockSpec((half, TILE), lambda i: (0, i))
    column_spec = pl.BlockSpec((2 * half, span), lambda i: (0, 0))
    flat = [piece for pieces in column_sets for piece in pieces]
    return pl.pallas_call(
        deferred(functools.partial(grads_kernel, sources), 16 + len(flat), len(after)),
        grid=(D // TILE,),
        out_shape=shaped((len(sources), span // BW, D, BW), BF16),
        in_specs=[pair_spec] * 8 + [row_spec] * 8 + [column_spec] * len(flat) + unread_specs(after),
        out_specs=pl.BlockSpec((len(sources), span // BW, TILE, BW), lambda i: (0, 0, i, 0)),
        compiler_params=params(60),
        cost_estimate=cost(2 * 8 * half * D * span * len(sources), 20_000_000),
        name=name,
    )(*pairs, *rows, *flat, *after)


def muon(grads, momentum, weights, offset, stride, begun=(), after=()):
    count = grads.shape[0]
    now = lambda i: jnp.minimum(i, count - 1)
    then = lambda i: jnp.maximum(i - count, 0)
    block = (None, D, BW)
    compact = pl.BlockSpec(block, lambda i: (now(i), 0, 0))
    early = pl.BlockSpec(block, lambda i: (stride * now(i) + offset, 0, 0))
    late = pl.BlockSpec(block, lambda i: (stride * then(i) + offset, 0, 0))
    return pl.pallas_call(
        deferred(muon_kernel, 3, len(begun) + len(after)),
        grid=(2 * count,),
        out_shape=(shaped(momentum.shape, F32),) * 3,
        in_specs=[compact, early, late] + unread_specs(begun) + unread_specs(after),
        out_specs=(early, early, late),
        input_output_aliases={3 + index: index for index in range(len(begun))},
        scratch_shapes=[pltpu.VMEM((count, D, BW), F32), pltpu.VMEM((count, BW, BW), F32)],
        compiler_params=params(40),
        cost_estimate=cost(1_000_000_000 * count, 5_500_000 * count),
        name="muon",
    )(grads, momentum, weights, *begun, *after)


def mirror(step):
    return [(place, place ^ step) for place in range(4)]


def ring(value, step=1):
    return lax.ppermute(value, "z", [(place, (place + step) % 4) for place in range(4)])


def swap(value):
    return lax.ppermute(value, "tensor", SWAP)


def nothing(value):
    first = value[(0,) * value.ndim].astype(F32)
    return (first * 0.0).astype(jnp.int32)


def hold(value, *others):
    zero = sum((nothing(other) for other in others), jnp.int32(0))
    return value + zero.astype(value.dtype)


def gather_rows(rows):
    mine = [rows]
    for _ in range(3):
        mine.append(ring(mine[-1]))
    return mine, [swap(part) for part in mine]


class Scatter:
    def __init__(self):
        self.moving = self.result = None
        self.payloads = []

    def add(self, step, mine, theirs):
        total = mine + swap(theirs).astype(F32)
        if self.moving is not None:
            total = total + self.moving.astype(F32)
        if step:
            self.payloads.append(total.astype(BF16))
            self.moving = ring(self.payloads[-1])
        else:
            self.result = total


def everywhere(value):
    value = value + swap(value)
    for axis in ("m", "z"):
        one, two, three = (lax.ppermute(value, axis, mirror(step)) for step in (1, 2, 3))
        value = (value + one) + (two + three)
    if lax.axis_size("r") > 1:
        value = lax.psum(value, "r")
    return value


def join(parts):
    if parts.shape[0] == 4:
        return parts
    width = parts.shape[3]
    parts = parts.reshape(4, 2, -1, D, width).transpose(0, 1, 3, 2, 4)
    return parts.reshape(4, 2, D, BW)


def unjoin(grads, width):
    if width == BW:
        return grads
    grads = grads.reshape(4, 2, D, -1, width).transpose(0, 1, 3, 2, 4)
    return grads.reshape(-1, 1, D, width)


def gather_plane(parts):
    return lax.all_gather(parts, ("m", "r"), axis=0, tiled=False)


def gather_part_direct(part, index, result):
    chip = lax.axis_index("m")
    result = lax.dynamic_update_slice(result, part[None, None], (chip, index, 0, 0))
    for step in (1, 2, 3):
        got = lax.ppermute(part, "m", mirror(step))
        result = lax.dynamic_update_slice(result, got[None, None], (chip ^ step, index, 0, 0))
    return result


def scatter_plane(grads):
    share = lax.psum_scatter(
        grads.reshape(grads.shape[0], -1, grads.shape[3]), ("m", "r"), scatter_dimension=0, tiled=False
    )
    return share.reshape(grads.shape[1:])


def scatter_plane_direct(grads):
    chip = lax.axis_index("m")

    def share_for(step):
        return lax.dynamic_index_in_dim(grads, chip ^ step, 0, keepdims=False)

    total = share_for(0).astype(F32)
    for step in (1, 2, 3):
        total = total + lax.ppermute(share_for(step), "m", mirror(step)).astype(F32)
    return total.astype(BF16)


def interleave(mine, other):
    return [rows for pair in zip(mine, other) for rows in pair]


def local(tokens, segments, weights, momentum, gains, gain_first, gain_second, cotangent):
    plane = lax.axis_index("z")
    core = lax.axis_index("tensor")
    block_count = weights.shape[0]

    if block_count == 8:
        shards = weights.reshape(4, 2, D, BW)
    else:
        width = block_count * BW // 4
        shards = weights.reshape(block_count, D, -1, width).transpose(0, 2, 1, 3).reshape(4, 1, D, width)
    parts, width = shards.shape[1], shards.shape[3]

    def shard(shift, part, *others):
        at = sum((nothing(other) for other in others), plane + shift)
        return lax.dynamic_slice(shards, (at % 4, part, 0, 0), (1, 1, D, width))[0, 0]

    rows_in = tokens.astype(F32)
    segment_own = segments.astype(F32)
    segment_parts = [segment_own] + [ring(segment_own, shift) for shift in (1, 2, 3)]
    segment_rows = jnp.concatenate(segment_parts, axis=0)
    def move(part, *others):
        return [shard(0, part)] + [ring(shard(shift, part, *others), shift) for shift in (1, 2, 3)]

    moved_even = move(0)

    def kind_part(source):
        return lax.select_n(plane, *(moved_even[(here - source) % 4] for here in range(4)))

    row_pair = lambda *others: jnp.stack([hold(rms_norm(rows_in, gains[0]), *others).astype(BF16), cotangent])
    if parts == 2:
        attn_even, mlp_even = sort_kinds(plane, moved_even, [segment_rows])
        w_attn = gather_part_direct(attn_even, 0, jnp.zeros((4, 2, D, BW), BF16))
        attn_odd, mlp_odd = sort_kinds(plane, move(1, attn_even), [w_attn])
        w_attn = gather_part_direct(attn_odd, 1, w_attn)
        w_mlp = [gather_plane(mlp_even), gather_plane(mlp_odd)]
        begun = [mlp_odd]
        first_mine, first_other = gather_rows(row_pair(attn_odd))
    else:
        w_attn = join(gather_plane(kind_part(0)[None]))
        w_mlp = gather_plane(jnp.stack([kind_part(kind) for kind in (1, 2, 3)]))
        w_mlp = jnp.stack([join(w_mlp[:, kind : kind + 1]) for kind in range(3)], axis=1)
        w_mlp = [w_mlp[:, :, 0], w_mlp[:, :, 1]]
        begun = []
        first_mine, first_other = gather_rows(row_pair())
    first_rows = interleave(first_mine, first_other)

    length = segment_rows.shape[1]
    half = length // 2
    place = jnp.arange(length)
    place = jnp.where(core == 0, place, (place + half) % length)
    segment_rows = jnp.where(core == 0, segment_rows, jnp.roll(segment_rows, half, axis=1))
    allowed = (place[None, None, :] <= place[None, :, None]) & (
        segment_rows[:, None, :] == segment_rows[:, :, None]
    )
    bias = jnp.where(allowed, 0.0, NEG_LARGE).astype(F32)
    cosine, sine = rope_tables(place)

    query, key, value, context = ([None] * 4 for _ in range(4))
    mixed = Scatter()
    for s in (1, 2, 3, 0):
        query[s], key[s], value[s], context[s], *both = attn_forward(
            first_mine[s], first_other[s], w_attn, bias[s], cosine, sine, mixed.payloads[:1] if s == 3 else begun if s == 1 else ()
        )
        mixed.add(s, *both)
    middle = rows_in + mixed.result
    two_mine, two_other = gather_rows(rms_norm(middle, gains[1]).astype(BF16))

    two_rows = interleave(two_mine, two_other)
    *even_half, grads_even = mlp_half(two_rows, first_rows, w_mlp[0])
    *odd_half, grads_odd = mlp_half(two_rows, first_rows, w_mlp[1])
    if parts == 2:
        mlp_share = [scatter_plane(grads_even), scatter_plane(grads_odd)]
    else:
        mlp_grads = jnp.stack([grads_even, grads_odd], axis=2)
        mlp_share = [
            jnp.concatenate([scatter_plane(unjoin(mlp_grads[:, kind], width)) for kind in range(3)])
        ]
    d_normed = Scatter()
    for s in (1, 2, 3, 0):
        d_normed.add(s, *mlp_back(s, (even_half, odd_half), *w_mlp))
    outward = mlp_out((even_half, odd_half), *w_mlp, d_normed.payloads[-1:])
    d_normed_two = hold(d_normed.result, outward[1])

    d_output = cotangent.astype(F32)
    d_middle_norm, d_gain_two = rms_norm_back(middle, gains[1], d_normed_two)
    d_middle = d_output + d_middle_norm
    e_mine, e_other = gather_rows(d_middle.astype(BF16))
    d_query, d_key, d_value, d_one = ([None] * 4 for _ in range(4))
    for s in range(4):
        d_query[s], d_key[s], d_value[s], *both = attn_backward(
            e_mine[s], e_other[s], w_attn, bias[s], cosine, sine, query[s], key[s], value[s]
        )
        d_one[s] = both
    attn_grads = weight_products(
        first_rows,
        interleave(e_mine, e_other),
        (d_query, d_key, d_value, context),
        (0, 0, 0, 1),
        "attn_products",
    )
    if parts == 2:
        attn_share = scatter_plane_direct(attn_grads)
    else:
        attn_share = scatter_plane(unjoin(attn_grads, width))

    last = Scatter()
    for s in (1, 2, 3, 0):
        mine, theirs = (jnp.stack([a, b[s]]) for a, b in zip(d_one[s], outward))
        if s == 2:
            mine = hold(mine, attn_grads)
        last.add(s, mine, theirs)
    d_normed_one, outward_sum = last.result
    d_rows_norm, d_gain_one = rms_norm_back(rows_in, gains[0], d_normed_one)
    input_grad = d_middle + d_rows_norm
    output = (middle + outward_sum).astype(BF16)
    gain_grads = jnp.stack([d_gain_one, d_gain_two])

    results = ()
    for part in range(parts):
        shares = jnp.concatenate([attn_share[part][None], mlp_share[part]])

        def share_of(shift):
            return lax.dynamic_index_in_dim(shares, (plane + shift) % 4, 0, keepdims=False)

        back = [share_of(0)] + [ring(share_of(shift), shift) for shift in (1, 2, 3)]
        if part == 0:
            gain_grads = everywhere(hold(gain_grads, back[1]))
        here = plane + nothing(results[1]) if part else plane
        summed = jnp.stack(
            [lax.select_n(here, *(back[(z - source) % 4] for z in range(4))) for source in range(4)]
        )
        if parts == 1:
            summed = summed.reshape(block_count, -1, D, width).transpose(0, 2, 1, 3).reshape(block_count, D, BW)
        results = muon(summed, momentum, weights, part, parts, results, (gain_grads,) if part else ())
    weight_grads, new_momentum, new_weights = results

    new_gain_first = BETA_FIRST * gain_first + (1.0 - BETA_FIRST) * gain_grads
    new_gain_second = BETA_SECOND * gain_second + (1.0 - BETA_SECOND) * gain_grads * gain_grads
    first_hat = new_gain_first / (1.0 - BETA_FIRST**STEP)
    second_hat = new_gain_second / (1.0 - BETA_SECOND**STEP)
    new_gains = gains - ADAM_RATE * first_hat / (jnp.sqrt(second_hat) + ADAM_EPS)
    return (
        output,
        input_grad,
        weight_grads,
        new_momentum,
        new_weights,
        new_gain_first,
        new_gain_second,
        new_gains,
    )


def solution(mesh):
    count = mesh.shape["dp"]
    fine = Mesh(
        np.asarray(mesh.devices).reshape(4, 4, count // 16, mesh.shape["tensor"]),
        ("z",) + PLANE,
    )
    every = ("z",) + PLANE
    in_specs = (
        P(every, None),
        P(every[:3], None),
        P(every, None, None),
        P(every, None, None),
        P(),
        P(),
        P(),
        P(every, None),
    )
    out_specs = (
        P(every, None),
        P(every, None),
        P(every, None, None),
        P(every, None, None),
        P(every, None, None),
        P(),
        P(),
        P(),
    )
    return jax.shard_map(local, mesh=fine, in_specs=in_specs, out_specs=out_specs, check_vma=False)
```

```python
import functools
import math

import jax
import jax.numpy as jnp
import numpy as np
from jax import lax
from jax.experimental import pallas as pl
from jax.experimental.pallas import tpu as pltpu
from jax.sharding import Mesh
from jax.sharding import PartitionSpec as P

D = 2048
FF = 8192
HD = 64
BW = 128
NS_ITERS = 5
STEP = 10

HIGHEST = lax.Precision.HIGHEST
ROPE_BASE = 130000.0
NORM_EPS = 1e-05
NEG_LARGE = -1e30
MOMENTUM_DECAY = 0.95
MUON_RATE = 0.25
COEFF_A = 3.4445
COEFF_B = -4.775
COEFF_C = 2.0315
BETA_FIRST = 0.9
BETA_SECOND = 0.95
ADAM_RATE = 1.0
ADAM_EPS = 1e-08

F32 = jnp.float32
BF16 = jnp.bfloat16
PLANE = ("m", "r", "tensor")
SWAP = [(0, 1), (1, 0)]
TILE = 256
SCORE_SCALE = 1.0 / math.sqrt(HD)


def rms_norm(values, gain):
    return values * lax.rsqrt(jnp.mean(values * values, axis=-1, keepdims=True) + NORM_EPS) * gain


def rms_norm_back(values, gain, grad):
    scale = lax.rsqrt(jnp.mean(values * values, axis=-1, keepdims=True) + NORM_EPS)
    scaled = gain * grad
    inner = jnp.mean(scaled * values, axis=-1, keepdims=True)
    gain_grad = jnp.sum(grad * values * scale, axis=0)
    return scale * scaled - values * (scale * scale * scale * inner), gain_grad


def rope_tables(place):
    exponent = jnp.arange(HD // 2).astype(F32) * (2.0 / HD)
    inverse = jnp.exp(-exponent * math.log(ROPE_BASE))
    angle = place.astype(F32)[:, None] * inverse[None, :]
    cosine, sine = jnp.cos(angle), jnp.sin(angle)
    heads = 2 * BW // HD
    return (
        jnp.tile(jnp.concatenate([cosine, cosine], axis=1), (1, heads)),
        jnp.tile(jnp.concatenate([-sine, sine], axis=1), (1, heads)),
    )


def dims(lhs, rhs):
    return (((lhs,), (rhs,)), ((), ()))


def mul(a, b):
    return lax.dot_general(a, b, dims(1, 0), preferred_element_type=F32)


def mul_bt(a, b):
    return lax.dot_general(a, b, dims(1, 1), preferred_element_type=F32)


def mul_at(a, b):
    return lax.dot_general(a, b, dims(0, 0), preferred_element_type=F32)


def side_by_side(ref, *index):
    return jnp.concatenate([ref[index + (0,)], ref[index + (1,)]], axis=-1)


def pair_rows(own_ref, other_ref):
    return jnp.concatenate([own_ref[...], other_ref[...]], axis=0)


def swap_halves(values):
    lane = lax.broadcasted_iota(jnp.int32, values.shape, 1)
    span = values.shape[1]
    ahead = pltpu.roll(values, span - HD // 2, 1)
    behind = pltpu.roll(values, HD // 2, 1)
    return jnp.where(lane % HD < HD // 2, ahead, behind)


def head_only(values, head):
    lane = lax.broadcasted_iota(jnp.int32, values.shape, 1)
    return jnp.where((lane >= head * HD) & (lane < (head + 1) * HD), values, jnp.zeros_like(values))


def head_probs(query, key, bias, head):
    scores = mul_bt(head_only(query, head), key) * SCORE_SCALE + bias
    weights = jnp.exp(scores - jnp.max(scores, axis=-1, keepdims=True))
    return weights / jnp.sum(weights, axis=-1, keepdims=True)


def attn_forward_kernel(
    own_ref, other_ref, w_ref, bias_ref, cos_ref, sin_ref, q_ref, k_ref, v_ref, c_ref, mine_ref, theirs_ref
):
    rows = pair_rows(own_ref, other_ref)
    cosine, sine = cos_ref[...], sin_ref[...]
    lin = mul(rows, side_by_side(w_ref, 0))
    query = (lin * cosine + swap_halves(lin) * sine).astype(BF16)
    lin = mul(rows, side_by_side(w_ref, 1))
    key = (lin * cosine + swap_halves(lin) * sine).astype(BF16)
    value = mul(rows, side_by_side(w_ref, 2)).astype(BF16)
    q_ref[...] = query
    k_ref[...] = key
    v_ref[...] = value
    context = jnp.zeros(query.shape, F32)
    for head in range(query.shape[1] // HD):
        probs = head_probs(query, key, bias_ref[...], head)
        context = context + mul(probs.astype(BF16), head_only(value, head))
    context = context.astype(BF16)
    c_ref[...] = context
    half = own_ref.shape[0]
    for tile in range(D // TILE):
        at = pl.ds(tile * TILE, TILE)
        w_out = jnp.concatenate([w_ref[3, 0, at, :], w_ref[3, 1, at, :]], axis=-1)
        mixed = mul_bt(context, w_out)
        mine_ref[:, at] = mixed[:half]
        theirs_ref[:, at] = mixed[half:].astype(BF16)


def attn_backward_kernel(
    own_ref, other_ref, own_normed, other_normed, w_ref, bias_ref, cos_ref, sin_ref, q_ref, k_ref, v_ref,
    dq_ref, dk_ref, dv_ref, mine_ref, theirs_ref, gain_ref,
):
    rows = pair_rows(own_ref, other_ref)
    query, key, value = q_ref[...], k_ref[...], v_ref[...]
    d_context = mul(rows, side_by_side(w_ref, 3)).astype(BF16)
    d_query = jnp.zeros(query.shape, F32)
    d_key = jnp.zeros(query.shape, F32)
    d_value = jnp.zeros(query.shape, F32)
    for head in range(query.shape[1] // HD):
        probs = head_probs(query, key, bias_ref[...], head)
        d_here = head_only(d_context, head)
        d_value = d_value + mul_at(probs.astype(BF16), d_here)
        d_probs = mul_bt(d_here, value)
        inner = jnp.sum(probs * d_probs, axis=-1, keepdims=True)
        d_scores = (probs * (d_probs - inner)).astype(BF16)
        d_query = d_query + mul(d_scores, head_only(key, head))
        d_key = d_key + mul_at(d_scores, head_only(query, head))
    cosine, sine = cos_ref[...], sin_ref[...]
    d_query = d_query * SCORE_SCALE
    d_key = d_key * SCORE_SCALE
    d_query = (d_query * cosine - swap_halves(d_query) * sine).astype(BF16)
    d_key = (d_key * cosine - swap_halves(d_key) * sine).astype(BF16)
    d_value = d_value.astype(BF16)
    dq_ref[...] = d_query
    dk_ref[...] = d_key
    dv_ref[...] = d_value
    half = own_ref.shape[0]
    for tile in range(D // TILE):
        at = pl.ds(tile * TILE, TILE)
        total = jnp.zeros((2 * half, TILE), F32)
        for matrix, columns in ((0, d_query), (1, d_key), (2, d_value)):
            w_here = jnp.concatenate([w_ref[matrix, 0, at, :], w_ref[matrix, 1, at, :]], axis=-1)
            total = total + mul_bt(columns, w_here)
        normed = jnp.concatenate([own_normed[:, at], other_normed[:, at]], axis=0).astype(F32)
        gain_ref[:, at] = jnp.sum(total * normed, axis=0, keepdims=True)
        mine_ref[:, at] = total[:half]
        theirs_ref[:, at] = total[half:].astype(BF16)


def mlp_half_kernel(*refs):
    rows, d_rows = refs[:8], refs[8:16]
    w_ref, hid_ref, dgate_ref, dup_ref, grad_ref = refs[16:]
    w_gate, w_up, w_down = (
        jnp.concatenate([w_ref[0, kind], w_ref[1, kind]], axis=-1) for kind in range(3)
    )
    for piece in range(4):
        here = pair_rows(rows[2 * piece], rows[2 * piece + 1])
        gate = mul(here, w_gate)
        up = mul(here, w_up)
        d_hidden = mul(pair_rows(d_rows[2 * piece], d_rows[2 * piece + 1]), w_down)
        sigmoid = 1.0 / (1.0 + jnp.exp(-gate))
        silu = gate * sigmoid
        at = pl.ds(piece * here.shape[0], here.shape[0])
        hid_ref[at, :] = (silu * up).astype(BF16)
        dgate_ref[at, :] = (d_hidden * up * sigmoid * (1.0 + gate * (1.0 - sigmoid))).astype(BF16)
        dup_ref[at, :] = (d_hidden * silu).astype(BF16)
    for tile in range(D // TILE):
        at = pl.ds(tile * TILE, TILE)
        across = jnp.concatenate([ref[:, at] for ref in rows], axis=0)
        d_across = jnp.concatenate([ref[:, at] for ref in d_rows], axis=0)
        for kind, left, right in ((0, across, dgate_ref), (1, across, dup_ref), (2, d_across, hid_ref)):
            grad = mul_at(left, right[...]).astype(BF16)
            for chip in range(2):
                grad_ref[chip, kind, at, :] = grad[:, chip * BW : (chip + 1) * BW]


def all_columns(kind, w_even, w_odd):
    return jnp.concatenate([ref[chip, kind] for ref in (w_even, w_odd) for chip in range(4)], axis=-1)


def both_columns(even, odd):
    return jnp.concatenate([even[...], odd[...]], axis=-1)


def mlp_back_kernel(dgate_even, dgate_odd, dup_even, dup_odd, w_even, w_odd, mine_ref, theirs_ref):
    total = mul_bt(both_columns(dgate_even, dgate_odd), all_columns(0, w_even, w_odd))
    total = total + mul_bt(both_columns(dup_even, dup_odd), all_columns(1, w_even, w_odd))
    half = mine_ref.shape[0]
    mine_ref[...] = total[:half]
    theirs_ref[...] = total[half:].astype(BF16)


def mlp_out_kernel(hid_even, hid_odd, w_even, w_odd, mine_ref, theirs_ref):
    total = mul_bt(both_columns(hid_even, hid_odd), all_columns(0, w_even, w_odd))
    half = mine_ref.shape[1]
    for piece in range(4):
        mine_ref[piece] = total[2 * piece * half : (2 * piece + 1) * half]
        theirs_ref[piece] = total[(2 * piece + 1) * half : 2 * (piece + 1) * half].astype(BF16)


def grads_kernel(sources, *refs):
    first, second = refs[:8], refs[8:16]
    columns = refs[16:-1]
    out_ref = refs[-1]
    row_sets = [jnp.concatenate([ref[...] for ref in part], axis=0) for part in (first, second)]
    for index, source in enumerate(sources):
        stacked = jnp.concatenate([ref[...] for ref in columns[4 * index : 4 * index + 4]], axis=0)
        grad = mul_at(row_sets[source], stacked).astype(BF16)
        for block in range(grad.shape[1] // BW):
            out_ref[index, block] = grad[:, block * BW : (block + 1) * BW]


def split(values):
    high = values.astype(BF16)
    return high, (values - high.astype(F32)).astype(BF16)


def mul_split(a, b):
    return mul(a[0], b[0]) + (mul(a[0], b[1]) + mul(a[1], b[0]))


def muon_kernel(grad_ref, momentum_ref, weight_ref, wg_ref, nm_ref, nw_ref, held, mixers):
    step = pl.program_id(0)
    count = held.shape[0]

    @pl.when(step < count)
    def _():
        grad = grad_ref[...].astype(F32)
        wg_ref[...] = grad
        block = MOMENTUM_DECAY * momentum_ref[...] + grad
        nm_ref[...] = block
        block = block * (1.0 / (jnp.sqrt(jnp.sum(block * block)) + 1e-07))
        held[step] = block
        high, low = split(block)
        cross = mul_at(high, low)
        mixers[step] = mul_at(high, high) + (cross + cross.T)

    @pl.when(step == count - 1)
    def _():
        row = lax.broadcasted_iota(jnp.int32, (BW, BW), 0)
        column = lax.broadcasted_iota(jnp.int32, (BW, BW), 1)
        eye = jnp.where(row == column, COEFF_A, 0.0).astype(F32)
        grams = [mixers[index] for index in range(count)]
        totals = [None] * count
        for turn in range(NS_ITERS):
            for index in range(count):
                pair = split(grams[index])
                mixer = eye + COEFF_B * grams[index] + COEFF_C * mul_split(pair, pair)
                mixed = split(mixer)
                if turn == 0:
                    totals[index] = mixer
                else:
                    totals[index] = mul_split(split(totals[index]), mixed)
                if turn < NS_ITERS - 1:
                    grams[index] = mul_split(split(mul_split(mixed, pair)), mixed)
        for index in range(count):
            mixers[index] = totals[index]

    @pl.when(step >= count)
    def _():
        at = step - count
        ortho = mul_split(split(held[at]), split(mixers[at]))
        nw_ref[...] = weight_ref[...].astype(F32) - (MUON_RATE * math.sqrt(D / BW)) * ortho


def deferred(kernel, inputs, unread):
    return lambda *refs: kernel(*refs[:inputs], *refs[inputs + unread :])


def unread_specs(after):
    return [pl.BlockSpec(memory_space=pl.ANY) for _ in after]


def cost(flops, accessed):
    return pl.CostEstimate(flops=flops // 6, bytes_accessed=accessed // 6, transcendentals=0)


def sort_kernel(plane_ref, *refs):
    moved, attn_ref, mlp_ref = refs[:4], refs[4], refs[5]
    for here in range(4):

        @pl.when(plane_ref[0] == here)
        def _():
            attn_ref[...] = moved[here][...]
            for kind in (1, 2, 3):
                mlp_ref[kind - 1] = moved[(here - kind) % 4][...]


def sort_kinds(plane, moved, after):
    shape = moved[0].shape
    return pl.pallas_call(
        deferred(sort_kernel, 5, len(after)),
        out_shape=(shaped(shape, BF16), shaped((3,) + shape, BF16)),
        in_specs=[pl.BlockSpec(memory_space=pltpu.SMEM)] + whole_specs(moved) + unread_specs(after),
        out_specs=tuple(whole_specs(range(2))),
        compiler_params=params(32),
        cost_estimate=cost(0, 4_000_000),
        name="sort_kinds",
    )(plane.astype(jnp.int32).reshape(1), *moved, *after)


def params(mebibytes):
    return pltpu.CompilerParams(vmem_limit_bytes=mebibytes * 1024 * 1024)


def whole_specs(arrays):
    return [pl.BlockSpec(memory_space=pltpu.VMEM) for _ in arrays]


def shaped(shape, dtype):
    return jax.ShapeDtypeStruct(shape, dtype)


def attn_forward(own, other, w_attn, bias, cosine, sine, after=()):
    half = own.shape[1]
    rows = pl.BlockSpec((None, half, D), lambda i: (0, 0, 0))
    span = w_attn.shape[1] * w_attn.shape[3]
    square = shaped((2 * half, span), BF16)
    args = (own, other, w_attn, bias, cosine, sine)
    return pl.pallas_call(
        deferred(attn_forward_kernel, len(args), len(after)),
        grid=(1,),
        out_shape=(square,) * 4 + (shaped((half, D), F32), shaped((half, D), BF16)),
        in_specs=[rows, rows] + whole_specs(args[2:]) + unread_specs(after),
        out_specs=tuple(whole_specs(range(6))),
        compiler_params=params(40),
        cost_estimate=cost(1_300_000_000, 9_000_000),
        name="attn_forward",
    )(*args, *after)


def attn_backward(own, other, own_pair, other_pair, w_attn, bias, cosine, sine, query, key, value):
    half = own.shape[0]
    square = shaped(query.shape, BF16)
    rows = pl.BlockSpec((None, half, D), lambda i: (0, 0, 0))
    args = (own, other, own_pair, other_pair, w_attn, bias, cosine, sine, query, key, value)
    return pl.pallas_call(
        attn_backward_kernel,
        grid=(1,),
        out_shape=(square,) * 3 + (shaped((half, D), F32), shaped((half, D), BF16), shaped((1, D), F32)),
        in_specs=whole_specs(args[:2]) + [rows, rows] + whole_specs(args[4:]),
        out_specs=tuple(whole_specs(range(6))),
        compiler_params=params(40),
        cost_estimate=cost(1_600_000_000, 9_000_000),
        name="attn_backward",
    )(*args)


def mlp_half(rows, pairs, w_half):
    half = rows[0].shape[0]
    columns = shaped((8 * half, 4 * BW), BF16)
    blocks = pl.BlockSpec((2, 3, D, BW), lambda j: (j, 0, 0, 0))
    return pl.pallas_call(
        mlp_half_kernel,
        grid=(2,),
        out_shape=(columns,) * 3 + (shaped(w_half.shape, BF16),),
        in_specs=[pl.BlockSpec((half, D), lambda j: (0, 0)) for _ in range(8)]
        + [pl.BlockSpec((None, half, D), lambda j: (1, 0, 0)) for _ in range(8)]
        + [blocks],
        out_specs=(pl.BlockSpec((8 * half, 2 * BW), lambda j: (0, j)),) * 3 + (blocks,),
        compiler_params=params(58),
        cost_estimate=cost(13_000_000_000, 20_000_000),
        name="mlp_half",
    )(*rows, *pairs, w_half)


def mlp_back(piece, halves, w_even, w_odd):
    rows = halves[0][0].shape[0] // 4
    wide = 2 * TILE
    args = [half[index] for index in (1, 2) for half in halves]
    tile = pl.BlockSpec((rows // 2, wide), lambda i: (0, i))
    weight = pl.BlockSpec((4, 2, wide, BW), lambda i: (0, 0, i, 0))
    return pl.pallas_call(
        mlp_back_kernel,
        grid=(D // wide,),
        out_shape=(shaped((rows // 2, D), F32), shaped((rows // 2, D), BF16)),
        in_specs=[pl.BlockSpec((rows, 4 * BW), lambda i: (piece, 0)) for _ in args] + [weight] * 2,
        out_specs=(tile,) * 2,
        compiler_params=params(58),
        cost_estimate=cost(2_200_000_000, 11_000_000),
        name="mlp_back",
    )(*args, w_even, w_odd)


def mlp_out(halves, w_even, w_odd, after):
    count = halves[0][0].shape[0]
    args = [half[0] for half in halves]
    wide = 2 * TILE
    tile = pl.BlockSpec((4, count // 8, wide), lambda i: (0, 0, i))
    weight = pl.BlockSpec((4, 1, wide, BW), lambda i: (0, 2, i, 0))
    return pl.pallas_call(
        deferred(mlp_out_kernel, 4, len(after)),
        grid=(D // wide,),
        out_shape=(shaped((4, count // 8, D), F32), shaped((4, count // 8, D), BF16)),
        in_specs=[pl.BlockSpec((count, 4 * BW), lambda i: (0, 0)) for _ in args] + [weight] * 2 + unread_specs(after),
        out_specs=(tile,) * 2,
        compiler_params=params(58),
        cost_estimate=cost(4_300_000_000, 18_000_000),
        name="mlp_out",
    )(*args, w_even, w_odd, *after)


def weight_products(pairs, rows, column_sets, sources, name, after=()):
    half = rows[0].shape[0]
    span = column_sets[0][0].shape[1]
    pair_spec = pl.BlockSpec((None, half, TILE), lambda i: (0, 0, i))
    row_spec = pl.BlockSpec((half, TILE), lambda i: (0, i))
    column_spec = pl.BlockSpec((2 * half, span), lambda i: (0, 0))
    flat = [piece for pieces in column_sets for piece in pieces]
    return pl.pallas_call(
        deferred(functools.partial(grads_kernel, sources), 16 + len(flat), len(after)),
        grid=(D // TILE,),
        out_shape=shaped((len(sources), span // BW, D, BW), BF16),
        in_specs=[pair_spec] * 8 + [row_spec] * 8 + [column_spec] * len(flat) + unread_specs(after),
        out_specs=pl.BlockSpec((len(sources), span // BW, TILE, BW), lambda i: (0, 0, i, 0)),
        compiler_params=params(60),
        cost_estimate=cost(2 * 8 * half * D * span * len(sources), 20_000_000),
        name=name,
    )(*pairs, *rows, *flat, *after)


def muon(grads, momentum, weights, offset, stride, begun=(), after=()):
    count = grads.shape[0]
    now = lambda i: jnp.minimum(i, count - 1)
    then = lambda i: jnp.maximum(i - count, 0)
    block = (None, D, BW)
    compact = pl.BlockSpec(block, lambda i: (now(i), 0, 0))
    early = pl.BlockSpec(block, lambda i: (stride * now(i) + offset, 0, 0))
    late = pl.BlockSpec(block, lambda i: (stride * then(i) + offset, 0, 0))
    return pl.pallas_call(
        deferred(muon_kernel, 3, len(begun) + len(after)),
        grid=(2 * count,),
        out_shape=(shaped(momentum.shape, F32),) * 3,
        in_specs=[compact, early, late] + unread_specs(begun) + unread_specs(after),
        out_specs=(early, early, late),
        input_output_aliases={3 + index: index for index in range(len(begun))},
        scratch_shapes=[pltpu.VMEM((count, D, BW), F32), pltpu.VMEM((count, BW, BW), F32)],
        compiler_params=params(40),
        cost_estimate=cost(1_000_000_000 * count, 5_500_000 * count),
        name="muon",
    )(grads, momentum, weights, *begun, *after)


def mirror(step):
    return [(place, place ^ step) for place in range(4)]


def ring(value, step=1):
    return lax.ppermute(value, "z", [(place, (place + step) % 4) for place in range(4)])


def swap(value):
    return lax.ppermute(value, "tensor", SWAP)


def nothing(value):
    first = value[(0,) * value.ndim].astype(F32)
    return (first * 0.0).astype(jnp.int32)


def hold(value, *others):
    zero = sum((nothing(other) for other in others), jnp.int32(0))
    return value + zero.astype(value.dtype)


def gather_rows(rows):
    mine = [rows]
    for _ in range(3):
        mine.append(ring(mine[-1]))
    return mine, [swap(part) for part in mine]


class Scatter:
    def __init__(self):
        self.moving = self.result = None
        self.payloads = []

    def add(self, step, mine, theirs):
        total = mine + swap(theirs).astype(F32)
        if self.moving is not None:
            total = total + self.moving.astype(F32)
        if step:
            self.payloads.append(total.astype(BF16))
            self.moving = ring(self.payloads[-1])
        else:
            self.result = total


def everywhere(value):
    value = value + swap(value)
    for axis in ("m", "z"):
        one, two, three = (lax.ppermute(value, axis, mirror(step)) for step in (1, 2, 3))
        value = (value + one) + (two + three)
    if lax.axis_size("r") > 1:
        value = lax.psum(value, "r")
    return value


def join(parts):
    if parts.shape[0] == 4:
        return parts
    width = parts.shape[3]
    parts = parts.reshape(4, 2, -1, D, width).transpose(0, 1, 3, 2, 4)
    return parts.reshape(4, 2, D, BW)


def unjoin(grads, width):
    if width == BW:
        return grads
    grads = grads.reshape(4, 2, D, -1, width).transpose(0, 1, 3, 2, 4)
    return grads.reshape(-1, 1, D, width)


def gather_plane(parts):
    return lax.all_gather(parts, ("m", "r"), axis=0, tiled=False)


def gather_part_direct(part, index, result):
    chip = lax.axis_index("m")
    result = lax.dynamic_update_slice(result, part[None, None], (chip, index, 0, 0))
    for step in (1, 2, 3):
        got = lax.ppermute(part, "m", mirror(step))
        result = lax.dynamic_update_slice(result, got[None, None], (chip ^ step, index, 0, 0))
    return result


def scatter_plane(grads):
    share = lax.psum_scatter(
        grads.reshape(grads.shape[0], -1, grads.shape[3]), ("m", "r"), scatter_dimension=0, tiled=False
    )
    return share.reshape(grads.shape[1:])


def scatter_plane_direct(grads, other):
    chip = lax.axis_index("m")

    def share_for(step):
        return lax.dynamic_index_in_dim(grads, chip ^ step, 0, keepdims=False)

    total = hold(share_for(0).astype(F32), other)
    for step in (1, 2, 3):
        total = total + lax.ppermute(share_for(step), "m", mirror(step)).astype(F32)
    return total.astype(BF16)


def interleave(mine, other):
    return [rows for pair in zip(mine, other) for rows in pair]


def local(tokens, segments, weights, momentum, gains, gain_first, gain_second, cotangent):
    plane = lax.axis_index("z")
    core = lax.axis_index("tensor")
    block_count = weights.shape[0]

    if block_count == 8:
        shards = weights.reshape(4, 2, D, BW)
    else:
        width = block_count * BW // 4
        shards = weights.reshape(block_count, D, -1, width).transpose(0, 2, 1, 3).reshape(4, 1, D, width)
    parts, width = shards.shape[1], shards.shape[3]

    def shard(shift, part, *others):
        at = sum((nothing(other) for other in others), plane + shift)
        return lax.dynamic_slice(shards, (at % 4, part, 0, 0), (1, 1, D, width))[0, 0]

    rows_in = tokens.astype(F32)
    segment_own = segments.astype(F32)
    segment_parts = [segment_own] + [ring(segment_own, shift) for shift in (1, 2, 3)]
    segment_rows = jnp.concatenate(segment_parts, axis=0)
    def move(part, *others):
        return [shard(0, part)] + [ring(shard(shift, part, *others), shift) for shift in (1, 2, 3)]

    moved_even = move(0)

    def kind_part(source):
        return lax.select_n(plane, *(moved_even[(here - source) % 4] for here in range(4)))

    row_pair = lambda *others: jnp.stack([hold(rms_norm(rows_in, gains[0]), *others).astype(BF16), cotangent])
    if parts == 2:
        attn_even, mlp_even = sort_kinds(plane, moved_even, [segment_rows])
        w_attn = gather_part_direct(attn_even, 0, jnp.zeros((4, 2, D, BW), BF16))
        attn_odd, mlp_odd = sort_kinds(plane, move(1, attn_even), [w_attn])
        w_attn = gather_part_direct(attn_odd, 1, w_attn)
        w_mlp = [gather_plane(mlp_even), gather_plane(mlp_odd)]
        begun = [mlp_odd]
        first_mine, first_other = gather_rows(row_pair(attn_odd))
    else:
        w_attn = join(gather_plane(kind_part(0)[None]))
        w_mlp = gather_plane(jnp.stack([kind_part(kind) for kind in (1, 2, 3)]))
        w_mlp = jnp.stack([join(w_mlp[:, kind : kind + 1]) for kind in range(3)], axis=1)
        w_mlp = [w_mlp[:, :, 0], w_mlp[:, :, 1]]
        begun = []
        first_mine, first_other = gather_rows(row_pair())
    first_rows = interleave(first_mine, first_other)

    length = segment_rows.shape[1]
    half = length // 2
    place = jnp.arange(length)
    place = jnp.where(core == 0, place, (place + half) % length)
    segment_rows = jnp.where(core == 0, segment_rows, jnp.roll(segment_rows, half, axis=1))
    allowed = (place[None, None, :] <= place[None, :, None]) & (
        segment_rows[:, None, :] == segment_rows[:, :, None]
    )
    bias = jnp.where(allowed, 0.0, NEG_LARGE).astype(F32)
    cosine, sine = rope_tables(place)

    query, key, value, context = ([None] * 4 for _ in range(4))
    mixed = Scatter()
    for s in (1, 2, 3, 0):
        query[s], key[s], value[s], context[s], *both = attn_forward(
            first_mine[s], first_other[s], w_attn, bias[s], cosine, sine, mixed.payloads[:1] if s == 3 else begun if s == 1 else ()
        )
        mixed.add(s, *both)
    middle = rows_in + mixed.result
    two_mine, two_other = gather_rows(rms_norm(middle, gains[1]).astype(BF16))

    two_rows = interleave(two_mine, two_other)
    *even_half, grads_even = mlp_half(two_rows, first_rows, w_mlp[0])
    *odd_half, grads_odd = mlp_half(two_rows, first_rows, w_mlp[1])
    if parts == 2:
        mlp_share = [scatter_plane(grads_even), scatter_plane(grads_odd)]
    else:
        mlp_grads = jnp.stack([grads_even, grads_odd], axis=2)
        mlp_share = [
            jnp.concatenate([scatter_plane(unjoin(mlp_grads[:, kind], width)) for kind in range(3)])
        ]
    d_normed = Scatter()
    for s in (1, 2, 3, 0):
        d_normed.add(s, *mlp_back(s, (even_half, odd_half), *w_mlp))
    outward = mlp_out((even_half, odd_half), *w_mlp, d_normed.payloads[-1:])
    d_normed_two = hold(d_normed.result, outward[1])

    d_output = cotangent.astype(F32)
    d_middle_norm, d_gain_two = rms_norm_back(middle, gains[1], d_normed_two)
    d_middle = d_output + d_middle_norm
    e_mine, e_other = gather_rows(d_middle.astype(BF16))
    d_query, d_key, d_value, d_one, gain_parts = ([None] * 4 for _ in range(5))
    for s in range(4):
        d_query[s], d_key[s], d_value[s], *both, gain_parts[s] = attn_backward(
            e_mine[s], e_other[s], first_mine[s], first_other[s], w_attn, bias[s], cosine, sine, query[s], key[s], value[s]
        )
        d_one[s] = both
    attn_grads = weight_products(
        first_rows,
        interleave(e_mine, e_other),
        (d_query, d_key, d_value, context),
        (0, 0, 0, 1),
        "attn_products",
    )
    d_gain_one = ((gain_parts[0] + gain_parts[1]) + (gain_parts[2] + gain_parts[3]))[0] / gains[0]
    gain_grads = everywhere(jnp.stack([d_gain_one, d_gain_two]))
    if parts == 2:
        attn_share = scatter_plane_direct(attn_grads, gain_grads)
    else:
        attn_share = scatter_plane(unjoin(attn_grads, width))

    last = Scatter()
    for s in (1, 2, 3, 0):
        mine, theirs = (jnp.stack([a, b[s]]) for a, b in zip(d_one[s], outward))
        if s == 2:
            mine = hold(mine, attn_grads)
        last.add(s, mine, theirs)
    d_normed_one, outward_sum = last.result
    d_rows_norm, _ = rms_norm_back(rows_in, gains[0], d_normed_one)
    input_grad = d_middle + d_rows_norm
    output = (middle + outward_sum).astype(BF16)

    results = ()
    for part in range(parts):
        shares = jnp.concatenate([attn_share[part][None], mlp_share[part]])

        def share_of(shift):
            return lax.dynamic_index_in_dim(shares, (plane + shift) % 4, 0, keepdims=False)

        back = [share_of(0)] + [ring(share_of(shift), shift) for shift in (1, 2, 3)]
        here = plane + nothing(results[1]) if part else plane
        summed = jnp.stack(
            [lax.select_n(here, *(back[(z - source) % 4] for z in range(4))) for source in range(4)]
        )
        if parts == 1:
            summed = summed.reshape(block_count, -1, D, width).transpose(0, 2, 1, 3).reshape(block_count, D, BW)
        results = muon(summed, momentum, weights, part, parts, results)
    weight_grads, new_momentum, new_weights = results

    new_gain_first = BETA_FIRST * gain_first + (1.0 - BETA_FIRST) * gain_grads
    new_gain_second = BETA_SECOND * gain_second + (1.0 - BETA_SECOND) * gain_grads * gain_grads
    first_hat = new_gain_first / (1.0 - BETA_FIRST**STEP)
    second_hat = new_gain_second / (1.0 - BETA_SECOND**STEP)
    new_gains = gains - ADAM_RATE * first_hat / (jnp.sqrt(second_hat) + ADAM_EPS)
    return (
        output,
        input_grad,
        weight_grads,
        new_momentum,
        new_weights,
        new_gain_first,
        new_gain_second,
        new_gains,
    )


def solution(mesh):
    count = mesh.shape["dp"]
    fine = Mesh(
        np.asarray(mesh.devices).reshape(4, 4, count // 16, mesh.shape["tensor"]),
        ("z",) + PLANE,
    )
    every = ("z",) + PLANE
    in_specs = (
        P(every, None),
        P(every[:3], None),
        P(every, None, None),
        P(every, None, None),
        P(),
        P(),
        P(),
        P(every, None),
    )
    out_specs = (
        P(every, None),
        P(every, None),
        P(every, None, None),
        P(every, None, None),
        P(every, None, None),
        P(),
        P(),
        P(),
    )
    return jax.shard_map(local, mesh=fine, in_specs=in_specs, out_specs=out_specs, check_vma=False)
```

```python
import functools
import math

import jax
import jax.numpy as jnp
import numpy as np
from jax import lax
from jax.experimental import pallas as pl
from jax.experimental.pallas import tpu as pltpu
from jax.sharding import Mesh
from jax.sharding import PartitionSpec as P

D = 2048
FF = 8192
HD = 64
BW = 128
NS_ITERS = 5
STEP = 10

HIGHEST = lax.Precision.HIGHEST
ROPE_BASE = 130000.0
NORM_EPS = 1e-05
NEG_LARGE = -1e30
MOMENTUM_DECAY = 0.95
MUON_RATE = 0.25
COEFF_A = 3.4445
COEFF_B = -4.775
COEFF_C = 2.0315
BETA_FIRST = 0.9
BETA_SECOND = 0.95
ADAM_RATE = 1.0
ADAM_EPS = 1e-08

F32 = jnp.float32
BF16 = jnp.bfloat16
PLANE = ("m", "r", "tensor")
SWAP = [(0, 1), (1, 0)]
TILE = 256
SCORE_SCALE = 1.0 / math.sqrt(HD)


def rms_norm(values, gain):
    return values * lax.rsqrt(jnp.mean(values * values, axis=-1, keepdims=True) + NORM_EPS) * gain


def rms_norm_back(values, gain, grad):
    scale = lax.rsqrt(jnp.mean(values * values, axis=-1, keepdims=True) + NORM_EPS)
    scaled = gain * grad
    inner = jnp.mean(scaled * values, axis=-1, keepdims=True)
    gain_grad = jnp.sum(grad * values * scale, axis=0)
    return scale * scaled - values * (scale * scale * scale * inner), gain_grad


def rope_tables(place):
    exponent = jnp.arange(HD // 2).astype(F32) * (2.0 / HD)
    inverse = jnp.exp(-exponent * math.log(ROPE_BASE))
    angle = place.astype(F32)[:, None] * inverse[None, :]
    cosine, sine = jnp.cos(angle), jnp.sin(angle)
    heads = 2 * BW // HD
    return (
        jnp.tile(jnp.concatenate([cosine, cosine], axis=1), (1, heads)),
        jnp.tile(jnp.concatenate([-sine, sine], axis=1), (1, heads)),
    )


def dims(lhs, rhs):
    return (((lhs,), (rhs,)), ((), ()))


def mul(a, b):
    return lax.dot_general(a, b, dims(1, 0), preferred_element_type=F32)


def mul_bt(a, b):
    return lax.dot_general(a, b, dims(1, 1), preferred_element_type=F32)


def mul_at(a, b):
    return lax.dot_general(a, b, dims(0, 0), preferred_element_type=F32)


def side_by_side(ref, *index):
    return jnp.concatenate([ref[index + (0,)], ref[index + (1,)]], axis=-1)


def pair_rows(own_ref, other_ref):
    return jnp.concatenate([own_ref[...], other_ref[...]], axis=0)


def swap_halves(values):
    lane = lax.broadcasted_iota(jnp.int32, values.shape, 1)
    span = values.shape[1]
    ahead = pltpu.roll(values, span - HD // 2, 1)
    behind = pltpu.roll(values, HD // 2, 1)
    return jnp.where(lane % HD < HD // 2, ahead, behind)


def head_only(values, head):
    lane = lax.broadcasted_iota(jnp.int32, values.shape, 1)
    return jnp.where((lane >= head * HD) & (lane < (head + 1) * HD), values, jnp.zeros_like(values))


def head_probs(query, key, bias, head):
    scores = mul_bt(head_only(query, head), key) * SCORE_SCALE + bias
    weights = jnp.exp(scores - jnp.max(scores, axis=-1, keepdims=True))
    return weights / jnp.sum(weights, axis=-1, keepdims=True)


def attn_forward_kernel(
    own_ref, other_ref, w_ref, bias_ref, cos_ref, sin_ref, q_ref, k_ref, v_ref, c_ref, mine_ref, theirs_ref
):
    rows = pair_rows(own_ref, other_ref)
    cosine, sine = cos_ref[...], sin_ref[...]
    lin = mul(rows, side_by_side(w_ref, 0))
    query = (lin * cosine + swap_halves(lin) * sine).astype(BF16)
    lin = mul(rows, side_by_side(w_ref, 1))
    key = (lin * cosine + swap_halves(lin) * sine).astype(BF16)
    value = mul(rows, side_by_side(w_ref, 2)).astype(BF16)
    q_ref[...] = query
    k_ref[...] = key
    v_ref[...] = value
    context = jnp.zeros(query.shape, F32)
    for head in range(query.shape[1] // HD):
        probs = head_probs(query, key, bias_ref[...], head)
        context = context + mul(probs.astype(BF16), head_only(value, head))
    context = context.astype(BF16)
    c_ref[...] = context
    half = own_ref.shape[0]
    for tile in range(D // TILE):
        at = pl.ds(tile * TILE, TILE)
        w_out = jnp.concatenate([w_ref[3, 0, at, :], w_ref[3, 1, at, :]], axis=-1)
        mixed = mul_bt(context, w_out)
        mine_ref[:, at] = mixed[:half]
        theirs_ref[:, at] = mixed[half:].astype(BF16)


def attn_backward_kernel(
    own_ref, other_ref, own_normed, other_normed, w_ref, bias_ref, cos_ref, sin_ref, q_ref, k_ref, v_ref,
    dq_ref, dk_ref, dv_ref, mine_ref, theirs_ref, gain_ref,
):
    rows = pair_rows(own_ref, other_ref)
    query, key, value = q_ref[...], k_ref[...], v_ref[...]
    d_context = mul(rows, side_by_side(w_ref, 3)).astype(BF16)
    d_query = jnp.zeros(query.shape, F32)
    d_key = jnp.zeros(query.shape, F32)
    d_value = jnp.zeros(query.shape, F32)
    for head in range(query.shape[1] // HD):
        probs = head_probs(query, key, bias_ref[...], head)
        d_here = head_only(d_context, head)
        d_value = d_value + mul_at(probs.astype(BF16), d_here)
        d_probs = mul_bt(d_here, value)
        inner = jnp.sum(probs * d_probs, axis=-1, keepdims=True)
        d_scores = (probs * (d_probs - inner)).astype(BF16)
        d_query = d_query + mul(d_scores, head_only(key, head))
        d_key = d_key + mul_at(d_scores, head_only(query, head))
    cosine, sine = cos_ref[...], sin_ref[...]
    d_query = d_query * SCORE_SCALE
    d_key = d_key * SCORE_SCALE
    d_query = (d_query * cosine - swap_halves(d_query) * sine).astype(BF16)
    d_key = (d_key * cosine - swap_halves(d_key) * sine).astype(BF16)
    d_value = d_value.astype(BF16)
    dq_ref[...] = d_query
    dk_ref[...] = d_key
    dv_ref[...] = d_value
    half = own_ref.shape[0]
    for tile in range(D // TILE):
        at = pl.ds(tile * TILE, TILE)
        total = jnp.zeros((2 * half, TILE), F32)
        for matrix, columns in ((0, d_query), (1, d_key), (2, d_value)):
            w_here = jnp.concatenate([w_ref[matrix, 0, at, :], w_ref[matrix, 1, at, :]], axis=-1)
            total = total + mul_bt(columns, w_here)
        normed = jnp.concatenate([own_normed[:, at], other_normed[:, at]], axis=0).astype(F32)
        gain_ref[:, at] = jnp.sum(total * normed, axis=0, keepdims=True)
        mine_ref[:, at] = total[:half]
        theirs_ref[:, at] = total[half:].astype(BF16)


def mlp_half_kernel(*refs):
    rows, d_rows = refs[:8], refs[8:16]
    w_ref, hid_ref, dgate_ref, dup_ref, grad_ref = refs[16:]
    w_gate, w_up, w_down = (
        jnp.concatenate([w_ref[0, kind], w_ref[1, kind]], axis=-1) for kind in range(3)
    )
    for piece in range(4):
        here = pair_rows(rows[2 * piece], rows[2 * piece + 1])
        gate = mul(here, w_gate)
        up = mul(here, w_up)
        d_hidden = mul(pair_rows(d_rows[2 * piece], d_rows[2 * piece + 1]), w_down)
        sigmoid = 1.0 / (1.0 + jnp.exp(-gate))
        silu = gate * sigmoid
        at = pl.ds(piece * here.shape[0], here.shape[0])
        hid_ref[at, :] = (silu * up).astype(BF16)
        dgate_ref[at, :] = (d_hidden * up * sigmoid * (1.0 + gate * (1.0 - sigmoid))).astype(BF16)
        dup_ref[at, :] = (d_hidden * silu).astype(BF16)
    for tile in range(D // TILE):
        at = pl.ds(tile * TILE, TILE)
        across = jnp.concatenate([ref[:, at] for ref in rows], axis=0)
        d_across = jnp.concatenate([ref[:, at] for ref in d_rows], axis=0)
        for kind, left, right in ((0, across, dgate_ref), (1, across, dup_ref), (2, d_across, hid_ref)):
            grad = mul_at(left, right[...]).astype(BF16)
            for chip in range(2):
                grad_ref[chip, kind, at, :] = grad[:, chip * BW : (chip + 1) * BW]


def all_columns(kind, w_even, w_odd):
    return jnp.concatenate([ref[chip, kind] for ref in (w_even, w_odd) for chip in range(4)], axis=-1)


def both_columns(even, odd):
    return jnp.concatenate([even[...], odd[...]], axis=-1)


def mlp_back_kernel(dgate_even, dgate_odd, dup_even, dup_odd, w_even, w_odd, mine_ref, theirs_ref):
    total = mul_bt(both_columns(dgate_even, dgate_odd), all_columns(0, w_even, w_odd))
    total = total + mul_bt(both_columns(dup_even, dup_odd), all_columns(1, w_even, w_odd))
    half = mine_ref.shape[0]
    mine_ref[...] = total[:half]
    theirs_ref[...] = total[half:].astype(BF16)


def mlp_out_kernel(hid_even, hid_odd, w_even, w_odd, mine_ref, theirs_ref):
    total = mul_bt(both_columns(hid_even, hid_odd), all_columns(0, w_even, w_odd))
    half = mine_ref.shape[1]
    for piece in range(4):
        mine_ref[piece] = total[2 * piece * half : (2 * piece + 1) * half]
        theirs_ref[piece] = total[(2 * piece + 1) * half : 2 * (piece + 1) * half].astype(BF16)


def grads_kernel(sources, *refs):
    first, second = refs[:8], refs[8:16]
    columns = refs[16:-1]
    out_ref = refs[-1]
    row_sets = [jnp.concatenate([ref[...] for ref in part], axis=0) for part in (first, second)]
    for index, source in enumerate(sources):
        stacked = jnp.concatenate([ref[...] for ref in columns[4 * index : 4 * index + 4]], axis=0)
        grad = mul_at(row_sets[source], stacked).astype(BF16)
        for block in range(grad.shape[1] // BW):
            out_ref[index, block] = grad[:, block * BW : (block + 1) * BW]


def split(values):
    high = values.astype(BF16)
    return high, (values - high.astype(F32)).astype(BF16)


def mul_split(a, b):
    return mul(a[0], b[0]) + (mul(a[0], b[1]) + mul(a[1], b[0]))


def muon_kernel(grad_ref, momentum_ref, weight_ref, wg_ref, nm_ref, nw_ref, held, mixers):
    step = pl.program_id(0)
    count = held.shape[0]

    @pl.when(step < count)
    def _():
        grad = grad_ref[...].astype(F32)
        wg_ref[...] = grad
        block = MOMENTUM_DECAY * momentum_ref[...] + grad
        nm_ref[...] = block
        block = block * (1.0 / (jnp.sqrt(jnp.sum(block * block)) + 1e-07))
        held[step] = block
        high, low = split(block)
        cross = mul_at(high, low)
        mixers[step] = mul_at(high, high) + (cross + cross.T)

    @pl.when(step == count - 1)
    def _():
        row = lax.broadcasted_iota(jnp.int32, (BW, BW), 0)
        column = lax.broadcasted_iota(jnp.int32, (BW, BW), 1)
        eye = jnp.where(row == column, COEFF_A, 0.0).astype(F32)
        grams = [mixers[index] for index in range(count)]
        totals = [None] * count
        for turn in range(NS_ITERS):
            for index in range(count):
                pair = split(grams[index])
                mixer = eye + COEFF_B * grams[index] + COEFF_C * mul_split(pair, pair)
                mixed = split(mixer)
                if turn == 0:
                    totals[index] = mixer
                else:
                    totals[index] = mul_split(split(totals[index]), mixed)
                if turn < NS_ITERS - 1:
                    grams[index] = mul_split(split(mul_split(mixed, pair)), mixed)
        for index in range(count):
            mixers[index] = totals[index]

    @pl.when(step >= count)
    def _():
        at = step - count
        ortho = mul_split(split(held[at]), split(mixers[at]))
        nw_ref[...] = weight_ref[...].astype(F32) - (MUON_RATE * math.sqrt(D / BW)) * ortho


def deferred(kernel, inputs, unread):
    return lambda *refs: kernel(*refs[:inputs], *refs[inputs + unread :])


def unread_specs(after):
    return [pl.BlockSpec(memory_space=pl.ANY) for _ in after]


def cost(flops, accessed):
    return pl.CostEstimate(flops=flops // 6, bytes_accessed=accessed // 6, transcendentals=0)


def sort_kernel(plane_ref, *refs):
    moved, attn_ref, mlp_ref = refs[:4], refs[4], refs[5]
    for here in range(4):

        @pl.when(plane_ref[0] == here)
        def _():
            attn_ref[...] = moved[here][...]
            for kind in (1, 2, 3):
                mlp_ref[kind - 1] = moved[(here - kind) % 4][...]


def sort_kinds(plane, moved, after):
    shape = moved[0].shape
    return pl.pallas_call(
        deferred(sort_kernel, 5, len(after)),
        out_shape=(shaped(shape, BF16), shaped((3,) + shape, BF16)),
        in_specs=[pl.BlockSpec(memory_space=pltpu.SMEM)] + whole_specs(moved) + unread_specs(after),
        out_specs=tuple(whole_specs(range(2))),
        compiler_params=params(32),
        cost_estimate=cost(0, 4_000_000),
        name="sort_kinds",
    )(plane.astype(jnp.int32).reshape(1), *moved, *after)


def params(mebibytes):
    return pltpu.CompilerParams(vmem_limit_bytes=mebibytes * 1024 * 1024)


def whole_specs(arrays):
    return [pl.BlockSpec(memory_space=pltpu.VMEM) for _ in arrays]


def shaped(shape, dtype):
    return jax.ShapeDtypeStruct(shape, dtype)


def attn_forward(own, other, w_attn, bias, cosine, sine, after=()):
    half = own.shape[1]
    rows = pl.BlockSpec((None, half, D), lambda i: (0, 0, 0))
    span = w_attn.shape[1] * w_attn.shape[3]
    square = shaped((2 * half, span), BF16)
    args = (own, other, w_attn, bias, cosine, sine)
    return pl.pallas_call(
        deferred(attn_forward_kernel, len(args), len(after)),
        grid=(1,),
        out_shape=(square,) * 4 + (shaped((half, D), F32), shaped((half, D), BF16)),
        in_specs=[rows, rows] + whole_specs(args[2:]) + unread_specs(after),
        out_specs=tuple(whole_specs(range(6))),
        compiler_params=params(40),
        cost_estimate=cost(1_300_000_000, 9_000_000),
        name="attn_forward",
    )(*args, *after)


def attn_backward(own, other, own_pair, other_pair, w_attn, bias, cosine, sine, query, key, value):
    half = own.shape[0]
    square = shaped(query.shape, BF16)
    rows = pl.BlockSpec((None, half, D), lambda i: (0, 0, 0))
    args = (own, other, own_pair, other_pair, w_attn, bias, cosine, sine, query, key, value)
    return pl.pallas_call(
        attn_backward_kernel,
        grid=(1,),
        out_shape=(square,) * 3 + (shaped((half, D), F32), shaped((half, D), BF16), shaped((1, D), F32)),
        in_specs=whole_specs(args[:2]) + [rows, rows] + whole_specs(args[4:]),
        out_specs=tuple(whole_specs(range(6))),
        compiler_params=params(40),
        cost_estimate=cost(1_600_000_000, 9_000_000),
        name="attn_backward",
    )(*args)


def mlp_half(rows, pairs, w_half):
    half = rows[0].shape[0]
    columns = shaped((8 * half, 4 * BW), BF16)
    blocks = pl.BlockSpec((2, 3, D, BW), lambda j: (j, 0, 0, 0))
    return pl.pallas_call(
        mlp_half_kernel,
        grid=(2,),
        out_shape=(columns,) * 3 + (shaped(w_half.shape, BF16),),
        in_specs=[pl.BlockSpec((half, D), lambda j: (0, 0)) for _ in range(8)]
        + [pl.BlockSpec((None, half, D), lambda j: (1, 0, 0)) for _ in range(8)]
        + [blocks],
        out_specs=(pl.BlockSpec((8 * half, 2 * BW), lambda j: (0, j)),) * 3 + (blocks,),
        compiler_params=params(58),
        cost_estimate=cost(13_000_000_000, 20_000_000),
        name="mlp_half",
    )(*rows, *pairs, w_half)


def mlp_back(piece, halves, w_even, w_odd):
    rows = halves[0][0].shape[0] // 4
    wide = 2 * TILE
    args = [half[index] for index in (1, 2) for half in halves]
    tile = pl.BlockSpec((rows // 2, wide), lambda i: (0, i))
    weight = pl.BlockSpec((4, 2, wide, BW), lambda i: (0, 0, i, 0))
    return pl.pallas_call(
        mlp_back_kernel,
        grid=(D // wide,),
        out_shape=(shaped((rows // 2, D), F32), shaped((rows // 2, D), BF16)),
        in_specs=[pl.BlockSpec((rows, 4 * BW), lambda i: (piece, 0)) for _ in args] + [weight] * 2,
        out_specs=(tile,) * 2,
        compiler_params=params(58),
        cost_estimate=cost(2_200_000_000, 11_000_000),
        name="mlp_back",
    )(*args, w_even, w_odd)


def mlp_out(halves, w_even, w_odd, after):
    count = halves[0][0].shape[0]
    args = [half[0] for half in halves]
    wide = 2 * TILE
    tile = pl.BlockSpec((4, count // 8, wide), lambda i: (0, 0, i))
    weight = pl.BlockSpec((4, 1, wide, BW), lambda i: (0, 2, i, 0))
    return pl.pallas_call(
        deferred(mlp_out_kernel, 4, len(after)),
        grid=(D // wide,),
        out_shape=(shaped((4, count // 8, D), F32), shaped((4, count // 8, D), BF16)),
        in_specs=[pl.BlockSpec((count, 4 * BW), lambda i: (0, 0)) for _ in args] + [weight] * 2 + unread_specs(after),
        out_specs=(tile,) * 2,
        compiler_params=params(58),
        cost_estimate=cost(4_300_000_000, 18_000_000),
        name="mlp_out",
    )(*args, w_even, w_odd, *after)


def weight_products(pairs, rows, column_sets, sources, name, after=()):
    half = rows[0].shape[0]
    span = column_sets[0][0].shape[1]
    pair_spec = pl.BlockSpec((None, half, TILE), lambda i: (0, 0, i))
    row_spec = pl.BlockSpec((half, TILE), lambda i: (0, i))
    column_spec = pl.BlockSpec((2 * half, span), lambda i: (0, 0))
    flat = [piece for pieces in column_sets for piece in pieces]
    return pl.pallas_call(
        deferred(functools.partial(grads_kernel, sources), 16 + len(flat), len(after)),
        grid=(D // TILE,),
        out_shape=shaped((len(sources), span // BW, D, BW), BF16),
        in_specs=[pair_spec] * 8 + [row_spec] * 8 + [column_spec] * len(flat) + unread_specs(after),
        out_specs=pl.BlockSpec((len(sources), span // BW, TILE, BW), lambda i: (0, 0, i, 0)),
        compiler_params=params(60),
        cost_estimate=cost(2 * 8 * half * D * span * len(sources), 20_000_000),
        name=name,
    )(*pairs, *rows, *flat, *after)


def muon(grads, momentum, weights, offset, stride, begun=(), after=()):
    count = grads.shape[0]
    now = lambda i: jnp.minimum(i, count - 1)
    then = lambda i: jnp.maximum(i - count, 0)
    block = (None, D, BW)
    compact = pl.BlockSpec(block, lambda i: (now(i), 0, 0))
    early = pl.BlockSpec(block, lambda i: (stride * now(i) + offset, 0, 0))
    late = pl.BlockSpec(block, lambda i: (stride * then(i) + offset, 0, 0))
    return pl.pallas_call(
        deferred(muon_kernel, 3, len(begun) + len(after)),
        grid=(2 * count,),
        out_shape=(shaped(momentum.shape, F32),) * 3,
        in_specs=[compact, early, late] + unread_specs(begun) + unread_specs(after),
        out_specs=(early, early, late),
        input_output_aliases={3 + index: index for index in range(len(begun))},
        scratch_shapes=[pltpu.VMEM((count, D, BW), F32), pltpu.VMEM((count, BW, BW), F32)],
        compiler_params=params(40),
        cost_estimate=cost(1_000_000_000 * count, 5_500_000 * count),
        name="muon",
    )(grads, momentum, weights, *begun, *after)


def mirror(step):
    return [(place, place ^ step) for place in range(4)]


def ring(value, step=1):
    return lax.ppermute(value, "z", [(place, (place + step) % 4) for place in range(4)])


def swap(value):
    return lax.ppermute(value, "tensor", SWAP)


def nothing(value):
    first = value[(0,) * value.ndim].astype(F32)
    return (first * 0.0).astype(jnp.int32)


def hold(value, *others):
    zero = sum((nothing(other) for other in others), jnp.int32(0))
    return value + zero.astype(value.dtype)


def gather_rows(rows):
    mine = [rows]
    for _ in range(3):
        mine.append(ring(mine[-1]))
    return mine, [swap(part) for part in mine]


class Scatter:
    def __init__(self):
        self.moving = self.result = None
        self.payloads = []

    def add(self, step, mine, theirs):
        total = mine + swap(theirs).astype(F32)
        if self.moving is not None:
            total = total + self.moving.astype(F32)
        if step:
            self.payloads.append(total.astype(BF16))
            self.moving = ring(self.payloads[-1])
        else:
            self.result = total


def everywhere(value):
    value = value + swap(value)
    for axis in ("m", "z"):
        one, two, three = (lax.ppermute(value, axis, mirror(step)) for step in (1, 2, 3))
        value = (value + one) + (two + three)
    if lax.axis_size("r") > 1:
        value = lax.psum(value, "r")
    return value


def join(parts):
    if parts.shape[0] == 4:
        return parts
    width = parts.shape[3]
    parts = parts.reshape(4, 2, -1, D, width).transpose(0, 1, 3, 2, 4)
    return parts.reshape(4, 2, D, BW)


def unjoin(grads, width):
    if width == BW:
        return grads
    grads = grads.reshape(4, 2, D, -1, width).transpose(0, 1, 3, 2, 4)
    return grads.reshape(-1, 1, D, width)


def gather_plane(parts):
    return lax.all_gather(parts, ("m", "r"), axis=0, tiled=False)


def gather_part_direct(part, index, result):
    chip = lax.axis_index("m")
    result = lax.dynamic_update_slice(result, part[None, None], (chip, index, 0, 0))
    for step in (1, 2, 3):
        got = lax.ppermute(part, "m", mirror(step))
        result = lax.dynamic_update_slice(result, got[None, None], (chip ^ step, index, 0, 0))
    return result


def scatter_plane(grads):
    share = lax.psum_scatter(
        grads.reshape(grads.shape[0], -1, grads.shape[3]), ("m", "r"), scatter_dimension=0, tiled=False
    )
    return share.reshape(grads.shape[1:])


def scatter_plane_direct(grads, gain_parts):
    chip = lax.axis_index("m")

    def share_for(step):
        return lax.dynamic_index_in_dim(grads, chip ^ step, 0, keepdims=False)

    arrived = [lax.ppermute(share_for(step), "m", mirror(step)) for step in (1, 2, 3)]
    gain_sums = everywhere(hold(gain_parts, arrived[0]))
    total = hold(share_for(0).astype(F32), gain_sums)
    for part in arrived:
        total = total + part.astype(F32)
    return total.astype(BF16), gain_sums


def interleave(mine, other):
    return [rows for pair in zip(mine, other) for rows in pair]


def local(tokens, segments, weights, momentum, gains, gain_first, gain_second, cotangent):
    plane = lax.axis_index("z")
    core = lax.axis_index("tensor")
    block_count = weights.shape[0]

    if block_count == 8:
        shards = weights.reshape(4, 2, D, BW)
    else:
        width = block_count * BW // 4
        shards = weights.reshape(block_count, D, -1, width).transpose(0, 2, 1, 3).reshape(4, 1, D, width)
    parts, width = shards.shape[1], shards.shape[3]

    def shard(shift, part, *others):
        at = sum((nothing(other) for other in others), plane + shift)
        return lax.dynamic_slice(shards, (at % 4, part, 0, 0), (1, 1, D, width))[0, 0]

    rows_in = tokens.astype(F32)
    segment_own = segments.astype(F32)
    segment_parts = [segment_own] + [ring(segment_own, shift) for shift in (1, 2, 3)]
    segment_rows = jnp.concatenate(segment_parts, axis=0)
    def move(part, *others):
        return [shard(0, part)] + [ring(shard(shift, part, *others), shift) for shift in (1, 2, 3)]

    moved_even = move(0)

    def kind_part(source):
        return lax.select_n(plane, *(moved_even[(here - source) % 4] for here in range(4)))

    row_pair = lambda *others: jnp.stack([hold(rms_norm(rows_in, gains[0]), *others).astype(BF16), cotangent])
    if parts == 2:
        attn_even, mlp_even = sort_kinds(plane, moved_even, [segment_rows])
        w_attn = gather_part_direct(attn_even, 0, jnp.zeros((4, 2, D, BW), BF16))
        attn_odd, mlp_odd = sort_kinds(plane, move(1, attn_even), [w_attn])
        w_attn = gather_part_direct(attn_odd, 1, w_attn)
        w_mlp = [gather_plane(mlp_even), gather_plane(mlp_odd)]
        begun = [mlp_odd]
        first_mine, first_other = gather_rows(row_pair(attn_odd))
    else:
        w_attn = join(gather_plane(kind_part(0)[None]))
        w_mlp = gather_plane(jnp.stack([kind_part(kind) for kind in (1, 2, 3)]))
        w_mlp = jnp.stack([join(w_mlp[:, kind : kind + 1]) for kind in range(3)], axis=1)
        w_mlp = [w_mlp[:, :, 0], w_mlp[:, :, 1]]
        begun = []
        first_mine, first_other = gather_rows(row_pair())
    first_rows = interleave(first_mine, first_other)

    length = segment_rows.shape[1]
    half = length // 2
    place = jnp.arange(length)
    place = jnp.where(core == 0, place, (place + half) % length)
    segment_rows = jnp.where(core == 0, segment_rows, jnp.roll(segment_rows, half, axis=1))
    allowed = (place[None, None, :] <= place[None, :, None]) & (
        segment_rows[:, None, :] == segment_rows[:, :, None]
    )
    bias = jnp.where(allowed, 0.0, NEG_LARGE).astype(F32)
    cosine, sine = rope_tables(place)

    query, key, value, context = ([None] * 4 for _ in range(4))
    mixed = Scatter()
    for s in (1, 2, 3, 0):
        query[s], key[s], value[s], context[s], *both = attn_forward(
            first_mine[s], first_other[s], w_attn, bias[s], cosine, sine, mixed.payloads[:1] if s == 3 else begun if s == 1 else ()
        )
        mixed.add(s, *both)
    middle = rows_in + mixed.result
    two_mine, two_other = gather_rows(rms_norm(middle, gains[1]).astype(BF16))

    two_rows = interleave(two_mine, two_other)
    *even_half, grads_even = mlp_half(two_rows, first_rows, w_mlp[0])
    *odd_half, grads_odd = mlp_half(two_rows, first_rows, w_mlp[1])
    if parts == 2:
        mlp_share = [scatter_plane(grads_even), scatter_plane(grads_odd)]
    else:
        mlp_grads = jnp.stack([grads_even, grads_odd], axis=2)
        mlp_share = [
            jnp.concatenate([scatter_plane(unjoin(mlp_grads[:, kind], width)) for kind in range(3)])
        ]
    d_normed = Scatter()
    for s in (1, 2, 3, 0):
        d_normed.add(s, *mlp_back(s, (even_half, odd_half), *w_mlp))
    outward = mlp_out((even_half, odd_half), *w_mlp, d_normed.payloads[-1:])
    d_normed_two = hold(d_normed.result, outward[1])

    d_output = cotangent.astype(F32)
    d_middle_norm, d_gain_two = rms_norm_back(middle, gains[1], d_normed_two)
    d_middle = d_output + d_middle_norm
    e_mine, e_other = gather_rows(d_middle.astype(BF16))
    d_query, d_key, d_value, d_one, gain_parts = ([None] * 4 for _ in range(5))
    for s in range(4):
        d_query[s], d_key[s], d_value[s], *both, gain_parts[s] = attn_backward(
            e_mine[s], e_other[s], first_mine[s], first_other[s], w_attn, bias[s], cosine, sine, query[s], key[s], value[s]
        )
        d_one[s] = both
    attn_grads = weight_products(
        first_rows,
        interleave(e_mine, e_other),
        (d_query, d_key, d_value, context),
        (0, 0, 0, 1),
        "attn_products",
    )
    d_gain_one = ((gain_parts[0] + gain_parts[1]) + (gain_parts[2] + gain_parts[3]))[0] / gains[0]
    gain_grads = jnp.stack([d_gain_one, d_gain_two])
    if parts == 2:
        attn_share, gain_grads = scatter_plane_direct(attn_grads, gain_grads)
    else:
        attn_share = scatter_plane(unjoin(attn_grads, width))
        gain_grads = everywhere(gain_grads)

    last = Scatter()
    for s in (1, 2, 3, 0):
        mine, theirs = (jnp.stack([a, b[s]]) for a, b in zip(d_one[s], outward))
        if s == 2:
            mine = hold(mine, attn_grads)
        last.add(s, mine, theirs)
    d_normed_one, outward_sum = last.result
    d_rows_norm, _ = rms_norm_back(rows_in, gains[0], d_normed_one)
    input_grad = d_middle + d_rows_norm
    output = (middle + outward_sum).astype(BF16)

    results = ()
    for part in range(parts):
        shares = jnp.concatenate([attn_share[part][None], mlp_share[part]])

        def share_of(shift):
            return lax.dynamic_index_in_dim(shares, (plane + shift) % 4, 0, keepdims=False)

        back = [share_of(0)] + [ring(share_of(shift), shift) for shift in (1, 2, 3)]
        here = plane + nothing(results[1]) if part else plane
        summed = jnp.stack(
            [lax.select_n(here, *(back[(z - source) % 4] for z in range(4))) for source in range(4)]
        )
        if parts == 1:
            summed = summed.reshape(block_count, -1, D, width).transpose(0, 2, 1, 3).reshape(block_count, D, BW)
        results = muon(summed, momentum, weights, part, parts, results)
    weight_grads, new_momentum, new_weights = results

    new_gain_first = BETA_FIRST * gain_first + (1.0 - BETA_FIRST) * gain_grads
    new_gain_second = BETA_SECOND * gain_second + (1.0 - BETA_SECOND) * gain_grads * gain_grads
    first_hat = new_gain_first / (1.0 - BETA_FIRST**STEP)
    second_hat = new_gain_second / (1.0 - BETA_SECOND**STEP)
    new_gains = gains - ADAM_RATE * first_hat / (jnp.sqrt(second_hat) + ADAM_EPS)
    return (
        output,
        input_grad,
        weight_grads,
        new_momentum,
        new_weights,
        new_gain_first,
        new_gain_second,
        new_gains,
    )


def solution(mesh):
    count = mesh.shape["dp"]
    fine = Mesh(
        np.asarray(mesh.devices).reshape(4, 4, count // 16, mesh.shape["tensor"]),
        ("z",) + PLANE,
    )
    every = ("z",) + PLANE
    in_specs = (
        P(every, None),
        P(every[:3], None),
        P(every, None, None),
        P(every, None, None),
        P(),
        P(),
        P(),
        P(every, None),
    )
    out_specs = (
        P(every, None),
        P(every, None),
        P(every, None, None),
        P(every, None, None),
        P(every, None, None),
        P(),
        P(),
        P(),
    )
    return jax.shard_map(local, mesh=fine, in_specs=in_specs, out_specs=out_specs, check_vma=False)
```

```python
import functools
import math

import jax
import jax.numpy as jnp
import numpy as np
from jax import lax
from jax.experimental import pallas as pl
from jax.experimental.pallas import tpu as pltpu
from jax.sharding import Mesh
from jax.sharding import PartitionSpec as P

D = 2048
FF = 8192
HD = 64
BW = 128
NS_ITERS = 5
STEP = 10

HIGHEST = lax.Precision.HIGHEST
ROPE_BASE = 130000.0
NORM_EPS = 1e-05
NEG_LARGE = -1e30
MOMENTUM_DECAY = 0.95
MUON_RATE = 0.25
COEFF_A = 3.4445
COEFF_B = -4.775
COEFF_C = 2.0315
BETA_FIRST = 0.9
BETA_SECOND = 0.95
ADAM_RATE = 1.0
ADAM_EPS = 1e-08

F32 = jnp.float32
BF16 = jnp.bfloat16
PLANE = ("m", "r", "tensor")
SWAP = [(0, 1), (1, 0)]
TILE = 256
SCORE_SCALE = 1.0 / math.sqrt(HD)


def rms_norm(values, gain):
    return values * lax.rsqrt(jnp.mean(values * values, axis=-1, keepdims=True) + NORM_EPS) * gain


def rms_norm_back(values, gain, grad):
    scale = lax.rsqrt(jnp.mean(values * values, axis=-1, keepdims=True) + NORM_EPS)
    scaled = gain * grad
    inner = jnp.mean(scaled * values, axis=-1, keepdims=True)
    gain_grad = jnp.sum(grad * values * scale, axis=0)
    return scale * scaled - values * (scale * scale * scale * inner), gain_grad


def rope_tables(place):
    exponent = jnp.arange(HD // 2).astype(F32) * (2.0 / HD)
    inverse = jnp.exp(-exponent * math.log(ROPE_BASE))
    angle = place.astype(F32)[:, None] * inverse[None, :]
    cosine, sine = jnp.cos(angle), jnp.sin(angle)
    heads = 2 * BW // HD
    return (
        jnp.tile(jnp.concatenate([cosine, cosine], axis=1), (1, heads)),
        jnp.tile(jnp.concatenate([-sine, sine], axis=1), (1, heads)),
    )


def dims(lhs, rhs):
    return (((lhs,), (rhs,)), ((), ()))


def mul(a, b):
    return lax.dot_general(a, b, dims(1, 0), preferred_element_type=F32)


def mul_bt(a, b):
    return lax.dot_general(a, b, dims(1, 1), preferred_element_type=F32)


def mul_at(a, b):
    return lax.dot_general(a, b, dims(0, 0), preferred_element_type=F32)


def side_by_side(ref, *index):
    return jnp.concatenate([ref[index + (0,)], ref[index + (1,)]], axis=-1)


def pair_rows(own_ref, other_ref):
    return jnp.concatenate([own_ref[...], other_ref[...]], axis=0)


def swap_halves(values):
    lane = lax.broadcasted_iota(jnp.int32, values.shape, 1)
    span = values.shape[1]
    ahead = pltpu.roll(values, span - HD // 2, 1)
    behind = pltpu.roll(values, HD // 2, 1)
    return jnp.where(lane % HD < HD // 2, ahead, behind)


def head_only(values, head):
    lane = lax.broadcasted_iota(jnp.int32, values.shape, 1)
    return jnp.where((lane >= head * HD) & (lane < (head + 1) * HD), values, jnp.zeros_like(values))


def head_probs(query, key, bias, head):
    scores = mul_bt(head_only(query, head), key) * SCORE_SCALE + bias
    weights = jnp.exp(scores - jnp.max(scores, axis=-1, keepdims=True))
    return weights / jnp.sum(weights, axis=-1, keepdims=True)


def attn_forward_kernel(
    own_ref, other_ref, w_ref, bias_ref, cos_ref, sin_ref, q_ref, k_ref, v_ref, c_ref, mine_ref, theirs_ref
):
    rows = pair_rows(own_ref, other_ref)
    cosine, sine = cos_ref[...], sin_ref[...]
    lin = mul(rows, side_by_side(w_ref, 0))
    query = (lin * cosine + swap_halves(lin) * sine).astype(BF16)
    lin = mul(rows, side_by_side(w_ref, 1))
    key = (lin * cosine + swap_halves(lin) * sine).astype(BF16)
    value = mul(rows, side_by_side(w_ref, 2)).astype(BF16)
    q_ref[...] = query
    k_ref[...] = key
    v_ref[...] = value
    context = jnp.zeros(query.shape, F32)
    for head in range(query.shape[1] // HD):
        probs = head_probs(query, key, bias_ref[...], head)
        context = context + mul(probs.astype(BF16), head_only(value, head))
    context = context.astype(BF16)
    c_ref[...] = context
    half = own_ref.shape[0]
    for tile in range(D // TILE):
        at = pl.ds(tile * TILE, TILE)
        w_out = jnp.concatenate([w_ref[3, 0, at, :], w_ref[3, 1, at, :]], axis=-1)
        mixed = mul_bt(context, w_out)
        mine_ref[:, at] = mixed[:half]
        theirs_ref[:, at] = mixed[half:].astype(BF16)


def attn_backward_kernel(
    own_ref, other_ref, own_normed, other_normed, w_ref, bias_ref, cos_ref, sin_ref, q_ref, k_ref, v_ref,
    dq_ref, dk_ref, dv_ref, mine_ref, theirs_ref, gain_ref,
):
    rows = pair_rows(own_ref, other_ref)
    query, key, value = q_ref[...], k_ref[...], v_ref[...]
    d_context = mul(rows, side_by_side(w_ref, 3)).astype(BF16)
    d_query = jnp.zeros(query.shape, F32)
    d_key = jnp.zeros(query.shape, F32)
    d_value = jnp.zeros(query.shape, F32)
    for head in range(query.shape[1] // HD):
        probs = head_probs(query, key, bias_ref[...], head)
        d_here = head_only(d_context, head)
        d_value = d_value + mul_at(probs.astype(BF16), d_here)
        d_probs = mul_bt(d_here, value)
        inner = jnp.sum(probs * d_probs, axis=-1, keepdims=True)
        d_scores = (probs * (d_probs - inner)).astype(BF16)
        d_query = d_query + mul(d_scores, head_only(key, head))
        d_key = d_key + mul_at(d_scores, head_only(query, head))
    cosine, sine = cos_ref[...], sin_ref[...]
    d_query = d_query * SCORE_SCALE
    d_key = d_key * SCORE_SCALE
    d_query = (d_query * cosine - swap_halves(d_query) * sine).astype(BF16)
    d_key = (d_key * cosine - swap_halves(d_key) * sine).astype(BF16)
    d_value = d_value.astype(BF16)
    dq_ref[...] = d_query
    dk_ref[...] = d_key
    dv_ref[...] = d_value
    half = own_ref.shape[0]
    for tile in range(D // TILE):
        at = pl.ds(tile * TILE, TILE)
        total = jnp.zeros((2 * half, TILE), F32)
        for matrix, columns in ((0, d_query), (1, d_key), (2, d_value)):
            w_here = jnp.concatenate([w_ref[matrix, 0, at, :], w_ref[matrix, 1, at, :]], axis=-1)
            total = total + mul_bt(columns, w_here)
        normed = jnp.concatenate([own_normed[:, at], other_normed[:, at]], axis=0).astype(F32)
        gain_ref[:, at] = jnp.sum(total * normed, axis=0, keepdims=True)
        mine_ref[:, at] = total[:half]
        theirs_ref[:, at] = total[half:].astype(BF16)


def mlp_half_kernel(*refs):
    rows, d_rows = refs[:8], refs[8:16]
    w_ref, hid_ref, dgate_ref, dup_ref, grad_ref = refs[16:]
    w_gate, w_up, w_down = (
        jnp.concatenate([w_ref[0, kind], w_ref[1, kind]], axis=-1) for kind in range(3)
    )
    for piece in range(4):
        here = pair_rows(rows[2 * piece], rows[2 * piece + 1])
        gate = mul(here, w_gate)
        up = mul(here, w_up)
        d_hidden = mul(pair_rows(d_rows[2 * piece], d_rows[2 * piece + 1]), w_down)
        sigmoid = 1.0 / (1.0 + jnp.exp(-gate))
        silu = gate * sigmoid
        at = pl.ds(piece * here.shape[0], here.shape[0])
        hid_ref[at, :] = (silu * up).astype(BF16)
        dgate_ref[at, :] = (d_hidden * up * sigmoid * (1.0 + gate * (1.0 - sigmoid))).astype(BF16)
        dup_ref[at, :] = (d_hidden * silu).astype(BF16)
    for tile in range(D // TILE):
        at = pl.ds(tile * TILE, TILE)
        across = jnp.concatenate([ref[:, at] for ref in rows], axis=0)
        d_across = jnp.concatenate([ref[:, at] for ref in d_rows], axis=0)
        for kind, left, right in ((0, across, dgate_ref), (1, across, dup_ref), (2, d_across, hid_ref)):
            grad = mul_at(left, right[...]).astype(BF16)
            for chip in range(2):
                grad_ref[chip, kind, at, :] = grad[:, chip * BW : (chip + 1) * BW]


def all_columns(kind, w_even, w_odd):
    return jnp.concatenate([ref[chip, kind] for ref in (w_even, w_odd) for chip in range(4)], axis=-1)


def both_columns(even, odd):
    return jnp.concatenate([even[...], odd[...]], axis=-1)


def mlp_back_kernel(dgate_even, dgate_odd, dup_even, dup_odd, w_even, w_odd, mine_ref, theirs_ref):
    total = mul_bt(both_columns(dgate_even, dgate_odd), all_columns(0, w_even, w_odd))
    total = total + mul_bt(both_columns(dup_even, dup_odd), all_columns(1, w_even, w_odd))
    half = mine_ref.shape[0]
    mine_ref[...] = total[:half]
    theirs_ref[...] = total[half:].astype(BF16)


def mlp_out_kernel(hid_even, hid_odd, w_even, w_odd, mine_ref, theirs_ref):
    total = mul_bt(both_columns(hid_even, hid_odd), all_columns(0, w_even, w_odd))
    half = mine_ref.shape[1]
    for piece in range(4):
        mine_ref[piece] = total[2 * piece * half : (2 * piece + 1) * half]
        theirs_ref[piece] = total[(2 * piece + 1) * half : 2 * (piece + 1) * half].astype(BF16)


def grads_kernel(sources, *refs):
    first, second = refs[:8], refs[8:16]
    columns = refs[16:-1]
    out_ref = refs[-1]
    row_sets = [jnp.concatenate([ref[...] for ref in part], axis=0) for part in (first, second)]
    for index, source in enumerate(sources):
        stacked = jnp.concatenate([ref[...] for ref in columns[4 * index : 4 * index + 4]], axis=0)
        grad = mul_at(row_sets[source], stacked).astype(BF16)
        for block in range(grad.shape[1] // BW):
            out_ref[index, block] = grad[:, block * BW : (block + 1) * BW]


def split(values):
    high = values.astype(BF16)
    return high, (values - high.astype(F32)).astype(BF16)


def mul_split(a, b):
    return mul(a[0], b[0]) + (mul(a[0], b[1]) + mul(a[1], b[0]))


def muon_kernel(grad_ref, momentum_ref, weight_ref, wg_ref, nm_ref, nw_ref, held, mixers):
    step = pl.program_id(0)
    count = held.shape[0]

    @pl.when(step < count)
    def _():
        grad = grad_ref[...].astype(F32)
        wg_ref[...] = grad
        block = MOMENTUM_DECAY * momentum_ref[...] + grad
        nm_ref[...] = block
        block = block * (1.0 / (jnp.sqrt(jnp.sum(block * block)) + 1e-07))
        held[step] = block
        high, low = split(block)
        cross = mul_at(high, low)
        mixers[step] = mul_at(high, high) + (cross + cross.T)

    @pl.when(step == count - 1)
    def _():
        row = lax.broadcasted_iota(jnp.int32, (BW, BW), 0)
        column = lax.broadcasted_iota(jnp.int32, (BW, BW), 1)
        eye = jnp.where(row == column, COEFF_A, 0.0).astype(F32)
        grams = [mixers[index] for index in range(count)]
        totals = [None] * count
        for turn in range(NS_ITERS):
            for index in range(count):
                pair = split(grams[index])
                mixer = eye + COEFF_B * grams[index] + COEFF_C * mul_split(pair, pair)
                mixed = split(mixer)
                if turn == 0:
                    totals[index] = mixer
                else:
                    totals[index] = mul_split(split(totals[index]), mixed)
                if turn < NS_ITERS - 1:
                    grams[index] = mul_split(split(mul_split(mixed, pair)), mixed)
        for index in range(count):
            mixers[index] = totals[index]

    @pl.when(step >= count)
    def _():
        at = step - count
        ortho = mul_split(split(held[at]), split(mixers[at]))
        nw_ref[...] = weight_ref[...].astype(F32) - (MUON_RATE * math.sqrt(D / BW)) * ortho


def deferred(kernel, inputs, unread):
    return lambda *refs: kernel(*refs[:inputs], *refs[inputs + unread :])


def unread_specs(after):
    return [pl.BlockSpec(memory_space=pl.ANY) for _ in after]


def cost(flops, accessed):
    return pl.CostEstimate(flops=flops // 6, bytes_accessed=accessed // 6, transcendentals=0)


def sort_kernel(plane_ref, *refs):
    moved, attn_ref, mlp_ref = refs[:4], refs[4], refs[5]
    for here in range(4):

        @pl.when(plane_ref[0] == here)
        def _():
            attn_ref[...] = moved[here][...]
            for kind in (1, 2, 3):
                mlp_ref[kind - 1] = moved[(here - kind) % 4][...]


def sort_kinds(plane, moved, after):
    shape = moved[0].shape
    return pl.pallas_call(
        deferred(sort_kernel, 5, len(after)),
        out_shape=(shaped(shape, BF16), shaped((3,) + shape, BF16)),
        in_specs=[pl.BlockSpec(memory_space=pltpu.SMEM)] + whole_specs(moved) + unread_specs(after),
        out_specs=tuple(whole_specs(range(2))),
        compiler_params=params(32),
        cost_estimate=cost(0, 4_000_000),
        name="sort_kinds",
    )(plane.astype(jnp.int32).reshape(1), *moved, *after)


def params(mebibytes):
    return pltpu.CompilerParams(vmem_limit_bytes=mebibytes * 1024 * 1024)


def whole_specs(arrays):
    return [pl.BlockSpec(memory_space=pltpu.VMEM) for _ in arrays]


def shaped(shape, dtype):
    return jax.ShapeDtypeStruct(shape, dtype)


def attn_forward(own, other, w_attn, bias, cosine, sine, after=()):
    half = own.shape[1]
    rows = pl.BlockSpec((None, half, D), lambda i: (0, 0, 0))
    span = w_attn.shape[1] * w_attn.shape[3]
    square = shaped((2 * half, span), BF16)
    args = (own, other, w_attn, bias, cosine, sine)
    return pl.pallas_call(
        deferred(attn_forward_kernel, len(args), len(after)),
        grid=(1,),
        out_shape=(square,) * 4 + (shaped((half, D), F32), shaped((half, D), BF16)),
        in_specs=[rows, rows] + whole_specs(args[2:]) + unread_specs(after),
        out_specs=tuple(whole_specs(range(6))),
        compiler_params=params(40),
        cost_estimate=cost(1_300_000_000, 9_000_000),
        name="attn_forward",
    )(*args, *after)


def attn_backward(own, other, own_pair, other_pair, w_attn, bias, cosine, sine, query, key, value):
    half = own.shape[0]
    square = shaped(query.shape, BF16)
    rows = pl.BlockSpec((None, half, D), lambda i: (0, 0, 0))
    args = (own, other, own_pair, other_pair, w_attn, bias, cosine, sine, query, key, value)
    return pl.pallas_call(
        attn_backward_kernel,
        grid=(1,),
        out_shape=(square,) * 3 + (shaped((half, D), F32), shaped((half, D), BF16), shaped((1, D), F32)),
        in_specs=whole_specs(args[:2]) + [rows, rows] + whole_specs(args[4:]),
        out_specs=tuple(whole_specs(range(6))),
        compiler_params=params(40),
        cost_estimate=cost(1_600_000_000, 9_000_000),
        name="attn_backward",
    )(*args)


def mlp_half(rows, pairs, w_half):
    half = rows[0].shape[0]
    columns = shaped((8 * half, 4 * BW), BF16)
    blocks = pl.BlockSpec((2, 3, D, BW), lambda j: (j, 0, 0, 0))
    return pl.pallas_call(
        mlp_half_kernel,
        grid=(2,),
        out_shape=(columns,) * 3 + (shaped(w_half.shape, BF16),),
        in_specs=[pl.BlockSpec((half, D), lambda j: (0, 0)) for _ in range(8)]
        + [pl.BlockSpec((None, half, D), lambda j: (1, 0, 0)) for _ in range(8)]
        + [blocks],
        out_specs=(pl.BlockSpec((8 * half, 2 * BW), lambda j: (0, j)),) * 3 + (blocks,),
        compiler_params=params(58),
        cost_estimate=cost(13_000_000_000, 20_000_000),
        name="mlp_half",
    )(*rows, *pairs, w_half)


def mlp_back(piece, halves, w_even, w_odd):
    rows = halves[0][0].shape[0] // 4
    wide = 2 * TILE
    args = [half[index] for index in (1, 2) for half in halves]
    tile = pl.BlockSpec((rows // 2, wide), lambda i: (0, i))
    weight = pl.BlockSpec((4, 2, wide, BW), lambda i: (0, 0, i, 0))
    return pl.pallas_call(
        mlp_back_kernel,
        grid=(D // wide,),
        out_shape=(shaped((rows // 2, D), F32), shaped((rows // 2, D), BF16)),
        in_specs=[pl.BlockSpec((rows, 4 * BW), lambda i: (piece, 0)) for _ in args] + [weight] * 2,
        out_specs=(tile,) * 2,
        compiler_params=params(58),
        cost_estimate=cost(2_200_000_000, 11_000_000),
        name="mlp_back",
    )(*args, w_even, w_odd)


def mlp_out(halves, w_even, w_odd, after):
    count = halves[0][0].shape[0]
    args = [half[0] for half in halves]
    wide = 2 * TILE
    tile = pl.BlockSpec((4, count // 8, wide), lambda i: (0, 0, i))
    weight = pl.BlockSpec((4, 1, wide, BW), lambda i: (0, 2, i, 0))
    return pl.pallas_call(
        deferred(mlp_out_kernel, 4, len(after)),
        grid=(D // wide,),
        out_shape=(shaped((4, count // 8, D), F32), shaped((4, count // 8, D), BF16)),
        in_specs=[pl.BlockSpec((count, 4 * BW), lambda i: (0, 0)) for _ in args] + [weight] * 2 + unread_specs(after),
        out_specs=(tile,) * 2,
        compiler_params=params(58),
        cost_estimate=cost(4_300_000_000, 18_000_000),
        name="mlp_out",
    )(*args, w_even, w_odd, *after)


def weight_products(pairs, rows, column_sets, sources, name, after=()):
    half = rows[0].shape[0]
    span = column_sets[0][0].shape[1]
    pair_spec = pl.BlockSpec((None, half, TILE), lambda i: (0, 0, i))
    row_spec = pl.BlockSpec((half, TILE), lambda i: (0, i))
    column_spec = pl.BlockSpec((2 * half, span), lambda i: (0, 0))
    flat = [piece for pieces in column_sets for piece in pieces]
    return pl.pallas_call(
        deferred(functools.partial(grads_kernel, sources), 16 + len(flat), len(after)),
        grid=(D // TILE,),
        out_shape=shaped((len(sources), span // BW, D, BW), BF16),
        in_specs=[pair_spec] * 8 + [row_spec] * 8 + [column_spec] * len(flat) + unread_specs(after),
        out_specs=pl.BlockSpec((len(sources), span // BW, TILE, BW), lambda i: (0, 0, i, 0)),
        compiler_params=params(60),
        cost_estimate=cost(2 * 8 * half * D * span * len(sources), 20_000_000),
        name=name,
    )(*pairs, *rows, *flat, *after)


def muon(grads, momentum, weights, offset, stride, begun=(), after=()):
    count = grads.shape[0]
    now = lambda i: jnp.minimum(i, count - 1)
    then = lambda i: jnp.maximum(i - count, 0)
    block = (None, D, BW)
    compact = pl.BlockSpec(block, lambda i: (now(i), 0, 0))
    early = pl.BlockSpec(block, lambda i: (stride * now(i) + offset, 0, 0))
    late = pl.BlockSpec(block, lambda i: (stride * then(i) + offset, 0, 0))
    return pl.pallas_call(
        deferred(muon_kernel, 3, len(begun) + len(after)),
        grid=(2 * count,),
        out_shape=(shaped(momentum.shape, F32),) * 3,
        in_specs=[compact, early, late] + unread_specs(begun) + unread_specs(after),
        out_specs=(early, early, late),
        input_output_aliases={3 + index: index for index in range(len(begun))},
        scratch_shapes=[pltpu.VMEM((count, D, BW), F32), pltpu.VMEM((count, BW, BW), F32)],
        compiler_params=params(40),
        cost_estimate=cost(1_000_000_000 * count, 5_500_000 * count),
        name="muon",
    )(grads, momentum, weights, *begun, *after)


def mirror(step):
    return [(place, place ^ step) for place in range(4)]


def ring(value, step=1):
    return lax.ppermute(value, "z", [(place, (place + step) % 4) for place in range(4)])


def swap(value):
    return lax.ppermute(value, "tensor", SWAP)


def nothing(value):
    first = value[(0,) * value.ndim].astype(F32)
    return (first * 0.0).astype(jnp.int32)


def hold(value, *others):
    zero = sum((nothing(other) for other in others), jnp.int32(0))
    return value + zero.astype(value.dtype)


def gather_rows(rows):
    mine = [rows]
    for _ in range(3):
        mine.append(ring(mine[-1]))
    return mine, [swap(part) for part in mine]


class Scatter:
    def __init__(self):
        self.moving = self.result = None
        self.payloads = []

    def add(self, step, mine, theirs):
        total = mine + swap(theirs).astype(F32)
        if self.moving is not None:
            total = total + self.moving.astype(F32)
        if step:
            self.payloads.append(total.astype(BF16))
            self.moving = ring(self.payloads[-1])
        else:
            self.result = total


def everywhere(value):
    value = value + swap(value)
    for axis in ("m", "z"):
        one, two, three = (lax.ppermute(value, axis, mirror(step)) for step in (1, 2, 3))
        value = (value + one) + (two + three)
    if lax.axis_size("r") > 1:
        value = lax.psum(value, "r")
    return value


def join(parts):
    if parts.shape[0] == 4:
        return parts
    width = parts.shape[3]
    parts = parts.reshape(4, 2, -1, D, width).transpose(0, 1, 3, 2, 4)
    return parts.reshape(4, 2, D, BW)


def unjoin(grads, width):
    if width == BW:
        return grads
    grads = grads.reshape(4, 2, D, -1, width).transpose(0, 1, 3, 2, 4)
    return grads.reshape(-1, 1, D, width)


def gather_plane(parts):
    return lax.all_gather(parts, ("m", "r"), axis=0, tiled=False)


def gather_part_direct(part, index, result):
    chip = lax.axis_index("m")
    result = lax.dynamic_update_slice(result, part[None, None], (chip, index, 0, 0))
    for step in (1, 2, 3):
        got = lax.ppermute(part, "m", mirror(step))
        result = lax.dynamic_update_slice(result, got[None, None], (chip ^ step, index, 0, 0))
    return result


def scatter_plane(grads):
    share = lax.psum_scatter(
        grads.reshape(grads.shape[0], -1, grads.shape[3]), ("m", "r"), scatter_dimension=0, tiled=False
    )
    return share.reshape(grads.shape[1:])


def scatter_plane_direct(grads):
    chip = lax.axis_index("m")

    def share_for(step):
        return lax.dynamic_index_in_dim(grads, chip ^ step, 0, keepdims=False)

    total = share_for(0).astype(F32)
    for step in (1, 2, 3):
        total = total + lax.ppermute(share_for(step), "m", mirror(step)).astype(F32)
    return total.astype(BF16)


def interleave(mine, other):
    return [rows for pair in zip(mine, other) for rows in pair]


def local(tokens, segments, weights, momentum, gains, gain_first, gain_second, cotangent):
    plane = lax.axis_index("z")
    core = lax.axis_index("tensor")
    block_count = weights.shape[0]

    if block_count == 8:
        shards = weights.reshape(4, 2, D, BW)
    else:
        width = block_count * BW // 4
        shards = weights.reshape(block_count, D, -1, width).transpose(0, 2, 1, 3).reshape(4, 1, D, width)
    parts, width = shards.shape[1], shards.shape[3]

    def shard(shift, part, *others):
        at = sum((nothing(other) for other in others), plane + shift)
        return lax.dynamic_slice(shards, (at % 4, part, 0, 0), (1, 1, D, width))[0, 0]

    rows_in = tokens.astype(F32)
    segment_own = segments.astype(F32)
    segment_parts = [segment_own] + [ring(segment_own, shift) for shift in (1, 2, 3)]
    segment_rows = jnp.concatenate(segment_parts, axis=0)
    def move(part, *others):
        return [shard(0, part)] + [ring(shard(shift, part, *others), shift) for shift in (1, 2, 3)]

    moved_even = move(0)

    def kind_part(source):
        return lax.select_n(plane, *(moved_even[(here - source) % 4] for here in range(4)))

    row_pair = lambda *others: jnp.stack([hold(rms_norm(rows_in, gains[0]), *others).astype(BF16), cotangent])
    if parts == 2:
        attn_even, mlp_even = sort_kinds(plane, moved_even, [segment_rows])
        w_attn = gather_part_direct(attn_even, 0, jnp.zeros((4, 2, D, BW), BF16))
        attn_odd, mlp_odd = sort_kinds(plane, move(1, attn_even), [w_attn])
        w_attn = gather_part_direct(attn_odd, 1, w_attn)
        w_mlp = [gather_plane(mlp_even), gather_plane(mlp_odd)]
        begun = [mlp_odd]
        first_mine, first_other = gather_rows(row_pair(attn_odd))
    else:
        w_attn = join(gather_plane(kind_part(0)[None]))
        w_mlp = gather_plane(jnp.stack([kind_part(kind) for kind in (1, 2, 3)]))
        w_mlp = jnp.stack([join(w_mlp[:, kind : kind + 1]) for kind in range(3)], axis=1)
        w_mlp = [w_mlp[:, :, 0], w_mlp[:, :, 1]]
        begun = []
        first_mine, first_other = gather_rows(row_pair())
    first_rows = interleave(first_mine, first_other)

    length = segment_rows.shape[1]
    half = length // 2
    place = jnp.arange(length)
    place = jnp.where(core == 0, place, (place + half) % length)
    segment_rows = jnp.where(core == 0, segment_rows, jnp.roll(segment_rows, half, axis=1))
    allowed = (place[None, None, :] <= place[None, :, None]) & (
        segment_rows[:, None, :] == segment_rows[:, :, None]
    )
    bias = jnp.where(allowed, 0.0, NEG_LARGE).astype(F32)
    cosine, sine = rope_tables(place)

    query, key, value, context = ([None] * 4 for _ in range(4))
    mixed = Scatter()
    for s in (1, 2, 3, 0):
        query[s], key[s], value[s], context[s], *both = attn_forward(
            first_mine[s], first_other[s], w_attn, bias[s], cosine, sine, mixed.payloads[:1] if s == 3 else begun if s == 1 else ()
        )
        mixed.add(s, *both)
    middle = rows_in + mixed.result
    two_mine, two_other = gather_rows(rms_norm(middle, gains[1]).astype(BF16))

    two_rows = interleave(two_mine, two_other)
    *even_half, grads_even = mlp_half(two_rows, first_rows, w_mlp[0])
    *odd_half, grads_odd = mlp_half(two_rows, first_rows, w_mlp[1])
    if parts == 2:
        mlp_share = [scatter_plane(grads_even), scatter_plane(grads_odd)]
    else:
        mlp_grads = jnp.stack([grads_even, grads_odd], axis=2)
        mlp_share = [
            jnp.concatenate([scatter_plane(unjoin(mlp_grads[:, kind], width)) for kind in range(3)])
        ]
    d_normed = Scatter()
    for s in (1, 2, 3, 0):
        d_normed.add(s, *mlp_back(s, (even_half, odd_half), *w_mlp))
    outward = mlp_out((even_half, odd_half), *w_mlp, d_normed.payloads[-1:])
    d_normed_two = hold(d_normed.result, outward[1])

    d_output = cotangent.astype(F32)
    d_middle_norm, d_gain_two = rms_norm_back(middle, gains[1], d_normed_two)
    d_middle = d_output + d_middle_norm
    e_mine, e_other = gather_rows(d_middle.astype(BF16))
    d_query, d_key, d_value, d_one, gain_parts = ([None] * 4 for _ in range(5))
    for s in range(4):
        d_query[s], d_key[s], d_value[s], *both, gain_parts[s] = attn_backward(
            e_mine[s], e_other[s], first_mine[s], first_other[s], w_attn, bias[s], cosine, sine, query[s], key[s], value[s]
        )
        d_one[s] = both
    attn_grads = weight_products(
        first_rows,
        interleave(e_mine, e_other),
        (d_query, d_key, d_value, context),
        (0, 0, 0, 1),
        "attn_products",
    )
    d_gain_one = ((gain_parts[0] + gain_parts[1]) + (gain_parts[2] + gain_parts[3]))[0] / gains[0]
    gain_grads = jnp.stack([d_gain_one, d_gain_two])
    if parts == 2:
        attn_share = scatter_plane_direct(attn_grads)
    else:
        attn_share = scatter_plane(unjoin(attn_grads, width))

    last = Scatter()
    for s in (1, 2, 3, 0):
        mine, theirs = (jnp.stack([a, b[s]]) for a, b in zip(d_one[s], outward))
        if s == 2:
            mine = hold(mine, attn_grads)
        last.add(s, mine, theirs)
    d_normed_one, outward_sum = last.result
    d_rows_norm, _ = rms_norm_back(rows_in, gains[0], d_normed_one)
    input_grad = d_middle + d_rows_norm
    output = (middle + outward_sum).astype(BF16)

    results = ()
    for part in range(parts):
        shares = jnp.concatenate([attn_share[part][None], mlp_share[part]])

        def share_of(shift):
            return lax.dynamic_index_in_dim(shares, (plane + shift) % 4, 0, keepdims=False)

        back = [share_of(0)] + [ring(share_of(shift), shift) for shift in (1, 2, 3)]
        zero = nothing(results[1]) if part else jnp.int32(0)
        here = plane + zero
        summed = jnp.stack(
            [lax.select_n(here, *(back[(z - source) % 4] for z in range(4))) for source in range(4)]
        )
        if parts == 1:
            summed = summed.reshape(block_count, -1, D, width).transpose(0, 2, 1, 3).reshape(block_count, D, BW)
        results = muon(summed, momentum, weights, part, parts, results)
    weight_grads, new_momentum, new_weights = results
    gain_grads = everywhere(gain_grads + zero.astype(F32))

    new_gain_first = BETA_FIRST * gain_first + (1.0 - BETA_FIRST) * gain_grads
    new_gain_second = BETA_SECOND * gain_second + (1.0 - BETA_SECOND) * gain_grads * gain_grads
    first_hat = new_gain_first / (1.0 - BETA_FIRST**STEP)
    second_hat = new_gain_second / (1.0 - BETA_SECOND**STEP)
    new_gains = gains - ADAM_RATE * first_hat / (jnp.sqrt(second_hat) + ADAM_EPS)
    return (
        output,
        input_grad,
        weight_grads,
        new_momentum,
        new_weights,
        new_gain_first,
        new_gain_second,
        new_gains,
    )


def solution(mesh):
    count = mesh.shape["dp"]
    fine = Mesh(
        np.asarray(mesh.devices).reshape(4, 4, count // 16, mesh.shape["tensor"]),
        ("z",) + PLANE,
    )
    every = ("z",) + PLANE
    in_specs = (
        P(every, None),
        P(every[:3], None),
        P(every, None, None),
        P(every, None, None),
        P(),
        P(),
        P(),
        P(every, None),
    )
    out_specs = (
        P(every, None),
        P(every, None),
        P(every, None, None),
        P(every, None, None),
        P(every, None, None),
        P(),
        P(),
        P(),
    )
    return jax.shard_map(local, mesh=fine, in_specs=in_specs, out_specs=out_specs, check_vma=False)
```
